32 devices in a mesh: replica: 2 (over x), shard: 16 (over z, y, core).
Axes of the slice: x: 2, y: 2, z: 4, core: 2. Of those that a mesh axis runs over, the one named last changes fastest.
Arguments:
- latents: bfloat16 [2, 256, 32, 640], P('replica', 'shard'), may hold values from -6 to 6
- cotangent: float32 [2, 256, 32, 640], P('replica', 'shard'), may hold values from -20.4 to 20.4
- kernel: float32 [2, 640, 5760], P('replica', 'shard'), may hold values from -4 to 4
- conv_bias: float32 [2, 640], P('replica'), may hold values from -3 to 3
- gn_gain: float32 [2, 640], P('replica'), may hold values from 0.25 to 1.75
- gn_shift: float32 [2, 640], P('replica'), may hold values from -3 to 3
- step: int32 [1], replicated, may hold values from 0 to 999
Outputs:
- block_out: bfloat16 [2, 256, 32, 640], P('replica', 'shard')
- new_kernel: float32 [2, 640, 5760], P('replica', 'shard')
- new_bias: float32 [2, 640], P('replica')
- new_gain: float32 [2, 640], P('replica')
- new_shift: float32 [2, 640], P('replica')
The draws below stay inside these ranges and needn't reach their ends.
All inputs are finite; a program needn't handle non-finite values.
Results may differ from the reference program's by a relative error of at most 0.005.
Values may be sent and summed in bfloat16 or wider, within the bound.
No kernel may reach another device: no remote copies, remote signals or barrier semaphores. Data moves between devices by JAX's collectives and lax.ppermute only.
A program may use at most 128 MiB of HBM per device.

```python
import jax
import jax.numpy as jnp
from jax import lax

C = 640
GROUPS = 32
LAT = 32
KC = 5760
PIX = 256
N_REPLICA = 2
N_SHARD = 16


def draw_cotangent(key, part):
    key = jax.random.fold_in(key, 7)
    shape = (N_REPLICA, PIX, LAT, C)
    ramp = 1.0 + 2.0 * jnp.arange(PIX, dtype=jnp.float32) / (PIX - 1)
    base = jnp.clip(jax.random.normal(key, shape, jnp.float32), -4.0, 4.0)
    return base * ramp[None, :, None, None]


def block_levels(stream_key, extent, shards, low, top_value):
    def one(axis_at, parts):
        heights = jax.random.uniform(jax.random.fold_in(jax.random.fold_in(stream_key, 6), axis_at), (parts,), jnp.float32, low / len(shards), top_value / len(shards))
        return jnp.repeat(jnp.exp(heights), extent[axis_at] // parts).reshape((-1,) + (1,) * (len(extent) - axis_at - 1))

    gain = one(*shards[0])
    for cut in shards[1:]:
        gain = gain * one(*cut)
    return gain


def normal_values(key, dims, width, bound, cuts=(), kind=jnp.bfloat16):
    array = width * jax.random.normal(key, dims, jnp.float32)
    if cuts:
        array = array * block_levels(key, dims, cuts, -0.22, 0.18)
    return jnp.clip(array, -bound, bound).astype(kind)


def setup_inputs(seed: int = 0) -> dict:
    key_of = jax.random.split(jax.random.key(seed), 8)
    latents = normal_values(key_of[0], (N_REPLICA, PIX, LAT, C), 1.0, 6.0, ((0, 2), (1, 16)))
    cotangent = draw_cotangent(jax.random.fold_in(key_of[7], 71), 0)
    kernel = normal_values(key_of[2], (N_REPLICA, C, KC), 1.0, 4.0, ((0, 2), (1, 16)), jnp.float32)
    conv_bias = normal_values(key_of[3], (N_REPLICA, C), 0.5, 3.0, ((0, 2),), jnp.float32)
    gn_gain = jnp.clip(1.0 + 0.15 * jax.random.normal(key_of[4], (N_REPLICA, C), jnp.float32), 0.25, 1.75)
    gn_shift = normal_values(key_of[5], (N_REPLICA, C), 0.5, 3.0, ((0, 2),), jnp.float32)
    step = jax.random.randint(key_of[6], (1,), 0, 1000).astype(jnp.int32)
    return dict(latents=latents, cotangent=cotangent, kernel=kernel, conv_bias=conv_bias, gn_gain=gn_gain, gn_shift=gn_shift, step=step)


eps = 1e-05
lr_kernel = 0.1
lr_vector = 0.01

def replica_pass(inputs, kernel_rate):
    latent, cotan, kernel, bias, norm_scale_vector, norm_offset_vector = inputs
    samples = PIX // LAT
    group_width = C // GROUPS
    weight_scale = (9 * C) ** (-0.5)
    row_count = samples * LAT * LAT
    latent_float = latent.astype(jnp.float32).reshape(samples, LAT, LAT, C)
    grouped = latent_float.reshape(samples, LAT * LAT, GROUPS, group_width)
    elements = LAT * LAT * group_width
    group_mean = lax.optimization_barrier(jnp.sum(grouped, axis=(1, 3))) / elements
    square = lax.optimization_barrier(jnp.sum(grouped * grouped, axis=(1, 3))) / elements
    rstd = lax.rsqrt(square - group_mean * group_mean + eps)
    channel_means = jnp.repeat(group_mean, group_width, axis=1)[:, None, None, :]
    channel_inverse_deviation = jnp.repeat(rstd, group_width, axis=1)[:, None, None, :]
    normalized_input = (latent_float - channel_means) * channel_inverse_deviation
    preactivation = norm_scale_vector * normalized_input + norm_offset_vector
    act = jax.nn.silu(preactivation).astype(jnp.bfloat16)
    padded = jnp.pad(act, ((0, 0), (1, 1), (1, 1), (0, 0)))
    patches = jnp.concatenate([padded[:, row_off:row_off + LAT, col_off:col_off + LAT].reshape(row_count, C) for row_off in range(3) for col_off in range(3)], axis=1)
    kernel_b = kernel.astype(jnp.bfloat16)
    conv_out = lax.dot_general(patches, kernel_b, (((1,), (1,)), ((), ())), preferred_element_type=jnp.float32)
    block = (weight_scale * conv_out + bias + latent_float.reshape(row_count, C)).astype(jnp.bfloat16)
    block = block.reshape(PIX, LAT, C)
    cot_b = cotan.reshape(row_count, C).astype(jnp.bfloat16)
    spread = jnp.zeros((samples, LAT + 2, LAT + 2, C), jnp.float32)
    for tap_index in range(9):
        row_off = tap_index // 3
        col_off = tap_index % 3
        contrib = jnp.dot(cot_b, kernel_b[:, tap_index * C:(tap_index + 1) * C], preferred_element_type=jnp.float32)
        spread = spread.at[:, row_off:row_off + LAT, col_off:col_off + LAT].add(contrib.reshape(samples, LAT, LAT, C))
    act_grad = weight_scale * spread[:, 1:LAT + 1, 1:LAT + 1]
    sigmoid_pre = jax.nn.sigmoid(preactivation)
    preactivation_gradient = act_grad * sigmoid_pre * (1.0 + preactivation * (1.0 - sigmoid_pre))
    scale_vector_gradient = lax.optimization_barrier(jnp.sum(preactivation_gradient * normalized_input, axis=(0, 1, 2)))
    shift_grad = lax.optimization_barrier(jnp.sum(preactivation_gradient, axis=(0, 1, 2)))
    bias_grad = lax.optimization_barrier(jnp.sum(cotan, axis=(0, 1)))
    device_rows = row_count // N_SHARD

    def add_device(running, device):
        offset = (device * device_rows).astype(jnp.int32)
        patch_block = lax.dynamic_slice_in_dim(patches, offset, device_rows, 0)
        cot_block = lax.dynamic_slice_in_dim(cot_b, offset, device_rows, 0)
        term = weight_scale * lax.dot_general(cot_block, patch_block, (((0,), (0,)), ((), ())), preferred_element_type=jnp.float32)
        rounded = lax.optimization_barrier(term.astype(jnp.bfloat16))
        return (running + rounded.astype(jnp.float32), None)
    kernel_grad, _ = lax.scan(add_device, jnp.zeros((C, 9 * C), jnp.float32), jnp.arange(N_SHARD, dtype=jnp.int32))
    return (block, kernel - kernel_rate * kernel_grad, bias - lr_vector * bias_grad, norm_scale_vector - lr_vector * scale_vector_gradient, norm_offset_vector - lr_vector * shift_grad)

def reference(latents, cotangent, kernel, conv_bias, gn_gain, gn_shift, step):
    kernel_rate = lr_kernel * (1.0 - (step[0] % 1000).astype(jnp.float32) / 2000.0)
    block, stepped_kernel, stepped_bias, stepped_gain, stepped_shift = lax.map(lambda inputs: replica_pass(inputs, kernel_rate), (latents, cotangent, kernel, conv_bias, gn_gain, gn_shift))
    levels = N_REPLICA.bit_length() - 1
    distance = jnp.left_shift(jnp.int32(1), (step[0] % levels).astype(jnp.int32))
    source = (jnp.arange(N_REPLICA, dtype=jnp.int32) - distance) % N_REPLICA

    def averaged(values):
        return 0.5 * (values + values[source])
    return (block, averaged(stepped_kernel), averaged(stepped_bias), averaged(stepped_gain), averaged(stepped_shift))
```

```python
import jax
import jax.numpy as jnp
from jax import lax
from jax.sharding import Mesh, PartitionSpec as P

GROUPS = 32
EPS = 1e-05
LR_KERNEL = 0.1
LR_VECTOR = 0.01
BF16 = jnp.bfloat16
F32 = jnp.float32


def swap_cores(value):
    return lax.ppermute(value, "core", [(0, 1), (1, 0)])


def from_behind(value, steps):
    count = lax.axis_size("replica")
    return lax.ppermute(value, "replica", [(s, (s + steps) % count) for s in range(count)])


def from_peer(level, levels, value):
    if levels == 1:
        return from_behind(value, 1)
    return lax.switch(level, [lambda v, by=1 << k: from_behind(v, by) for k in range(levels)], value)


def column_shifts(rows):
    zero = jnp.zeros_like(rows[:, :1])
    return [
        jnp.concatenate([zero, rows[:, :-1]], axis=1),
        rows,
        jnp.concatenate([rows[:, 1:], zero], axis=1),
    ]


def per_device(latents, cotangent, kernel, conv_bias, gn_gain, gn_shift, step):
    latent, cotan, shard = latents[0], cotangent[0], kernel[0]
    bias, gain, shift = conv_bias[0], gn_gain[0], gn_shift[0]
    half, width, chans = latent.shape
    own_rows, taps_in = shard.shape
    cells = half * width
    nodes = lax.axis_size("node")
    core = lax.axis_index("core")
    lower = core == 0
    scale = taps_in ** (-0.5)
    group_width = chans // GROUPS
    levels = lax.axis_size("replica").bit_length() - 1
    level = step[0] % levels
    rate = LR_KERNEL * (1.0 - (step[0] % 1000).astype(F32) / 2000.0)

    own = lax.all_gather(shard.astype(BF16), "node", axis=0, tiled=False)

    cot_b = cotan.astype(BF16)
    edges = jnp.stack([
        jnp.where(lower, latent[-1], latent[0]),
        jnp.where(lower, cot_b[-1], cot_b[0]),
    ])
    far_lat, far_cot = swap_cores(edges)
    lat = latent.astype(F32)
    flat = lat.reshape(cells, chans)
    sums = jnp.stack([jnp.sum(flat, axis=0), jnp.sum(flat * flat, axis=0)])
    sums = sums.reshape(2, GROUPS, group_width).sum(axis=2)
    sums = (sums + swap_cores(sums)) / (2 * cells * group_width)
    rstd = lax.rsqrt(sums[1] - sums[0] * sums[0] + EPS)
    mean_c = jnp.repeat(sums[0], group_width)
    rstd_c = jnp.repeat(rstd, group_width)

    def pre_of(values):
        xhat = (values - mean_c) * rstd_c
        return xhat, gain * xhat + shift

    xhat, pre = pre_of(lat)
    act = jax.nn.silu(pre).astype(BF16)
    far_act = jax.nn.silu(pre_of(far_lat.astype(F32))[1]).astype(BF16)

    def with_halo(rows, far):
        zero = jnp.zeros_like(far)
        top = jnp.where(lower, zero, far)[None]
        bottom = jnp.where(lower, far, zero)[None]
        return jnp.concatenate([top, rows, bottom], axis=0)

    act_s = column_shifts(with_halo(act, far_act))
    cot_s = column_shifts(with_halo(cot_b, far_cot))
    patches = jnp.concatenate(
        [act_s[b][a:a + half].reshape(cells, chans) for a in range(3) for b in range(3)], axis=1
    )
    cot_flat = cot_b.reshape(cells, chans)
    grad = scale * lax.dot_general(
        cot_flat, patches, (((0,), (0,)), ((), ())), preferred_element_type=F32
    )
    grad = grad.astype(BF16).reshape(nodes, 2, own_rows, taps_in)
    keep = lax.dynamic_index_in_dim(grad, core, 1, keepdims=False)
    send = lax.dynamic_index_in_dim(grad, 1 - core, 1, keepdims=False)
    pair = (keep.astype(F32) + swap_cores(send).astype(F32)).astype(BF16)

    other = swap_cores(own)
    whole = jnp.where(
        lower, jnp.stack([own, other], axis=1), jnp.stack([other, own], axis=1)
    ).reshape(chans, taps_in)

    kernel_grad = lax.psum_scatter(pair, "node", scatter_dimension=0, tiled=False).astype(F32)

    conv = lax.dot_general(patches, whole, (((1,), (1,)), ((), ())), preferred_element_type=F32)
    block = (scale * conv + bias + flat).astype(BF16)

    back = jnp.zeros((cells, chans), F32)
    for a in range(3):
        for b in range(3):
            tap = (a * 3 + b) * chans
            shifted = cot_s[2 - b][2 - a:2 - a + half].reshape(cells, chans)
            back = back + jnp.dot(shifted, whole[:, tap:tap + chans], preferred_element_type=F32)
    act_grad = (scale * back).reshape(half, width, chans)
    sig = jax.nn.sigmoid(pre)
    pre_grad = act_grad * sig * (1.0 + pre * (1.0 - sig))
    vectors = jnp.stack([
        jnp.sum(cotan, axis=(0, 1)),
        jnp.sum(pre_grad * xhat, axis=(0, 1)),
        jnp.sum(pre_grad, axis=(0, 1)),
    ])
    vectors = lax.psum(vectors, ("node", "core"))
    stepped_v = jnp.stack([bias, gain, shift]) - LR_VECTOR * vectors
    peer_v = from_peer(level, levels, stepped_v.astype(BF16)).astype(F32)
    new_v = 0.5 * (stepped_v + peer_v)

    stepped = shard - rate * kernel_grad
    peer = from_peer(level, levels, stepped.astype(BF16)).astype(F32)
    new_kernel = 0.5 * (stepped + peer)
    return (
        block.reshape(1, half, width, chans),
        new_kernel[None],
        new_v[0][None],
        new_v[1][None],
        new_v[2][None],
    )


def solution(mesh):
    replicas, shards = mesh.shape["replica"], mesh.shape["shard"]
    split = Mesh(mesh.devices.reshape(replicas, shards // 2, 2), ("replica", "node", "core"))
    shard = ("node", "core")
    return jax.shard_map(
        per_device,
        mesh=split,
        in_specs=(
            P("replica", shard, None, None),
            P("replica", shard, None, None),
            P("replica", shard, None),
            P("replica", None),
            P("replica", None),
            P("replica", None),
            P(),
        ),
        out_specs=(
            P("replica", shard, None, None),
            P("replica", shard, None),
            P("replica", None),
            P("replica", None),
            P("replica", None),
        ),
        check_vma=False,
    )
```

```python
from functools import partial

import jax
import jax.numpy as jnp
import numpy as np
from jax import lax
from jax.experimental import pallas as pl
from jax.experimental.pallas import tpu as pltpu
from jax.sharding import Mesh, PartitionSpec as P

GROUPS = 32
EPS = 1e-05
LR_KERNEL = 0.1
LR_VECTOR = 0.01
LANES = 128
BF16 = jnp.bfloat16
F32 = jnp.float32
VMEM_BYTES = 56 * 2**20

SMEM_SPEC = pl.BlockSpec(memory_space=pltpu.SMEM)
VMEM_SPEC = pl.BlockSpec(memory_space=pltpu.VMEM)
HBM_SPEC = pl.BlockSpec(memory_space=pl.ANY)


class Columns:
    def __init__(self, chans):
        tiles = 9 * chans // LANES
        self.total = 9 * chans
        self.lead = (tiles + 1) // 2 * LANES
        self.start = self.total - self.lead
        self.both = 2 * self.lead - self.total
        self.mid = self.lead - 4 * chans
        self.mid_start = chans - self.mid

    def tap(self, core, k, chans):
        tap = jnp.where(core == 0, k, 5 + k)
        return tap, pl.multiple_of(jnp.where(core == 0, k * chans, self.mid + k * chans), LANES)

    def middle(self, core, chans):
        place = jnp.where(core == 0, 4 * chans, 0)
        channel = jnp.where(core == 0, 0, self.mid_start)
        return pl.multiple_of(place, LANES), pl.multiple_of(channel, LANES)


def fill_shifts(shifts, row, values):
    width = values.shape[0]
    at = lax.broadcasted_iota(jnp.int32, values.shape, 0)
    left = jnp.where(at == 0, 0.0, pltpu.roll(values, 1, 0))
    right = jnp.where(at == width - 1, 0.0, pltpu.roll(values, width - 1, 0))
    shifts[0, row] = left.astype(BF16)
    shifts[1, row] = values.astype(BF16)
    shifts[2, row] = right.astype(BF16)


def clear_edges(shifts):
    zero = jnp.zeros(shifts.shape[2:], shifts.dtype)
    for b in range(3):
        shifts[b, 0] = zero
        shifts[b, shifts.shape[1] - 1] = zero


def grad_kernel(cols, zs, ys, info, lat_own, lat_far, cot_own, cot_far, gain, shift,
                act, stats, keep, send, acts, cot_t, grad):
    core, which, flip = info[0], info[1], info[2]
    half, width, chans = lat_own.shape
    rows = 2 * half
    cells = rows * width
    group_width = chans // GROUPS
    own_at = core * half
    far_at = half - own_at
    clear_edges(acts)

    def add_row(i, sums):
        total, square = sums
        a = lat_own[i].astype(F32)
        b = lat_far[i].astype(F32)
        return total + (a + b), square + (a * a + b * b)

    zero = jnp.zeros((width, chans), F32)
    total, square = lax.fori_loop(0, half, add_row, (zero, zero))
    sums = jnp.concatenate(
        [jnp.sum(total, axis=0, keepdims=True), jnp.sum(square, axis=0, keepdims=True),
         jnp.zeros((6, chans), F32)], axis=0
    )
    first = lax.broadcasted_iota(jnp.int32, (chans, chans), 0) // group_width
    second = lax.broadcasted_iota(jnp.int32, (chans, chans), 1) // group_width
    member = jnp.where(first == second, 1.0, 0.0)
    sums = jnp.dot(sums, member, precision=lax.Precision.HIGHEST, preferred_element_type=F32)
    sums = sums / (cells * group_width)
    mean = sums[0:1]
    rstd = lax.rsqrt(sums[1:2] - mean * mean + EPS)
    stats[0:1] = mean
    stats[1:2] = rstd
    gain_v, shift_v = gain[...], shift[...]

    def act_row(values):
        pre = gain_v * ((values.astype(F32) - mean) * rstd) + shift_v
        return pre / (1.0 + jnp.exp(-pre))

    def act_rows(i, _):
        for ref, base in ((lat_own, own_at), (lat_far, far_at)):
            value = act_row(ref[i])
            act[base + i] = value.astype(BF16)
            fill_shifts(acts, base + i + 1, value)
        return 0

    lax.fori_loop(0, half, act_rows, 0)

    chunk = LANES // width
    for ref, base in ((cot_own, own_at), (cot_far, far_at)):
        for i in range(half // chunk):
            piece = ref[i * chunk:(i + 1) * chunk].reshape(LANES, chans).astype(F32)
            place = pl.multiple_of(base * width + i * LANES, LANES)
            cot_t[:, pl.ds(place, LANES)] = piece.T.astype(BF16)

    scale = cols.total ** (-0.5)
    unit = chans // (zs * ys)
    part = unit // 2

    def emit(value, place, count):
        grad[:, :count] = value
        for z in range(zs):
            for y in range(ys):
                at = (z * ys + y) * unit
                first_half = (scale * grad[at:at + part, :count]).astype(BF16)
                second_half = (scale * grad[at + part:at + unit, :count]).astype(BF16)
                slot = info[3 + z]
                other = y ^ flip
                keep[slot, other, :, pl.ds(place, count)] = jnp.where(which == 0, first_half, second_half)
                send[slot, other, :, pl.ds(place, count)] = jnp.where(which == 0, second_half, first_half)

    def full_tap(k, _):
        tap, place = cols.tap(core, k, chans)
        window = acts[tap % 3, pl.ds(tap // 3, rows)].reshape(cells, chans)
        emit(jnp.dot(cot_t[...], window, preferred_element_type=F32), place, chans)
        return 0

    lax.fori_loop(0, 4, full_tap, 0)
    place, channel = cols.middle(core, chans)
    window = acts[1, 1:rows + 1, :, pl.ds(channel, cols.mid)].reshape(cells, cols.mid)
    emit(jnp.dot(cot_t[...], window, preferred_element_type=F32), place, cols.mid)


def load_blocks(info, blocks, whole, sems):
    copies = []
    for i, block in enumerate(blocks):
        count = block.shape[0]
        at = pl.multiple_of(info[8 + i] * count, count)
        copies.append(pltpu.make_async_copy(block, whole.at[pl.ds(at, count)], sems.at[i]))
    for copy in copies:
        copy.start()
    return copies


def split_halves(core, total, own, far):
    count = own.shape[0]
    own[...] = total[pl.ds(pl.multiple_of(core * count, count), count)]
    far[...] = total[pl.ds(pl.multiple_of((1 - core) * count, count), count)].astype(far.dtype)


def conv_kernel(cols, count, info, act, *refs):
    blocks, (own, far, whole, acts, total, sems) = refs[:count], refs[count:]
    core = info[0]
    rows, width, chans = act.shape
    cells = rows * width
    copies = load_blocks(info, blocks, whole, sems)
    clear_edges(acts)

    def shift_row(i, _):
        fill_shifts(acts, i + 1, act[i].astype(F32))
        return 0

    lax.fori_loop(0, rows, shift_row, 0)
    for copy in copies:
        copy.wait()
    nt = (((1,), (1,)), ((), ()))
    place, channel = cols.middle(core, chans)
    window = acts[1, 1:rows + 1, :, pl.ds(channel, cols.mid)].reshape(cells, cols.mid)
    lane = lax.broadcasted_iota(jnp.int32, window.shape, 1)
    window = jnp.where((core == 1) & (lane < cols.both), jnp.zeros_like(window), window)
    total[...] = lax.dot_general(window, whole[:, pl.ds(place, cols.mid)], nt, preferred_element_type=F32)

    def full_tap(k, _):
        tap, place = cols.tap(core, k, chans)
        window = acts[tap % 3, pl.ds(tap // 3, rows)].reshape(cells, chans)
        total[...] += lax.dot_general(window, whole[:, pl.ds(place, chans)], nt, preferred_element_type=F32)
        return 0

    lax.fori_loop(0, 4, full_tap, 0)
    split_halves(core, total, own, far)


def back_kernel(cols, count, info, cot_own, cot_far, *refs):
    blocks, (own, far, whole, cots, total, sems) = refs[:count], refs[count:]
    core = info[0]
    half, width, chans = cot_own.shape
    rows = 2 * half
    cells = rows * width
    copies = load_blocks(info, blocks, whole, sems)
    clear_edges(cots)

    def shift_row(i, _):
        fill_shifts(cots, core * half + i + 1, cot_own[i].astype(F32))
        fill_shifts(cots, (1 - core) * half + i + 1, cot_far[i].astype(F32))
        return 0

    lax.fori_loop(0, half, shift_row, 0)
    for copy in copies:
        copy.wait()
    total[...] = jnp.zeros_like(total)
    place, channel = cols.middle(core, chans)
    window = cots[1, 1:rows + 1].reshape(cells, chans)
    value = jnp.dot(window, whole[:, pl.ds(place, cols.mid)], preferred_element_type=F32)
    lane = lax.broadcasted_iota(jnp.int32, value.shape, 1)
    total[:, pl.ds(channel, cols.mid)] = jnp.where((core == 1) & (lane < cols.both), 0.0, value)

    def full_tap(k, _):
        tap, place = cols.tap(core, k, chans)
        window = cots[2 - tap % 3, pl.ds(2 - tap // 3, rows)].reshape(cells, chans)
        total[...] += jnp.dot(window, whole[:, pl.ds(place, chans)], preferred_element_type=F32)
        return 0

    lax.fori_loop(0, 4, full_tap, 0)
    split_halves(core, total, own, far)


def swap(value, axis):
    return lax.ppermute(value, axis, [(0, 1), (1, 0)])


def from_peer(level, value):
    count = lax.axis_size("replica")
    levels = count.bit_length() - 1
    moves = [[(s, (s + (1 << k)) % count) for s in range(count)] for k in range(levels)]
    if levels == 1:
        return lax.ppermute(value, "replica", moves[0])
    return lax.switch(level, [lambda v, m=m: lax.ppermute(v, "replica", m) for m in moves], value)


PAIRS = [(0, 1), (1, 0), (2, 3), (3, 2)]
MIDDLE = [(1, 2), (2, 1)]
INWARD = [(0, 1), (3, 2)]
OUTWARD = [(1, 0), (2, 3)]
GATHER_FROM = [[1, 2, 3], [0, 2, 3], [3, 1, 0], [2, 1, 0]]
SLOT_OF = [[3, 2, 1, 0], [2, 3, 1, 0], [0, 1, 3, 2], [0, 1, 2, 3]]


def gather_line(unit, inner):
    along = partial(lax.ppermute, axis_name="z")
    r1 = along(unit, perm=PAIRS)
    mid = along(unit, perm=MIDDLE)
    mid_far = along(r1, perm=MIDDLE)
    out = along(mid, perm=OUTWARD)
    out_far = along(mid_far, perm=OUTWARD)
    r2 = jnp.where(inner, mid, out)
    r3 = jnp.where(inner, mid_far, out_far)
    held = [unit, r1, r2, r3]
    return held + [swap(block, "y") for block in held]


def add(*values):
    total = values[0].astype(F32)
    for value in values[1:]:
        total = total + value.astype(F32)
    return total.astype(BF16)


def reduce_all(keep, send):
    slots = [add(keep[j], swap(send[j], "replica")) for j in range(4)]
    along = partial(lax.ppermute, axis_name="z")
    in1 = along(slots[0], perm=INWARD)
    mid2 = along(add(in1, slots[0]), perm=MIDDLE)
    in2 = along(slots[1], perm=INWARD)
    in3 = along(slots[2], perm=INWARD)
    mid3 = along(add(in2, slots[1]), perm=MIDDLE)
    out3 = along(add(mid2, slots[2]), perm=OUTWARD)
    line = add(slots[3], in3, mid3, out3)
    return add(line[0], swap(line[1], "y"))


def per_device(latents, cotangent, kernel, conv_bias, gn_gain, gn_shift, step):
    latent, cotan, shard = latents[0], cotangent[0], kernel[0]
    half, width, chans = latent.shape
    own_rows = shard.shape[0]
    cols = Columns(chans)
    cells = half * width
    zs, ys, replicas = lax.axis_size("z"), lax.axis_size("y"), lax.axis_size("replica")
    core, z, y, replica = (lax.axis_index(a) for a in ("core", "z", "y", "replica"))
    lower = core == 0
    paired = replicas == 2 and zs == 4 and ys == 2
    scale = cols.total ** (-0.5)
    level = step[0] % (replicas.bit_length() - 1)
    rate = LR_KERNEL * (1.0 - (step[0] % 1000).astype(F32) / 2000.0)
    params = jnp.stack([conv_bias[0], gn_gain[0], gn_shift[0]])

    kernel_b = shard.astype(BF16)
    mine = lax.dynamic_slice_in_dim(kernel_b, core * cols.start, cols.lead, 1)
    theirs = lax.dynamic_slice_in_dim(kernel_b, (1 - core) * cols.start, cols.lead, 1)
    got = swap(theirs, "core")
    unit = jnp.where(lower, jnp.concatenate([mine, got]), jnp.concatenate([got, mine]))
    cot_b = cotan.astype(BF16)
    lat_far = swap(latent, "core")
    cot_far = swap(cot_b, "core")

    if paired:
        blocks = gather_line(unit, (z == 1) | (z == 2))
        order = jnp.asarray(np.array(GATHER_FROM, np.int32))[z]
        nodes = jnp.concatenate([z[None], order]) * 2
        places = jnp.concatenate([nodes + y, nodes + 1 - y])
        slots = jnp.asarray(np.array(SLOT_OF, np.int32))[z]
        head = jnp.stack([core, replica, y, jnp.int32(0)])
        info = jnp.concatenate([head[:3], slots, head[3:], places])
    else:
        blocks = [lax.all_gather(unit, ("z", "y"), axis=0, tiled=True)]
        places = jnp.zeros((1,), jnp.int32)
        head = jnp.stack([core, jnp.int32(0), jnp.int32(0)])
        info = None
    count = len(blocks)
    if info is None:
        slots = jnp.arange(zs, dtype=jnp.int32)
        grad_info = jnp.concatenate([head, slots])
        info = jnp.concatenate([head, jnp.zeros((5,), jnp.int32), places])
    else:
        grad_info = info

    params_of = pltpu.CompilerParams(vmem_limit_bytes=VMEM_BYTES)
    flops = 2 * 2 * cells * chans * cols.lead
    pieces = jax.ShapeDtypeStruct((zs, ys, own_rows, cols.lead), BF16)
    act, stats, keep, send = pl.pallas_call(
        partial(grad_kernel, cols, zs, ys),
        out_shape=(
            jax.ShapeDtypeStruct((2 * half, width, chans), BF16),
            jax.ShapeDtypeStruct((2, chans), F32),
            pieces,
            pieces,
        ),
        in_specs=[SMEM_SPEC] + [VMEM_SPEC] * 6,
        out_specs=(VMEM_SPEC,) * 4,
        scratch_shapes=[
            pltpu.VMEM((3, 2 * half + 2, width, chans), BF16),
            pltpu.VMEM((chans, 2 * cells), BF16),
            pltpu.VMEM((chans, chans), F32),
        ],
        compiler_params=params_of,
        cost_estimate=pl.CostEstimate(flops=2 * flops, bytes_accessed=10 * 2**20, transcendentals=2 * cells * chans),
        name="act_and_kernel_grad",
    )(grad_info, latent, lat_far, cot_b, cot_far, params[1:2], params[2:3])

    if paired:
        peer_b = from_peer(level, kernel_b)
        total = reduce_all(keep, send)
        a = lax.ppermute(total, ("replica", "core"), [(1, 0), (2, 3), (0, 2), (3, 1)])
        b = lax.ppermute(total, ("replica", "core"), [(1, 2), (2, 1)])
        left = jnp.where(replica == core, jnp.where(lower, total, a), jnp.where(lower, a, b))
        right = jnp.where(replica == core, jnp.where(lower, a, total), jnp.where(lower, b, a))
    else:
        terms = jnp.stack([keep, send], axis=2).reshape(zs * ys, 2, own_rows, cols.lead)
        summed = lax.psum_scatter(terms, ("z", "y"), scatter_dimension=0, tiled=False)
        ours = lax.dynamic_index_in_dim(summed, core, 0, keepdims=False)
        got = swap(lax.dynamic_index_in_dim(summed, 1 - core, 0, keepdims=False), "core")
        left, right = jnp.where(lower, ours, got), jnp.where(lower, got, ours)
    kernel_grad = jnp.concatenate([left, right[:, cols.both:]], axis=1).astype(F32)
    if paired:
        new_kernel = 0.5 * (shard + peer_b.astype(F32)) - (0.5 * rate) * kernel_grad
    else:
        stepped = shard - rate * kernel_grad
        new_kernel = 0.5 * (stepped + from_peer(level, stepped.astype(BF16)).astype(F32))

    block_rows = blocks[0].shape[0]
    product = partial(
        pl.pallas_call,
        out_shape=(
            jax.ShapeDtypeStruct((cells, chans), F32),
            jax.ShapeDtypeStruct((cells, chans), BF16),
        ),
        out_specs=(VMEM_SPEC,) * 2,
        scratch_shapes=[
            pltpu.VMEM((chans, cols.lead), BF16),
            pltpu.VMEM((3, 2 * half + 2, width, chans), BF16),
            pltpu.VMEM((2 * cells, chans), F32),
            pltpu.SemaphoreType.DMA((count,)),
        ],
        compiler_params=params_of,
        cost_estimate=pl.CostEstimate(flops=2 * flops, bytes_accessed=8 * 2**20, transcendentals=0),
    )
    back_own, back_send = product(
        partial(back_kernel, cols, count),
        in_specs=[SMEM_SPEC] + [VMEM_SPEC] * 2 + [HBM_SPEC] * count,
        name="act_grad_part",
    )(info, cot_b, cot_far, *blocks)
    back = back_own + swap(back_send, "core").astype(F32)

    lat = latent.astype(F32).reshape(cells, chans)
    xhat = (lat - stats[0]) * stats[1]
    pre = params[1] * xhat + params[2]
    sig = jax.nn.sigmoid(pre)
    pre_grad = (scale * back) * sig * (1.0 + pre * (1.0 - sig))
    vectors = jnp.stack([
        jnp.sum(cotan, axis=(0, 1)),
        jnp.sum(pre_grad * xhat, axis=0),
        jnp.sum(pre_grad, axis=0),
    ])
    vectors = vectors + swap(vectors, "core")
    vectors = vectors + swap(vectors, "y")
    reach = 1
    while reach < zs:
        vectors = vectors + lax.ppermute(vectors, "z", [(s, s ^ reach) for s in range(zs)])
        reach *= 2
    stepped_v = params - LR_VECTOR * vectors
    new_v = 0.5 * (stepped_v + from_peer(level, stepped_v))

    conv_own, conv_send = product(
        partial(conv_kernel, cols, count),
        in_specs=[SMEM_SPEC] + [VMEM_SPEC] + [HBM_SPEC] * count,
        name="conv_part",
    )(info, act, *blocks)
    conv = conv_own + swap(conv_send, "core").astype(F32)
    block = (scale * conv + params[0] + lat).astype(BF16)
    return (
        block.reshape(1, half, width, chans),
        new_kernel[None],
        new_v[0][None],
        new_v[1][None],
        new_v[2][None],
    )


def solution(mesh):
    replicas, shards = mesh.shape["replica"], mesh.shape["shard"]
    split = Mesh(mesh.devices.reshape(replicas, shards // 4, 2, 2), ("replica", "z", "y", "core"))
    shard = ("z", "y", "core")
    return jax.shard_map(
        per_device,
        mesh=split,
        in_specs=(
            P("replica", shard, None, None),
            P("replica", shard, None, None),
            P("replica", shard, None),
            P("replica", None),
            P("replica", None),
            P("replica", None),
            P(),
        ),
        out_specs=(
            P("replica", shard, None, None),
            P("replica", shard, None),
            P("replica", None),
            P("replica", None),
            P("replica", None),
        ),
        check_vma=False,
    )
```

```python
from functools import partial

import jax
import jax.numpy as jnp
import numpy as np
from jax import lax
from jax.experimental import pallas as pl
from jax.experimental.pallas import tpu as pltpu
from jax.sharding import Mesh, PartitionSpec as P

GROUPS = 32
EPS = 1e-05
LR_KERNEL = 0.1
LR_VECTOR = 0.01
LANES = 128
BF16 = jnp.bfloat16
F32 = jnp.float32

SMEM_SPEC = pl.BlockSpec(memory_space=pltpu.SMEM)
VMEM_SPEC = pl.BlockSpec(memory_space=pltpu.VMEM)


class Columns:
    def __init__(self, chans):
        tiles = 9 * chans // LANES
        self.total = 9 * chans
        self.lead = (tiles + 1) // 2 * LANES
        self.start = self.total - self.lead
        self.both = 2 * self.lead - self.total
        self.mid = self.lead - 4 * chans
        self.mid_start = chans - self.mid

    def tap(self, core, k, chans):
        tap = jnp.where(core == 0, k, 5 + k)
        return tap, pl.multiple_of(jnp.where(core == 0, k * chans, self.mid + k * chans), LANES)

    def middle(self, core, chans):
        place = jnp.where(core == 0, 4 * chans, 0)
        channel = jnp.where(core == 0, 0, self.mid_start)
        return pl.multiple_of(place, LANES), pl.multiple_of(channel, LANES)


def fill_shifts(shifts, row, values):
    width = values.shape[0]
    at = lax.broadcasted_iota(jnp.int32, values.shape, 0)
    left = jnp.where(at == 0, 0.0, pltpu.roll(values, 1, 0))
    right = jnp.where(at == width - 1, 0.0, pltpu.roll(values, width - 1, 0))
    shifts[0, row] = left.astype(BF16)
    shifts[1, row] = values.astype(BF16)
    shifts[2, row] = right.astype(BF16)


def clear_edges(shifts):
    zero = jnp.zeros(shifts.shape[2:], shifts.dtype)
    for b in range(3):
        shifts[b, 0] = zero
        shifts[b, shifts.shape[1] - 1] = zero


def act_kernel(order, dev, table, lat_own, lat_far, cot_own, cot_far, gain, shift,
               stats, acts, cot_t, cot_f):
    me = dev[0]
    core = me % 2
    half, width, chans = lat_own.shape
    cells = 2 * half * width
    group_width = chans // GROUPS
    own_at = core * half
    far_at = half - own_at
    clear_edges(acts)

    def add_row(i, sums):
        total, square = sums
        a = lat_own[i].astype(F32)
        b = lat_far[i].astype(F32)
        return total + (a + b), square + (a * a + b * b)

    zero = jnp.zeros((width, chans), F32)
    total, square = lax.fori_loop(0, half, add_row, (zero, zero))
    sums = jnp.concatenate(
        [jnp.sum(total, axis=0, keepdims=True), jnp.sum(square, axis=0, keepdims=True),
         jnp.zeros((6, chans), F32)], axis=0
    )
    first = lax.broadcasted_iota(jnp.int32, (chans, LANES), 0)
    start = lax.broadcasted_iota(jnp.int32, (chans, LANES), 1) * group_width
    member = jnp.where((first >= start) & (first < start + group_width), 1.0, 0.0)
    exact = partial(lax.dot_general, precision=lax.Precision.HIGHEST, preferred_element_type=F32)
    sums = exact(sums, member, (((1,), (0,)), ((), ()))) / (cells * group_width)
    sums = exact(sums, member, (((1,), (1,)), ((), ())))
    mean = sums[0:1]
    rstd = lax.rsqrt(sums[1:2] - mean * mean + EPS)
    stats[0:1] = mean
    stats[1:2] = rstd
    gain_v, shift_v = gain[...], shift[...]

    def act_rows(i, _):
        for ref, base in ((lat_own, own_at), (lat_far, far_at)):
            pre = gain_v * ((ref[i].astype(F32) - mean) * rstd) + shift_v
            fill_shifts(acts, base + i + 1, pre * (0.5 + 0.5 * jnp.tanh(0.5 * pre)))
        return 0

    lax.fori_loop(0, half, act_rows, 0)

    chunk = LANES // width
    for ref, base in ((cot_own, own_at), (cot_far, far_at)):
        for i in range(half // chunk):
            piece = ref[i * chunk:(i + 1) * chunk].reshape(LANES, chans).astype(F32)
            place = pl.multiple_of(base * width + i * LANES, LANES)
            if order is None:
                cot_t[:, pl.ds(place, LANES)] = piece.T.astype(BF16)
            else:
                cot_f[:, pl.ds(place, LANES)] = piece.T
    if order is not None:
        first_at, part, count = order
        for q in range(count // 2):
            pair = [
                cot_f[pl.ds(pl.multiple_of(table[me, first_at + 2 * q + i], 8), part)]
                for i in range(2)
            ]
            cot_t[2 * q * part:(2 * q + 2) * part] = jnp.concatenate(pair).astype(BF16)


def grad_kernel(cols, dev, acts, cot_t, *pieces):
    core = dev[0] % 2
    rows, width, chans = acts.shape[1] - 2, acts.shape[2], acts.shape[3]
    cells = rows * width
    count = pieces[0].shape[0]

    def emit(window, place, wide):
        value = jnp.dot(cot_t[...], window, preferred_element_type=F32)
        for q, piece in enumerate(pieces):
            piece[:, pl.ds(place, wide)] = value[q * count:(q + 1) * count].astype(BF16)

    def full_tap(k, _):
        tap, place = cols.tap(core, k, chans)
        emit(acts[tap % 3, pl.ds(tap // 3, rows)].reshape(cells, chans), place, chans)
        return 0

    lax.fori_loop(0, 4, full_tap, 0)
    place, channel = cols.middle(core, chans)
    emit(acts[1, 1:rows + 1, :, pl.ds(channel, cols.mid)].reshape(cells, cols.mid), place, cols.mid)


def slope_kernel(dev, stats, gain, shift, lat_own, lat_far, cot_own, cot_far, cots, slope, slope_x):
    core = dev[0] % 2
    half = lat_own.shape[0]
    clear_edges(cots)
    mean, rstd = stats[0:1], stats[1:2]
    gain_v, shift_v = gain[...], shift[...]

    def one_row(i, _):
        for lat, cot, base in ((lat_own, cot_own, core * half), (lat_far, cot_far, half - core * half)):
            fill_shifts(cots, base + i + 1, cot[i].astype(F32))
            xhat = (lat[i].astype(F32) - mean) * rstd
            pre = gain_v * xhat + shift_v
            sig = 0.5 + 0.5 * jnp.tanh(0.5 * pre)
            value = sig * (1.0 + pre * (1.0 - sig))
            slope[base + i] = value.astype(BF16)
            slope_x[base + i] = (value * xhat).astype(BF16)
        return 0

    lax.fori_loop(0, half, one_row, 0)


def place_blocks(first_at, me, table, blocks, whole):
    for i, block in enumerate(blocks):
        count = block.shape[0]
        at = pl.multiple_of(table[me, first_at + i] * count, count)
        whole[pl.ds(at, count)] = block[...]


def conv_kernel(cols, first_at, count, dev, table, acts, *refs):
    blocks, (own, far, whole, total) = refs[:count], refs[count:]
    me = dev[0]
    core = me % 2
    rows, width, chans = acts.shape[1] - 2, acts.shape[2], acts.shape[3]
    cells = rows * width
    place_blocks(first_at, me, table, blocks, whole)
    nt = (((1,), (1,)), ((), ()))
    place, channel = cols.middle(core, chans)
    window = acts[1, 1:rows + 1, :, pl.ds(channel, cols.mid)].reshape(cells, cols.mid)
    lane = lax.broadcasted_iota(jnp.int32, window.shape, 1)
    window = jnp.where((core == 1) & (lane < cols.both), jnp.zeros_like(window), window)
    total[...] = lax.dot_general(window, whole[:, pl.ds(place, cols.mid)], nt, preferred_element_type=F32)

    def full_tap(k, _):
        tap, place = cols.tap(core, k, chans)
        window = acts[tap % 3, pl.ds(tap // 3, rows)].reshape(cells, chans)
        total[...] += lax.dot_general(window, whole[:, pl.ds(place, chans)], nt, preferred_element_type=F32)
        return 0

    lax.fori_loop(0, 4, full_tap, 0)
    half = cells // 2
    own[...] = total[pl.ds(pl.multiple_of(core * half, half), half)]
    far[...] = total[pl.ds(pl.multiple_of((1 - core) * half, half), half)].astype(BF16)


def back_kernel(cols, first_at, count, dev, table, cots, slope, slope_x, *refs):
    blocks, (sums, whole, total) = refs[:count], refs[count:]
    me = dev[0]
    core = me % 2
    rows, width, chans = slope.shape
    cells = rows * width
    place_blocks(first_at, me, table, blocks, whole)
    total[...] = jnp.zeros_like(total)
    place, channel = cols.middle(core, chans)
    window = cots[1, 1:rows + 1].reshape(cells, chans)
    value = jnp.dot(window, whole[:, pl.ds(place, cols.mid)], preferred_element_type=F32)
    lane = lax.broadcasted_iota(jnp.int32, value.shape, 1)
    total[:, pl.ds(channel, cols.mid)] = jnp.where((core == 1) & (lane < cols.both), 0.0, value)

    def full_tap(k, _):
        tap, place = cols.tap(core, k, chans)
        window = cots[2 - tap % 3, pl.ds(2 - tap // 3, rows)].reshape(cells, chans)
        total[...] += jnp.dot(window, whole[:, pl.ds(place, chans)], preferred_element_type=F32)
        return 0

    lax.fori_loop(0, 4, full_tap, 0)

    def add_row(i, carry):
        gains, shifts = carry
        value = total[pl.ds(pl.multiple_of(i * width, width), width)]
        return gains + value * slope_x[i].astype(F32), shifts + value * slope[i].astype(F32)

    zero = jnp.zeros((width, chans), F32)
    gains, shifts = lax.fori_loop(0, rows, add_row, (zero, zero))
    scale = cols.total ** (-0.5)
    sums[0:1] = scale * jnp.sum(gains, axis=0, keepdims=True)
    sums[1:2] = scale * jnp.sum(shifts, axis=0, keepdims=True)


NODE = ("z", "y")


def swap(value, axis):
    return lax.ppermute(value, axis, [(0, 1), (1, 0)])


def from_peer(level, value):
    count = lax.axis_size("replica")
    levels = count.bit_length() - 1
    moves = [[(s, (s + (1 << k)) % count) for s in range(count)] for k in range(levels)]
    if levels == 1:
        return lax.ppermute(value, "replica", moves[0])
    return lax.switch(level, [lambda v, m=m: lax.ppermute(v, "replica", m) for m in moves], value)


class Ring:
    def __init__(self, zs):
        self.count = 2 * zs
        self.reach = zs
        self.nodes = [2 * z for z in range(zs)] + [2 * z + 1 for z in reversed(range(zs))]
        ahead = list(zip(self.nodes, self.nodes[1:] + self.nodes[:1]))
        self.ahead = ahead
        self.behind = [(b, a) for a, b in ahead]

    def node(self, at, offset):
        return self.nodes[(at + offset) % self.count]

    def up(self, value):
        return lax.ppermute(value, NODE, self.ahead)

    def down(self, value):
        return lax.ppermute(value, NODE, self.behind)

    def table(self, part):
        rows = np.zeros((2, self.count, 2, 3 * self.count), np.int32)
        for replica in range(2):
            for at, node in enumerate(self.nodes):
                line = [node]
                for k in range(1, self.reach + 1):
                    line.append(self.node(at, -k))
                    if k < self.reach:
                        line.append(self.node(at, k))
                for j in range(self.reach):
                    targets = [self.node(at, self.reach - j), self.node(at, j + 1 - self.reach)]
                    for which in (replica, 1 - replica):
                        line += [(2 * target + which) * part for target in targets]
                rows[replica, node, :] = line
        return rows.reshape(-1, 3 * self.count)


def add(*values):
    total = values[0].astype(F32)
    for value in values[1:]:
        total = total + value.astype(F32)
    return total.astype(BF16)


def tied(*values):
    return lax.optimization_barrier(values)


def per_device(latents, cotangent, kernel, conv_bias, gn_gain, gn_shift, step):
    latent, cotan, shard = latents[0], cotangent[0], kernel[0]
    half, width, chans = latent.shape
    part = shard.shape[0]
    cols = Columns(chans)
    cells = half * width
    zs, replicas = lax.axis_size("z"), lax.axis_size("replica")
    core, z, y, replica = (lax.axis_index(a) for a in ("core", "z", "y", "replica"))
    lower = core == 0
    paired = replicas == 2
    ring = Ring(zs)
    scale = cols.total ** (-0.5)
    level = step[0] % (replicas.bit_length() - 1)
    rate = LR_KERNEL * (1.0 - (step[0] % 1000).astype(F32) / 2000.0)
    dev = (((replica * zs + z) * 2 + y) * 2 + core).reshape(1)

    kernel_b = shard.astype(BF16)
    mine = lax.dynamic_slice_in_dim(kernel_b, core * cols.start, cols.lead, 1)
    theirs = lax.dynamic_slice_in_dim(kernel_b, (1 - core) * cols.start, cols.lead, 1)
    got = swap(theirs, "core")
    unit = jnp.where(lower, jnp.concatenate([mine, got]), jnp.concatenate([got, mine]))
    lat_far = swap(latent, "core")
    cot_b = cotan.astype(BF16)
    cot_far = swap(cot_b, "core")

    if paired:
        table = jnp.asarray(ring.table(part))
        order = (ring.count, part, 2 * ring.count)
        up1, down1 = ring.up(unit), ring.down(unit)
        peer_b = from_peer(level, kernel_b)
    else:
        table = jnp.zeros((replicas * zs * 4, 1), jnp.int32)
        order = None

    def call(body, outs, ins, scratch, megabytes, flops, extra=0):
        return pl.pallas_call(
            body,
            out_shape=outs,
            in_specs=ins,
            out_specs=jax.tree.map(lambda _: VMEM_SPEC, outs),
            scratch_shapes=scratch,
            compiler_params=pltpu.CompilerParams(vmem_limit_bytes=megabytes * 2**20),
            cost_estimate=pl.CostEstimate(flops=flops, bytes_accessed=8 * 2**20, transcendentals=extra),
        )

    image = (2 * half, width, chans)
    shifted = jax.ShapeDtypeStruct((3, 2 * half + 2, width, chans), BF16)
    flops = 2 * 2 * cells * chans * cols.lead
    stats, acts, cot_t = call(
        partial(act_kernel, order),
        (jax.ShapeDtypeStruct((2, chans), F32), shifted, jax.ShapeDtypeStruct((chans, 2 * cells), BF16)),
        [SMEM_SPEC] * 2 + [VMEM_SPEC] * 6,
        [pltpu.VMEM((chans, 2 * cells), F32)],
        24, flops, 2 * cells * chans,
    )(dev, table, latent, lat_far, cot_b, cot_far, gn_gain, gn_shift)
    if paired:
        up1, down1, acts = tied(up1, down1, acts)
        up2, down2 = ring.up(up1), ring.down(down1)

    pieces = call(
        partial(grad_kernel, cols),
        [jax.ShapeDtypeStruct((2 * part, cols.lead), BF16)] * (2 * zs),
        [SMEM_SPEC] + [VMEM_SPEC] * 2,
        [],
        24, 2 * flops,
    )(dev, acts, cot_t)
    cots, slope, slope_x = call(
        slope_kernel,
        (shifted, jax.ShapeDtypeStruct(image, BF16), jax.ShapeDtypeStruct(image, BF16)),
        [SMEM_SPEC] + [VMEM_SPEC] * 7,
        [],
        24, flops, 2 * cells * chans,
    )(dev, stats, gn_gain, gn_shift, latent, lat_far, cot_b, cot_far)

    if paired:
        blocks = [unit, up1, down1, up2, down2]
        ups, downs = [up1, up2], [down1, down2]
        for k in range(3, zs + 1):
            ups.append(ring.up(ups[-1]))
            blocks.append(ups[-1])
            if k < zs:
                downs.append(ring.down(downs[-1]))
                blocks.append(downs[-1])
        slots = [add(pieces[2 * j], swap(pieces[2 * j + 1], "replica")) for j in range(zs)]
        up_sum = down_sum = None
        for j in range(zs):
            ahead, behind = slots[j][:part], slots[j][part:]
            if j > 0:
                ahead, behind = add(ahead, up_sum), add(behind, down_sum)
            up_sum = ring.up(ahead)
            if j < zs - 1:
                down_sum = ring.down(behind)
        total = add(behind, up_sum)
        a = lax.ppermute(total, ("replica", "core"), [(1, 0), (2, 3), (0, 2), (3, 1)])
        b = lax.ppermute(total, ("replica", "core"), [(1, 2), (2, 1)])
        left = jnp.where(replica == core, jnp.where(lower, total, a), jnp.where(lower, a, b))
        right = jnp.where(replica == core, jnp.where(lower, a, total), jnp.where(lower, b, a))
    else:
        blocks = [lax.all_gather(unit, NODE, axis=0, tiled=True)]
        terms = jnp.concatenate(pieces).reshape(2 * zs, 2, part, cols.lead)
        summed = lax.psum_scatter(terms, NODE, scatter_dimension=0, tiled=False)
        ours = lax.dynamic_index_in_dim(summed, core, 0, keepdims=False)
        got = swap(lax.dynamic_index_in_dim(summed, 1 - core, 0, keepdims=False), "core")
        left, right = jnp.where(lower, ours, got), jnp.where(lower, got, ours)
    kernel_grad = jnp.concatenate([left, right[:, cols.both:]], axis=1).astype(F32)
    if paired:
        new_kernel = 0.5 * (shard + peer_b.astype(F32)) - (0.5 * scale * rate) * kernel_grad
    else:
        stepped = shard - (scale * rate) * kernel_grad
        new_kernel = 0.5 * (stepped + from_peer(level, stepped.astype(BF16)).astype(F32))

    count = len(blocks)
    whole = pltpu.VMEM((chans, cols.lead), BF16)
    total_f = pltpu.VMEM((2 * cells, chans), F32)
    sums = call(
        partial(back_kernel, cols, 0, count),
        jax.ShapeDtypeStruct((2, chans), F32),
        [SMEM_SPEC] * 2 + [VMEM_SPEC] * (3 + count),
        [whole, total_f],
        24, 2 * flops,
    )(dev, table, cots, slope, slope_x, *blocks)
    conv_own, conv_send = call(
        partial(conv_kernel, cols, 0, count),
        (jax.ShapeDtypeStruct((cells, chans), F32), jax.ShapeDtypeStruct((cells, chans), BF16)),
        [SMEM_SPEC] * 2 + [VMEM_SPEC] * (1 + count),
        [whole, total_f],
        24, 2 * flops,
    )(dev, table, acts, *blocks)

    vectors = jnp.concatenate([jnp.sum(cotan, axis=(0, 1))[None], sums])
    vectors = vectors + swap(vectors, "core")
    vectors = vectors + swap(vectors, "y")
    reach = 1
    while reach < zs:
        vectors = vectors + lax.ppermute(vectors, "z", [(s, s ^ reach) for s in range(zs)])
        reach *= 2
    stepped_v = jnp.concatenate([conv_bias, gn_gain, gn_shift]) - LR_VECTOR * vectors
    new_v = 0.5 * (stepped_v + from_peer(level, stepped_v))

    conv = conv_own + swap(conv_send, "core").astype(F32)
    block = (scale * conv + conv_bias + latent.astype(F32).reshape(cells, chans)).astype(BF16)
    return (
        block.reshape(1, half, width, chans),
        new_kernel[None],
        new_v[0][None],
        new_v[1][None],
        new_v[2][None],
    )


def solution(mesh):
    replicas, shards = mesh.shape["replica"], mesh.shape["shard"]
    split = Mesh(mesh.devices.reshape(replicas, shards // 4, 2, 2), ("replica", "z", "y", "core"))
    shard = ("z", "y", "core")
    return jax.shard_map(
        per_device,
        mesh=split,
        in_specs=(
            P("replica", shard, None, None),
            P("replica", shard, None, None),
            P("replica", shard, None),
            P("replica", None),
            P("replica", None),
            P("replica", None),
            P(),
        ),
        out_specs=(
            P("replica", shard, None, None),
            P("replica", shard, None),
            P("replica", None),
            P("replica", None),
            P("replica", None),
        ),
        check_vma=False,
    )
```

```python
from functools import partial

import jax
import jax.numpy as jnp
import numpy as np
from jax import lax
from jax.experimental import pallas as pl
from jax.experimental.pallas import tpu as pltpu
from jax.sharding import Mesh, PartitionSpec as P

GROUPS = 32
EPS = 1e-05
LR_KERNEL = 0.1
LR_VECTOR = 0.01
LANES = 128
BF16 = jnp.bfloat16
F32 = jnp.float32

SMEM_SPEC = pl.BlockSpec(memory_space=pltpu.SMEM)
VMEM_SPEC = pl.BlockSpec(memory_space=pltpu.VMEM)


class Columns:
    def __init__(self, chans):
        tiles = 9 * chans // LANES
        self.total = 9 * chans
        self.lead = (tiles + 1) // 2 * LANES
        self.start = self.total - self.lead
        self.both = 2 * self.lead - self.total
        self.mid = self.lead - 4 * chans
        self.mid_start = chans - self.mid

    def pair(self, core, k, chans):
        first = jnp.where(core == 0, 2 * k, 5 + 2 * k)
        place = jnp.where(core == 0, 2 * k * chans, self.mid + 2 * k * chans)
        return (first, first + 1), pl.multiple_of(place, LANES)

    def middle(self, core, chans):
        place = jnp.where(core == 0, 4 * chans, 0)
        channel = jnp.where(core == 0, 0, self.mid_start)
        return pl.multiple_of(place, LANES), pl.multiple_of(channel, LANES)


def fill_shifts(shifts, row, values):
    width = values.shape[0]
    at = lax.broadcasted_iota(jnp.int32, values.shape, 0)
    left = jnp.where(at == 0, 0.0, pltpu.roll(values, 1, 0))
    right = jnp.where(at == width - 1, 0.0, pltpu.roll(values, width - 1, 0))
    shifts[0, row] = left.astype(BF16)
    shifts[1, row] = values.astype(BF16)
    shifts[2, row] = right.astype(BF16)


def clear_edges(shifts):
    zero = jnp.zeros(shifts.shape[2:], shifts.dtype)
    for b in range(3):
        shifts[b, 0] = zero
        shifts[b, shifts.shape[1] - 1] = zero


def act_kernel(order, dev, table, lat_own, lat_far, cot_own, cot_far, gain, shift,
               stats, acts, cot_t, cot_f):
    me = dev[0]
    core = me % 2
    half, width, chans = lat_own.shape
    cells = 2 * half * width
    group_width = chans // GROUPS
    own_at = core * half
    far_at = half - own_at
    clear_edges(acts)

    def add_row(i, sums):
        total, square = sums
        a = lat_own[i].astype(F32)
        b = lat_far[i].astype(F32)
        return total + (a + b), square + (a * a + b * b)

    zero = jnp.zeros((width, chans), F32)
    total, square = lax.fori_loop(0, half, add_row, (zero, zero))
    sums = jnp.concatenate(
        [jnp.sum(total, axis=0, keepdims=True), jnp.sum(square, axis=0, keepdims=True),
         jnp.zeros((6, chans), F32)], axis=0
    )
    first = lax.broadcasted_iota(jnp.int32, (chans, LANES), 0)
    start = lax.broadcasted_iota(jnp.int32, (chans, LANES), 1) * group_width
    member = jnp.where((first >= start) & (first < start + group_width), 1.0, 0.0)
    exact = partial(lax.dot_general, precision=lax.Precision.HIGHEST, preferred_element_type=F32)
    sums = exact(sums, member, (((1,), (0,)), ((), ()))) / (cells * group_width)
    sums = exact(sums, member, (((1,), (1,)), ((), ())))
    mean = sums[0:1]
    rstd = lax.rsqrt(sums[1:2] - mean * mean + EPS)
    stats[0:1] = mean
    stats[1:2] = rstd
    gain_v, shift_v = gain[...], shift[...]

    def act_rows(i, _):
        for ref, base in ((lat_own, own_at), (lat_far, far_at)):
            pre = gain_v * ((ref[i].astype(F32) - mean) * rstd) + shift_v
            fill_shifts(acts, base + i + 1, pre * (0.5 + 0.5 * jnp.tanh(0.5 * pre)))
        return 0

    lax.fori_loop(0, half, act_rows, 0)

    chunk = LANES // width
    for ref, base in ((cot_own, own_at), (cot_far, far_at)):
        for i in range(half // chunk):
            piece = ref[i * chunk:(i + 1) * chunk].reshape(LANES, chans).astype(F32)
            place = pl.multiple_of(base * width + i * LANES, LANES)
            if order is None:
                cot_t[:, pl.ds(place, LANES)] = piece.T.astype(BF16)
            else:
                cot_f[:, pl.ds(place, LANES)] = piece.T
    if order is not None:
        first_at, part, count = order
        for q in range(count // 2):
            pair = [
                cot_f[pl.ds(pl.multiple_of(table[me, first_at + 2 * q + i], 8), part)]
                for i in range(2)
            ]
            cot_t[2 * q * part:(2 * q + 2) * part] = jnp.concatenate(pair).astype(BF16)


def grad_kernel(cols, dev, acts, cot_t, *pieces):
    core = dev[0] % 2
    rows, width, chans = acts.shape[1] - 2, acts.shape[2], acts.shape[3]
    cells = rows * width
    count = pieces[0].shape[0]

    def emit(window, place, wide):
        value = jnp.dot(cot_t[...], window, preferred_element_type=F32)
        for q, piece in enumerate(pieces):
            piece[:, pl.ds(place, wide)] = value[q * count:(q + 1) * count].astype(BF16)

    def two_taps(k, _):
        taps, place = cols.pair(core, k, chans)
        windows = [acts[t % 3, pl.ds(t // 3, rows)].reshape(cells, chans) for t in taps]
        emit(jnp.concatenate(windows, axis=1), place, 2 * chans)
        return 0

    lax.fori_loop(0, 2, two_taps, 0)
    place, channel = cols.middle(core, chans)
    emit(acts[1, 1:rows + 1, :, pl.ds(channel, cols.mid)].reshape(cells, cols.mid), place, cols.mid)


def slope_kernel(dev, stats, gain, shift, lat_own, lat_far, cot_own, cot_far, cots, slope, slope_x):
    core = dev[0] % 2
    half = lat_own.shape[0]
    clear_edges(cots)
    mean, rstd = stats[0:1], stats[1:2]
    gain_v, shift_v = gain[...], shift[...]

    def one_row(i, _):
        for lat, cot, base in ((lat_own, cot_own, core * half), (lat_far, cot_far, half - core * half)):
            fill_shifts(cots, base + i + 1, cot[i].astype(F32))
            xhat = (lat[i].astype(F32) - mean) * rstd
            pre = gain_v * xhat + shift_v
            sig = 0.5 + 0.5 * jnp.tanh(0.5 * pre)
            value = sig * (1.0 + pre * (1.0 - sig))
            slope[base + i] = value.astype(BF16)
            slope_x[base + i] = (value * xhat).astype(BF16)
        return 0

    lax.fori_loop(0, half, one_row, 0)


def place_kernel(dev, table, *refs):
    blocks, whole = refs[:-1], refs[-1]
    for i, block in enumerate(blocks):
        count = block.shape[0]
        at = pl.multiple_of(table[dev[0], i] * count, count)
        whole[pl.ds(at, count)] = block[...]


def conv_sum(cols, core, first, half, acts, whole, total):
    width, chans = acts.shape[2:]
    cells = half * width
    nt = (((1,), (1,)), ((), ()))
    place, channel = cols.middle(core, chans)
    window = acts[1, pl.ds(first + 1, half), :, pl.ds(channel, cols.mid)].reshape(cells, cols.mid)
    lane = lax.broadcasted_iota(jnp.int32, window.shape, 1)
    window = jnp.where((core == 1) & (lane < cols.both), jnp.zeros_like(window), window)
    total[...] = lax.dot_general(window, whole[:, pl.ds(place, cols.mid)], nt, preferred_element_type=F32)

    def two_taps(k, _):
        taps, place = cols.pair(core, k, chans)
        windows = [acts[t % 3, pl.ds(first + t // 3, half)].reshape(cells, chans) for t in taps]
        total[...] += lax.dot_general(
            jnp.concatenate(windows, axis=1), whole[:, pl.ds(place, 2 * chans)], nt, preferred_element_type=F32
        )
        return 0

    lax.fori_loop(0, 2, two_taps, 0)


def conv_far_kernel(cols, dev, acts, whole, far, total):
    core = dev[0] % 2
    half = (acts.shape[1] - 2) // 2
    conv_sum(cols, core, (1 - core) * half, half, acts, whole, total)
    far[...] = total[...].astype(BF16)


def conv_own_kernel(cols, dev, acts, whole, got, latent, bias, block, total):
    core = dev[0] % 2
    half, width, chans = latent.shape
    conv_sum(cols, core, core * half, half, acts, whole, total)
    scale = cols.total ** (-0.5)
    conv = scale * (total[...] + got[...].astype(F32)) + bias[...]
    block[...] = (conv.reshape(half, width, chans) + latent[...].astype(F32)).astype(BF16)


def back_kernel(cols, dev, cots, slope, slope_x, whole, sums, total):
    core = dev[0] % 2
    rows, width, chans = slope.shape
    cells = rows * width
    total[...] = jnp.zeros_like(total)
    place, channel = cols.middle(core, chans)
    window = cots[1, 1:rows + 1].reshape(cells, chans)
    value = jnp.dot(window, whole[:, pl.ds(place, cols.mid)], preferred_element_type=F32)
    lane = lax.broadcasted_iota(jnp.int32, value.shape, 1)
    total[:, pl.ds(channel, cols.mid)] = jnp.where((core == 1) & (lane < cols.both), 0.0, value)

    def two_taps(k, _):
        taps, place = cols.pair(core, k, chans)
        windows = [cots[2 - t % 3, pl.ds(2 - t // 3, rows)].reshape(cells, chans) for t in taps]
        second = pl.multiple_of(place + chans, LANES)
        kernels = [whole[:, pl.ds(place, chans)], whole[:, pl.ds(second, chans)]]
        total[...] += jnp.dot(
            jnp.concatenate(windows, axis=1), jnp.concatenate(kernels, axis=0), preferred_element_type=F32
        )
        return 0

    lax.fori_loop(0, 2, two_taps, 0)

    def add_row(i, carry):
        gains, shifts = carry
        value = total[pl.ds(pl.multiple_of(i * width, width), width)]
        return gains + value * slope_x[i].astype(F32), shifts + value * slope[i].astype(F32)

    zero = jnp.zeros((width, chans), F32)
    gains, shifts = lax.fori_loop(0, rows, add_row, (zero, zero))
    scale = cols.total ** (-0.5)
    sums[0:1] = scale * jnp.sum(gains, axis=0, keepdims=True)
    sums[1:2] = scale * jnp.sum(shifts, axis=0, keepdims=True)


NODE = ("z", "y")


def swap(value, axis):
    return lax.ppermute(value, axis, [(0, 1), (1, 0)])


def from_peer(level, value):
    count = lax.axis_size("replica")
    levels = count.bit_length() - 1
    moves = [[(s, (s + (1 << k)) % count) for s in range(count)] for k in range(levels)]
    if levels == 1:
        return lax.ppermute(value, "replica", moves[0])
    return lax.switch(level, [lambda v, m=m: lax.ppermute(v, "replica", m) for m in moves], value)


class Ring:
    def __init__(self, zs):
        self.count = 2 * zs
        self.reach = zs
        self.nodes = [2 * z for z in range(zs)] + [2 * z + 1 for z in reversed(range(zs))]
        ahead = list(zip(self.nodes, self.nodes[1:] + self.nodes[:1]))
        self.ahead = ahead
        self.behind = [(b, a) for a, b in ahead]

    def node(self, at, offset):
        return self.nodes[(at + offset) % self.count]

    def up(self, value):
        return lax.ppermute(value, NODE, self.ahead)

    def down(self, value):
        return lax.ppermute(value, NODE, self.behind)

    def table(self, part):
        rows = np.zeros((2, self.count, 2, 3 * self.count), np.int32)
        for replica in range(2):
            for at, node in enumerate(self.nodes):
                line = [node]
                for k in range(1, self.reach + 1):
                    line.append(self.node(at, -k))
                    if k < self.reach:
                        line.append(self.node(at, k))
                for j in range(self.reach):
                    targets = [self.node(at, self.reach - j), self.node(at, j + 1 - self.reach)]
                    for which in (replica, 1 - replica):
                        line += [(2 * target + which) * part for target in targets]
                rows[replica, node, :] = line
        return rows.reshape(-1, 3 * self.count)


def add(*values):
    total = values[0].astype(F32)
    for value in values[1:]:
        total = total + value.astype(F32)
    return total.astype(BF16)


def tied(*values):
    return lax.optimization_barrier(values)


def per_device(latents, cotangent, kernel, conv_bias, gn_gain, gn_shift, step):
    latent, cotan, shard = latents[0], cotangent[0], kernel[0]
    half, width, chans = latent.shape
    part = shard.shape[0]
    cols = Columns(chans)
    cells = half * width
    zs, replicas = lax.axis_size("z"), lax.axis_size("replica")
    core, z, y, replica = (lax.axis_index(a) for a in ("core", "z", "y", "replica"))
    lower = core == 0
    paired = replicas == 2
    ring = Ring(zs)
    scale = cols.total ** (-0.5)
    level = step[0] % (replicas.bit_length() - 1)
    rate = LR_KERNEL * (1.0 - (step[0] % 1000).astype(F32) / 2000.0)
    dev = (((replica * zs + z) * 2 + y) * 2 + core).reshape(1)

    mine = lax.dynamic_slice_in_dim(shard, core * cols.start, cols.lead, 1).astype(BF16)
    theirs = lax.dynamic_slice_in_dim(shard, (1 - core) * cols.start, cols.lead, 1).astype(BF16)
    got = swap(theirs, "core")
    unit = jnp.where(lower, jnp.concatenate([mine, got]), jnp.concatenate([got, mine]))
    lat_far = swap(latent, "core")
    cot_b = cotan.astype(BF16)
    cot_far = swap(cot_b, "core")

    if paired:
        table = jnp.asarray(ring.table(part))
        order = (ring.count, part, 2 * ring.count)
        up1, down1 = ring.up(unit), ring.down(unit)
    else:
        table = jnp.zeros((replicas * zs * 4, 1), jnp.int32)
        order = None

    def call(body, outs, ins, scratch, megabytes, flops):
        return pl.pallas_call(
            body,
            out_shape=outs,
            in_specs=ins,
            out_specs=jax.tree.map(lambda _: VMEM_SPEC, outs),
            scratch_shapes=scratch,
            compiler_params=pltpu.CompilerParams(vmem_limit_bytes=megabytes * 2**20),
            cost_estimate=pl.CostEstimate(flops=flops, bytes_accessed=0, transcendentals=0),
        )

    image = (2 * half, width, chans)
    shifted = jax.ShapeDtypeStruct((3, 2 * half + 2, width, chans), BF16)
    flops = 2 * 2 * cells * chans * cols.lead
    stats, acts, cot_t = call(
        partial(act_kernel, order),
        (jax.ShapeDtypeStruct((2, chans), F32), shifted, jax.ShapeDtypeStruct((chans, 2 * cells), BF16)),
        [SMEM_SPEC] * 2 + [VMEM_SPEC] * 6,
        [pltpu.VMEM((chans, 2 * cells), F32)],
        24, flops // 4,
    )(dev, table, latent, lat_far, cot_b, cot_far, gn_gain, gn_shift)
    pieces = call(
        partial(grad_kernel, cols),
        [jax.ShapeDtypeStruct((2 * part, cols.lead), BF16)] * (2 * zs),
        [SMEM_SPEC] + [VMEM_SPEC] * 2,
        [],
        24, flops // 2,
    )(dev, acts, cot_t)
    def slopes_of(stats):
        return call(
            slope_kernel,
            (shifted, jax.ShapeDtypeStruct(image, BF16), jax.ShapeDtypeStruct(image, BF16)),
            [SMEM_SPEC] + [VMEM_SPEC] * 7,
            [],
            24, flops // 4,
        )(dev, stats, gn_gain, gn_shift, latent, lat_far, cot_b, cot_far)

    def back_of(blocks, slopes):
        whole = call(
            place_kernel, jax.ShapeDtypeStruct((chans, cols.lead), BF16),
            [SMEM_SPEC] * 2 + [VMEM_SPEC] * len(blocks), [], 16, flops // 16,
        )(dev, table, *blocks)
        return whole, call(
            partial(back_kernel, cols), jax.ShapeDtypeStruct((2, chans), F32),
            [SMEM_SPEC] + [VMEM_SPEC] * 4, [pltpu.VMEM((2 * cells, chans), F32)], 24, flops // 2,
        )(dev, *slopes, whole)

    half_sum = [pltpu.VMEM((cells, chans), F32)]

    def conv_far(whole):
        return call(
            partial(conv_far_kernel, cols), jax.ShapeDtypeStruct((cells, chans), BF16),
            [SMEM_SPEC] + [VMEM_SPEC] * 2, half_sum, 24, flops // 4,
        )(dev, acts, whole)

    def chip_pair_sum(sums):
        vectors = jnp.concatenate([jnp.sum(cotan, axis=(0, 1))[None], sums])
        vectors = vectors + swap(vectors, "core")
        return vectors + swap(vectors, "y")

    if paired:
        pieces = list(pieces)
        up, down, pieces[1] = tied(up1, down1, pieces[1])
        blocks = [unit, up, down]
        sums_in = [(), ()]
        for j in range(zs):
            crossed = swap(pieces[2 * j + 1], "replica")
            if j < zs - 1:
                up = ring.up(up)
                blocks.append(up)
            if j < zs - 2:
                down = ring.down(down)
                blocks.append(down)
            if j == zs - 2:
                slopes = slopes_of(tied(stats, blocks[-2])[0])
                kernel_f = tied(shard, blocks[-2])[0]
                up, crossed, slopes, *received = tied(up, crossed, slopes, *sums_in[0], *sums_in[1])
            elif j < zs - 2:
                up, down, crossed, *received = tied(up, down, crossed, *sums_in[0], *sums_in[1])
            else:
                whole, sums = back_of(blocks, slopes)
                crossed, sums, *received = tied(crossed, sums, *sums_in[0], *sums_in[1])
            if j < zs - 2:
                blocks[-2:] = [up, down]
            elif j == zs - 2:
                blocks[-1] = up
            sums_in = [tuple(received[:1]), tuple(received[1:])]
            kept = pieces[2 * j]
            ahead = add(kept[:part], crossed[:part], *sums_in[0])
            behind = (kept[part:], crossed[part:], *sums_in[1])
            sums_in = [(ring.up(ahead),), ()]
            if j < zs - 1:
                sums_in[1] = (ring.down(add(*behind)),)
        last, conv_send, vectors = tied(*sums_in[0], conv_far(whole), chip_pair_sum(sums))
        total = add(*behind, last)
        peer_b = from_peer(level, kernel_f.astype(BF16))
        a = lax.ppermute(total, ("replica", "core"), [(1, 0), (2, 3), (0, 2), (3, 1)])
        b = lax.ppermute(total, ("replica", "core"), [(1, 2), (2, 1)])
        left = jnp.where(replica == core, jnp.where(lower, total, a), jnp.where(lower, a, b))
        right = jnp.where(replica == core, jnp.where(lower, a, total), jnp.where(lower, b, a))
    else:
        whole, sums = back_of([lax.all_gather(unit, NODE, axis=0, tiled=True)], slopes_of(stats))
        conv_send, vectors = conv_far(whole), chip_pair_sum(sums)
        terms = jnp.concatenate(pieces).reshape(2 * zs, 2, part, cols.lead)
        summed = lax.psum_scatter(terms, NODE, scatter_dimension=0, tiled=False)
        ours = lax.dynamic_index_in_dim(summed, core, 0, keepdims=False)
        got = swap(lax.dynamic_index_in_dim(summed, 1 - core, 0, keepdims=False), "core")
        left, right = jnp.where(lower, ours, got), jnp.where(lower, got, ours)
    kernel_grad = jnp.concatenate([left, right[:, cols.both:]], axis=1).astype(F32)
    if paired:
        new_kernel = 0.5 * (shard + peer_b.astype(F32)) - (0.5 * scale * rate) * kernel_grad
    else:
        stepped = shard - (scale * rate) * kernel_grad
        new_kernel = 0.5 * (stepped + from_peer(level, stepped.astype(BF16)).astype(F32))

    block = call(
        partial(conv_own_kernel, cols), jax.ShapeDtypeStruct((half, width, chans), BF16),
        [SMEM_SPEC] + [VMEM_SPEC] * 5, half_sum, 24, flops // 4,
    )(dev, acts, whole, swap(conv_send, "core"), latent, conv_bias)

    reach = 1
    while reach < zs:
        vectors = vectors + lax.ppermute(vectors, "z", [(s, s ^ reach) for s in range(zs)])
        reach *= 2
    stepped_v = jnp.concatenate([conv_bias, gn_gain, gn_shift]) - LR_VECTOR * vectors
    new_v = 0.5 * (stepped_v + from_peer(level, stepped_v))

    return (
        block[None],
        new_kernel[None],
        new_v[0][None],
        new_v[1][None],
        new_v[2][None],
    )


def solution(mesh):
    replicas, shards = mesh.shape["replica"], mesh.shape["shard"]
    split = Mesh(mesh.devices.reshape(replicas, shards // 4, 2, 2), ("replica", "z", "y", "core"))
    shard = ("z", "y", "core")
    return jax.shard_map(
        per_device,
        mesh=split,
        in_specs=(
            P("replica", shard, None, None),
            P("replica", shard, None, None),
            P("replica", shard, None),
            P("replica", None),
            P("replica", None),
            P("replica", None),
            P(),
        ),
        out_specs=(
            P("replica", shard, None, None),
            P("replica", shard, None),
            P("replica", None),
            P("replica", None),
            P("replica", None),
        ),
        check_vma=False,
    )
```

```python
from functools import partial

import jax
import jax.numpy as jnp
import numpy as np
from jax import lax
from jax.experimental import pallas as pl
from jax.experimental.pallas import tpu as pltpu
from jax.sharding import Mesh, PartitionSpec as P

GROUPS = 32
EPS = 1e-05
LR_KERNEL = 0.1
LR_VECTOR = 0.01
LANES = 128
BF16 = jnp.bfloat16
F32 = jnp.float32

SMEM_SPEC = pl.BlockSpec(memory_space=pltpu.SMEM)
VMEM_SPEC = pl.BlockSpec(memory_space=pltpu.VMEM)


class Columns:
    def __init__(self, chans):
        tiles = 9 * chans // LANES
        self.total = 9 * chans
        self.lead = (tiles + 1) // 2 * LANES
        self.start = self.total - self.lead
        self.both = 2 * self.lead - self.total
        self.mid = self.lead - 4 * chans
        self.mid_start = chans - self.mid

    def pair(self, core, k, chans):
        first = jnp.where(core == 0, 2 * k, 5 + 2 * k)
        place = jnp.where(core == 0, 2 * k * chans, self.mid + 2 * k * chans)
        return (first, first + 1), pl.multiple_of(place, LANES)

    def middle(self, core, chans):
        place = jnp.where(core == 0, 4 * chans, 0)
        channel = jnp.where(core == 0, 0, self.mid_start)
        return pl.multiple_of(place, LANES), pl.multiple_of(channel, LANES)


def fill_shifts(shifts, row, values):
    width = values.shape[0]
    at = lax.broadcasted_iota(jnp.int32, values.shape, 0)
    left = jnp.where(at == 0, 0.0, pltpu.roll(values, 1, 0))
    right = jnp.where(at == width - 1, 0.0, pltpu.roll(values, width - 1, 0))
    shifts[0, row] = left.astype(BF16)
    shifts[1, row] = values.astype(BF16)
    shifts[2, row] = right.astype(BF16)


def clear_edges(shifts):
    zero = jnp.zeros(shifts.shape[2:], shifts.dtype)
    for b in range(3):
        shifts[b, 0] = zero
        shifts[b, shifts.shape[1] - 1] = zero


def act_kernel(order, dev, table, lat_own, lat_far, cot_own, cot_far, gain, shift,
               stats, acts, cot_t, cot_f):
    me = dev[0]
    core = me % 2
    half, width, chans = lat_own.shape
    cells = 2 * half * width
    group_width = chans // GROUPS
    own_at = core * half
    far_at = half - own_at
    clear_edges(acts)

    def add_row(i, sums):
        total, square = sums
        a = lat_own[i].astype(F32)
        b = lat_far[i].astype(F32)
        return total + (a + b), square + (a * a + b * b)

    zero = jnp.zeros((width, chans), F32)
    total, square = lax.fori_loop(0, half, add_row, (zero, zero))
    sums = jnp.concatenate(
        [jnp.sum(total, axis=0, keepdims=True), jnp.sum(square, axis=0, keepdims=True),
         jnp.zeros((6, chans), F32)], axis=0
    )
    first = lax.broadcasted_iota(jnp.int32, (chans, LANES), 0)
    start = lax.broadcasted_iota(jnp.int32, (chans, LANES), 1) * group_width
    member = jnp.where((first >= start) & (first < start + group_width), 1.0, 0.0)
    exact = partial(lax.dot_general, precision=lax.Precision.HIGHEST, preferred_element_type=F32)
    sums = exact(sums, member, (((1,), (0,)), ((), ()))) / (cells * group_width)
    sums = exact(sums, member, (((1,), (1,)), ((), ())))
    mean = sums[0:1]
    rstd = lax.rsqrt(sums[1:2] - mean * mean + EPS)
    stats[0:1] = mean
    stats[1:2] = rstd
    gain_v, shift_v = gain[...], shift[...]

    def act_rows(i, _):
        for ref, base in ((lat_own, own_at), (lat_far, far_at)):
            pre = gain_v * ((ref[i].astype(F32) - mean) * rstd) + shift_v
            fill_shifts(acts, base + i + 1, pre * (0.5 + 0.5 * jnp.tanh(0.5 * pre)))
        return 0

    lax.fori_loop(0, half, act_rows, 0)

    chunk = LANES // width
    for ref, base in ((cot_own, own_at), (cot_far, far_at)):
        for i in range(half // chunk):
            piece = ref[i * chunk:(i + 1) * chunk].reshape(LANES, chans).astype(F32)
            place = pl.multiple_of(base * width + i * LANES, LANES)
            if order is None:
                cot_t[:, pl.ds(place, LANES)] = piece.T.astype(BF16)
            else:
                cot_f[:, pl.ds(place, LANES)] = piece.T
    if order is not None:
        first_at, part, count = order
        for q in range(count // 2):
            pair = [
                cot_f[pl.ds(pl.multiple_of(table[me, first_at + 2 * q + i], 8), part)]
                for i in range(2)
            ]
            cot_t[2 * q * part:(2 * q + 2) * part] = jnp.concatenate(pair).astype(BF16)


def grad_kernel(cols, dev, acts, cot_t, *pieces):
    core = dev[0] % 2
    rows, width, chans = acts.shape[1] - 2, acts.shape[2], acts.shape[3]
    cells = rows * width
    count = pieces[0].shape[0]

    def emit(window, place, wide):
        value = jnp.dot(cot_t[...], window, preferred_element_type=F32)
        for q, piece in enumerate(pieces):
            piece[:, pl.ds(place, wide)] = value[q * count:(q + 1) * count].astype(BF16)

    def two_taps(k, _):
        taps, place = cols.pair(core, k, chans)
        windows = [acts[t % 3, pl.ds(t // 3, rows)].reshape(cells, chans) for t in taps]
        emit(jnp.concatenate(windows, axis=1), place, 2 * chans)
        return 0

    lax.fori_loop(0, 2, two_taps, 0)
    place, channel = cols.middle(core, chans)
    emit(acts[1, 1:rows + 1, :, pl.ds(channel, cols.mid)].reshape(cells, cols.mid), place, cols.mid)


def slope_kernel(dev, stats, gain, shift, lat_own, lat_far, cot_own, cot_far, cots, slope, slope_x):
    core = dev[0] % 2
    half = lat_own.shape[0]
    clear_edges(cots)
    mean, rstd = stats[0:1], stats[1:2]
    gain_v, shift_v = gain[...], shift[...]

    def one_row(i, _):
        for lat, cot, base in ((lat_own, cot_own, core * half), (lat_far, cot_far, half - core * half)):
            fill_shifts(cots, base + i + 1, cot[i].astype(F32))
            xhat = (lat[i].astype(F32) - mean) * rstd
            pre = gain_v * xhat + shift_v
            sig = 0.5 + 0.5 * jnp.tanh(0.5 * pre)
            value = sig * (1.0 + pre * (1.0 - sig))
            slope[base + i] = value.astype(BF16)
            slope_x[base + i] = (value * xhat).astype(BF16)
        return 0

    lax.fori_loop(0, half, one_row, 0)


def place_kernel(dev, table, *refs):
    blocks, whole = list(refs[:-1]), refs[-1]
    if blocks[-1].shape != blocks[0].shape:
        blocks[-2:] = [jnp.concatenate([blocks[-2][...], blocks[-1][...]])]
    for i, block in enumerate(blocks):
        count = block.shape[0]
        at = pl.multiple_of(table[dev[0], i] * count, count)
        whole[pl.ds(at, count)] = block[...]


def conv_sum(cols, core, first, half, acts, whole, total):
    width, chans = acts.shape[2:]
    cells = half * width
    nt = (((1,), (1,)), ((), ()))
    place, channel = cols.middle(core, chans)
    window = acts[1, pl.ds(first + 1, half), :, pl.ds(channel, cols.mid)].reshape(cells, cols.mid)
    lane = lax.broadcasted_iota(jnp.int32, window.shape, 1)
    window = jnp.where((core == 1) & (lane < cols.both), jnp.zeros_like(window), window)
    total[...] = lax.dot_general(window, whole[:, pl.ds(place, cols.mid)], nt, preferred_element_type=F32)

    def two_taps(k, _):
        taps, place = cols.pair(core, k, chans)
        windows = [acts[t % 3, pl.ds(first + t // 3, half)].reshape(cells, chans) for t in taps]
        total[...] += lax.dot_general(
            jnp.concatenate(windows, axis=1), whole[:, pl.ds(place, 2 * chans)], nt, preferred_element_type=F32
        )
        return 0

    lax.fori_loop(0, 2, two_taps, 0)


def conv_far_kernel(cols, dev, acts, whole, far, total):
    core = dev[0] % 2
    half = (acts.shape[1] - 2) // 2
    conv_sum(cols, core, (1 - core) * half, half, acts, whole, total)
    far[...] = total[...].astype(BF16)


def conv_own_kernel(cols, dev, acts, whole, got, latent, bias, block, total):
    core = dev[0] % 2
    half, width, chans = latent.shape
    conv_sum(cols, core, core * half, half, acts, whole, total)
    scale = cols.total ** (-0.5)
    conv = scale * (total[...] + got[...].astype(F32)) + bias[...]
    block[...] = (conv.reshape(half, width, chans) + latent[...].astype(F32)).astype(BF16)


def back_kernel(cols, dev, cots, slope, slope_x, whole, sums, total):
    core = dev[0] % 2
    rows, width, chans = slope.shape
    cells = rows * width
    total[...] = jnp.zeros_like(total)
    place, channel = cols.middle(core, chans)
    window = cots[1, 1:rows + 1].reshape(cells, chans)
    value = jnp.dot(window, whole[:, pl.ds(place, cols.mid)], preferred_element_type=F32)
    lane = lax.broadcasted_iota(jnp.int32, value.shape, 1)
    total[:, pl.ds(channel, cols.mid)] = jnp.where((core == 1) & (lane < cols.both), 0.0, value)

    def two_taps(k, _):
        taps, place = cols.pair(core, k, chans)
        windows = [cots[2 - t % 3, pl.ds(2 - t // 3, rows)].reshape(cells, chans) for t in taps]
        second = pl.multiple_of(place + chans, LANES)
        kernels = [whole[:, pl.ds(place, chans)], whole[:, pl.ds(second, chans)]]
        total[...] += jnp.dot(
            jnp.concatenate(windows, axis=1), jnp.concatenate(kernels, axis=0), preferred_element_type=F32
        )
        return 0

    lax.fori_loop(0, 2, two_taps, 0)

    def add_row(i, carry):
        gains, shifts = carry
        value = total[pl.ds(pl.multiple_of(i * width, width), width)]
        return gains + value * slope_x[i].astype(F32), shifts + value * slope[i].astype(F32)

    zero = jnp.zeros((width, chans), F32)
    gains, shifts = lax.fori_loop(0, rows, add_row, (zero, zero))
    scale = cols.total ** (-0.5)
    sums[0:1] = scale * jnp.sum(gains, axis=0, keepdims=True)
    sums[1:2] = scale * jnp.sum(shifts, axis=0, keepdims=True)


NODE = ("z", "y")


def swap(value, axis):
    return lax.ppermute(value, axis, [(0, 1), (1, 0)])


def from_peer(level, value):
    count = lax.axis_size("replica")
    levels = count.bit_length() - 1
    moves = [[(s, (s + (1 << k)) % count) for s in range(count)] for k in range(levels)]
    if levels == 1:
        return lax.ppermute(value, "replica", moves[0])
    return lax.switch(level, [lambda v, m=m: lax.ppermute(v, "replica", m) for m in moves], value)


class Ring:
    def __init__(self, zs):
        self.count = 2 * zs
        self.reach = zs
        self.nodes = [2 * z for z in range(zs)] + [2 * z + 1 for z in reversed(range(zs))]
        ahead = list(zip(self.nodes, self.nodes[1:] + self.nodes[:1]))
        self.ahead = ahead
        self.behind = [(b, a) for a, b in ahead]

    def node(self, at, offset):
        return self.nodes[(at + offset) % self.count]

    def up(self, value):
        return lax.ppermute(value, NODE, self.ahead)

    def down(self, value):
        return lax.ppermute(value, NODE, self.behind)

    def table(self, part):
        rows = np.zeros((2, self.count, 2, 3 * self.count), np.int32)
        for replica in range(2):
            for at, node in enumerate(self.nodes):
                line = [node]
                for k in range(1, self.reach + 1):
                    line.append(self.node(at, -k))
                    if k < self.reach:
                        line.append(self.node(at, k))
                for j in range(self.reach):
                    targets = [self.node(at, self.reach - j), self.node(at, j + 1 - self.reach)]
                    for which in (replica, 1 - replica):
                        line += [(2 * target + which) * part for target in targets]
                rows[replica, node, :] = line
        return rows.reshape(-1, 3 * self.count)


def sum_over(value, axes, masks):
    count = lax.axis_size(axes)
    for mask in (masks[0], masks[1], masks[0] | masks[1]):
        value_in = lax.ppermute(value, axes, [(s, s ^ mask) for s in range(count)])
        total = value_in if mask == masks[0] else total + value_in
    return value + total


def add(*values):
    total = values[0].astype(F32)
    for value in values[1:]:
        total = total + value.astype(F32)
    return total.astype(BF16)


def tied(*values):
    return lax.optimization_barrier(values)


def per_device(latents, cotangent, kernel, conv_bias, gn_gain, gn_shift, step):
    latent, cotan, shard = latents[0], cotangent[0], kernel[0]
    half, width, chans = latent.shape
    part = shard.shape[0]
    cols = Columns(chans)
    cells = half * width
    zs, replicas = lax.axis_size("z"), lax.axis_size("replica")
    core, z, y, replica = (lax.axis_index(a) for a in ("core", "z", "y", "replica"))
    lower = core == 0
    paired = replicas == 2
    ring = Ring(zs)
    scale = cols.total ** (-0.5)
    level = step[0] % (replicas.bit_length() - 1)
    params = jnp.concatenate([conv_bias, gn_gain, gn_shift])
    rate = LR_KERNEL * (1.0 - (step[0] % 1000).astype(F32) / 2000.0)
    dev = (((replica * zs + z) * 2 + y) * 2 + core).reshape(1)

    mine = lax.dynamic_slice_in_dim(shard, core * cols.start, cols.lead, 1).astype(BF16)
    theirs = lax.dynamic_slice_in_dim(shard, (1 - core) * cols.start, cols.lead, 1).astype(BF16)
    got = swap(theirs, "core")
    unit = jnp.where(lower, jnp.concatenate([mine, got]), jnp.concatenate([got, mine]))
    lat_far = swap(latent, "core")
    cot_b = cotan.astype(BF16)
    cot_far = swap(cot_b, "core")

    if paired:
        table = jnp.asarray(ring.table(part))
        order = (ring.count, part, 2 * ring.count)
        up1, down1 = ring.up(unit), ring.down(unit)
        peer_b = from_peer(level, shard.astype(BF16))
    else:
        table = jnp.zeros((replicas * zs * 4, 1), jnp.int32)
        order = None

    def call(body, outs, ins, scratch, megabytes, flops):
        return pl.pallas_call(
            body,
            out_shape=outs,
            in_specs=ins,
            out_specs=jax.tree.map(lambda _: VMEM_SPEC, outs),
            scratch_shapes=scratch,
            compiler_params=pltpu.CompilerParams(vmem_limit_bytes=megabytes * 2**20),
            cost_estimate=pl.CostEstimate(flops=flops, bytes_accessed=0, transcendentals=0),
        )

    image = (2 * half, width, chans)
    shifted = jax.ShapeDtypeStruct((3, 2 * half + 2, width, chans), BF16)
    flops = 2 * 2 * cells * chans * cols.lead
    stats, acts, cot_t = call(
        partial(act_kernel, order),
        (jax.ShapeDtypeStruct((2, chans), F32), shifted, jax.ShapeDtypeStruct((chans, 2 * cells), BF16)),
        [SMEM_SPEC] * 2 + [VMEM_SPEC] * 6,
        [pltpu.VMEM((chans, 2 * cells), F32)],
        16, flops // 4,
    )(dev, table, latent, lat_far, cot_b, cot_far, gn_gain, gn_shift)
    pieces = call(
        partial(grad_kernel, cols),
        [jax.ShapeDtypeStruct((2 * part, cols.lead), BF16)] * (2 * zs),
        [SMEM_SPEC] + [VMEM_SPEC] * 2,
        [],
        20, flops // 2,
    )(dev, acts, cot_t)
    def slopes_of(stats):
        return call(
            slope_kernel,
            (shifted, jax.ShapeDtypeStruct(image, BF16), jax.ShapeDtypeStruct(image, BF16)),
            [SMEM_SPEC] + [VMEM_SPEC] * 7,
            [],
            12, flops // 4,
        )(dev, stats, gn_gain, gn_shift, latent, lat_far, cot_b, cot_far)

    def back_of(blocks, slopes):
        whole = call(
            place_kernel, jax.ShapeDtypeStruct((chans, cols.lead), BF16),
            [SMEM_SPEC] * 2 + [VMEM_SPEC] * len(blocks), [], 10, flops // 16,
        )(dev, table, *blocks)
        return whole, call(
            partial(back_kernel, cols), jax.ShapeDtypeStruct((2, chans), F32),
            [SMEM_SPEC] + [VMEM_SPEC] * 4, [pltpu.VMEM((2 * cells, chans), F32)], 24, flops // 2,
        )(dev, *slopes, whole)

    half_sum = [pltpu.VMEM((cells, chans), F32)]

    def conv_far(whole):
        return call(
            partial(conv_far_kernel, cols), jax.ShapeDtypeStruct((cells, chans), BF16),
            [SMEM_SPEC] + [VMEM_SPEC] * 2, half_sum, 16, flops // 4,
        )(dev, acts, whole)

    def chip_sum(sums):
        vectors = jnp.concatenate([jnp.sum(cotan, axis=(0, 1))[None], sums])
        vectors = params / (4 * zs) - LR_VECTOR * vectors
        return vectors + swap(vectors, "core")

    if paired:
        kept, sent = pieces[::2], pieces[1::2]
        slopes = slopes_of(tied(stats, sent[0])[0])
        up, down, peer_b, slopes = tied(up1, down1, peer_b, slopes)
        blocks = [unit, up, down]
        crossed = [swap(piece, "replica") for piece in sent]
        up_sum = down_sum = ()
        for j in range(zs):
            if j < zs - 2:
                up, down = ring.up(up), ring.down(down)
                blocks += [up, down]
                up, down, crossed[j], *received = tied(up, down, crossed[j], *up_sum, *down_sum)
                up_sum, down_sum = tuple(received[:1]), tuple(received[1:])
            elif j == zs - 2:
                halves = ring.up(up[:part]), ring.down(down[part:])
                *halves, crossed[j] = tied(*halves, crossed[j])
                whole, sums = back_of(blocks + halves, slopes)
            else:
                crossed[j], sums, *received = tied(crossed[j], sums, *up_sum, *down_sum)
                up_sum, down_sum = tuple(received[:1]), tuple(received[1:])
            ahead = add(kept[j][:part], crossed[j][:part], *up_sum)
            behind = (kept[j][part:], crossed[j][part:], *down_sum)
            up_sum = (ring.up(ahead),)
            if j < zs - 1:
                down_sum = (ring.down(add(*behind)),)
        vectors = sum_over(chip_sum(sums), ("z", "y"), (1, 2))
        last, conv_got, vectors = tied(*up_sum, swap(conv_far(whole), "core"), vectors)
        total = add(*behind, last)
        a = lax.ppermute(total, ("replica", "core"), [(1, 0), (2, 3), (0, 2), (3, 1)])
        b = lax.ppermute(total, ("replica", "core"), [(1, 2), (2, 1)])
        left = jnp.where(replica == core, jnp.where(lower, total, a), jnp.where(lower, a, b))
        right = jnp.where(replica == core, jnp.where(lower, a, total), jnp.where(lower, b, a))
    else:
        whole, sums = back_of([lax.all_gather(unit, NODE, axis=0, tiled=True)], slopes_of(stats))
        conv_got, vectors = swap(conv_far(whole), "core"), chip_sum(sums)
        terms = jnp.concatenate(pieces).reshape(2 * zs, 2, part, cols.lead)
        summed = lax.psum_scatter(terms, NODE, scatter_dimension=0, tiled=False)
        ours = lax.dynamic_index_in_dim(summed, core, 0, keepdims=False)
        got = swap(lax.dynamic_index_in_dim(summed, 1 - core, 0, keepdims=False), "core")
        left, right = jnp.where(lower, ours, got), jnp.where(lower, got, ours)
    kernel_grad = jnp.concatenate([left, right[:, cols.both:]], axis=1).astype(F32)
    if paired:
        new_kernel = 0.5 * (shard + peer_b.astype(F32)) - (0.5 * scale * rate) * kernel_grad
    else:
        stepped = shard - (scale * rate) * kernel_grad
        new_kernel = 0.5 * (stepped + from_peer(level, stepped.astype(BF16)).astype(F32))

    block = call(
        partial(conv_own_kernel, cols), jax.ShapeDtypeStruct((half, width, chans), BF16),
        [SMEM_SPEC] + [VMEM_SPEC] * 5, half_sum, 16, flops // 4,
    )(dev, acts, whole, conv_got, latent, conv_bias)

    if paired:
        new_v = 0.5 * sum_over(vectors, ("replica", "z"), (2, zs))
    else:
        stepped_v = lax.psum(vectors, NODE)
        new_v = 0.5 * (stepped_v + from_peer(level, stepped_v))

    return (
        block[None],
        new_kernel[None],
        new_v[0][None],
        new_v[1][None],
        new_v[2][None],
    )


def solution(mesh):
    replicas, shards = mesh.shape["replica"], mesh.shape["shard"]
    split = Mesh(mesh.devices.reshape(replicas, shards // 4, 2, 2), ("replica", "z", "y", "core"))
    shard = ("z", "y", "core")
    return jax.shard_map(
        per_device,
        mesh=split,
        in_specs=(
            P("replica", shard, None, None),
            P("replica", shard, None, None),
            P("replica", shard, None),
            P("replica", None),
            P("replica", None),
            P("replica", None),
            P(),
        ),
        out_specs=(
            P("replica", shard, None, None),
            P("replica", shard, None),
            P("replica", None),
            P("replica", None),
            P("replica", None),
        ),
        check_vma=False,
    )
```

```python
from functools import partial

import jax
import jax.numpy as jnp
import numpy as np
from jax import lax
from jax.experimental import pallas as pl
from jax.experimental.pallas import tpu as pltpu
from jax.sharding import Mesh, PartitionSpec as P

GROUPS = 32
EPS = 1e-05
LR_KERNEL = 0.1
LR_VECTOR = 0.01
LANES = 128
BF16 = jnp.bfloat16
F32 = jnp.float32

SMEM_SPEC = pl.BlockSpec(memory_space=pltpu.SMEM)
VMEM_SPEC = pl.BlockSpec(memory_space=pltpu.VMEM)


class Columns:
    def __init__(self, chans):
        tiles = 9 * chans // LANES
        self.total = 9 * chans
        self.lead = (tiles + 1) // 2 * LANES
        self.start = self.total - self.lead
        self.both = 2 * self.lead - self.total
        self.mid = self.lead - 4 * chans
        self.mid_start = chans - self.mid

    def pair(self, core, k, chans):
        first = jnp.where(core == 0, 2 * k, 5 + 2 * k)
        place = jnp.where(core == 0, 2 * k * chans, self.mid + 2 * k * chans)
        return (first, first + 1), pl.multiple_of(place, LANES)

    def middle(self, core, chans):
        place = jnp.where(core == 0, 4 * chans, 0)
        channel = jnp.where(core == 0, 0, self.mid_start)
        return pl.multiple_of(place, LANES), pl.multiple_of(channel, LANES)


def fill_shifts(shifts, row, values):
    width = values.shape[0]
    at = lax.broadcasted_iota(jnp.int32, values.shape, 0)
    left = jnp.where(at == 0, 0.0, pltpu.roll(values, 1, 0))
    right = jnp.where(at == width - 1, 0.0, pltpu.roll(values, width - 1, 0))
    shifts[0, row] = left.astype(BF16)
    shifts[1, row] = values.astype(BF16)
    shifts[2, row] = right.astype(BF16)


def clear_edges(shifts):
    zero = jnp.zeros(shifts.shape[2:], shifts.dtype)
    for b in range(3):
        shifts[b, 0] = zero
        shifts[b, shifts.shape[1] - 1] = zero


def act_kernel(order, dev, table, lat_own, lat_far, cot_own, cot_far, gain, shift,
               stats, acts, cot_t, cot_f):
    me = dev[0]
    core = me % 2
    half, width, chans = lat_own.shape
    cells = 2 * half * width
    group_width = chans // GROUPS
    own_at = core * half
    far_at = half - own_at
    clear_edges(acts)

    def add_row(i, sums):
        total, square = sums
        a = lat_own[i].astype(F32)
        b = lat_far[i].astype(F32)
        return total + (a + b), square + (a * a + b * b)

    zero = jnp.zeros((width, chans), F32)
    total, square = lax.fori_loop(0, half, add_row, (zero, zero))
    sums = jnp.concatenate(
        [jnp.sum(total, axis=0, keepdims=True), jnp.sum(square, axis=0, keepdims=True),
         jnp.zeros((6, chans), F32)], axis=0
    )
    first = lax.broadcasted_iota(jnp.int32, (chans, LANES), 0)
    start = lax.broadcasted_iota(jnp.int32, (chans, LANES), 1) * group_width
    member = jnp.where((first >= start) & (first < start + group_width), 1.0, 0.0)
    exact = partial(lax.dot_general, precision=lax.Precision.HIGHEST, preferred_element_type=F32)
    sums = exact(sums, member, (((1,), (0,)), ((), ()))) / (cells * group_width)
    sums = exact(sums, member, (((1,), (1,)), ((), ())))
    mean = sums[0:1]
    rstd = lax.rsqrt(sums[1:2] - mean * mean + EPS)
    stats[0:1] = mean
    stats[1:2] = rstd
    gain_v, shift_v = gain[...], shift[...]

    def act_rows(i, _):
        for ref, base in ((lat_own, own_at), (lat_far, far_at)):
            pre = gain_v * ((ref[i].astype(F32) - mean) * rstd) + shift_v
            fill_shifts(acts, base + i + 1, pre * (0.5 + 0.5 * jnp.tanh(0.5 * pre)))
        return 0

    lax.fori_loop(0, half, act_rows, 0)

    chunk = LANES // width
    for ref, base in ((cot_own, own_at), (cot_far, far_at)):
        for i in range(half // chunk):
            piece = ref[i * chunk:(i + 1) * chunk].reshape(LANES, chans).astype(F32)
            place = pl.multiple_of(base * width + i * LANES, LANES)
            if order is None:
                cot_t[:, pl.ds(place, LANES)] = piece.T.astype(BF16)
            else:
                cot_f[:, pl.ds(place, LANES)] = piece.T
    if order is not None:
        first_at, part, count = order
        for q in range(count // 2):
            pair = [
                cot_f[pl.ds(pl.multiple_of(table[me, first_at + 2 * q + i], 8), part)]
                for i in range(2)
            ]
            cot_t[2 * q * part:(2 * q + 2) * part] = jnp.concatenate(pair).astype(BF16)


def grad_kernel(cols, dev, acts, cot_t, *pieces):
    core = dev[0] % 2
    rows, width, chans = acts.shape[1] - 2, acts.shape[2], acts.shape[3]
    cells = rows * width
    count = pieces[0].shape[0]

    def emit(window, place, wide):
        value = jnp.dot(cot_t[...], window, preferred_element_type=F32)
        for q, piece in enumerate(pieces):
            piece[:, pl.ds(place, wide)] = value[q * count:(q + 1) * count].astype(BF16)

    def two_taps(k, _):
        taps, place = cols.pair(core, k, chans)
        windows = [acts[t % 3, pl.ds(t // 3, rows)].reshape(cells, chans) for t in taps]
        emit(jnp.concatenate(windows, axis=1), place, 2 * chans)
        return 0

    lax.fori_loop(0, 2, two_taps, 0)
    place, channel = cols.middle(core, chans)
    emit(acts[1, 1:rows + 1, :, pl.ds(channel, cols.mid)].reshape(cells, cols.mid), place, cols.mid)


class Stages:
    def __init__(self, counts, rows):
        self.rows = rows
        self.counts = counts
        self.widths = [-(-n * rows // LANES) * LANES for n in counts]
        self.starts = [sum(self.widths[:i]) for i in range(len(counts))]
        self.width = sum(self.widths)

    def lanes(self, stage):
        return slice(self.starts[stage], self.starts[stage] + self.widths[stage])

    def columns(self, stage, blocks, place, wide):
        parts = [ref[:, pl.ds(place, wide)] for ref in blocks]
        if len(parts) == self.counts[stage] + 1:
            parts[-2:] = [jnp.concatenate(parts[-2:])]
        spare = self.widths[stage] - self.counts[stage] * self.rows
        if spare:
            parts.append(jnp.zeros((spare, wide), BF16))
        return jnp.concatenate(parts) if len(parts) > 1 else parts[0]

    def order(self, me, table, order, chans):
        lane = lax.broadcasted_iota(jnp.int32, (1, self.width), 1)
        source = jnp.full((1, self.width), -1, jnp.int32)
        at = 0
        for start, count in zip(self.starts, self.counts):
            for i in range(count):
                first = start + i * self.rows
                inside = (lane >= first) & (lane < first + self.rows)
                source = jnp.where(inside, table[me, at] * self.rows + lane - first, source)
                at += 1
        channel = lax.broadcasted_iota(jnp.int32, (chans, self.width), 0)
        order[...] = jnp.where(channel == source, 1.0, 0.0).astype(BF16)


def slope_kernel(stages, dev, table, stats, gain, shift, lat_own, lat_far, cot_own, cot_far,
                 cots, slope, slope_x, *refs):
    me = dev[0]
    core = me % 2
    half, width, chans = lat_own.shape
    clear_edges(cots)
    mean, rstd = stats[0:1], stats[1:2]
    gain_v, shift_v = gain[...], shift[...]
    far_at = half - core * half
    if len(stages.counts) > 1:
        order, placed = refs
        stages.order(me, table, order, chans)
        for ref, base in ((cot_own, core * half), (cot_far, far_at)):
            value = jnp.dot(ref[...].reshape(half * width, chans), order[...], preferred_element_type=F32)
            placed[pl.ds(base, half)] = value.reshape(half, width, stages.width)

    def one_row(i, _):
        for lat, cot, base in ((lat_own, cot_own, core * half), (lat_far, cot_far, far_at)):
            value = placed[base + i] if len(stages.counts) > 1 else cot[i].astype(F32)
            fill_shifts(cots, base + i + 1, value)
            xhat = (lat[i].astype(F32) - mean) * rstd
            pre = gain_v * xhat + shift_v
            sig = 0.5 + 0.5 * jnp.tanh(0.5 * pre)
            value = sig * (1.0 + pre * (1.0 - sig))
            slope[base + i] = value.astype(BF16)
            slope_x[base + i] = (value * xhat).astype(BF16)
        return 0

    lax.fori_loop(0, half, one_row, 0)


def conv_sum(cols, stages, stage, core, first, half, acts, blocks, total):
    width, chans = acts.shape[2:]
    cells = half * width
    nt = (((1,), (1,)), ((), ()))
    place, channel = cols.middle(core, chans)
    window = acts[1, pl.ds(first + 1, half), :, pl.ds(channel, cols.mid)].reshape(cells, cols.mid)
    lane = lax.broadcasted_iota(jnp.int32, window.shape, 1)
    window = jnp.where((core == 1) & (lane < cols.both), jnp.zeros_like(window), window)
    kernel = stages.columns(stage, blocks, place, cols.mid)
    total[...] = lax.dot_general(window, kernel, nt, preferred_element_type=F32)

    def two_taps(k, _):
        taps, place = cols.pair(core, k, chans)
        windows = [acts[t % 3, pl.ds(first + t // 3, half)].reshape(cells, chans) for t in taps]
        kernel = stages.columns(stage, blocks, place, 2 * chans)
        total[...] += lax.dot_general(
            jnp.concatenate(windows, axis=1), kernel, nt, preferred_element_type=F32
        )
        return 0

    lax.fori_loop(0, 2, two_taps, 0)


def conv_both_kernel(cols, stages, stage, dev, acts, *refs):
    blocks, (own, far, total) = refs[:-3], refs[-3:]
    core = dev[0] % 2
    rows = acts.shape[1] - 2
    conv_sum(cols, stages, stage, core, 0, rows, acts, blocks, total)
    half = own.shape[0]
    own[...] = total[pl.ds(pl.multiple_of(core * half, half), half)]
    far[...] = total[pl.ds(pl.multiple_of((1 - core) * half, half), half)].astype(BF16)


def conv_far_kernel(cols, stages, stage, dev, acts, *refs):
    blocks, (far, total) = refs[:-2], refs[-2:]
    core = dev[0] % 2
    half = (acts.shape[1] - 2) // 2
    conv_sum(cols, stages, stage, core, (1 - core) * half, half, acts, blocks, total)
    far[...] = total[...].astype(BF16)


def conv_own_kernel(cols, stages, dev, acts, got, latent, bias, *refs):
    core = dev[0] % 2
    half, width, chans = latent.shape
    scale = cols.total ** (-0.5)
    stage = len(stages.counts) - 1
    before = 3 * stage
    blocks, (block, total) = refs[before:-2], refs[-2:]
    conv_sum(cols, stages, stage, core, core * half, half, acts, blocks, total)
    conv = total[...] + got[...].astype(F32)
    if stage:
        first_own, first_got, order = refs[:before]
        conv = jnp.concatenate([first_own[...] + first_got[...].astype(F32), conv], axis=1)
        high = conv.astype(BF16)
        low = (conv - high.astype(F32)).astype(BF16)
        nt = (((1,), (1,)), ((), ()))
        conv = sum(
            lax.dot_general(value, order[...], nt, preferred_element_type=F32) for value in (low, high)
        )
    conv = scale * conv + bias[...]
    block[...] = (conv.reshape(half, width, chans) + latent[...].astype(F32)).astype(BF16)


def back_kernel(cols, stages, stage, dev, cots, *refs):
    last = stage == len(stages.counts) - 1
    before = (1 if stage else 0) + (2 if last else 0)
    blocks = refs[before:-2] if last else refs[before:-1]
    total = refs[-1]
    core = dev[0] % 2
    rows, width = cots.shape[1] - 2, cots.shape[2]
    cells, chans = total.shape
    lanes = stages.lanes(stage)

    total[...] = refs[0][...] if stage else jnp.zeros_like(total)
    place, channel = cols.middle(core, chans)
    window = cots[1, 1:rows + 1, :, lanes].reshape(cells, stages.widths[stage])
    kernel = stages.columns(stage, blocks, place, cols.mid)
    value = jnp.dot(window, kernel, preferred_element_type=F32)
    lane = lax.broadcasted_iota(jnp.int32, value.shape, 1)
    total[:, pl.ds(channel, cols.mid)] += jnp.where((core == 1) & (lane < cols.both), 0.0, value)

    def taps_from(first, place, count):
        windows, kernels = [], []
        for i in range(count):
            tap = first + i
            window = cots[2 - tap % 3, pl.ds(2 - tap // 3, rows), :, lanes]
            windows.append(window.reshape(cells, stages.widths[stage]))
            kernels.append(stages.columns(stage, blocks, pl.multiple_of(place + i * chans, LANES), chans))
        total[...] += jnp.dot(
            jnp.concatenate(windows, axis=1), jnp.concatenate(kernels), preferred_element_type=F32
        )

    def two_taps(k, _):
        taps, place = cols.pair(core, k, chans)
        taps_from(taps[0], place, 2)
        return 0

    if stage:
        taps, place = cols.pair(core, 0, chans)
        taps_from(taps[0], place, 4)
    else:
        lax.fori_loop(0, 2, two_taps, 0)

    if last:
        slope, slope_x = refs[before - 2:before]
        sums = refs[-2]

        def add_row(i, carry):
            gains, shifts = carry
            value = total[pl.ds(pl.multiple_of(i * width, width), width)]
            return gains + value * slope_x[i].astype(F32), shifts + value * slope[i].astype(F32)

        zero = jnp.zeros((width, chans), F32)
        gains, shifts = lax.fori_loop(0, rows, add_row, (zero, zero))
        scale = cols.total ** (-0.5)
        sums[0:1] = scale * jnp.sum(gains, axis=0, keepdims=True)
        sums[1:2] = scale * jnp.sum(shifts, axis=0, keepdims=True)


NODE = ("z", "y")


def swap(value, axis):
    return lax.ppermute(value, axis, [(0, 1), (1, 0)])


def from_peer(level, value):
    count = lax.axis_size("replica")
    levels = count.bit_length() - 1
    moves = [[(s, (s + (1 << k)) % count) for s in range(count)] for k in range(levels)]
    if levels == 1:
        return lax.ppermute(value, "replica", moves[0])
    return lax.switch(level, [lambda v, m=m: lax.ppermute(v, "replica", m) for m in moves], value)


class Ring:
    def __init__(self, zs):
        self.count = 2 * zs
        self.reach = zs
        self.nodes = [2 * z for z in range(zs)] + [2 * z + 1 for z in reversed(range(zs))]
        ahead = list(zip(self.nodes, self.nodes[1:] + self.nodes[:1]))
        self.ahead = ahead
        self.behind = [(b, a) for a, b in ahead]

    def node(self, at, offset):
        return self.nodes[(at + offset) % self.count]

    def up(self, value):
        return lax.ppermute(value, NODE, self.ahead)

    def down(self, value):
        return lax.ppermute(value, NODE, self.behind)

    def table(self, part):
        rows = np.zeros((2, self.count, 2, 3 * self.count), np.int32)
        for replica in range(2):
            for at, node in enumerate(self.nodes):
                line = [node]
                for k in range(1, self.reach + 1):
                    line.append(self.node(at, -k))
                    if k < self.reach:
                        line.append(self.node(at, k))
                for j in range(self.reach):
                    targets = [self.node(at, self.reach - j), self.node(at, j + 1 - self.reach)]
                    for which in (replica, 1 - replica):
                        line += [(2 * target + which) * part for target in targets]
                rows[replica, node, :] = line
        return rows.reshape(-1, 3 * self.count)


def sum_over(value, axes, masks):
    count = lax.axis_size(axes)
    for mask in (masks[0], masks[1], masks[0] | masks[1]):
        value_in = lax.ppermute(value, axes, [(s, s ^ mask) for s in range(count)])
        total = value_in if mask == masks[0] else total + value_in
    return value + total


def add(*values):
    total = values[0].astype(F32)
    for value in values[1:]:
        total = total + value.astype(F32)
    return total.astype(BF16)


def tied(*values):
    return lax.optimization_barrier(values)


def per_device(latents, cotangent, kernel, conv_bias, gn_gain, gn_shift, step):
    latent, cotan, shard = latents[0], cotangent[0], kernel[0]
    half, width, chans = latent.shape
    part = shard.shape[0]
    cols = Columns(chans)
    cells = half * width
    zs, replicas = lax.axis_size("z"), lax.axis_size("replica")
    core, z, y, replica = (lax.axis_index(a) for a in ("core", "z", "y", "replica"))
    lower = core == 0
    paired = replicas == 2
    ring = Ring(zs)
    scale = cols.total ** (-0.5)
    level = step[0] % (replicas.bit_length() - 1)
    params = jnp.concatenate([conv_bias, gn_gain, gn_shift])
    rate = LR_KERNEL * (1.0 - (step[0] % 1000).astype(F32) / 2000.0)
    dev = (((replica * zs + z) * 2 + y) * 2 + core).reshape(1)

    mine = lax.dynamic_slice_in_dim(shard, core * cols.start, cols.lead, 1).astype(BF16)
    theirs = lax.dynamic_slice_in_dim(shard, (1 - core) * cols.start, cols.lead, 1).astype(BF16)
    got = swap(theirs, "core")
    unit = jnp.where(lower, jnp.concatenate([mine, got]), jnp.concatenate([got, mine]))
    lat_far = swap(latent, "core")
    cot_b = cotan.astype(BF16)
    cot_far = swap(cot_b, "core")

    if paired:
        table = jnp.asarray(ring.table(part))
        order = (ring.count, part, 2 * ring.count)
        up1, down1 = ring.up(unit), ring.down(unit)
        peer = from_peer(level, mine), from_peer(level, theirs)
    else:
        table = jnp.zeros((replicas * zs * 4, 1), jnp.int32)
        order = None

    def call(body, outs, ins, scratch, megabytes, flops):
        return pl.pallas_call(
            body,
            out_shape=outs,
            in_specs=ins,
            out_specs=jax.tree.map(lambda _: VMEM_SPEC, outs),
            scratch_shapes=scratch,
            compiler_params=pltpu.CompilerParams(vmem_limit_bytes=megabytes * 2**20),
            cost_estimate=pl.CostEstimate(flops=flops, bytes_accessed=0, transcendentals=0),
        )

    image = (2 * half, width, chans)
    shifted = jax.ShapeDtypeStruct((3, 2 * half + 2, width, chans), BF16)
    flops = 2 * 2 * cells * chans * cols.lead
    stats, acts, cot_t = call(
        partial(act_kernel, order),
        (jax.ShapeDtypeStruct((2, chans), F32), shifted, jax.ShapeDtypeStruct((chans, 2 * cells), BF16)),
        [SMEM_SPEC] * 2 + [VMEM_SPEC] * 6,
        [pltpu.VMEM((chans, 2 * cells), F32)],
        16, flops // 4,
    )(dev, table, latent, lat_far, cot_b, cot_far, gn_gain, gn_shift)
    pieces = call(
        partial(grad_kernel, cols),
        [jax.ShapeDtypeStruct((2 * part, cols.lead), BF16)] * (2 * zs),
        [SMEM_SPEC] + [VMEM_SPEC] * 2,
        [],
        20, flops // 2,
    )(dev, acts, cot_t)
    stages = Stages([2 * zs - 3, 3] if paired else [1], 2 * part if paired else chans)
    staged = paired

    def slopes_of(stats):
        extra = (jax.ShapeDtypeStruct((chans, stages.width), BF16),) if staged else ()
        return call(
            partial(slope_kernel, stages),
            (jax.ShapeDtypeStruct((3, 2 * half + 2, width, stages.width), BF16),
             jax.ShapeDtypeStruct(image, BF16), jax.ShapeDtypeStruct(image, BF16)) + extra,
            [SMEM_SPEC] * 2 + [VMEM_SPEC] * 7,
            [pltpu.VMEM((2 * half, width, stages.width), F32)] if staged else [],
            18, flops // 4,
        )(dev, table, stats, gn_gain, gn_shift, latent, lat_far, cot_b, cot_far)

    total_of = jax.ShapeDtypeStruct((2 * cells, chans), F32)

    def back_first(cots, blocks):
        return call(
            partial(back_kernel, cols, stages, 0), total_of,
            [SMEM_SPEC] + [VMEM_SPEC] * (1 + len(blocks)), [], 20, flops // 4,
        )(dev, cots, *blocks)

    def back_last(cots, earlier, slopes, blocks):
        return call(
            partial(back_kernel, cols, stages, len(stages.counts) - 1), jax.ShapeDtypeStruct((2, chans), F32),
            [SMEM_SPEC] + [VMEM_SPEC] * (3 + len(earlier) + len(blocks)),
            [pltpu.VMEM(total_of.shape, F32)], 24, flops // 4,
        )(dev, cots, *earlier, *slopes, *blocks)

    def conv_first(blocks):
        wide = stages.widths[0]
        return call(
            partial(conv_both_kernel, cols, stages, 0),
            (jax.ShapeDtypeStruct((cells, wide), F32), jax.ShapeDtypeStruct((cells, wide), BF16)),
            [SMEM_SPEC] + [VMEM_SPEC] * (1 + len(blocks)),
            [pltpu.VMEM((2 * cells, wide), F32)], 18, flops // 4,
        )(dev, acts, *blocks)

    def conv_far(blocks):
        wide = stages.widths[-1]
        return call(
            partial(conv_far_kernel, cols, stages, len(stages.counts) - 1),
            jax.ShapeDtypeStruct((cells, wide), BF16),
            [SMEM_SPEC] + [VMEM_SPEC] * (1 + len(blocks)),
            [pltpu.VMEM((cells, wide), F32)], 16, flops // 8,
        )(dev, acts, *blocks)

    def conv_own(got, earlier, blocks):
        return call(
            partial(conv_own_kernel, cols, stages), jax.ShapeDtypeStruct((half, width, chans), BF16),
            [SMEM_SPEC] + [VMEM_SPEC] * (4 + len(earlier) + len(blocks)),
            [pltpu.VMEM((cells, stages.widths[-1]), F32)], 18, flops // 4,
        )(dev, acts, got, latent, conv_bias, *earlier, *blocks)

    def chip_sum(sums):
        vectors = jnp.concatenate([jnp.sum(cotan, axis=(0, 1))[None], sums])
        vectors = params / (4 * zs) - LR_VECTOR * vectors
        return vectors + swap(vectors, "core")

    if paired:
        kept, sent = pieces[::2], list(pieces[1::2])
        up, down, peer, sent[0] = tied(up1, down1, peer, sent[0])
        blocks = [unit, up, down]
        crossed = [swap(piece, "replica") for piece in sent]
        up_sum = down_sum = ()
        for j in range(zs):
            if j < zs - 2:
                up, down = ring.up(up), ring.down(down)
                if j == zs - 3:
                    total_first = back_first(cots, blocks)
                    conv_first_own, conv_send = conv_first(blocks)
                    up, down, crossed[j], total_first, conv_send = tied(
                        up, down, crossed[j], total_first, conv_send
                    )
                    conv_first_got = swap(conv_send, "core")
                    late = [up, down]
                else:
                    blocks += [up, down]
                    up, down, crossed[j], cots, slope, slope_x, order = tied(
                        up, down, crossed[j], *slopes_of(stats)
                    )
                    blocks[-2:] = [up, down]
            elif j == zs - 2:
                halves = ring.up(up[:part]), ring.down(down[part:])
                *halves, crossed[j], conv_first_got = tied(*halves, crossed[j], conv_first_got)
                late += halves
                sums = back_last(cots, [total_first], [slope, slope_x], late)
                conv_got = swap(conv_far(late), "core")
            else:
                crossed[j], sums, *received = tied(crossed[j], sums, *up_sum, *down_sum)
                up_sum, down_sum = tuple(received[:1]), tuple(received[1:])
            ahead = add(kept[j][:part], crossed[j][:part], *up_sum)
            behind = (kept[j][part:], crossed[j][part:], *down_sum)
            up_sum = (ring.up(ahead),)
            if j < zs - 1:
                down_sum = (ring.down(add(*behind)),)
        vectors = sum_over(chip_sum(sums), ("z", "y"), (1, 2))
        last, conv_got, vectors = tied(*up_sum, conv_got, vectors)
        total = add(*behind, last)
        earlier = [conv_first_own, conv_first_got, order]
        a = lax.ppermute(total, ("replica", "core"), [(1, 0), (2, 3), (0, 2), (3, 1)])
        b = lax.ppermute(total, ("replica", "core"), [(1, 2), (2, 1)])
        left = jnp.where(replica == core, jnp.where(lower, total, a), jnp.where(lower, a, b))
        right = jnp.where(replica == core, jnp.where(lower, a, total), jnp.where(lower, b, a))
    else:
        late, earlier = [lax.all_gather(unit, NODE, axis=0, tiled=True)], []
        cots, slope, slope_x = slopes_of(stats)
        sums = back_last(cots, [], [slope, slope_x], late)
        conv_got, vectors = swap(conv_far(late), "core"), chip_sum(sums)
        terms = jnp.concatenate(pieces).reshape(2 * zs, 2, part, cols.lead)
        summed = lax.psum_scatter(terms, NODE, scatter_dimension=0, tiled=False)
        ours = lax.dynamic_index_in_dim(summed, core, 0, keepdims=False)
        got = swap(lax.dynamic_index_in_dim(summed, 1 - core, 0, keepdims=False), "core")
        left, right = jnp.where(lower, ours, got), jnp.where(lower, got, ours)

    def all_columns(left, right):
        return jnp.concatenate([left, right[:, cols.both:]], axis=1).astype(F32)

    kernel_grad = all_columns(left, right)
    if paired:
        peer = all_columns(jnp.where(lower, *peer), jnp.where(lower, *peer[::-1]))
        new_kernel = 0.5 * (shard + peer) - (0.5 * scale * rate) * kernel_grad
    else:
        stepped = shard - (scale * rate) * kernel_grad
        new_kernel = 0.5 * (stepped + from_peer(level, stepped.astype(BF16)).astype(F32))

    block = conv_own(conv_got, earlier, late)
    if paired:
        new_v = 0.5 * sum_over(vectors, ("replica", "z"), (2, zs))
    else:
        stepped_v = lax.psum(vectors, NODE)
        new_v = 0.5 * (stepped_v + from_peer(level, stepped_v))

    return (
        block[None],
        new_kernel[None],
        new_v[0][None],
        new_v[1][None],
        new_v[2][None],
    )


def solution(mesh):
    replicas, shards = mesh.shape["replica"], mesh.shape["shard"]
    split = Mesh(mesh.devices.reshape(replicas, shards // 4, 2, 2), ("replica", "z", "y", "core"))
    shard = ("z", "y", "core")
    return jax.shard_map(
        per_device,
        mesh=split,
        in_specs=(
            P("replica", shard, None, None),
            P("replica", shard, None, None),
            P("replica", shard, None),
            P("replica", None),
            P("replica", None),
            P("replica", None),
            P(),
        ),
        out_specs=(
            P("replica", shard, None, None),
            P("replica", shard, None),
            P("replica", None),
            P("replica", None),
            P("replica", None),
        ),
        check_vma=False,
    )
```

```python
from functools import partial

import jax
import jax.numpy as jnp
import numpy as np
from jax import lax
from jax.experimental import pallas as pl
from jax.experimental.pallas import tpu as pltpu
from jax.sharding import Mesh, PartitionSpec as P

GROUPS = 32
EPS = 1e-05
LR_KERNEL = 0.1
LR_VECTOR = 0.01
LANES = 128
BF16 = jnp.bfloat16
F32 = jnp.float32

SMEM_SPEC = pl.BlockSpec(memory_space=pltpu.SMEM)
VMEM_SPEC = pl.BlockSpec(memory_space=pltpu.VMEM)


class Columns:
    def __init__(self, chans):
        tiles = 9 * chans // LANES
        self.total = 9 * chans
        self.lead = (tiles + 1) // 2 * LANES
        self.start = self.total - self.lead
        self.both = 2 * self.lead - self.total
        self.mid = self.lead - 4 * chans
        self.mid_start = chans - self.mid

    def pair(self, core, k, chans):
        first = jnp.where(core == 0, 2 * k, 5 + 2 * k)
        place = jnp.where(core == 0, 2 * k * chans, self.mid + 2 * k * chans)
        return (first, first + 1), pl.multiple_of(place, LANES)

    def middle(self, core, chans):
        place = jnp.where(core == 0, 4 * chans, 0)
        channel = jnp.where(core == 0, 0, self.mid_start)
        return pl.multiple_of(place, LANES), pl.multiple_of(channel, LANES)


def fill_shifts(shifts, row, values):
    width = values.shape[0]
    at = lax.broadcasted_iota(jnp.int32, values.shape, 0)
    left = jnp.where(at == 0, 0.0, pltpu.roll(values, 1, 0))
    right = jnp.where(at == width - 1, 0.0, pltpu.roll(values, width - 1, 0))
    shifts[0, row] = left.astype(BF16)
    shifts[1, row] = values.astype(BF16)
    shifts[2, row] = right.astype(BF16)


def clear_edges(shifts):
    zero = jnp.zeros(shifts.shape[2:], shifts.dtype)
    for b in range(3):
        shifts[b, 0] = zero
        shifts[b, shifts.shape[1] - 1] = zero


def act_kernel(order, dev, table, lat_own, lat_far, cot_own, cot_far, gain, shift,
               stats, acts, cot_t, cot_f):
    me = dev[0]
    core = me % 2
    half, width, chans = lat_own.shape
    cells = 2 * half * width
    group_width = chans // GROUPS
    own_at = core * half
    far_at = half - own_at
    clear_edges(acts)

    def add_row(i, sums):
        total, square = sums
        a = lat_own[i].astype(F32)
        b = lat_far[i].astype(F32)
        return total + (a + b), square + (a * a + b * b)

    zero = jnp.zeros((width, chans), F32)
    total, square = lax.fori_loop(0, half, add_row, (zero, zero))
    sums = jnp.concatenate(
        [jnp.sum(total, axis=0, keepdims=True), jnp.sum(square, axis=0, keepdims=True),
         jnp.zeros((6, chans), F32)], axis=0
    )
    first = lax.broadcasted_iota(jnp.int32, (chans, LANES), 0)
    start = lax.broadcasted_iota(jnp.int32, (chans, LANES), 1) * group_width
    member = jnp.where((first >= start) & (first < start + group_width), 1.0, 0.0)
    exact = partial(lax.dot_general, precision=lax.Precision.HIGHEST, preferred_element_type=F32)
    sums = exact(sums, member, (((1,), (0,)), ((), ()))) / (cells * group_width)
    sums = exact(sums, member, (((1,), (1,)), ((), ())))
    mean = sums[0:1]
    rstd = lax.rsqrt(sums[1:2] - mean * mean + EPS)
    stats[0:1] = mean
    stats[1:2] = rstd
    gain_v, shift_v = gain[...], shift[...]

    def act_rows(i, _):
        for ref, base in ((lat_own, own_at), (lat_far, far_at)):
            pre = gain_v * ((ref[i].astype(F32) - mean) * rstd) + shift_v
            fill_shifts(acts, base + i + 1, pre * (0.5 + 0.5 * jnp.tanh(0.5 * pre)))
        return 0

    lax.fori_loop(0, half, act_rows, 0)

    chunk = LANES // width
    for ref, base in ((cot_own, own_at), (cot_far, far_at)):
        for i in range(half // chunk):
            piece = ref[i * chunk:(i + 1) * chunk].reshape(LANES, chans).astype(F32)
            place = pl.multiple_of(base * width + i * LANES, LANES)
            if order is None:
                cot_t[:, pl.ds(place, LANES)] = piece.T.astype(BF16)
            else:
                cot_f[:, pl.ds(place, LANES)] = piece.T
    if order is not None:
        first_at, part, count = order
        for q in range(count // 2):
            pair = [
                cot_f[pl.ds(pl.multiple_of(table[me, first_at + 2 * q + i], 8), part)]
                for i in range(2)
            ]
            cot_t[2 * q * part:(2 * q + 2) * part] = jnp.concatenate(pair).astype(BF16)


def grad_kernel(cols, dev, acts, cot_t, *pieces):
    core = dev[0] % 2
    rows, width, chans = acts.shape[1] - 2, acts.shape[2], acts.shape[3]
    cells = rows * width
    count = pieces[0].shape[0]

    def emit(window, place, wide):
        value = jnp.dot(cot_t[...], window, preferred_element_type=F32)
        for q, piece in enumerate(pieces):
            piece[:, pl.ds(place, wide)] = value[q * count:(q + 1) * count].astype(BF16)

    def two_taps(k, _):
        taps, place = cols.pair(core, k, chans)
        windows = [acts[t % 3, pl.ds(t // 3, rows)].reshape(cells, chans) for t in taps]
        emit(jnp.concatenate(windows, axis=1), place, 2 * chans)
        return 0

    lax.fori_loop(0, 2, two_taps, 0)
    place, channel = cols.middle(core, chans)
    emit(acts[1, 1:rows + 1, :, pl.ds(channel, cols.mid)].reshape(cells, cols.mid), place, cols.mid)


class Stages:
    def __init__(self, counts, rows):
        self.rows = rows
        self.counts = counts
        self.widths = [-(-n * rows // LANES) * LANES for n in counts]
        self.starts = [sum(self.widths[:i]) for i in range(len(counts))]
        self.width = sum(self.widths)

    def lanes(self, stage):
        return slice(self.starts[stage], self.starts[stage] + self.widths[stage])

    def columns(self, stage, blocks, place, wide):
        parts = [ref[:, pl.ds(place, wide)] for ref in blocks]
        if len(parts) == self.counts[stage] + 1:
            parts[-2:] = [jnp.concatenate(parts[-2:])]
        spare = self.widths[stage] - self.counts[stage] * self.rows
        if spare:
            parts.append(jnp.zeros((spare, wide), BF16))
        return jnp.concatenate(parts) if len(parts) > 1 else parts[0]

    def order(self, me, table, order, chans):
        lane = lax.broadcasted_iota(jnp.int32, (1, self.width), 1)
        source = jnp.full((1, self.width), -1, jnp.int32)
        at = 0
        for start, count in zip(self.starts, self.counts):
            for i in range(count):
                first = start + i * self.rows
                inside = (lane >= first) & (lane < first + self.rows)
                source = jnp.where(inside, table[me, at] * self.rows + lane - first, source)
                at += 1
        channel = lax.broadcasted_iota(jnp.int32, (chans, self.width), 0)
        order[...] = jnp.where(channel == source, 1.0, 0.0).astype(BF16)


def slope_kernel(stages, dev, table, stats, gain, shift, lat_own, lat_far, cot_own, cot_far,
                 cots, slope, slope_x, *refs):
    me = dev[0]
    core = me % 2
    half, width, chans = lat_own.shape
    clear_edges(cots)
    mean, rstd = stats[0:1], stats[1:2]
    gain_v, shift_v = gain[...], shift[...]
    far_at = half - core * half
    if len(stages.counts) > 1:
        order, placed = refs
        stages.order(me, table, order, chans)
        for ref, base in ((cot_own, core * half), (cot_far, far_at)):
            value = jnp.dot(ref[...].reshape(half * width, chans), order[...], preferred_element_type=F32)
            placed[pl.ds(base, half)] = value.reshape(half, width, stages.width)

    def one_row(i, _):
        for lat, cot, base in ((lat_own, cot_own, core * half), (lat_far, cot_far, far_at)):
            value = placed[base + i] if len(stages.counts) > 1 else cot[i].astype(F32)
            fill_shifts(cots, base + i + 1, value)
            xhat = (lat[i].astype(F32) - mean) * rstd
            pre = gain_v * xhat + shift_v
            sig = 0.5 + 0.5 * jnp.tanh(0.5 * pre)
            value = sig * (1.0 + pre * (1.0 - sig))
            slope[base + i] = value.astype(BF16)
            slope_x[base + i] = (value * xhat).astype(BF16)
        return 0

    lax.fori_loop(0, half, one_row, 0)


def conv_sum(cols, stages, stage, core, first, half, acts, blocks, total):
    width, chans = acts.shape[2:]
    cells = half * width
    nt = (((1,), (1,)), ((), ()))
    place, channel = cols.middle(core, chans)
    window = acts[1, pl.ds(first + 1, half), :, pl.ds(channel, cols.mid)].reshape(cells, cols.mid)
    lane = lax.broadcasted_iota(jnp.int32, window.shape, 1)
    window = jnp.where((core == 1) & (lane < cols.both), jnp.zeros_like(window), window)
    kernel = stages.columns(stage, blocks, place, cols.mid)
    total[...] = lax.dot_general(window, kernel, nt, preferred_element_type=F32)

    def two_taps(k, _):
        taps, place = cols.pair(core, k, chans)
        windows = [acts[t % 3, pl.ds(first + t // 3, half)].reshape(cells, chans) for t in taps]
        kernel = stages.columns(stage, blocks, place, 2 * chans)
        total[...] += lax.dot_general(
            jnp.concatenate(windows, axis=1), kernel, nt, preferred_element_type=F32
        )
        return 0

    lax.fori_loop(0, 2, two_taps, 0)


def conv_both_kernel(cols, stages, stage, dev, acts, *refs):
    blocks, (own, far, total) = refs[:-3], refs[-3:]
    core = dev[0] % 2
    rows = acts.shape[1] - 2
    conv_sum(cols, stages, stage, core, 0, rows, acts, blocks, total)
    half = own.shape[0]
    own[...] = total[pl.ds(pl.multiple_of(core * half, half), half)]
    far[...] = total[pl.ds(pl.multiple_of((1 - core) * half, half), half)].astype(BF16)


def conv_far_kernel(cols, stages, stage, dev, acts, *refs):
    blocks, (far, total) = refs[:-2], refs[-2:]
    core = dev[0] % 2
    half = (acts.shape[1] - 2) // 2
    conv_sum(cols, stages, stage, core, (1 - core) * half, half, acts, blocks, total)
    far[...] = total[...].astype(BF16)


def conv_own_kernel(cols, stages, dev, acts, got, latent, bias, *refs):
    core = dev[0] % 2
    half, width, chans = latent.shape
    scale = cols.total ** (-0.5)
    stage = len(stages.counts) - 1
    before = 3 * stage
    blocks, (block, total) = refs[before:-2], refs[-2:]
    conv_sum(cols, stages, stage, core, core * half, half, acts, blocks, total)
    conv = total[...] + got[...].astype(F32)
    if stage:
        first_own, first_got, order = refs[:before]
        conv = jnp.concatenate([first_own[...] + first_got[...].astype(F32), conv], axis=1)
        high = conv.astype(BF16)
        low = (conv - high.astype(F32)).astype(BF16)
        nt = (((1,), (1,)), ((), ()))
        conv = sum(
            lax.dot_general(value, order[...], nt, preferred_element_type=F32) for value in (low, high)
        )
    conv = scale * conv + bias[...]
    block[...] = (conv.reshape(half, width, chans) + latent[...].astype(F32)).astype(BF16)


def back_kernel(cols, stages, stage, dev, cots, *refs):
    last = stage == len(stages.counts) - 1
    before = (1 if stage else 0) + (2 if last else 0)
    blocks = refs[before:-2] if last else refs[before:-1]
    total = refs[-1]
    core = dev[0] % 2
    rows, width = cots.shape[1] - 2, cots.shape[2]
    cells, chans = total.shape
    lanes = stages.lanes(stage)

    total[...] = refs[0][...] if stage else jnp.zeros_like(total)
    place, channel = cols.middle(core, chans)
    window = cots[1, 1:rows + 1, :, lanes].reshape(cells, stages.widths[stage])
    kernel = stages.columns(stage, blocks, place, cols.mid)
    value = jnp.dot(window, kernel, preferred_element_type=F32)
    lane = lax.broadcasted_iota(jnp.int32, value.shape, 1)
    total[:, pl.ds(channel, cols.mid)] += jnp.where((core == 1) & (lane < cols.both), 0.0, value)

    def taps_from(first, place, count):
        windows, kernels = [], []
        for i in range(count):
            tap = first + i
            window = cots[2 - tap % 3, pl.ds(2 - tap // 3, rows), :, lanes]
            windows.append(window.reshape(cells, stages.widths[stage]))
            kernels.append(stages.columns(stage, blocks, pl.multiple_of(place + i * chans, LANES), chans))
        total[...] += jnp.dot(
            jnp.concatenate(windows, axis=1), jnp.concatenate(kernels), preferred_element_type=F32
        )

    def two_taps(k, _):
        taps, place = cols.pair(core, k, chans)
        taps_from(taps[0], place, 2)
        return 0

    if stage:
        taps, place = cols.pair(core, 0, chans)
        taps_from(taps[0], place, 4)
    else:
        lax.fori_loop(0, 2, two_taps, 0)

    if last:
        slope, slope_x = refs[before - 2:before]
        sums = refs[-2]

        def add_row(i, carry):
            gains, shifts = carry
            value = total[pl.ds(pl.multiple_of(i * width, width), width)]
            return gains + value * slope_x[i].astype(F32), shifts + value * slope[i].astype(F32)

        zero = jnp.zeros((width, chans), F32)
        gains, shifts = lax.fori_loop(0, rows, add_row, (zero, zero))
        scale = cols.total ** (-0.5)
        sums[0:1] = scale * jnp.sum(gains, axis=0, keepdims=True)
        sums[1:2] = scale * jnp.sum(shifts, axis=0, keepdims=True)


NODE = ("z", "y")


def swap(value, axis):
    return lax.ppermute(value, axis, [(0, 1), (1, 0)])


def from_peer(level, value):
    count = lax.axis_size("replica")
    levels = count.bit_length() - 1
    moves = [[(s, (s + (1 << k)) % count) for s in range(count)] for k in range(levels)]
    if levels == 1:
        return lax.ppermute(value, "replica", moves[0])
    return lax.switch(level, [lambda v, m=m: lax.ppermute(v, "replica", m) for m in moves], value)


class Ring:
    def __init__(self, zs):
        self.count = 2 * zs
        self.reach = zs
        self.nodes = [2 * z for z in range(zs)] + [2 * z + 1 for z in reversed(range(zs))]
        ahead = list(zip(self.nodes, self.nodes[1:] + self.nodes[:1]))
        self.ahead = ahead
        self.behind = [(b, a) for a, b in ahead]

    def node(self, at, offset):
        return self.nodes[(at + offset) % self.count]

    def up(self, value):
        return lax.ppermute(value, NODE, self.ahead)

    def down(self, value):
        return lax.ppermute(value, NODE, self.behind)

    def table(self, part):
        rows = np.zeros((2, self.count, 2, 3 * self.count), np.int32)
        for replica in range(2):
            for at, node in enumerate(self.nodes):
                line = [node]
                for k in range(1, self.reach + 1):
                    line.append(self.node(at, -k))
                    if k < self.reach:
                        line.append(self.node(at, k))
                for j in range(self.reach):
                    targets = [self.node(at, self.reach - j), self.node(at, j + 1 - self.reach)]
                    for which in (replica, 1 - replica):
                        line += [(2 * target + which) * part for target in targets]
                rows[replica, node, :] = line
        return rows.reshape(-1, 3 * self.count)


def sum_over(value, axes, masks):
    count = lax.axis_size(axes)
    for mask in (masks[0], masks[1], masks[0] | masks[1]):
        value_in = lax.ppermute(value, axes, [(s, s ^ mask) for s in range(count)])
        total = value_in if mask == masks[0] else total + value_in
    return value + total


def add(*values):
    total = values[0].astype(F32)
    for value in values[1:]:
        total = total + value.astype(F32)
    return total.astype(BF16)


def tied(*values):
    return lax.optimization_barrier(values)


def per_device(latents, cotangent, kernel, conv_bias, gn_gain, gn_shift, step):
    latent, cotan, shard = latents[0], cotangent[0], kernel[0]
    half, width, chans = latent.shape
    part = shard.shape[0]
    cols = Columns(chans)
    cells = half * width
    zs, replicas = lax.axis_size("z"), lax.axis_size("replica")
    core, z, y, replica = (lax.axis_index(a) for a in ("core", "z", "y", "replica"))
    lower = core == 0
    paired = replicas == 2
    ring = Ring(zs)
    scale = cols.total ** (-0.5)
    level = step[0] % (replicas.bit_length() - 1)
    params = jnp.concatenate([conv_bias, gn_gain, gn_shift])
    rate = LR_KERNEL * (1.0 - (step[0] % 1000).astype(F32) / 2000.0)
    dev = (((replica * zs + z) * 2 + y) * 2 + core).reshape(1)

    mine = lax.dynamic_slice_in_dim(shard, core * cols.start, cols.lead, 1).astype(BF16)
    theirs = lax.dynamic_slice_in_dim(shard, (1 - core) * cols.start, cols.lead, 1).astype(BF16)
    got = swap(theirs, "core")
    unit = jnp.where(lower, jnp.concatenate([mine, got]), jnp.concatenate([got, mine]))
    lat_far = swap(latent, "core")
    cot_b = cotan.astype(BF16)
    cot_far = swap(cot_b, "core")

    if paired:
        table = jnp.asarray(ring.table(part))
        order = (ring.count, part, 2 * ring.count)
        up1, down1 = ring.up(unit), ring.down(unit)
        peer = from_peer(level, mine), from_peer(level, theirs)
    else:
        table = jnp.zeros((replicas * zs * 4, 1), jnp.int32)
        order = None

    def call(body, outs, ins, scratch, megabytes, flops):
        return pl.pallas_call(
            body,
            out_shape=outs,
            in_specs=ins,
            out_specs=jax.tree.map(lambda _: VMEM_SPEC, outs),
            scratch_shapes=scratch,
            compiler_params=pltpu.CompilerParams(vmem_limit_bytes=megabytes * 2**20),
            cost_estimate=pl.CostEstimate(flops=flops, bytes_accessed=0, transcendentals=0),
        )

    image = (2 * half, width, chans)
    shifted = jax.ShapeDtypeStruct((3, 2 * half + 2, width, chans), BF16)
    flops = 2 * 2 * cells * chans * cols.lead
    stats, acts, cot_t = call(
        partial(act_kernel, order),
        (jax.ShapeDtypeStruct((2, chans), F32), shifted, jax.ShapeDtypeStruct((chans, 2 * cells), BF16)),
        [SMEM_SPEC] * 2 + [VMEM_SPEC] * 6,
        [pltpu.VMEM((chans, 2 * cells), F32)],
        8, flops // 4,
    )(dev, table, latent, lat_far, cot_b, cot_far, gn_gain, gn_shift)
    pieces = call(
        partial(grad_kernel, cols),
        [jax.ShapeDtypeStruct((2 * part, cols.lead), BF16)] * (2 * zs),
        [SMEM_SPEC] + [VMEM_SPEC] * 2,
        [],
        4, flops // 2,
    )(dev, acts, cot_t)
    stages = Stages([2 * zs - 3, 3] if paired else [1], 2 * part if paired else chans)
    staged = paired

    def slopes_of(stats):
        extra = (jax.ShapeDtypeStruct((chans, stages.width), BF16),) if staged else ()
        return call(
            partial(slope_kernel, stages),
            (jax.ShapeDtypeStruct((3, 2 * half + 2, width, stages.width), BF16),
             jax.ShapeDtypeStruct(image, BF16), jax.ShapeDtypeStruct(image, BF16)) + extra,
            [SMEM_SPEC] * 2 + [VMEM_SPEC] * 7,
            [pltpu.VMEM((2 * half, width, stages.width), F32)] if staged else [],
            8, flops // 4,
        )(dev, table, stats, gn_gain, gn_shift, latent, lat_far, cot_b, cot_far)

    total_of = jax.ShapeDtypeStruct((2 * cells, chans), F32)

    def back_first(cots, blocks):
        return call(
            partial(back_kernel, cols, stages, 0), total_of,
            [SMEM_SPEC] + [VMEM_SPEC] * (1 + len(blocks)), [], 4, flops // 4,
        )(dev, cots, *blocks)

    def back_last(cots, earlier, slopes, blocks):
        return call(
            partial(back_kernel, cols, stages, len(stages.counts) - 1), jax.ShapeDtypeStruct((2, chans), F32),
            [SMEM_SPEC] + [VMEM_SPEC] * (3 + len(earlier) + len(blocks)),
            [pltpu.VMEM(total_of.shape, F32)], 8, flops // 4,
        )(dev, cots, *earlier, *slopes, *blocks)

    def conv_first(blocks):
        wide = stages.widths[0]
        return call(
            partial(conv_both_kernel, cols, stages, 0),
            (jax.ShapeDtypeStruct((cells, wide), F32), jax.ShapeDtypeStruct((cells, wide), BF16)),
            [SMEM_SPEC] + [VMEM_SPEC] * (1 + len(blocks)),
            [pltpu.VMEM((2 * cells, wide), F32)], 6, flops // 4,
        )(dev, acts, *blocks)

    def conv_far(blocks):
        wide = stages.widths[-1]
        return call(
            partial(conv_far_kernel, cols, stages, len(stages.counts) - 1),
            jax.ShapeDtypeStruct((cells, wide), BF16),
            [SMEM_SPEC] + [VMEM_SPEC] * (1 + len(blocks)),
            [pltpu.VMEM((cells, wide), F32)], 4, flops // 8,
        )(dev, acts, *blocks)

    def conv_own(got, earlier, blocks):
        return call(
            partial(conv_own_kernel, cols, stages), jax.ShapeDtypeStruct((half, width, chans), BF16),
            [SMEM_SPEC] + [VMEM_SPEC] * (4 + len(earlier) + len(blocks)),
            [pltpu.VMEM((cells, stages.widths[-1]), F32)], 8, flops // 4,
        )(dev, acts, got, latent, conv_bias, *earlier, *blocks)

    def chip_sum(sums):
        vectors = jnp.concatenate([jnp.sum(cotan, axis=(0, 1))[None], sums])
        vectors = params / (4 * zs) - LR_VECTOR * vectors
        return vectors + swap(vectors, "core")

    if paired:
        kept, sent = pieces[::2], list(pieces[1::2])
        up, down, peer, sent[0] = tied(up1, down1, peer, sent[0])
        blocks = [unit, up, down]
        crossed = [swap(piece, "replica") for piece in sent]
        up_sum = down_sum = ()
        for j in range(zs):
            if j < zs - 2:
                up, down = ring.up(up), ring.down(down)
                if j == zs - 3:
                    total_first = back_first(cots, blocks)
                    conv_first_own, conv_send = conv_first(blocks)
                    up, down, crossed[j], total_first, conv_send = tied(
                        up, down, crossed[j], total_first, conv_send
                    )
                    conv_first_got = swap(conv_send, "core")
                    late = [up, down]
                else:
                    blocks += [up, down]
                    up, down, crossed[j], cots, slope, slope_x, order = tied(
                        up, down, crossed[j], *slopes_of(stats)
                    )
                    blocks[-2:] = [up, down]
            elif j == zs - 2:
                halves = ring.up(up[:part]), ring.down(down[part:])
                *halves, crossed[j], conv_first_got = tied(*halves, crossed[j], conv_first_got)
                late += halves
                sums = back_last(cots, [total_first], [slope, slope_x], late)
                conv_got = swap(conv_far(late), "core")
            else:
                crossed[j], sums, *received = tied(crossed[j], sums, *up_sum, *down_sum)
                up_sum, down_sum = tuple(received[:1]), tuple(received[1:])
            ahead = add(kept[j][:part], crossed[j][:part], *up_sum)
            behind = (kept[j][part:], crossed[j][part:], *down_sum)
            up_sum = (ring.up(ahead),)
            if j < zs - 1:
                down_sum = (ring.down(add(*behind)),)
        vectors = sum_over(chip_sum(sums), ("z", "y"), (1, 2))
        last, conv_got, vectors = tied(*up_sum, conv_got, vectors)
        total = add(*behind, last)
        earlier = [conv_first_own, conv_first_got, order]
        a = lax.ppermute(total, ("replica", "core"), [(1, 0), (2, 3), (0, 2), (3, 1)])
        b = lax.ppermute(total, ("replica", "core"), [(1, 2), (2, 1)])
        left = jnp.where(replica == core, jnp.where(lower, total, a), jnp.where(lower, a, b))
        right = jnp.where(replica == core, jnp.where(lower, a, total), jnp.where(lower, b, a))
    else:
        late, earlier = [lax.all_gather(unit, NODE, axis=0, tiled=True)], []
        cots, slope, slope_x = slopes_of(stats)
        sums = back_last(cots, [], [slope, slope_x], late)
        conv_got, vectors = swap(conv_far(late), "core"), chip_sum(sums)
        terms = jnp.concatenate(pieces).reshape(2 * zs, 2, part, cols.lead)
        summed = lax.psum_scatter(terms, NODE, scatter_dimension=0, tiled=False)
        ours = lax.dynamic_index_in_dim(summed, core, 0, keepdims=False)
        got = swap(lax.dynamic_index_in_dim(summed, 1 - core, 0, keepdims=False), "core")
        left, right = jnp.where(lower, ours, got), jnp.where(lower, got, ours)

    def all_columns(left, right):
        return jnp.concatenate([left, right[:, cols.both:]], axis=1).astype(F32)

    kernel_grad = all_columns(left, right)
    if paired:
        peer = all_columns(jnp.where(lower, *peer), jnp.where(lower, *peer[::-1]))
        new_kernel = 0.5 * (shard + peer) - (0.5 * scale * rate) * kernel_grad
    else:
        stepped = shard - (scale * rate) * kernel_grad
        new_kernel = 0.5 * (stepped + from_peer(level, stepped.astype(BF16)).astype(F32))

    block = conv_own(conv_got, earlier, late)
    if paired:
        new_v = 0.5 * sum_over(vectors, ("replica", "z"), (2, zs))
    else:
        stepped_v = lax.psum(vectors, NODE)
        new_v = 0.5 * (stepped_v + from_peer(level, stepped_v))

    return (
        block[None],
        new_kernel[None],
        new_v[0][None],
        new_v[1][None],
        new_v[2][None],
    )


def solution(mesh):
    replicas, shards = mesh.shape["replica"], mesh.shape["shard"]
    split = Mesh(mesh.devices.reshape(replicas, shards // 4, 2, 2), ("replica", "z", "y", "core"))
    shard = ("z", "y", "core")
    return jax.shard_map(
        per_device,
        mesh=split,
        in_specs=(
            P("replica", shard, None, None),
            P("replica", shard, None, None),
            P("replica", shard, None),
            P("replica", None),
            P("replica", None),
            P("replica", None),
            P(),
        ),
        out_specs=(
            P("replica", shard, None, None),
            P("replica", shard, None),
            P("replica", None),
            P("replica", None),
            P("replica", None),
        ),
        check_vma=False,
    )
```

```python
from functools import partial

import jax
import jax.numpy as jnp
import numpy as np
from jax import lax
from jax.experimental import pallas as pl
from jax.experimental.pallas import tpu as pltpu
from jax.sharding import Mesh, PartitionSpec as P

GROUPS = 32
EPS = 1e-05
LR_KERNEL = 0.1
LR_VECTOR = 0.01
LANES = 128
BF16 = jnp.bfloat16
F32 = jnp.float32

SMEM_SPEC = pl.BlockSpec(memory_space=pltpu.SMEM)
VMEM_SPEC = pl.BlockSpec(memory_space=pltpu.VMEM)


class Columns:
    def __init__(self, chans):
        tiles = 9 * chans // LANES
        self.total = 9 * chans
        self.lead = (tiles + 1) // 2 * LANES
        self.start = self.total - self.lead
        self.both = 2 * self.lead - self.total
        self.mid = self.lead - 4 * chans
        self.mid_start = chans - self.mid

    def pair(self, core, k, chans):
        first = jnp.where(core == 0, 2 * k, 5 + 2 * k)
        place = jnp.where(core == 0, 2 * k * chans, self.mid + 2 * k * chans)
        return (first, first + 1), pl.multiple_of(place, LANES)

    def middle(self, core, chans):
        place = jnp.where(core == 0, 4 * chans, 0)
        channel = jnp.where(core == 0, 0, self.mid_start)
        return pl.multiple_of(place, LANES), pl.multiple_of(channel, LANES)


def fill_shifts(shifts, row, values):
    width = values.shape[0]
    at = lax.broadcasted_iota(jnp.int32, values.shape, 0)
    left = jnp.where(at == 0, 0.0, pltpu.roll(values, 1, 0))
    right = jnp.where(at == width - 1, 0.0, pltpu.roll(values, width - 1, 0))
    shifts[0, row] = left.astype(BF16)
    shifts[1, row] = values.astype(BF16)
    shifts[2, row] = right.astype(BF16)


def clear_edges(shifts):
    zero = jnp.zeros(shifts.shape[2:], shifts.dtype)
    for b in range(3):
        shifts[b, 0] = zero
        shifts[b, shifts.shape[1] - 1] = zero


def act_kernel(order, dev, table, lat_own, lat_far, cot_own, cot_far, gain, shift,
               stats, acts, cot_t, cot_f):
    me = dev[0]
    core = me % 2
    half, width, chans = lat_own.shape
    cells = 2 * half * width
    group_width = chans // GROUPS
    own_at = core * half
    far_at = half - own_at
    clear_edges(acts)

    def add_row(i, sums):
        total, square = sums
        a = lat_own[i].astype(F32)
        b = lat_far[i].astype(F32)
        return total + (a + b), square + (a * a + b * b)

    zero = jnp.zeros((width, chans), F32)
    total, square = lax.fori_loop(0, half, add_row, (zero, zero))
    sums = jnp.concatenate(
        [jnp.sum(total, axis=0, keepdims=True), jnp.sum(square, axis=0, keepdims=True),
         jnp.zeros((6, chans), F32)], axis=0
    )
    first = lax.broadcasted_iota(jnp.int32, (chans, LANES), 0)
    start = lax.broadcasted_iota(jnp.int32, (chans, LANES), 1) * group_width
    member = jnp.where((first >= start) & (first < start + group_width), 1.0, 0.0)
    exact = partial(lax.dot_general, precision=lax.Precision.HIGHEST, preferred_element_type=F32)
    sums = exact(sums, member, (((1,), (0,)), ((), ()))) / (cells * group_width)
    sums = exact(sums, member, (((1,), (1,)), ((), ())))
    mean = sums[0:1]
    rstd = lax.rsqrt(sums[1:2] - mean * mean + EPS)
    stats[0:1] = mean
    stats[1:2] = rstd
    gain_v, shift_v = gain[...], shift[...]

    def act_rows(i, _):
        for ref, base in ((lat_own, own_at), (lat_far, far_at)):
            pre = gain_v * ((ref[i].astype(F32) - mean) * rstd) + shift_v
            fill_shifts(acts, base + i + 1, pre * (0.5 + 0.5 * jnp.tanh(0.5 * pre)))
        return 0

    lax.fori_loop(0, half, act_rows, 0)

    chunk = LANES // width
    for ref, base in ((cot_own, own_at), (cot_far, far_at)):
        for i in range(half // chunk):
            piece = ref[i * chunk:(i + 1) * chunk].reshape(LANES, chans).astype(F32)
            place = pl.multiple_of(base * width + i * LANES, LANES)
            if order is None:
                cot_t[:, pl.ds(place, LANES)] = piece.T.astype(BF16)
            else:
                cot_f[:, pl.ds(place, LANES)] = piece.T
    if order is not None:
        first_at, part, count = order
        for q in range(count // 2):
            pair = [
                cot_f[pl.ds(pl.multiple_of(table[me, first_at + 2 * q + i], 8), part)]
                for i in range(2)
            ]
            cot_t[2 * q * part:(2 * q + 2) * part] = jnp.concatenate(pair).astype(BF16)


def grad_kernel(cols, dev, acts, cot_t, *pieces):
    core = dev[0] % 2
    rows, width, chans = acts.shape[1] - 2, acts.shape[2], acts.shape[3]
    cells = rows * width
    count = pieces[0].shape[0]

    def emit(window, place, wide):
        value = jnp.dot(cot_t[...], window, preferred_element_type=F32)
        for q, piece in enumerate(pieces):
            piece[:, pl.ds(place, wide)] = value[q * count:(q + 1) * count].astype(BF16)

    def two_taps(k, _):
        taps, place = cols.pair(core, k, chans)
        windows = [acts[t % 3, pl.ds(t // 3, rows)].reshape(cells, chans) for t in taps]
        emit(jnp.concatenate(windows, axis=1), place, 2 * chans)
        return 0

    lax.fori_loop(0, 2, two_taps, 0)
    place, channel = cols.middle(core, chans)
    emit(acts[1, 1:rows + 1, :, pl.ds(channel, cols.mid)].reshape(cells, cols.mid), place, cols.mid)


class Stages:
    def __init__(self, counts, rows):
        self.rows = rows
        self.counts = counts
        self.widths = [-(-n * rows // LANES) * LANES for n in counts]
        self.starts = [sum(self.widths[:i]) for i in range(len(counts))]
        self.width = sum(self.widths)

    def lanes(self, stage):
        return slice(self.starts[stage], self.starts[stage] + self.widths[stage])

    def columns(self, stage, blocks, place, wide):
        parts = [ref[:, pl.ds(place, wide)] for ref in blocks]
        if len(parts) == self.counts[stage] + 1:
            parts[-2:] = [jnp.concatenate(parts[-2:])]
        spare = self.widths[stage] - self.counts[stage] * self.rows
        if spare:
            parts.append(jnp.zeros((spare, wide), BF16))
        return jnp.concatenate(parts) if len(parts) > 1 else parts[0]

    def order(self, me, table, order, chans):
        lane = lax.broadcasted_iota(jnp.int32, (1, self.width), 1)
        source = jnp.full((1, self.width), -1, jnp.int32)
        at = 0
        for start, count in zip(self.starts, self.counts):
            for i in range(count):
                first = start + i * self.rows
                inside = (lane >= first) & (lane < first + self.rows)
                source = jnp.where(inside, table[me, at] * self.rows + lane - first, source)
                at += 1
        channel = lax.broadcasted_iota(jnp.int32, (chans, self.width), 0)
        order[...] = jnp.where(channel == source, 1.0, 0.0).astype(BF16)


def slope_kernel(stages, dev, table, stats, gain, shift, lat_own, lat_far, cot_own, cot_far,
                 cots, slope, slope_x, *refs):
    me = dev[0]
    core = me % 2
    half, width, chans = lat_own.shape
    clear_edges(cots)
    mean, rstd = stats[0:1], stats[1:2]
    gain_v, shift_v = gain[...], shift[...]
    far_at = half - core * half
    if len(stages.counts) > 1:
        order, placed = refs
        stages.order(me, table, order, chans)
        for ref, base in ((cot_own, core * half), (cot_far, far_at)):
            value = jnp.dot(ref[...].reshape(half * width, chans), order[...], preferred_element_type=F32)
            placed[pl.ds(base, half)] = value.reshape(half, width, stages.width)

    def one_row(i, _):
        for lat, cot, base in ((lat_own, cot_own, core * half), (lat_far, cot_far, far_at)):
            value = placed[base + i] if len(stages.counts) > 1 else cot[i].astype(F32)
            fill_shifts(cots, base + i + 1, value)
            xhat = (lat[i].astype(F32) - mean) * rstd
            pre = gain_v * xhat + shift_v
            sig = 0.5 + 0.5 * jnp.tanh(0.5 * pre)
            value = sig * (1.0 + pre * (1.0 - sig))
            slope[base + i] = value.astype(BF16)
            slope_x[base + i] = (value * xhat).astype(BF16)
        return 0

    lax.fori_loop(0, half, one_row, 0)


def conv_sum(cols, stages, stage, core, first, half, acts, blocks, total):
    width, chans = acts.shape[2:]
    cells = half * width
    nt = (((1,), (1,)), ((), ()))
    place, channel = cols.middle(core, chans)
    window = acts[1, pl.ds(first + 1, half), :, pl.ds(channel, cols.mid)].reshape(cells, cols.mid)
    lane = lax.broadcasted_iota(jnp.int32, window.shape, 1)
    window = jnp.where((core == 1) & (lane < cols.both), jnp.zeros_like(window), window)
    kernel = stages.columns(stage, blocks, place, cols.mid)
    total[...] = lax.dot_general(window, kernel, nt, preferred_element_type=F32)

    def two_taps(k, _):
        taps, place = cols.pair(core, k, chans)
        windows = [acts[t % 3, pl.ds(first + t // 3, half)].reshape(cells, chans) for t in taps]
        kernel = stages.columns(stage, blocks, place, 2 * chans)
        total[...] += lax.dot_general(
            jnp.concatenate(windows, axis=1), kernel, nt, preferred_element_type=F32
        )
        return 0

    lax.fori_loop(0, 2, two_taps, 0)


def conv_both_kernel(cols, stages, stage, dev, acts, *refs):
    blocks, (own, far, total) = refs[:-3], refs[-3:]
    core = dev[0] % 2
    rows = acts.shape[1] - 2
    conv_sum(cols, stages, stage, core, 0, rows, acts, blocks, total)
    half = own.shape[0]
    own[...] = total[pl.ds(pl.multiple_of(core * half, half), half)]
    far[...] = total[pl.ds(pl.multiple_of((1 - core) * half, half), half)].astype(BF16)


def conv_far_kernel(cols, stages, stage, dev, acts, *refs):
    blocks, (far, total) = refs[:-2], refs[-2:]
    core = dev[0] % 2
    half = (acts.shape[1] - 2) // 2
    conv_sum(cols, stages, stage, core, (1 - core) * half, half, acts, blocks, total)
    far[...] = total[...].astype(BF16)


def conv_own_kernel(cols, stages, dev, acts, got, latent, bias, *refs):
    core = dev[0] % 2
    half, width, chans = latent.shape
    scale = cols.total ** (-0.5)
    stage = len(stages.counts) - 1
    before = 3 * stage
    blocks, (block, total) = refs[before:-2], refs[-2:]
    conv_sum(cols, stages, stage, core, core * half, half, acts, blocks, total)
    conv = total[...] + got[...].astype(F32)
    if stage:
        first_own, first_got, order = refs[:before]
        conv = jnp.concatenate([first_own[...] + first_got[...].astype(F32), conv], axis=1)
        high = conv.astype(BF16)
        low = (conv - high.astype(F32)).astype(BF16)
        nt = (((1,), (1,)), ((), ()))
        conv = sum(
            lax.dot_general(value, order[...], nt, preferred_element_type=F32) for value in (low, high)
        )
    conv = scale * conv + bias[...]
    block[...] = (conv.reshape(half, width, chans) + latent[...].astype(F32)).astype(BF16)


def back_kernel(cols, stages, stage, dev, cots, slope, slope_x, *refs):
    blocks, (sums, total) = refs[:-2], refs[-2:]
    core = dev[0] % 2
    rows, width = cots.shape[1] - 2, cots.shape[2]
    cells, chans = total.shape
    lanes = stages.lanes(stage)

    def taps_from(first, place, count):
        windows, kernels = [], []
        for i in range(count):
            tap = first + i
            window = cots[2 - tap % 3, pl.ds(2 - tap // 3, rows), :, lanes]
            windows.append(window.reshape(cells, stages.widths[stage]))
            kernels.append(stages.columns(stage, blocks, pl.multiple_of(place + i * chans, LANES), chans))
        return jnp.dot(
            jnp.concatenate(windows, axis=1), jnp.concatenate(kernels), preferred_element_type=F32
        )

    if stages.widths[stage] * 4 <= 2 * chans:
        taps, place = cols.pair(core, 0, chans)
        total[...] = taps_from(taps[0], place, 4)
    else:
        total[...] = jnp.zeros_like(total)

        def two_taps(k, _):
            taps, place = cols.pair(core, k, chans)
            total[...] += taps_from(taps[0], place, 2)
            return 0

        lax.fori_loop(0, 2, two_taps, 0)

    place, channel = cols.middle(core, chans)
    window = cots[1, 1:rows + 1, :, lanes].reshape(cells, stages.widths[stage])
    kernel = stages.columns(stage, blocks, place, cols.mid)
    value = jnp.dot(window, kernel, preferred_element_type=F32)
    lane = lax.broadcasted_iota(jnp.int32, value.shape, 1)
    total[:, pl.ds(channel, cols.mid)] += jnp.where((core == 1) & (lane < cols.both), 0.0, value)

    def add_row(i, carry):
        gains, shifts = carry
        value = total[pl.ds(pl.multiple_of(i * width, width), width)]
        return gains + value * slope_x[i].astype(F32), shifts + value * slope[i].astype(F32)

    zero = jnp.zeros((width, chans), F32)
    gains, shifts = lax.fori_loop(0, rows, add_row, (zero, zero))
    scale = cols.total ** (-0.5)
    sums[0:1] = scale * jnp.sum(gains, axis=0, keepdims=True)
    sums[1:2] = scale * jnp.sum(shifts, axis=0, keepdims=True)


def finish_kernel(cols, dev, step, shard, mine, theirs, total, across, aside, out):
    me = dev[0]
    core = me % 2
    same = me // (dev[1] // 2) == core
    lower = core == 0
    rate = LR_KERNEL * (1.0 - (step[0] % 1000).astype(F32) / 2000.0)
    factor = 0.5 * cols.total ** (-0.5) * rate
    total, across, aside = (ref[...].astype(F32) for ref in (total, across, aside))
    left = jnp.where(same, jnp.where(lower, total, across), jnp.where(lower, across, aside))
    right = jnp.where(same, jnp.where(lower, across, total), jnp.where(lower, aside, across))
    mine, theirs = mine[...].astype(F32), theirs[...].astype(F32)
    peer_left, peer_right = jnp.where(lower, mine, theirs), jnp.where(lower, theirs, mine)
    out[:, :cols.lead] = 0.5 * (shard[:, :cols.lead] + peer_left) - factor * left
    out[:, cols.lead:] = (
        0.5 * (shard[:, cols.lead:] + peer_right[:, cols.both:]) - factor * right[:, cols.both:]
    )


NODE = ("z", "y")


def swap(value, axis):
    return lax.ppermute(value, axis, [(0, 1), (1, 0)])


def from_peer(level, value):
    count = lax.axis_size("replica")
    levels = count.bit_length() - 1
    moves = [[(s, (s + (1 << k)) % count) for s in range(count)] for k in range(levels)]
    if levels == 1:
        return lax.ppermute(value, "replica", moves[0])
    return lax.switch(level, [lambda v, m=m: lax.ppermute(v, "replica", m) for m in moves], value)


class Ring:
    def __init__(self, zs):
        self.count = 2 * zs
        self.reach = zs
        self.nodes = [2 * z for z in range(zs)] + [2 * z + 1 for z in reversed(range(zs))]
        ahead = list(zip(self.nodes, self.nodes[1:] + self.nodes[:1]))
        self.ahead = ahead
        self.behind = [(b, a) for a, b in ahead]

    def node(self, at, offset):
        return self.nodes[(at + offset) % self.count]

    def up(self, value):
        return lax.ppermute(value, NODE, self.ahead)

    def down(self, value):
        return lax.ppermute(value, NODE, self.behind)

    def table(self, part):
        rows = np.zeros((2, self.count, 2, 3 * self.count), np.int32)
        for replica in range(2):
            for at, node in enumerate(self.nodes):
                line = [node]
                for k in range(1, self.reach + 1):
                    line.append(self.node(at, -k))
                    if k < self.reach:
                        line.append(self.node(at, k))
                for j in range(self.reach):
                    targets = [self.node(at, self.reach - j), self.node(at, j + 1 - self.reach)]
                    for which in (replica, 1 - replica):
                        line += [(2 * target + which) * part for target in targets]
                rows[replica, node, :] = line
        return rows.reshape(-1, 3 * self.count)


def hop(value, axis, mask):
    count = lax.axis_size(axis)
    return value + lax.ppermute(value, axis, [(s, s ^ mask) for s in range(count)])


def add(*values):
    total = values[0].astype(F32)
    for value in values[1:]:
        total = total + value.astype(F32)
    return total.astype(BF16)


def tied(*values):
    return lax.optimization_barrier(values)


def per_device(latents, cotangent, kernel, conv_bias, gn_gain, gn_shift, step):
    latent, cotan, shard = latents[0], cotangent[0], kernel[0]
    half, width, chans = latent.shape
    part = shard.shape[0]
    cols = Columns(chans)
    cells = half * width
    zs, replicas = lax.axis_size("z"), lax.axis_size("replica")
    core, z, y, replica = (lax.axis_index(a) for a in ("core", "z", "y", "replica"))
    lower = core == 0
    paired = replicas == 2
    ring = Ring(zs)
    scale = cols.total ** (-0.5)
    params = jnp.concatenate([conv_bias, gn_gain, gn_shift])
    me = ((replica * zs + z) * 2 + y) * 2 + core
    core, lower, me = tied(core, lower, me)
    dev = jnp.stack([me, jnp.int32(4 * zs * replicas)])

    mine = lax.dynamic_slice_in_dim(shard, core * cols.start, cols.lead, 1).astype(BF16)
    theirs = lax.dynamic_slice_in_dim(shard, (1 - core) * cols.start, cols.lead, 1).astype(BF16)
    got = swap(theirs, "core")
    unit = jnp.where(lower, jnp.concatenate([mine, got]), jnp.concatenate([got, mine]))
    lat_far = swap(latent, "core")
    cot_b = cotan.astype(BF16)
    cot_far = swap(cot_b, "core")

    if paired:
        table = jnp.asarray(ring.table(part))
        order = (ring.count, part, 2 * ring.count)
        up1, down1 = ring.up(unit), ring.down(unit)
        peer = swap(mine, "replica"), swap(theirs, "replica")
    else:
        table = jnp.zeros((replicas * zs * 4, 1), jnp.int32)
        order = None

    def call(body, outs, ins, scratch, megabytes, flops):
        return pl.pallas_call(
            body,
            out_shape=outs,
            in_specs=ins,
            out_specs=jax.tree.map(lambda _: VMEM_SPEC, outs),
            scratch_shapes=scratch,
            compiler_params=pltpu.CompilerParams(vmem_limit_bytes=megabytes * 2**20),
            cost_estimate=pl.CostEstimate(flops=flops, bytes_accessed=0, transcendentals=0),
        )

    image = (2 * half, width, chans)
    shifted = jax.ShapeDtypeStruct((3, 2 * half + 2, width, chans), BF16)
    flops = 2 * 2 * cells * chans * cols.lead
    stats, acts, cot_t = call(
        partial(act_kernel, order),
        (jax.ShapeDtypeStruct((2, chans), F32), shifted, jax.ShapeDtypeStruct((chans, 2 * cells), BF16)),
        [SMEM_SPEC] * 2 + [VMEM_SPEC] * 6,
        [pltpu.VMEM((chans, 2 * cells), F32)],
        8, flops // 4,
    )(dev, table, latent, lat_far, cot_b, cot_far, gn_gain, gn_shift)
    pieces = call(
        partial(grad_kernel, cols),
        [jax.ShapeDtypeStruct((2 * part, cols.lead), BF16)] * (2 * zs),
        [SMEM_SPEC] + [VMEM_SPEC] * 2,
        [],
        4, flops // 2,
    )(dev, acts, cot_t)
    stages = Stages([2 * zs - 3, 3] if paired else [1], 2 * part if paired else chans)
    staged = paired

    def slopes_of(stats):
        extra = (jax.ShapeDtypeStruct((chans, stages.width), BF16),) if staged else ()
        return call(
            partial(slope_kernel, stages),
            (jax.ShapeDtypeStruct((3, 2 * half + 2, width, stages.width), BF16),
             jax.ShapeDtypeStruct(image, BF16), jax.ShapeDtypeStruct(image, BF16)) + extra,
            [SMEM_SPEC] * 2 + [VMEM_SPEC] * 7,
            [pltpu.VMEM((2 * half, width, stages.width), F32)] if staged else [],
            8, flops // 4,
        )(dev, table, stats, gn_gain, gn_shift, latent, lat_far, cot_b, cot_far)

    def back(stage, cots, slopes, blocks):
        return call(
            partial(back_kernel, cols, stages, stage), jax.ShapeDtypeStruct((2, chans), F32),
            [SMEM_SPEC] + [VMEM_SPEC] * (3 + len(blocks)),
            [pltpu.VMEM((2 * cells, chans), F32)], 8, flops // 4,
        )(dev, cots, *slopes, *blocks)

    def conv_first(blocks):
        wide = stages.widths[0]
        return call(
            partial(conv_both_kernel, cols, stages, 0),
            (jax.ShapeDtypeStruct((cells, wide), F32), jax.ShapeDtypeStruct((cells, wide), BF16)),
            [SMEM_SPEC] + [VMEM_SPEC] * (1 + len(blocks)),
            [pltpu.VMEM((2 * cells, wide), F32)], 6, flops // 4,
        )(dev, acts, *blocks)

    def conv_far(acts, blocks):
        wide = stages.widths[-1]
        return call(
            partial(conv_far_kernel, cols, stages, len(stages.counts) - 1),
            jax.ShapeDtypeStruct((cells, wide), BF16),
            [SMEM_SPEC] + [VMEM_SPEC] * (1 + len(blocks)),
            [pltpu.VMEM((cells, wide), F32)], 4, flops // 8,
        )(dev, acts, *blocks)

    def conv_own(got, earlier, blocks):
        return call(
            partial(conv_own_kernel, cols, stages), jax.ShapeDtypeStruct((half, width, chans), BF16),
            [SMEM_SPEC] + [VMEM_SPEC] * (4 + len(earlier) + len(blocks)),
            [pltpu.VMEM((cells, stages.widths[-1]), F32)], 8, flops // 4,
        )(dev, acts, got, latent, conv_bias, *earlier, *blocks)

    def chip_sum(sums):
        vectors = jnp.concatenate([jnp.sum(cotan, axis=(0, 1))[None], sums])
        vectors = params / (4 * zs) - LR_VECTOR * vectors
        return vectors + swap(vectors, "core")

    if paired:
        kept, sent = pieces[::2], list(pieces[1::2])
        up, down, peer, sent[0] = tied(up1, down1, peer, sent[0])
        blocks = [unit, up, down]
        crossed = [swap(piece, "replica") for piece in sent]
        up_sum = down_sum = ()
        for j in range(zs):
            if j < zs - 2:
                up, down = ring.up(up), ring.down(down)
                if j < zs - 3:
                    up, down, cots, *slopes, order = tied(up, down, *slopes_of(stats))
                    blocks += [up, down]
                    crossed[j] = tied(crossed[j], up)[0]
                else:
                    cots, crossed[j - 1] = tied(cots, crossed[j - 1])
                    first_sums = back(0, cots, slopes, blocks)
                    conv_first_own, conv_send = conv_first(blocks)
                    up, down, crossed[j], first_sums, conv_send = tied(
                        up, down, crossed[j], first_sums, conv_send
                    )
                    conv_first_got = swap(conv_send, "core")
                    late = [up, down]
            elif j == zs - 2:
                halves = ring.up(up[:part]), ring.down(down[part:])
                *halves, crossed[j], conv_first_got = tied(*halves, crossed[j], conv_first_got)
                late += halves
                sums = back(1, cots, slopes, late)
            else:
                crossed[j], sums, acts, *received = tied(crossed[j], sums, acts, *up_sum, *down_sum)
                up_sum, down_sum = tuple(received[:1]), tuple(received[1:])
                conv_got = swap(conv_far(acts, late), "core")
            ahead = add(kept[j][:part], crossed[j][:part], *up_sum)
            behind = (kept[j][part:], crossed[j][part:], *down_sum)
            up_sum = (ring.up(ahead),)
            if j < zs - 1:
                down_sum = (ring.down(add(*behind)),)
        vectors = hop(hop(chip_sum(first_sums + sums), "y", 1), "z", 1)
        last, conv_got, vectors = tied(*up_sum, conv_got, vectors)
        total = add(*behind, last)
        earlier = [conv_first_own, conv_first_got, order]
        across = lax.ppermute(total, ("replica", "core"), [(1, 0), (2, 3), (0, 2), (3, 1)])
        aside = lax.ppermute(total, ("replica", "core"), [(1, 2), (2, 1)])
        new_kernel = call(
            partial(finish_kernel, cols), jax.ShapeDtypeStruct(shard.shape, F32),
            [SMEM_SPEC] * 2 + [VMEM_SPEC] * 6, [], 8, flops // 16,
        )(dev, step, shard, *peer, total, across, aside)
        vectors = hop(vectors, "z", 2)
        new_v = 0.5 * hop(vectors, "replica", 1)
    else:
        late, earlier = [lax.all_gather(unit, NODE, axis=0, tiled=True)], []
        cots, slope, slope_x = slopes_of(stats)
        sums = back(0, cots, [slope, slope_x], late)
        conv_got, vectors = swap(conv_far(acts, late), "core"), chip_sum(sums)
        terms = jnp.concatenate(pieces).reshape(2 * zs, 2, part, cols.lead)
        summed = lax.psum_scatter(terms, NODE, scatter_dimension=0, tiled=False)
        ours = lax.dynamic_index_in_dim(summed, core, 0, keepdims=False)
        got = swap(lax.dynamic_index_in_dim(summed, 1 - core, 0, keepdims=False), "core")
        left, right = jnp.where(lower, ours, got), jnp.where(lower, got, ours)
        kernel_grad = jnp.concatenate([left, right[:, cols.both:]], axis=1).astype(F32)
        level = step[0] % (replicas.bit_length() - 1)
        rate = LR_KERNEL * (1.0 - (step[0] % 1000).astype(F32) / 2000.0)
        stepped = shard - (scale * rate) * kernel_grad
        new_kernel = 0.5 * (stepped + from_peer(level, stepped.astype(BF16)).astype(F32))
        stepped_v = lax.psum(vectors, NODE)
        new_v = 0.5 * (stepped_v + from_peer(level, stepped_v))

    block = conv_own(conv_got, earlier, late)
    return (
        block[None],
        new_kernel[None],
        new_v[0][None],
        new_v[1][None],
        new_v[2][None],
    )


def solution(mesh):
    replicas, shards = mesh.shape["replica"], mesh.shape["shard"]
    split = Mesh(mesh.devices.reshape(replicas, shards // 4, 2, 2), ("replica", "z", "y", "core"))
    shard = ("z", "y", "core")
    return jax.shard_map(
        per_device,
        mesh=split,
        in_specs=(
            P("replica", shard, None, None),
            P("replica", shard, None, None),
            P("replica", shard, None),
            P("replica", None),
            P("replica", None),
            P("replica", None),
            P(),
        ),
        out_specs=(
            P("replica", shard, None, None),
            P("replica", shard, None),
            P("replica", None),
            P("replica", None),
            P("replica", None),
        ),
        check_vma=False,
    )
```

```python
from functools import partial

import jax
import jax.numpy as jnp
import numpy as np
from jax import lax
from jax.experimental import pallas as pl
from jax.experimental.pallas import tpu as pltpu
from jax.sharding import Mesh, PartitionSpec as P

GROUPS = 32
EPS = 1e-05
LR_KERNEL = 0.1
LR_VECTOR = 0.01
LANES = 128
BF16 = jnp.bfloat16
F32 = jnp.float32

SMEM_SPEC = pl.BlockSpec(memory_space=pltpu.SMEM)
VMEM_SPEC = pl.BlockSpec(memory_space=pltpu.VMEM)


class Columns:
    def __init__(self, chans):
        tiles = 9 * chans // LANES
        self.total = 9 * chans
        self.lead = (tiles + 1) // 2 * LANES
        self.start = self.total - self.lead
        self.both = 2 * self.lead - self.total
        self.mid = self.lead - 4 * chans
        self.mid_start = chans - self.mid

    def pair(self, core, k, chans):
        first = jnp.where(core == 0, 2 * k, 5 + 2 * k)
        place = jnp.where(core == 0, 2 * k * chans, self.mid + 2 * k * chans)
        return (first, first + 1), pl.multiple_of(place, LANES)

    def middle(self, core, chans):
        place = jnp.where(core == 0, 4 * chans, 0)
        channel = jnp.where(core == 0, 0, self.mid_start)
        return pl.multiple_of(place, LANES), pl.multiple_of(channel, LANES)


def fill_shifts(shifts, row, values):
    width = values.shape[0]
    at = lax.broadcasted_iota(jnp.int32, values.shape, 0)
    left = jnp.where(at == 0, 0.0, pltpu.roll(values, 1, 0))
    right = jnp.where(at == width - 1, 0.0, pltpu.roll(values, width - 1, 0))
    shifts[0, row] = left.astype(BF16)
    shifts[1, row] = values.astype(BF16)
    shifts[2, row] = right.astype(BF16)


def clear_edges(shifts):
    zero = jnp.zeros(shifts.shape[2:], shifts.dtype)
    for b in range(3):
        shifts[b, 0] = zero
        shifts[b, shifts.shape[1] - 1] = zero


def act_kernel(order, dev, table, lat_own, lat_far, cot_own, cot_far, gain, shift,
               stats, acts, cot_t, cot_f):
    me = dev[0]
    core = me % 2
    half, width, chans = lat_own.shape
    cells = 2 * half * width
    group_width = chans // GROUPS
    own_at = core * half
    far_at = half - own_at
    clear_edges(acts)

    def add_row(i, sums):
        total, square = sums
        a = lat_own[i].astype(F32)
        b = lat_far[i].astype(F32)
        return total + (a + b), square + (a * a + b * b)

    zero = jnp.zeros((width, chans), F32)
    total, square = lax.fori_loop(0, half, add_row, (zero, zero))
    sums = jnp.concatenate(
        [jnp.sum(total, axis=0, keepdims=True), jnp.sum(square, axis=0, keepdims=True),
         jnp.zeros((6, chans), F32)], axis=0
    )
    first = lax.broadcasted_iota(jnp.int32, (chans, LANES), 0)
    start = lax.broadcasted_iota(jnp.int32, (chans, LANES), 1) * group_width
    member = jnp.where((first >= start) & (first < start + group_width), 1.0, 0.0)
    exact = partial(lax.dot_general, precision=lax.Precision.HIGHEST, preferred_element_type=F32)
    sums = exact(sums, member, (((1,), (0,)), ((), ()))) / (cells * group_width)
    sums = exact(sums, member, (((1,), (1,)), ((), ())))
    mean = sums[0:1]
    rstd = lax.rsqrt(sums[1:2] - mean * mean + EPS)
    stats[0:1] = mean
    stats[1:2] = rstd
    gain_v, shift_v = gain[...], shift[...]

    def act_rows(i, _):
        for ref, base in ((lat_own, own_at), (lat_far, far_at)):
            pre = gain_v * ((ref[i].astype(F32) - mean) * rstd) + shift_v
            fill_shifts(acts, base + i + 1, pre * (0.5 + 0.5 * jnp.tanh(0.5 * pre)))
        return 0

    lax.fori_loop(0, half, act_rows, 0)

    chunk = LANES // width
    for ref, base in ((cot_own, own_at), (cot_far, far_at)):
        for i in range(half // chunk):
            piece = ref[i * chunk:(i + 1) * chunk].reshape(LANES, chans).astype(F32)
            place = pl.multiple_of(base * width + i * LANES, LANES)
            if order is None:
                cot_t[:, pl.ds(place, LANES)] = piece.T.astype(BF16)
            else:
                cot_f[:, pl.ds(place, LANES)] = piece.T
    if order is not None:
        first_at, part, count = order
        for q in range(count // 2):
            pair = [
                cot_f[pl.ds(pl.multiple_of(table[me, first_at + 2 * q + i], 8), part)]
                for i in range(2)
            ]
            cot_t[2 * q * part:(2 * q + 2) * part] = jnp.concatenate(pair).astype(BF16)


def grad_kernel(cols, dev, acts, cot_t, *pieces):
    core = dev[0] % 2
    rows, width, chans = acts.shape[1] - 2, acts.shape[2], acts.shape[3]
    cells = rows * width

    def emit(window, place, wide):
        value = jnp.dot(cot_t[...], window, preferred_element_type=F32)
        at = 0
        for piece in pieces:
            piece[:, pl.ds(place, wide)] = value[at:at + piece.shape[0]].astype(BF16)
            at += piece.shape[0]

    def two_taps(k, _):
        taps, place = cols.pair(core, k, chans)
        windows = [acts[t % 3, pl.ds(t // 3, rows)].reshape(cells, chans) for t in taps]
        emit(jnp.concatenate(windows, axis=1), place, 2 * chans)
        return 0

    lax.fori_loop(0, 2, two_taps, 0)
    place, channel = cols.middle(core, chans)
    emit(acts[1, 1:rows + 1, :, pl.ds(channel, cols.mid)].reshape(cells, cols.mid), place, cols.mid)


class Stages:
    def __init__(self, counts, rows):
        self.rows = rows
        self.counts = counts
        self.widths = [-(-n * rows // LANES) * LANES for n in counts]
        self.starts = [sum(self.widths[:i]) for i in range(len(counts))]
        self.width = sum(self.widths)

    def lanes(self, stage):
        return slice(self.starts[stage], self.starts[stage] + self.widths[stage])

    def columns(self, stage, blocks, place, wide):
        parts = [ref[:, pl.ds(place, wide)] for ref in blocks]
        if len(parts) == self.counts[stage] + 1:
            parts[-2:] = [jnp.concatenate(parts[-2:])]
        spare = self.widths[stage] - self.counts[stage] * self.rows
        if spare:
            parts.append(jnp.zeros((spare, wide), BF16))
        return jnp.concatenate(parts) if len(parts) > 1 else parts[0]

    def order(self, me, table, order, chans):
        lane = lax.broadcasted_iota(jnp.int32, (1, self.width), 1)
        source = jnp.full((1, self.width), -1, jnp.int32)
        at = 0
        for start, count in zip(self.starts, self.counts):
            for i in range(count):
                first = start + i * self.rows
                inside = (lane >= first) & (lane < first + self.rows)
                source = jnp.where(inside, table[me, at] * self.rows + lane - first, source)
                at += 1
        channel = lax.broadcasted_iota(jnp.int32, (chans, self.width), 0)
        order[...] = jnp.where(channel == source, 1.0, 0.0).astype(BF16)


def slope_kernel(stages, dev, table, stats, gain, shift, lat_own, lat_far, cot_own, cot_far,
                 cots, slope, slope_x, *refs):
    me = dev[0]
    core = me % 2
    half, width, chans = lat_own.shape
    clear_edges(cots)
    mean, rstd = stats[0:1], stats[1:2]
    gain_v, shift_v = gain[...], shift[...]
    far_at = half - core * half
    if len(stages.counts) > 1:
        order, placed = refs
        stages.order(me, table, order, chans)
        for ref, base in ((cot_own, core * half), (cot_far, far_at)):
            value = jnp.dot(ref[...].reshape(half * width, chans), order[...], preferred_element_type=F32)
            placed[pl.ds(base, half)] = value.reshape(half, width, stages.width)

    def one_row(i, _):
        for lat, cot, base in ((lat_own, cot_own, core * half), (lat_far, cot_far, far_at)):
            value = placed[base + i] if len(stages.counts) > 1 else cot[i].astype(F32)
            fill_shifts(cots, base + i + 1, value)
            xhat = (lat[i].astype(F32) - mean) * rstd
            pre = gain_v * xhat + shift_v
            sig = 0.5 + 0.5 * jnp.tanh(0.5 * pre)
            value = sig * (1.0 + pre * (1.0 - sig))
            slope[base + i] = value.astype(BF16)
            slope_x[base + i] = (value * xhat).astype(BF16)
        return 0

    lax.fori_loop(0, half, one_row, 0)


def conv_sum(cols, stages, stage, core, first, half, acts, blocks, total):
    width, chans = acts.shape[2:]
    cells = half * width
    nt = (((1,), (1,)), ((), ()))
    place, channel = cols.middle(core, chans)
    window = acts[1, pl.ds(first + 1, half), :, pl.ds(channel, cols.mid)].reshape(cells, cols.mid)
    lane = lax.broadcasted_iota(jnp.int32, window.shape, 1)
    window = jnp.where((core == 1) & (lane < cols.both), jnp.zeros_like(window), window)
    kernel = stages.columns(stage, blocks, place, cols.mid)
    total[...] = lax.dot_general(window, kernel, nt, preferred_element_type=F32)

    def two_taps(k, _):
        taps, place = cols.pair(core, k, chans)
        windows = [acts[t % 3, pl.ds(first + t // 3, half)].reshape(cells, chans) for t in taps]
        kernel = stages.columns(stage, blocks, place, 2 * chans)
        total[...] += lax.dot_general(
            jnp.concatenate(windows, axis=1), kernel, nt, preferred_element_type=F32
        )
        return 0

    lax.fori_loop(0, 2, two_taps, 0)


def conv_both_kernel(cols, stages, stage, dev, acts, *refs):
    blocks, (own, far, total) = refs[:-3], refs[-3:]
    core = dev[0] % 2
    rows = acts.shape[1] - 2
    conv_sum(cols, stages, stage, core, 0, rows, acts, blocks, total)
    half = own.shape[0]
    own[...] = total[pl.ds(pl.multiple_of(core * half, half), half)]
    far[...] = total[pl.ds(pl.multiple_of((1 - core) * half, half), half)].astype(BF16)


def conv_far_kernel(cols, stages, stage, dev, acts, *refs):
    blocks, (far, total) = refs[:-2], refs[-2:]
    core = dev[0] % 2
    half = (acts.shape[1] - 2) // 2
    conv_sum(cols, stages, stage, core, (1 - core) * half, half, acts, blocks, total)
    far[...] = total[...].astype(BF16)


def conv_own_kernel(cols, stages, dev, acts, got, latent, bias, *refs):
    core = dev[0] % 2
    half, width, chans = latent.shape
    scale = cols.total ** (-0.5)
    stage = len(stages.counts) - 1
    before = 3 * stage
    blocks, (block, total) = refs[before:-2], refs[-2:]
    conv_sum(cols, stages, stage, core, core * half, half, acts, blocks, total)
    conv = total[...] + got[...].astype(F32)
    if stage:
        first_own, first_got, order = refs[:before]
        conv = jnp.concatenate([first_own[...] + first_got[...].astype(F32), conv], axis=1)
        high = conv.astype(BF16)
        low = (conv - high.astype(F32)).astype(BF16)
        nt = (((1,), (1,)), ((), ()))
        conv = sum(
            lax.dot_general(value, order[...], nt, preferred_element_type=F32) for value in (low, high)
        )
    conv = scale * conv + bias[...]
    block[...] = (conv.reshape(half, width, chans) + latent[...].astype(F32)).astype(BF16)


def back_kernel(cols, stages, stage, dev, cots, slope, slope_x, *refs):
    blocks, (sums, total) = refs[:-2], refs[-2:]
    core = dev[0] % 2
    rows, width = cots.shape[1] - 2, cots.shape[2]
    cells, chans = total.shape
    lanes = stages.lanes(stage)

    def taps_from(first, place, count):
        windows, kernels = [], []
        for i in range(count):
            tap = first + i
            window = cots[2 - tap % 3, pl.ds(2 - tap // 3, rows), :, lanes]
            windows.append(window.reshape(cells, stages.widths[stage]))
            kernels.append(stages.columns(stage, blocks, pl.multiple_of(place + i * chans, LANES), chans))
        return jnp.dot(
            jnp.concatenate(windows, axis=1), jnp.concatenate(kernels), preferred_element_type=F32
        )

    if stages.widths[stage] * 4 <= 2 * chans:
        taps, place = cols.pair(core, 0, chans)
        total[...] = taps_from(taps[0], place, 4)
    else:
        total[...] = jnp.zeros_like(total)

        def two_taps(k, _):
            taps, place = cols.pair(core, k, chans)
            total[...] += taps_from(taps[0], place, 2)
            return 0

        lax.fori_loop(0, 2, two_taps, 0)

    place, channel = cols.middle(core, chans)
    window = cots[1, 1:rows + 1, :, lanes].reshape(cells, stages.widths[stage])
    kernel = stages.columns(stage, blocks, place, cols.mid)
    value = jnp.dot(window, kernel, preferred_element_type=F32)
    lane = lax.broadcasted_iota(jnp.int32, value.shape, 1)
    total[:, pl.ds(channel, cols.mid)] += jnp.where((core == 1) & (lane < cols.both), 0.0, value)

    def add_row(i, carry):
        gains, shifts = carry
        value = total[pl.ds(pl.multiple_of(i * width, width), width)]
        return gains + value * slope_x[i].astype(F32), shifts + value * slope[i].astype(F32)

    zero = jnp.zeros((width, chans), F32)
    gains, shifts = lax.fori_loop(0, rows, add_row, (zero, zero))
    scale = cols.total ** (-0.5)
    sums[0:1] = scale * jnp.sum(gains, axis=0, keepdims=True)
    sums[1:2] = scale * jnp.sum(shifts, axis=0, keepdims=True)


def finish_kernel(cols, dev, step, shard, mine, theirs, ours, aside, out):
    lower = dev[0] % 2 == 0
    rate = LR_KERNEL * (1.0 - (step[0] % 1000).astype(F32) / 2000.0)
    factor = 0.5 * cols.total ** (-0.5) * rate
    here = 0.5 * mine[...].astype(F32) - factor * ours[...].astype(F32)
    there = 0.5 * theirs[...].astype(F32) - factor * aside[...].astype(F32)
    left, right = jnp.where(lower, here, there), jnp.where(lower, there, here)
    out[:, :cols.lead] = 0.5 * shard[:, :cols.lead] + left
    out[:, cols.lead:] = 0.5 * shard[:, cols.lead:] + right[:, cols.both:]


NODE = ("z", "y")


def swap(value, axis):
    return lax.ppermute(value, axis, [(0, 1), (1, 0)])


def from_peer(level, value):
    count = lax.axis_size("replica")
    levels = count.bit_length() - 1
    moves = [[(s, (s + (1 << k)) % count) for s in range(count)] for k in range(levels)]
    if levels == 1:
        return lax.ppermute(value, "replica", moves[0])
    return lax.switch(level, [lambda v, m=m: lax.ppermute(v, "replica", m) for m in moves], value)


class Ring:
    def __init__(self, zs):
        self.count = 2 * zs
        self.reach = zs
        self.nodes = [2 * z for z in range(zs)] + [2 * z + 1 for z in reversed(range(zs))]
        ahead = list(zip(self.nodes, self.nodes[1:] + self.nodes[:1]))
        self.ahead = ahead
        self.behind = [(b, a) for a, b in ahead]

    def node(self, at, offset):
        return self.nodes[(at + offset) % self.count]

    def up(self, value):
        return lax.ppermute(value, NODE, self.ahead)

    def down(self, value):
        return lax.ppermute(value, NODE, self.behind)

    def table(self, part):
        rows = np.zeros((2, self.count, 2, 3 * self.count), np.int32)
        for replica in range(2):
            for at, node in enumerate(self.nodes):
                line = [node]
                for k in range(1, self.reach + 1):
                    line.append(self.node(at, -k))
                    if k < self.reach:
                        line.append(self.node(at, k))
                for which in (replica, 1 - replica):
                    for j in range(self.reach):
                        targets = [self.node(at, self.reach - j), self.node(at, j + 1 - self.reach)]
                        line += [(2 * target + which) * part for target in targets]
                rows[replica, node, :] = line
        return rows.reshape(-1, 3 * self.count)


def hop(value, axis, mask):
    count = lax.axis_size(axis)
    return value + lax.ppermute(value, axis, [(s, s ^ mask) for s in range(count)])


def add(*values):
    total = values[0].astype(F32)
    for value in values[1:]:
        total = total + value.astype(F32)
    return total.astype(BF16)


def tied(*values):
    return lax.optimization_barrier(values)


def per_device(latents, cotangent, kernel, conv_bias, gn_gain, gn_shift, step):
    latent, cotan, shard = latents[0], cotangent[0], kernel[0]
    half, width, chans = latent.shape
    part = shard.shape[0]
    cols = Columns(chans)
    cells = half * width
    zs, replicas = lax.axis_size("z"), lax.axis_size("replica")
    core, z, y, replica = (lax.axis_index(a) for a in ("core", "z", "y", "replica"))
    lower = core == 0
    paired = replicas == 2
    ring = Ring(zs)
    scale = cols.total ** (-0.5)
    params = jnp.concatenate([conv_bias, gn_gain, gn_shift])
    me = ((replica * zs + z) * 2 + y) * 2 + core
    core, lower, same, me = tied(core, lower, replica == core, me)
    dev = me.reshape(1)

    mine = lax.dynamic_slice_in_dim(shard, core * cols.start, cols.lead, 1).astype(BF16)
    theirs = lax.dynamic_slice_in_dim(shard, (1 - core) * cols.start, cols.lead, 1).astype(BF16)
    got = swap(theirs, "core")
    unit = jnp.where(lower, jnp.concatenate([mine, got]), jnp.concatenate([got, mine]))
    lat_far = swap(latent, "core")
    cot_b = cotan.astype(BF16)
    cot_far = swap(cot_b, "core")

    if paired:
        table = jnp.asarray(ring.table(part))
        order = (ring.count, part, 2 * ring.count)
        up1, down1 = ring.up(unit), ring.down(unit)
        peer = swap(mine, "replica"), swap(theirs, "replica")
    else:
        table = jnp.zeros((replicas * zs * 4, 1), jnp.int32)
        order = None

    def call(body, outs, ins, scratch, megabytes, flops):
        return pl.pallas_call(
            body,
            out_shape=outs,
            in_specs=ins,
            out_specs=jax.tree.map(lambda _: VMEM_SPEC, outs),
            scratch_shapes=scratch,
            compiler_params=pltpu.CompilerParams(vmem_limit_bytes=megabytes * 2**20),
            cost_estimate=pl.CostEstimate(flops=flops, bytes_accessed=0, transcendentals=0),
        )

    image = (2 * half, width, chans)
    shifted = jax.ShapeDtypeStruct((3, 2 * half + 2, width, chans), BF16)
    flops = 2 * 2 * cells * chans * cols.lead
    stats, acts, cot_t = call(
        partial(act_kernel, order),
        (jax.ShapeDtypeStruct((2, chans), F32), shifted, jax.ShapeDtypeStruct((chans, 2 * cells), BF16)),
        [SMEM_SPEC] * 2 + [VMEM_SPEC] * 6,
        [pltpu.VMEM((chans, 2 * cells), F32)],
        8, flops // 4,
    )(dev, table, latent, lat_far, cot_b, cot_far, gn_gain, gn_shift)
    counts = [zs, 1, zs - 2, 1] if paired else [2 * zs]
    pieces = call(
        partial(grad_kernel, cols),
        [jax.ShapeDtypeStruct((n * 2 * part, cols.lead), BF16) for n in counts],
        [SMEM_SPEC] + [VMEM_SPEC] * 2,
        [],
        4, flops // 2,
    )(dev, acts, cot_t)
    stages = Stages([2 * zs - 3, 3] if paired else [1], 2 * part if paired else chans)
    staged = paired

    def slopes_of(stats):
        extra = (jax.ShapeDtypeStruct((chans, stages.width), BF16),) if staged else ()
        return call(
            partial(slope_kernel, stages),
            (jax.ShapeDtypeStruct((3, 2 * half + 2, width, stages.width), BF16),
             jax.ShapeDtypeStruct(image, BF16), jax.ShapeDtypeStruct(image, BF16)) + extra,
            [SMEM_SPEC] * 2 + [VMEM_SPEC] * 7,
            [pltpu.VMEM((2 * half, width, stages.width), F32)] if staged else [],
            8, flops // 4,
        )(dev, table, stats, gn_gain, gn_shift, latent, lat_far, cot_b, cot_far)

    def back(stage, cots, slopes, blocks):
        return call(
            partial(back_kernel, cols, stages, stage), jax.ShapeDtypeStruct((2, chans), F32),
            [SMEM_SPEC] + [VMEM_SPEC] * (3 + len(blocks)),
            [pltpu.VMEM((2 * cells, chans), F32)], 8, flops // 4,
        )(dev, cots, *slopes, *blocks)

    def conv_first(blocks):
        wide = stages.widths[0]
        return call(
            partial(conv_both_kernel, cols, stages, 0),
            (jax.ShapeDtypeStruct((cells, wide), F32), jax.ShapeDtypeStruct((cells, wide), BF16)),
            [SMEM_SPEC] + [VMEM_SPEC] * (1 + len(blocks)),
            [pltpu.VMEM((2 * cells, wide), F32)], 6, flops // 4,
        )(dev, acts, *blocks)

    def conv_far(acts, blocks):
        wide = stages.widths[-1]
        return call(
            partial(conv_far_kernel, cols, stages, len(stages.counts) - 1),
            jax.ShapeDtypeStruct((cells, wide), BF16),
            [SMEM_SPEC] + [VMEM_SPEC] * (1 + len(blocks)),
            [pltpu.VMEM((cells, wide), F32)], 4, flops // 8,
        )(dev, acts, *blocks)

    def conv_own(got, earlier, blocks):
        return call(
            partial(conv_own_kernel, cols, stages), jax.ShapeDtypeStruct((half, width, chans), BF16),
            [SMEM_SPEC] + [VMEM_SPEC] * (4 + len(earlier) + len(blocks)),
            [pltpu.VMEM((cells, stages.widths[-1]), F32)], 8, flops // 4,
        )(dev, acts, got, latent, conv_bias, *earlier, *blocks)

    def chip_sum(sums):
        vectors = jnp.concatenate([jnp.sum(cotan, axis=(0, 1))[None], sums])
        vectors = params / (4 * zs) - LR_VECTOR * vectors
        return vectors + swap(vectors, "core")

    if paired:
        kept, *sent = pieces
        up, down, sent[0], mine, theirs = tied(up1, down1, sent[0], *peer)
        blocks = [unit, up, down]
        first, middle, final = (swap(piece, "replica") for piece in sent)
        up, down = ring.up(up), ring.down(down)
        up, down, cots, *slopes, order = tied(up, down, *slopes_of(stats))
        blocks += [up, down]

        def ring_step(j, crossed, *received):
            rows = slice(2 * j * part, (2 * j + 2) * part)
            parts = kept[rows], crossed
            ahead, behind = (tuple(x[half] for x in parts) for half in (slice(part), slice(part, None)))
            up_sum = ring.up(add(*ahead, *received[:1]))
            if j < zs - 1:
                return up_sum, ring.down(add(*behind, *received[1:]))
            return up_sum, behind + tuple(received[1:])

        up, down = ring.up(up), ring.down(down)
        conv_first_own, conv_send = conv_first(blocks)
        first, conv_send = tied(first, conv_send)
        received = ring_step(0, first)
        up, down, conv_send = tied(up, down, conv_send)
        late = [up, down]

        halves = ring.up(up[:part]), ring.down(down[part:])
        conv_first_got = swap(conv_send, "core")
        cots, conv_send = tied(cots, conv_send)
        middle, first_sums = tied(middle, back(0, cots, slopes, blocks))
        for j in range(1, zs - 2):
            received = ring_step(j, middle[(2 * j - 2) * part:2 * j * part], *received)
        *halves, conv_first_got = tied(*halves, conv_first_got)
        late += halves

        sums = back(1, cots, slopes, late)
        middle, sums, *received = tied(middle, sums, *received)
        acts_last, *_ = tied(acts, sums, *received)
        received = ring_step(zs - 2, middle[(2 * zs - 6) * part:], *received)
        conv_got = swap(conv_far(acts_last, late), "core")
        vectors = hop(chip_sum(first_sums + sums), "replica", 1)
        final, conv_got, *received = tied(final, conv_got, *received)
        last, behind = ring_step(zs - 1, final, *received)
        block = conv_own(conv_got, [conv_first_own, conv_first_got, order], late)
        last, block, vectors = tied(last, block, vectors)
        total = add(*behind, last)
        across = swap(total, "replica")
        ours, others = jnp.where(same, total, across), jnp.where(same, across, total)
        aside = swap(others, "core")
        new_kernel = call(
            partial(finish_kernel, cols), jax.ShapeDtypeStruct(shard.shape, F32),
            [SMEM_SPEC] * 2 + [VMEM_SPEC] * 5, [], 8, flops // 16,
        )(dev, step, shard, mine, theirs, ours, aside)
        vectors = hop(vectors, "z", 1)
        vectors = hop(vectors, "y", 1)
        reach = 2
        while reach < zs:
            vectors = hop(vectors, "z", reach)
            reach *= 2
        new_v = 0.5 * vectors
    else:
        late = [lax.all_gather(unit, NODE, axis=0, tiled=True)]
        cots, slope, slope_x = slopes_of(stats)
        sums = back(0, cots, [slope, slope_x], late)
        vectors = chip_sum(sums)
        block = conv_own(swap(conv_far(acts, late), "core"), [], late)
        terms = pieces[0].reshape(2 * zs, 2, part, cols.lead)
        summed = lax.psum_scatter(terms, NODE, scatter_dimension=0, tiled=False)
        ours = lax.dynamic_index_in_dim(summed, core, 0, keepdims=False)
        got = swap(lax.dynamic_index_in_dim(summed, 1 - core, 0, keepdims=False), "core")
        left, right = jnp.where(lower, ours, got), jnp.where(lower, got, ours)
        kernel_grad = jnp.concatenate([left, right[:, cols.both:]], axis=1).astype(F32)
        level = step[0] % (replicas.bit_length() - 1)
        rate = LR_KERNEL * (1.0 - (step[0] % 1000).astype(F32) / 2000.0)
        stepped = shard - (scale * rate) * kernel_grad
        new_kernel = 0.5 * (stepped + from_peer(level, stepped.astype(BF16)).astype(F32))
        stepped_v = lax.psum(vectors, NODE)
        new_v = 0.5 * (stepped_v + from_peer(level, stepped_v))

    return (
        block[None],
        new_kernel[None],
        new_v[0][None],
        new_v[1][None],
        new_v[2][None],
    )


def solution(mesh):
    replicas, shards = mesh.shape["replica"], mesh.shape["shard"]
    split = Mesh(mesh.devices.reshape(replicas, shards // 4, 2, 2), ("replica", "z", "y", "core"))
    shard = ("z", "y", "core")
    return jax.shard_map(
        per_device,
        mesh=split,
        in_specs=(
            P("replica", shard, None, None),
            P("replica", shard, None, None),
            P("replica", shard, None),
            P("replica", None),
            P("replica", None),
            P("replica", None),
            P(),
        ),
        out_specs=(
            P("replica", shard, None, None),
            P("replica", shard, None),
            P("replica", None),
            P("replica", None),
            P("replica", None),
        ),
        check_vma=False,
    )
```

```python
from functools import partial

import jax
import jax.numpy as jnp
import numpy as np
from jax import lax
from jax.experimental import pallas as pl
from jax.experimental.pallas import tpu as pltpu
from jax.sharding import Mesh, PartitionSpec as P

GROUPS = 32
EPS = 1e-05
LR_KERNEL = 0.1
LR_VECTOR = 0.01
LANES = 128
BF16 = jnp.bfloat16
F32 = jnp.float32

SMEM_SPEC = pl.BlockSpec(memory_space=pltpu.SMEM)
VMEM_SPEC = pl.BlockSpec(memory_space=pltpu.VMEM)


class Columns:
    def __init__(self, chans):
        tiles = 9 * chans // LANES
        self.total = 9 * chans
        self.lead = (tiles + 1) // 2 * LANES
        self.start = self.total - self.lead
        self.both = 2 * self.lead - self.total
        self.mid = self.lead - 4 * chans
        self.mid_start = chans - self.mid

    def pair(self, core, k, chans):
        first = jnp.where(core == 0, 2 * k, 5 + 2 * k)
        place = jnp.where(core == 0, 2 * k * chans, self.mid + 2 * k * chans)
        return (first, first + 1), pl.multiple_of(place, LANES)

    def middle(self, core, chans):
        place = jnp.where(core == 0, 4 * chans, 0)
        channel = jnp.where(core == 0, 0, self.mid_start)
        return pl.multiple_of(place, LANES), pl.multiple_of(channel, LANES)


def fill_shifts(shifts, row, values):
    width = values.shape[0]
    at = lax.broadcasted_iota(jnp.int32, values.shape, 0)
    left = jnp.where(at == 0, 0.0, pltpu.roll(values, 1, 0))
    right = jnp.where(at == width - 1, 0.0, pltpu.roll(values, width - 1, 0))
    shifts[0, row] = left.astype(BF16)
    shifts[1, row] = values.astype(BF16)
    shifts[2, row] = right.astype(BF16)


def clear_edges(shifts):
    zero = jnp.zeros(shifts.shape[2:], shifts.dtype)
    for b in range(3):
        shifts[b, 0] = zero
        shifts[b, shifts.shape[1] - 1] = zero


def act_kernel(order, dev, table, lat_own, lat_far, cot_own, cot_far, gain, shift,
               stats, acts, cot_t, cot_f):
    me = dev[0]
    core = me % 2
    half, width, chans = lat_own.shape
    cells = 2 * half * width
    group_width = chans // GROUPS
    own_at = core * half
    far_at = half - own_at
    clear_edges(acts)

    def add_row(i, sums):
        total, square = sums
        a = lat_own[i].astype(F32)
        b = lat_far[i].astype(F32)
        return total + (a + b), square + (a * a + b * b)

    zero = jnp.zeros((width, chans), F32)
    total, square = lax.fori_loop(0, half, add_row, (zero, zero))
    sums = jnp.concatenate(
        [jnp.sum(total, axis=0, keepdims=True), jnp.sum(square, axis=0, keepdims=True),
         jnp.zeros((6, chans), F32)], axis=0
    )
    first = lax.broadcasted_iota(jnp.int32, (chans, LANES), 0)
    start = lax.broadcasted_iota(jnp.int32, (chans, LANES), 1) * group_width
    member = jnp.where((first >= start) & (first < start + group_width), 1.0, 0.0)
    exact = partial(lax.dot_general, precision=lax.Precision.HIGHEST, preferred_element_type=F32)
    sums = exact(sums, member, (((1,), (0,)), ((), ()))) / (cells * group_width)
    sums = exact(sums, member, (((1,), (1,)), ((), ())))
    mean = sums[0:1]
    rstd = lax.rsqrt(sums[1:2] - mean * mean + EPS)
    stats[0:1] = mean
    stats[1:2] = rstd
    gain_v, shift_v = gain[...], shift[...]

    def act_rows(i, _):
        for ref, base in ((lat_own, own_at), (lat_far, far_at)):
            pre = gain_v * ((ref[i].astype(F32) - mean) * rstd) + shift_v
            fill_shifts(acts, base + i + 1, pre * (0.5 + 0.5 * jnp.tanh(0.5 * pre)))
        return 0

    lax.fori_loop(0, half, act_rows, 0)

    chunk = LANES // width
    for ref, base in ((cot_own, own_at), (cot_far, far_at)):
        for i in range(half // chunk):
            piece = ref[i * chunk:(i + 1) * chunk].reshape(LANES, chans).astype(F32)
            place = pl.multiple_of(base * width + i * LANES, LANES)
            if order is None:
                cot_t[:, pl.ds(place, LANES)] = piece.T.astype(BF16)
            else:
                cot_f[:, pl.ds(place, LANES)] = piece.T
    if order is not None:
        first_at, part, count = order
        for q in range(count // 2):
            pair = [
                cot_f[pl.ds(pl.multiple_of(table[me, first_at + 2 * q + i], 8), part)]
                for i in range(2)
            ]
            cot_t[2 * q * part:(2 * q + 2) * part] = jnp.concatenate(pair).astype(BF16)


def grad_kernel(cols, dev, acts, cot_t, *pieces):
    core = dev[0] % 2
    rows, width, chans = acts.shape[1] - 2, acts.shape[2], acts.shape[3]
    cells = rows * width

    def emit(window, place, wide):
        value = jnp.dot(cot_t[...], window, preferred_element_type=F32)
        at = 0
        for piece in pieces:
            piece[:, pl.ds(place, wide)] = value[at:at + piece.shape[0]].astype(BF16)
            at += piece.shape[0]

    def two_taps(k, _):
        taps, place = cols.pair(core, k, chans)
        windows = [acts[t % 3, pl.ds(t // 3, rows)].reshape(cells, chans) for t in taps]
        emit(jnp.concatenate(windows, axis=1), place, 2 * chans)
        return 0

    lax.fori_loop(0, 2, two_taps, 0)
    place, channel = cols.middle(core, chans)
    emit(acts[1, 1:rows + 1, :, pl.ds(channel, cols.mid)].reshape(cells, cols.mid), place, cols.mid)


class Stages:
    def __init__(self, counts, rows):
        self.rows = rows
        self.counts = counts
        self.widths = [-(-n * rows // LANES) * LANES for n in counts]
        self.starts = [sum(self.widths[:i]) for i in range(len(counts))]
        self.width = sum(self.widths)

    def lanes(self, stage):
        return slice(self.starts[stage], self.starts[stage] + self.widths[stage])

    def columns(self, stage, blocks, place, wide):
        parts = [ref[:, pl.ds(place, wide)] for ref in blocks]
        if len(parts) == self.counts[stage] + 1:
            parts[-2:] = [jnp.concatenate(parts[-2:])]
        spare = self.widths[stage] - self.counts[stage] * self.rows
        if spare:
            parts.append(jnp.zeros((spare, wide), BF16))
        return jnp.concatenate(parts) if len(parts) > 1 else parts[0]

    def order(self, me, table, order, chans):
        lane = lax.broadcasted_iota(jnp.int32, (1, self.width), 1)
        source = jnp.full((1, self.width), -1, jnp.int32)
        at = 0
        for start, count in zip(self.starts, self.counts):
            for i in range(count):
                first = start + i * self.rows
                inside = (lane >= first) & (lane < first + self.rows)
                source = jnp.where(inside, table[me, at] * self.rows + lane - first, source)
                at += 1
        channel = lax.broadcasted_iota(jnp.int32, (chans, self.width), 0)
        order[...] = jnp.where(channel == source, 1.0, 0.0).astype(BF16)


def slope_kernel(stages, dev, table, stats, gain, shift, lat_own, lat_far, cot_own, cot_far,
                 cots, slope, slope_x, *refs):
    me = dev[0]
    core = me % 2
    half, width, chans = lat_own.shape
    clear_edges(cots)
    mean, rstd = stats[0:1], stats[1:2]
    gain_v, shift_v = gain[...], shift[...]
    far_at = half - core * half
    if len(stages.counts) > 1:
        order, placed = refs
        stages.order(me, table, order, chans)
        for ref, base in ((cot_own, core * half), (cot_far, far_at)):
            value = jnp.dot(ref[...].reshape(half * width, chans), order[...], preferred_element_type=F32)
            placed[pl.ds(base, half)] = value.reshape(half, width, stages.width)

    def one_row(i, _):
        for lat, cot, base in ((lat_own, cot_own, core * half), (lat_far, cot_far, far_at)):
            value = placed[base + i] if len(stages.counts) > 1 else cot[i].astype(F32)
            fill_shifts(cots, base + i + 1, value)
            xhat = (lat[i].astype(F32) - mean) * rstd
            pre = gain_v * xhat + shift_v
            sig = 0.5 + 0.5 * jnp.tanh(0.5 * pre)
            value = sig * (1.0 + pre * (1.0 - sig))
            slope[base + i] = value.astype(BF16)
            slope_x[base + i] = (value * xhat).astype(BF16)
        return 0

    lax.fori_loop(0, half, one_row, 0)


def conv_sum(cols, stages, stage, core, first, half, acts, blocks, total):
    width, chans = acts.shape[2:]
    cells = half * width
    nt = (((1,), (1,)), ((), ()))
    place, channel = cols.middle(core, chans)
    window = acts[1, pl.ds(first + 1, half), :, pl.ds(channel, cols.mid)].reshape(cells, cols.mid)
    lane = lax.broadcasted_iota(jnp.int32, window.shape, 1)
    window = jnp.where((core == 1) & (lane < cols.both), jnp.zeros_like(window), window)
    kernel = stages.columns(stage, blocks, place, cols.mid)
    total[...] = lax.dot_general(window, kernel, nt, preferred_element_type=F32)

    def two_taps(k, _):
        taps, place = cols.pair(core, k, chans)
        windows = [acts[t % 3, pl.ds(first + t // 3, half)].reshape(cells, chans) for t in taps]
        kernel = stages.columns(stage, blocks, place, 2 * chans)
        total[...] += lax.dot_general(
            jnp.concatenate(windows, axis=1), kernel, nt, preferred_element_type=F32
        )
        return 0

    lax.fori_loop(0, 2, two_taps, 0)


def conv_both_kernel(cols, stages, stage, dev, acts, *refs):
    blocks, (own, far, total) = refs[:-3], refs[-3:]
    core = dev[0] % 2
    rows = acts.shape[1] - 2
    conv_sum(cols, stages, stage, core, 0, rows, acts, blocks, total)
    half = own.shape[0]
    own[...] = total[pl.ds(pl.multiple_of(core * half, half), half)]
    far[...] = total[pl.ds(pl.multiple_of((1 - core) * half, half), half)].astype(BF16)


def conv_far_kernel(cols, stages, stage, dev, acts, *refs):
    blocks, (far, total) = refs[:-2], refs[-2:]
    core = dev[0] % 2
    half = (acts.shape[1] - 2) // 2
    conv_sum(cols, stages, stage, core, (1 - core) * half, half, acts, blocks, total)
    far[...] = total[...].astype(BF16)


def conv_own_kernel(cols, stages, dev, acts, got, latent, bias, *refs):
    core = dev[0] % 2
    half, width, chans = latent.shape
    scale = cols.total ** (-0.5)
    stage = len(stages.counts) - 1
    before = 3 * stage
    blocks, (block, total) = refs[before:-2], refs[-2:]
    conv_sum(cols, stages, stage, core, core * half, half, acts, blocks, total)
    conv = total[...] + got[...].astype(F32)
    if stage:
        first_own, first_got, order = refs[:before]
        conv = jnp.concatenate([first_own[...] + first_got[...].astype(F32), conv], axis=1)
        high = conv.astype(BF16)
        low = (conv - high.astype(F32)).astype(BF16)
        nt = (((1,), (1,)), ((), ()))
        conv = sum(
            lax.dot_general(value, order[...], nt, preferred_element_type=F32) for value in (low, high)
        )
    conv = scale * conv + bias[...]
    block[...] = (conv.reshape(half, width, chans) + latent[...].astype(F32)).astype(BF16)


def back_kernel(cols, stages, stage, dev, cots, slope, slope_x, *refs):
    blocks, (sums, total) = refs[:-2], refs[-2:]
    core = dev[0] % 2
    rows, width = cots.shape[1] - 2, cots.shape[2]
    cells, chans = total.shape
    lanes = stages.lanes(stage)

    def taps_from(first, place, count):
        windows, kernels = [], []
        for i in range(count):
            tap = first + i
            window = cots[2 - tap % 3, pl.ds(2 - tap // 3, rows), :, lanes]
            windows.append(window.reshape(cells, stages.widths[stage]))
            kernels.append(stages.columns(stage, blocks, pl.multiple_of(place + i * chans, LANES), chans))
        return jnp.dot(
            jnp.concatenate(windows, axis=1), jnp.concatenate(kernels), preferred_element_type=F32
        )

    if stages.widths[stage] * 4 <= 2 * chans:
        taps, place = cols.pair(core, 0, chans)
        total[...] = taps_from(taps[0], place, 4)
    else:
        total[...] = jnp.zeros_like(total)

        def two_taps(k, _):
            taps, place = cols.pair(core, k, chans)
            total[...] += taps_from(taps[0], place, 2)
            return 0

        lax.fori_loop(0, 2, two_taps, 0)

    place, channel = cols.middle(core, chans)
    window = cots[1, 1:rows + 1, :, lanes].reshape(cells, stages.widths[stage])
    kernel = stages.columns(stage, blocks, place, cols.mid)
    value = jnp.dot(window, kernel, preferred_element_type=F32)
    lane = lax.broadcasted_iota(jnp.int32, value.shape, 1)
    total[:, pl.ds(channel, cols.mid)] += jnp.where((core == 1) & (lane < cols.both), 0.0, value)

    def add_row(i, carry):
        gains, shifts = carry
        value = total[pl.ds(pl.multiple_of(i * width, width), width)]
        return gains + value * slope_x[i].astype(F32), shifts + value * slope[i].astype(F32)

    zero = jnp.zeros((width, chans), F32)
    gains, shifts = lax.fori_loop(0, rows, add_row, (zero, zero))
    scale = cols.total ** (-0.5)
    sums[0:1] = scale * jnp.sum(gains, axis=0, keepdims=True)
    sums[1:2] = scale * jnp.sum(shifts, axis=0, keepdims=True)


def finish_kernel(cols, dev, step, shard, mine, theirs, ours, aside, out):
    lower = dev[0] % 2 == 0
    rate = LR_KERNEL * (1.0 - (step[0] % 1000).astype(F32) / 2000.0)
    factor = 0.5 * cols.total ** (-0.5) * rate
    here = 0.5 * mine[...].astype(F32) - factor * ours[...].astype(F32)
    there = 0.5 * theirs[...].astype(F32) - factor * aside[...].astype(F32)
    left, right = jnp.where(lower, here, there), jnp.where(lower, there, here)
    out[:, :cols.lead] = 0.5 * shard[:, :cols.lead] + left
    out[:, cols.lead:] = 0.5 * shard[:, cols.lead:] + right[:, cols.both:]


NODE = ("z", "y")


def swap(value, axis):
    return lax.ppermute(value, axis, [(0, 1), (1, 0)])


def from_peer(level, value):
    count = lax.axis_size("replica")
    levels = count.bit_length() - 1
    moves = [[(s, (s + (1 << k)) % count) for s in range(count)] for k in range(levels)]
    if levels == 1:
        return lax.ppermute(value, "replica", moves[0])
    return lax.switch(level, [lambda v, m=m: lax.ppermute(v, "replica", m) for m in moves], value)


class Ring:
    def __init__(self, zs):
        self.count = 2 * zs
        self.reach = zs
        self.nodes = [2 * z for z in range(zs)] + [2 * z + 1 for z in reversed(range(zs))]
        ahead = list(zip(self.nodes, self.nodes[1:] + self.nodes[:1]))
        self.ahead = ahead
        self.behind = [(b, a) for a, b in ahead]

    def node(self, at, offset):
        return self.nodes[(at + offset) % self.count]

    def up(self, value):
        return lax.ppermute(value, NODE, self.ahead)

    def down(self, value):
        return lax.ppermute(value, NODE, self.behind)

    def table(self, part):
        rows = np.zeros((2, self.count, 2, 3 * self.count), np.int32)
        for replica in range(2):
            for at, node in enumerate(self.nodes):
                line = [node]
                for k in range(1, self.reach + 1):
                    line.append(self.node(at, -k))
                    if k < self.reach:
                        line.append(self.node(at, k))
                for which in (replica, 1 - replica):
                    for j in range(self.reach):
                        targets = [self.node(at, self.reach - j), self.node(at, j + 1 - self.reach)]
                        line += [(2 * target + which) * part for target in targets]
                rows[replica, node, :] = line
        return rows.reshape(-1, 3 * self.count)


def hop(value, axis, mask):
    count = lax.axis_size(axis)
    return value + lax.ppermute(value, axis, [(s, s ^ mask) for s in range(count)])


def add(*values):
    total = values[0].astype(F32)
    for value in values[1:]:
        total = total + value.astype(F32)
    return total.astype(BF16)


def tied(*values):
    return lax.optimization_barrier(values)


def per_device(latents, cotangent, kernel, conv_bias, gn_gain, gn_shift, step):
    latent, cotan, shard = latents[0], cotangent[0], kernel[0]
    half, width, chans = latent.shape
    part = shard.shape[0]
    cols = Columns(chans)
    cells = half * width
    zs, replicas = lax.axis_size("z"), lax.axis_size("replica")
    core, z, y, replica = (lax.axis_index(a) for a in ("core", "z", "y", "replica"))
    lower = core == 0
    paired = replicas == 2
    ring = Ring(zs)
    scale = cols.total ** (-0.5)
    params = jnp.concatenate([conv_bias, gn_gain, gn_shift])
    me = ((replica * zs + z) * 2 + y) * 2 + core
    core, lower, same, me = tied(core, lower, replica == core, me)
    dev = me.reshape(1)

    mine = lax.dynamic_slice_in_dim(shard, core * cols.start, cols.lead, 1).astype(BF16)
    theirs = lax.dynamic_slice_in_dim(shard, (1 - core) * cols.start, cols.lead, 1).astype(BF16)
    got = swap(theirs, "core")
    unit = jnp.where(lower, jnp.concatenate([mine, got]), jnp.concatenate([got, mine]))
    lat_far = swap(latent, "core")
    cot_b = cotan.astype(BF16)
    cot_far = swap(cot_b, "core")

    if paired:
        table = jnp.asarray(ring.table(part))
        order = (ring.count, part, 2 * ring.count)
        up1, down1 = ring.up(unit), ring.down(unit)
        peer = swap(mine, "replica"), swap(theirs, "replica")
    else:
        table = jnp.zeros((replicas * zs * 4, 1), jnp.int32)
        order = None

    def call(body, outs, ins, scratch, megabytes, flops):
        return pl.pallas_call(
            body,
            out_shape=outs,
            in_specs=ins,
            out_specs=jax.tree.map(lambda _: VMEM_SPEC, outs),
            scratch_shapes=scratch,
            compiler_params=pltpu.CompilerParams(vmem_limit_bytes=megabytes * 2**20),
            cost_estimate=pl.CostEstimate(flops=flops, bytes_accessed=0, transcendentals=0),
        )

    image = (2 * half, width, chans)
    shifted = jax.ShapeDtypeStruct((3, 2 * half + 2, width, chans), BF16)
    flops = 2 * 2 * cells * chans * cols.lead
    stats, acts, cot_t = call(
        partial(act_kernel, order),
        (jax.ShapeDtypeStruct((2, chans), F32), shifted, jax.ShapeDtypeStruct((chans, 2 * cells), BF16)),
        [SMEM_SPEC] * 2 + [VMEM_SPEC] * 6,
        [pltpu.VMEM((chans, 2 * cells), F32)],
        8, flops // 4,
    )(dev, table, latent, lat_far, cot_b, cot_far, gn_gain, gn_shift)
    counts = [zs] + [1] * zs if paired else [2 * zs]
    pieces = call(
        partial(grad_kernel, cols),
        [jax.ShapeDtypeStruct((n * 2 * part, cols.lead), BF16) for n in counts],
        [SMEM_SPEC] + [VMEM_SPEC] * 2,
        [],
        4, flops // 2,
    )(dev, acts, cot_t)
    stages = Stages([2 * zs - 3, 3] if paired else [1], 2 * part if paired else chans)
    staged = paired

    def slopes_of(stats):
        extra = (jax.ShapeDtypeStruct((chans, stages.width), BF16),) if staged else ()
        return call(
            partial(slope_kernel, stages),
            (jax.ShapeDtypeStruct((3, 2 * half + 2, width, stages.width), BF16),
             jax.ShapeDtypeStruct(image, BF16), jax.ShapeDtypeStruct(image, BF16)) + extra,
            [SMEM_SPEC] * 2 + [VMEM_SPEC] * 7,
            [pltpu.VMEM((2 * half, width, stages.width), F32)] if staged else [],
            8, flops // 4,
        )(dev, table, stats, gn_gain, gn_shift, latent, lat_far, cot_b, cot_far)

    def back(stage, cots, slopes, blocks):
        return call(
            partial(back_kernel, cols, stages, stage), jax.ShapeDtypeStruct((2, chans), F32),
            [SMEM_SPEC] + [VMEM_SPEC] * (3 + len(blocks)),
            [pltpu.VMEM((2 * cells, chans), F32)], 8, flops // 4,
        )(dev, cots, *slopes, *blocks)

    def conv_first(blocks):
        wide = stages.widths[0]
        return call(
            partial(conv_both_kernel, cols, stages, 0),
            (jax.ShapeDtypeStruct((cells, wide), F32), jax.ShapeDtypeStruct((cells, wide), BF16)),
            [SMEM_SPEC] + [VMEM_SPEC] * (1 + len(blocks)),
            [pltpu.VMEM((2 * cells, wide), F32)], 6, flops // 4,
        )(dev, acts, *blocks)

    def conv_far(acts, blocks):
        wide = stages.widths[-1]
        return call(
            partial(conv_far_kernel, cols, stages, len(stages.counts) - 1),
            jax.ShapeDtypeStruct((cells, wide), BF16),
            [SMEM_SPEC] + [VMEM_SPEC] * (1 + len(blocks)),
            [pltpu.VMEM((cells, wide), F32)], 4, flops // 8,
        )(dev, acts, *blocks)

    def conv_own(got, earlier, blocks):
        return call(
            partial(conv_own_kernel, cols, stages), jax.ShapeDtypeStruct((half, width, chans), BF16),
            [SMEM_SPEC] + [VMEM_SPEC] * (4 + len(earlier) + len(blocks)),
            [pltpu.VMEM((cells, stages.widths[-1]), F32)], 8, flops // 4,
        )(dev, acts, got, latent, conv_bias, *earlier, *blocks)

    def chip_sum(sums):
        vectors = jnp.concatenate([jnp.sum(cotan, axis=(0, 1))[None], sums])
        vectors = params / (4 * zs) - LR_VECTOR * vectors
        return vectors + swap(vectors, "core")

    if paired:
        kept, *sent = pieces
        up, down, sent[0], mine, theirs = tied(up1, down1, sent[0], *peer)
        blocks = [unit, up, down]
        crossed = [swap(piece, "replica") for piece in sent]
        up, down = ring.up(up), ring.down(down)
        up, down, cots, *slopes, order = tied(up, down, *slopes_of(stats))
        blocks += [up, down]

        def ring_step(j, *received):
            parts = kept[2 * j * part:(2 * j + 2) * part], crossed[j]
            ahead, behind = (tuple(x[half] for x in parts) for half in (slice(part), slice(part, None)))
            up_sum = ring.up(add(*ahead, *received[:1]))
            if j < zs - 1:
                return up_sum, ring.down(add(*behind, *received[1:]))
            return up_sum, behind + tuple(received[1:])

        up, down = ring.up(up), ring.down(down)
        conv_first_own, conv_send = conv_first(blocks)
        crossed[0], conv_send = tied(crossed[0], conv_send)
        received = ring_step(0)
        cots, conv_send = tied(cots, conv_send)
        first_sums = back(0, cots, slopes, blocks)
        up, down, first_sums, crossed[1] = tied(up, down, first_sums, crossed[1])
        late = [up, down]

        halves = ring.up(up[:part]), ring.down(down[part:])
        conv_send, *received = tied(conv_send, *received)
        conv_first_got = swap(conv_send, "core")
        for j in range(1, zs - 2):
            received = ring_step(j, *received)
        late += halves

        sums = back(1, cots, slopes, late)
        crossed[-2], sums, *received = tied(crossed[-2], sums, *received)
        acts_last, *_ = tied(acts, sums, *received)
        received = ring_step(zs - 2, *received)
        conv_got = swap(conv_far(acts_last, late), "core")
        vectors = hop(chip_sum(first_sums + sums), "replica", 1)
        crossed[-1], conv_got, vectors, *received = tied(crossed[-1], conv_got, vectors, *received)
        last, behind = ring_step(zs - 1, *received)
        block = conv_own(conv_got, [conv_first_own, conv_first_got, order], late)
        vectors = hop(vectors, "z", 1)
        last, block, vectors = tied(last, block, vectors)
        total = add(*behind, last)
        across = swap(total, "replica")
        ours, others = jnp.where(same, total, across), jnp.where(same, across, total)
        aside = swap(others, "core")
        new_kernel = call(
            partial(finish_kernel, cols), jax.ShapeDtypeStruct(shard.shape, F32),
            [SMEM_SPEC] * 2 + [VMEM_SPEC] * 5, [], 8, flops // 16,
        )(dev, step, shard, mine, theirs, ours, aside)
        vectors = hop(vectors, "y", 1)
        reach = 2
        while reach < zs:
            vectors = hop(vectors, "z", reach)
            reach *= 2
        new_v = 0.5 * vectors
    else:
        late = [lax.all_gather(unit, NODE, axis=0, tiled=True)]
        cots, slope, slope_x = slopes_of(stats)
        sums = back(0, cots, [slope, slope_x], late)
        vectors = chip_sum(sums)
        block = conv_own(swap(conv_far(acts, late), "core"), [], late)
        terms = pieces[0].reshape(2 * zs, 2, part, cols.lead)
        summed = lax.psum_scatter(terms, NODE, scatter_dimension=0, tiled=False)
        ours = lax.dynamic_index_in_dim(summed, core, 0, keepdims=False)
        got = swap(lax.dynamic_index_in_dim(summed, 1 - core, 0, keepdims=False), "core")
        left, right = jnp.where(lower, ours, got), jnp.where(lower, got, ours)
        kernel_grad = jnp.concatenate([left, right[:, cols.both:]], axis=1).astype(F32)
        level = step[0] % (replicas.bit_length() - 1)
        rate = LR_KERNEL * (1.0 - (step[0] % 1000).astype(F32) / 2000.0)
        stepped = shard - (scale * rate) * kernel_grad
        new_kernel = 0.5 * (stepped + from_peer(level, stepped.astype(BF16)).astype(F32))
        stepped_v = lax.psum(vectors, NODE)
        new_v = 0.5 * (stepped_v + from_peer(level, stepped_v))

    return (
        block[None],
        new_kernel[None],
        new_v[0][None],
        new_v[1][None],
        new_v[2][None],
    )


def solution(mesh):
    replicas, shards = mesh.shape["replica"], mesh.shape["shard"]
    split = Mesh(mesh.devices.reshape(replicas, shards // 4, 2, 2), ("replica", "z", "y", "core"))
    shard = ("z", "y", "core")
    return jax.shard_map(
        per_device,
        mesh=split,
        in_specs=(
            P("replica", shard, None, None),
            P("replica", shard, None, None),
            P("replica", shard, None),
            P("replica", None),
            P("replica", None),
            P("replica", None),
            P(),
        ),
        out_specs=(
            P("replica", shard, None, None),
            P("replica", shard, None),
            P("replica", None),
            P("replica", None),
            P("replica", None),
        ),
        check_vma=False,
    )
```

```python
from functools import partial

import jax
import jax.numpy as jnp
import numpy as np
from jax import lax
from jax.experimental import pallas as pl
from jax.experimental.pallas import tpu as pltpu
from jax.sharding import Mesh, PartitionSpec as P

GROUPS = 32
EPS = 1e-05
LR_KERNEL = 0.1
LR_VECTOR = 0.01
LANES = 128
BF16 = jnp.bfloat16
F32 = jnp.float32

SMEM_SPEC = pl.BlockSpec(memory_space=pltpu.SMEM)
VMEM_SPEC = pl.BlockSpec(memory_space=pltpu.VMEM)


class Columns:
    def __init__(self, chans):
        tiles = 9 * chans // LANES
        self.total = 9 * chans
        self.lead = (tiles + 1) // 2 * LANES
        self.start = self.total - self.lead
        self.both = 2 * self.lead - self.total
        self.mid = self.lead - 4 * chans
        self.mid_start = chans - self.mid

    def pair(self, core, k, chans):
        first = jnp.where(core == 0, 2 * k, 5 + 2 * k)
        place = jnp.where(core == 0, 2 * k * chans, self.mid + 2 * k * chans)
        return (first, first + 1), pl.multiple_of(place, LANES)

    def middle(self, core, chans):
        place = jnp.where(core == 0, 4 * chans, 0)
        channel = jnp.where(core == 0, 0, self.mid_start)
        return pl.multiple_of(place, LANES), pl.multiple_of(channel, LANES)


def fill_shifts(shifts, row, values):
    width = values.shape[0]
    at = lax.broadcasted_iota(jnp.int32, values.shape, 0)
    left = jnp.where(at == 0, 0.0, pltpu.roll(values, 1, 0))
    right = jnp.where(at == width - 1, 0.0, pltpu.roll(values, width - 1, 0))
    shifts[0, row] = left.astype(BF16)
    shifts[1, row] = values.astype(BF16)
    shifts[2, row] = right.astype(BF16)


def clear_edges(shifts):
    zero = jnp.zeros(shifts.shape[2:], shifts.dtype)
    for b in range(3):
        shifts[b, 0] = zero
        shifts[b, shifts.shape[1] - 1] = zero


def act_kernel(order, dev, table, lat_own, lat_far, cot_own, cot_far, gain, shift,
               stats, acts, cot_t, cot_f):
    me = dev[0]
    core = me % 2
    half, width, chans = lat_own.shape
    cells = 2 * half * width
    group_width = chans // GROUPS
    own_at = core * half
    far_at = half - own_at
    clear_edges(acts)

    def add_row(i, sums):
        total, square = sums
        a = lat_own[i].astype(F32)
        b = lat_far[i].astype(F32)
        return total + (a + b), square + (a * a + b * b)

    zero = jnp.zeros((width, chans), F32)
    total, square = lax.fori_loop(0, half, add_row, (zero, zero))
    sums = jnp.concatenate(
        [jnp.sum(total, axis=0, keepdims=True), jnp.sum(square, axis=0, keepdims=True),
         jnp.zeros((6, chans), F32)], axis=0
    )
    first = lax.broadcasted_iota(jnp.int32, (chans, LANES), 0)
    start = lax.broadcasted_iota(jnp.int32, (chans, LANES), 1) * group_width
    member = jnp.where((first >= start) & (first < start + group_width), 1.0, 0.0)
    exact = partial(lax.dot_general, precision=lax.Precision.HIGHEST, preferred_element_type=F32)
    sums = exact(sums, member, (((1,), (0,)), ((), ()))) / (cells * group_width)
    sums = exact(sums, member, (((1,), (1,)), ((), ())))
    mean = sums[0:1]
    rstd = lax.rsqrt(sums[1:2] - mean * mean + EPS)
    stats[0:1] = mean
    stats[1:2] = rstd
    gain_v, shift_v = gain[...], shift[...]

    def act_rows(i, _):
        for ref, base in ((lat_own, own_at), (lat_far, far_at)):
            pre = gain_v * ((ref[i].astype(F32) - mean) * rstd) + shift_v
            fill_shifts(acts, base + i + 1, pre * (0.5 + 0.5 * jnp.tanh(0.5 * pre)))
        return 0

    lax.fori_loop(0, half, act_rows, 0)

    chunk = LANES // width
    for ref, base in ((cot_own, own_at), (cot_far, far_at)):
        for i in range(half // chunk):
            piece = ref[i * chunk:(i + 1) * chunk].reshape(LANES, chans).astype(F32)
            place = pl.multiple_of(base * width + i * LANES, LANES)
            if order is None:
                cot_t[:, pl.ds(place, LANES)] = piece.T.astype(BF16)
            else:
                cot_f[:, pl.ds(place, LANES)] = piece.T
    if order is not None:
        first_at, part, count = order
        for q in range(count // 2):
            pair = [
                cot_f[pl.ds(pl.multiple_of(table[me, first_at + 2 * q + i], 8), part)]
                for i in range(2)
            ]
            cot_t[2 * q * part:(2 * q + 2) * part] = jnp.concatenate(pair).astype(BF16)


def grad_kernel(cols, dev, acts, cot_t, *pieces):
    core = dev[0] % 2
    rows, width, chans = acts.shape[1] - 2, acts.shape[2], acts.shape[3]
    cells = rows * width

    def emit(window, place, wide):
        value = jnp.dot(cot_t[...], window, preferred_element_type=F32)
        at = 0
        for piece in pieces:
            piece[:, pl.ds(place, wide)] = value[at:at + piece.shape[0]].astype(BF16)
            at += piece.shape[0]

    def two_taps(k, _):
        taps, place = cols.pair(core, k, chans)
        windows = [acts[t % 3, pl.ds(t // 3, rows)].reshape(cells, chans) for t in taps]
        emit(jnp.concatenate(windows, axis=1), place, 2 * chans)
        return 0

    lax.fori_loop(0, 2, two_taps, 0)
    place, channel = cols.middle(core, chans)
    emit(acts[1, 1:rows + 1, :, pl.ds(channel, cols.mid)].reshape(cells, cols.mid), place, cols.mid)


class Stages:
    def __init__(self, counts, rows):
        self.rows = rows
        self.counts = counts
        self.widths = [-(-n * rows // LANES) * LANES for n in counts]
        self.starts = [sum(self.widths[:i]) for i in range(len(counts))]
        self.width = sum(self.widths)

    def lanes(self, stage):
        return slice(self.starts[stage], self.starts[stage] + self.widths[stage])

    def columns(self, stage, blocks, place, wide):
        parts = [ref[:, pl.ds(place, wide)] for ref in blocks]
        if len(parts) == self.counts[stage] + 1:
            parts[-2:] = [jnp.concatenate(parts[-2:])]
        spare = self.widths[stage] - self.counts[stage] * self.rows
        if spare:
            parts.append(jnp.zeros((spare, wide), BF16))
        return jnp.concatenate(parts) if len(parts) > 1 else parts[0]

    def order(self, me, table, order, chans):
        lane = lax.broadcasted_iota(jnp.int32, (1, self.width), 1)
        source = jnp.full((1, self.width), -1, jnp.int32)
        at = 0
        for start, count in zip(self.starts, self.counts):
            for i in range(count):
                first = start + i * self.rows
                inside = (lane >= first) & (lane < first + self.rows)
                source = jnp.where(inside, table[me, at] * self.rows + lane - first, source)
                at += 1
        channel = lax.broadcasted_iota(jnp.int32, (chans, self.width), 0)
        order[...] = jnp.where(channel == source, 1.0, 0.0).astype(BF16)


def slope_kernel(stages, dev, table, stats, gain, shift, lat_own, lat_far, cot_own, cot_far,
                 cots, slope, slope_x, *refs):
    me = dev[0]
    core = me % 2
    half, width, chans = lat_own.shape
    clear_edges(cots)
    mean, rstd = stats[0:1], stats[1:2]
    gain_v, shift_v = gain[...], shift[...]
    far_at = half - core * half
    if len(stages.counts) > 1:
        order, placed = refs
        stages.order(me, table, order, chans)
        for ref, base in ((cot_own, core * half), (cot_far, far_at)):
            value = jnp.dot(ref[...].reshape(half * width, chans), order[...], preferred_element_type=F32)
            placed[pl.ds(base, half)] = value.reshape(half, width, stages.width)

    def one_row(i, _):
        for lat, cot, base in ((lat_own, cot_own, core * half), (lat_far, cot_far, far_at)):
            value = placed[base + i] if len(stages.counts) > 1 else cot[i].astype(F32)
            fill_shifts(cots, base + i + 1, value)
            xhat = (lat[i].astype(F32) - mean) * rstd
            pre = gain_v * xhat + shift_v
            sig = 0.5 + 0.5 * jnp.tanh(0.5 * pre)
            value = sig * (1.0 + pre * (1.0 - sig))
            slope[base + i] = value.astype(BF16)
            slope_x[base + i] = (value * xhat).astype(BF16)
        return 0

    lax.fori_loop(0, half, one_row, 0)


def conv_sum(cols, stages, stage, core, first, half, acts, blocks, total):
    width, chans = acts.shape[2:]
    cells = half * width
    nt = (((1,), (1,)), ((), ()))
    place, channel = cols.middle(core, chans)
    window = acts[1, pl.ds(first + 1, half), :, pl.ds(channel, cols.mid)].reshape(cells, cols.mid)
    lane = lax.broadcasted_iota(jnp.int32, window.shape, 1)
    window = jnp.where((core == 1) & (lane < cols.both), jnp.zeros_like(window), window)
    kernel = stages.columns(stage, blocks, place, cols.mid)
    total[...] = lax.dot_general(window, kernel, nt, preferred_element_type=F32)

    def two_taps(k, _):
        taps, place = cols.pair(core, k, chans)
        windows = [acts[t % 3, pl.ds(first + t // 3, half)].reshape(cells, chans) for t in taps]
        kernel = stages.columns(stage, blocks, place, 2 * chans)
        total[...] += lax.dot_general(
            jnp.concatenate(windows, axis=1), kernel, nt, preferred_element_type=F32
        )
        return 0

    lax.fori_loop(0, 2, two_taps, 0)


def conv_both_kernel(cols, stages, stage, dev, acts, *refs):
    blocks, (own, far, total) = refs[:-3], refs[-3:]
    core = dev[0] % 2
    rows = acts.shape[1] - 2
    conv_sum(cols, stages, stage, core, 0, rows, acts, blocks, total)
    half = own.shape[0]
    own[...] = total[pl.ds(pl.multiple_of(core * half, half), half)]
    far[...] = total[pl.ds(pl.multiple_of((1 - core) * half, half), half)].astype(BF16)


def conv_far_kernel(cols, stages, stage, dev, acts, *refs):
    blocks, (far, total) = refs[:-2], refs[-2:]
    core = dev[0] % 2
    half = (acts.shape[1] - 2) // 2
    conv_sum(cols, stages, stage, core, (1 - core) * half, half, acts, blocks, total)
    far[...] = total[...].astype(BF16)


def conv_own_kernel(cols, stages, dev, acts, got, latent, bias, *refs):
    core = dev[0] % 2
    half, width, chans = latent.shape
    scale = cols.total ** (-0.5)
    stage = len(stages.counts) - 1
    before = 3 * stage
    blocks, (block, total) = refs[before:-2], refs[-2:]
    conv_sum(cols, stages, stage, core, core * half, half, acts, blocks, total)
    conv = total[...] + got[...].astype(F32)
    if stage:
        first_own, first_got, order = refs[:before]
        conv = jnp.concatenate([first_own[...] + first_got[...].astype(F32), conv], axis=1)
        high = conv.astype(BF16)
        low = (conv - high.astype(F32)).astype(BF16)
        nt = (((1,), (1,)), ((), ()))
        conv = sum(
            lax.dot_general(value, order[...], nt, preferred_element_type=F32) for value in (low, high)
        )
    conv = scale * conv + bias[...]
    block[...] = (conv.reshape(half, width, chans) + latent[...].astype(F32)).astype(BF16)


def back_kernel(cols, stages, stage, dev, cots, slope, slope_x, *refs):
    blocks, (sums, total) = refs[:-2], refs[-2:]
    core = dev[0] % 2
    rows, width = cots.shape[1] - 2, cots.shape[2]
    cells, chans = total.shape
    lanes = stages.lanes(stage)

    def taps_from(first, place, count):
        windows, kernels = [], []
        for i in range(count):
            tap = first + i
            window = cots[2 - tap % 3, pl.ds(2 - tap // 3, rows), :, lanes]
            windows.append(window.reshape(cells, stages.widths[stage]))
            kernels.append(stages.columns(stage, blocks, pl.multiple_of(place + i * chans, LANES), chans))
        return jnp.dot(
            jnp.concatenate(windows, axis=1), jnp.concatenate(kernels), preferred_element_type=F32
        )

    if stages.widths[stage] * 4 <= 2 * chans:
        taps, place = cols.pair(core, 0, chans)
        total[...] = taps_from(taps[0], place, 4)
    else:
        total[...] = jnp.zeros_like(total)

        def two_taps(k, _):
            taps, place = cols.pair(core, k, chans)
            total[...] += taps_from(taps[0], place, 2)
            return 0

        lax.fori_loop(0, 2, two_taps, 0)

    place, channel = cols.middle(core, chans)
    window = cots[1, 1:rows + 1, :, lanes].reshape(cells, stages.widths[stage])
    kernel = stages.columns(stage, blocks, place, cols.mid)
    value = jnp.dot(window, kernel, preferred_element_type=F32)
    lane = lax.broadcasted_iota(jnp.int32, value.shape, 1)
    total[:, pl.ds(channel, cols.mid)] += jnp.where((core == 1) & (lane < cols.both), 0.0, value)

    def add_row(i, carry):
        gains, shifts = carry
        value = total[pl.ds(pl.multiple_of(i * width, width), width)]
        return gains + value * slope_x[i].astype(F32), shifts + value * slope[i].astype(F32)

    zero = jnp.zeros((width, chans), F32)
    gains, shifts = lax.fori_loop(0, rows, add_row, (zero, zero))
    scale = cols.total ** (-0.5)
    sums[0:1] = scale * jnp.sum(gains, axis=0, keepdims=True)
    sums[1:2] = scale * jnp.sum(shifts, axis=0, keepdims=True)


def finish_kernel(cols, dev, step, shard, mine, theirs, ours, aside, vectors, out, new_bias, new_gain, new_shift):
    lower = dev[0] % 2 == 0
    rate = LR_KERNEL * (1.0 - (step[0] % 1000).astype(F32) / 2000.0)
    factor = 0.5 * cols.total ** (-0.5) * rate
    here = 0.5 * mine[...].astype(F32) - factor * ours[...].astype(F32)
    there = 0.5 * theirs[...].astype(F32) - factor * aside[...].astype(F32)
    left, right = jnp.where(lower, here, there), jnp.where(lower, there, here)
    out[:, :cols.lead] = 0.5 * shard[:, :cols.lead] + left
    out[:, cols.lead:] = 0.5 * shard[:, cols.lead:] + right[:, cols.both:]
    for i, new in enumerate((new_bias, new_gain, new_shift)):
        new[...] = 0.5 * vectors[i:i + 1]


NODE = ("z", "y")


def swap(value, axis):
    return lax.ppermute(value, axis, [(0, 1), (1, 0)])


def from_peer(level, value):
    count = lax.axis_size("replica")
    levels = count.bit_length() - 1
    moves = [[(s, (s + (1 << k)) % count) for s in range(count)] for k in range(levels)]
    if levels == 1:
        return lax.ppermute(value, "replica", moves[0])
    return lax.switch(level, [lambda v, m=m: lax.ppermute(v, "replica", m) for m in moves], value)


class Ring:
    def __init__(self, zs):
        self.count = 2 * zs
        self.reach = zs
        self.nodes = [2 * z for z in range(zs)] + [2 * z + 1 for z in reversed(range(zs))]
        ahead = list(zip(self.nodes, self.nodes[1:] + self.nodes[:1]))
        self.ahead = ahead
        self.behind = [(b, a) for a, b in ahead]

    def node(self, at, offset):
        return self.nodes[(at + offset) % self.count]

    def up(self, value):
        return lax.ppermute(value, NODE, self.ahead)

    def down(self, value):
        return lax.ppermute(value, NODE, self.behind)

    def table(self, part):
        rows = np.zeros((2, self.count, 2, 3 * self.count), np.int32)
        for replica in range(2):
            for at, node in enumerate(self.nodes):
                line = [node]
                for k in range(1, self.reach + 1):
                    line.append(self.node(at, -k))
                    if k < self.reach:
                        line.append(self.node(at, k))
                for which in (replica, 1 - replica):
                    for j in range(self.reach):
                        targets = [self.node(at, self.reach - j), self.node(at, j + 1 - self.reach)]
                        line += [(2 * target + which) * part for target in targets]
                rows[replica, node, :] = line
        return rows.reshape(-1, 3 * self.count)


def hop(value, axis, mask):
    count = lax.axis_size(axis)
    return value + lax.ppermute(value, axis, [(s, s ^ mask) for s in range(count)])


def add(*values):
    total = values[0].astype(F32)
    for value in values[1:]:
        total = total + value.astype(F32)
    return total.astype(BF16)


def tied(*values):
    return lax.optimization_barrier(values)


def per_device(latents, cotangent, kernel, conv_bias, gn_gain, gn_shift, step):
    latent, cotan, shard = latents[0], cotangent[0], kernel[0]
    half, width, chans = latent.shape
    part = shard.shape[0]
    cols = Columns(chans)
    cells = half * width
    zs, replicas = lax.axis_size("z"), lax.axis_size("replica")
    core, z, y, replica = (lax.axis_index(a) for a in ("core", "z", "y", "replica"))
    lower = core == 0
    paired = replicas == 2
    ring = Ring(zs)
    scale = cols.total ** (-0.5)
    params = jnp.concatenate([conv_bias, gn_gain, gn_shift])
    me = ((replica * zs + z) * 2 + y) * 2 + core
    core, lower, same, me = tied(core, lower, replica == core, me)
    dev = me.reshape(1)

    mine = lax.dynamic_slice_in_dim(shard, core * cols.start, cols.lead, 1).astype(BF16)
    theirs = lax.dynamic_slice_in_dim(shard, (1 - core) * cols.start, cols.lead, 1).astype(BF16)
    got = swap(theirs, "core")
    unit = jnp.where(lower, jnp.concatenate([mine, got]), jnp.concatenate([got, mine]))
    lat_far = swap(latent, "core")
    cot_b = cotan.astype(BF16)
    cot_far = swap(cot_b, "core")

    if paired:
        table = jnp.asarray(ring.table(part))
        order = (ring.count, part, 2 * ring.count)
        up1, down1 = ring.up(unit), ring.down(unit)
        peer = swap(mine, "replica"), swap(theirs, "replica")
    else:
        table = jnp.zeros((replicas * zs * 4, 1), jnp.int32)
        order = None

    def call(body, outs, ins, scratch, megabytes, flops):
        return pl.pallas_call(
            body,
            out_shape=outs,
            in_specs=ins,
            out_specs=jax.tree.map(lambda _: VMEM_SPEC, outs),
            scratch_shapes=scratch,
            compiler_params=pltpu.CompilerParams(vmem_limit_bytes=megabytes * 2**20),
            cost_estimate=pl.CostEstimate(flops=flops, bytes_accessed=0, transcendentals=0),
        )

    image = (2 * half, width, chans)
    shifted = jax.ShapeDtypeStruct((3, 2 * half + 2, width, chans), BF16)
    flops = 2 * 2 * cells * chans * cols.lead
    stats, acts, cot_t = call(
        partial(act_kernel, order),
        (jax.ShapeDtypeStruct((2, chans), F32), shifted, jax.ShapeDtypeStruct((chans, 2 * cells), BF16)),
        [SMEM_SPEC] * 2 + [VMEM_SPEC] * 6,
        [pltpu.VMEM((chans, 2 * cells), F32)],
        8, flops // 4,
    )(dev, table, latent, lat_far, cot_b, cot_far, gn_gain, gn_shift)
    counts = [zs] + [1] * zs if paired else [2 * zs]
    pieces = call(
        partial(grad_kernel, cols),
        [jax.ShapeDtypeStruct((n * 2 * part, cols.lead), BF16) for n in counts],
        [SMEM_SPEC] + [VMEM_SPEC] * 2,
        [],
        4, flops // 2,
    )(dev, acts, cot_t)
    stages = Stages([2 * zs - 3, 3] if paired else [1], 2 * part if paired else chans)
    staged = paired

    def slopes_of(stats):
        extra = (jax.ShapeDtypeStruct((chans, stages.width), BF16),) if staged else ()
        return call(
            partial(slope_kernel, stages),
            (jax.ShapeDtypeStruct((3, 2 * half + 2, width, stages.width), BF16),
             jax.ShapeDtypeStruct(image, BF16), jax.ShapeDtypeStruct(image, BF16)) + extra,
            [SMEM_SPEC] * 2 + [VMEM_SPEC] * 7,
            [pltpu.VMEM((2 * half, width, stages.width), F32)] if staged else [],
            8, flops // 4,
        )(dev, table, stats, gn_gain, gn_shift, latent, lat_far, cot_b, cot_far)

    def back(stage, cots, slopes, blocks):
        return call(
            partial(back_kernel, cols, stages, stage), jax.ShapeDtypeStruct((2, chans), F32),
            [SMEM_SPEC] + [VMEM_SPEC] * (3 + len(blocks)),
            [pltpu.VMEM((2 * cells, chans), F32)], 8, flops // 4,
        )(dev, cots, *slopes, *blocks)

    def conv_first(blocks):
        wide = stages.widths[0]
        return call(
            partial(conv_both_kernel, cols, stages, 0),
            (jax.ShapeDtypeStruct((cells, wide), F32), jax.ShapeDtypeStruct((cells, wide), BF16)),
            [SMEM_SPEC] + [VMEM_SPEC] * (1 + len(blocks)),
            [pltpu.VMEM((2 * cells, wide), F32)], 6, flops // 4,
        )(dev, acts, *blocks)

    def conv_far(acts, blocks):
        wide = stages.widths[-1]
        return call(
            partial(conv_far_kernel, cols, stages, len(stages.counts) - 1),
            jax.ShapeDtypeStruct((cells, wide), BF16),
            [SMEM_SPEC] + [VMEM_SPEC] * (1 + len(blocks)),
            [pltpu.VMEM((cells, wide), F32)], 4, flops // 8,
        )(dev, acts, *blocks)

    def conv_own(got, earlier, blocks):
        return call(
            partial(conv_own_kernel, cols, stages), jax.ShapeDtypeStruct((half, width, chans), BF16),
            [SMEM_SPEC] + [VMEM_SPEC] * (4 + len(earlier) + len(blocks)),
            [pltpu.VMEM((cells, stages.widths[-1]), F32)], 8, flops // 4,
        )(dev, acts, got, latent, conv_bias, *earlier, *blocks)

    def chip_sum(sums):
        vectors = jnp.concatenate([jnp.sum(cotan, axis=(0, 1))[None], sums])
        vectors = params / (4 * zs) - LR_VECTOR * vectors
        return vectors + swap(vectors, "core")

    if paired:
        kept, *sent = pieces
        up, down, sent[0], mine, theirs = tied(up1, down1, sent[0], *peer)
        blocks = [unit, up, down]
        crossed = [swap(piece, "replica") for piece in sent]
        up, down = ring.up(up), ring.down(down)
        up, down, cots, *slopes, order = tied(up, down, *slopes_of(stats))
        blocks += [up, down]

        def ring_step(j, *received):
            parts = kept[2 * j * part:(2 * j + 2) * part], crossed[j]
            ahead, behind = (tuple(x[half] for x in parts) for half in (slice(part), slice(part, None)))
            up_sum = ring.up(add(*ahead, *received[:1]))
            if j < zs - 1:
                return up_sum, ring.down(add(*behind, *received[1:]))
            return up_sum, behind + tuple(received[1:])

        up, down = ring.up(up), ring.down(down)
        conv_first_own, conv_send = conv_first(blocks)
        crossed[0], conv_send = tied(crossed[0], conv_send)
        received = ring_step(0)
        cots, conv_send = tied(cots, conv_send)
        first_sums = back(0, cots, slopes, blocks)
        up, down, first_sums, crossed[1] = tied(up, down, first_sums, crossed[1])
        late = [up, down]

        halves = ring.up(up[:part]), ring.down(down[part:])
        conv_send, *received = tied(conv_send, *received)
        conv_first_got = swap(conv_send, "core")
        for j in range(1, zs - 2):
            received = ring_step(j, *received)
        late += halves

        conv_send = conv_far(acts, late)
        cots, conv_send = tied(cots, conv_send)
        conv_got = swap(conv_send, "core")
        sums = back(1, cots, slopes, late)
        crossed[-2], sums, *received = tied(crossed[-2], sums, *received)
        received = ring_step(zs - 2, *received)
        vectors = hop(chip_sum(first_sums + sums), "replica", 1)
        vectors = hop(vectors, "z", 1)
        crossed[-1], conv_got, vectors, *received = tied(crossed[-1], conv_got, vectors, *received)
        last, behind = ring_step(zs - 1, *received)
        block = conv_own(conv_got, [conv_first_own, conv_first_got, order], late)
        vectors = hop(vectors, "y", 1)
        last, block, vectors = tied(last, block, vectors)
        total = add(*behind, last)
        reach = 2
        while reach < zs:
            vectors = hop(vectors, "z", reach)
            reach *= 2
        across, vectors = tied(swap(total, "replica"), vectors)
        ours, others = jnp.where(same, total, across), jnp.where(same, across, total)
        aside = swap(others, "core")
        vector = jax.ShapeDtypeStruct((1, chans), F32)
        new_kernel, *new_v = call(
            partial(finish_kernel, cols),
            (jax.ShapeDtypeStruct(shard.shape, F32), vector, vector, vector),
            [SMEM_SPEC] * 2 + [VMEM_SPEC] * 6, [], 8, flops // 16,
        )(dev, step, shard, mine, theirs, ours, aside, vectors)
    else:
        late = [lax.all_gather(unit, NODE, axis=0, tiled=True)]
        cots, slope, slope_x = slopes_of(stats)
        sums = back(0, cots, [slope, slope_x], late)
        vectors = chip_sum(sums)
        block = conv_own(swap(conv_far(acts, late), "core"), [], late)
        terms = pieces[0].reshape(2 * zs, 2, part, cols.lead)
        summed = lax.psum_scatter(terms, NODE, scatter_dimension=0, tiled=False)
        ours = lax.dynamic_index_in_dim(summed, core, 0, keepdims=False)
        got = swap(lax.dynamic_index_in_dim(summed, 1 - core, 0, keepdims=False), "core")
        left, right = jnp.where(lower, ours, got), jnp.where(lower, got, ours)
        kernel_grad = jnp.concatenate([left, right[:, cols.both:]], axis=1).astype(F32)
        level = step[0] % (replicas.bit_length() - 1)
        rate = LR_KERNEL * (1.0 - (step[0] % 1000).astype(F32) / 2000.0)
        stepped = shard - (scale * rate) * kernel_grad
        new_kernel = 0.5 * (stepped + from_peer(level, stepped.astype(BF16)).astype(F32))
        stepped_v = lax.psum(vectors, NODE)
        new_v = jnp.split(0.5 * (stepped_v + from_peer(level, stepped_v)), 3)

    return (
        block[None],
        new_kernel[None],
        new_v[0],
        new_v[1],
        new_v[2],
    )


def solution(mesh):
    replicas, shards = mesh.shape["replica"], mesh.shape["shard"]
    split = Mesh(mesh.devices.reshape(replicas, shards // 4, 2, 2), ("replica", "z", "y", "core"))
    shard = ("z", "y", "core")
    return jax.shard_map(
        per_device,
        mesh=split,
        in_specs=(
            P("replica", shard, None, None),
            P("replica", shard, None, None),
            P("replica", shard, None),
            P("replica", None),
            P("replica", None),
            P("replica", None),
            P(),
        ),
        out_specs=(
            P("replica", shard, None, None),
            P("replica", shard, None),
            P("replica", None),
            P("replica", None),
            P("replica", None),
        ),
        check_vma=False,
    )
```

```python
from functools import partial

import jax
import jax.numpy as jnp
import numpy as np
from jax import lax
from jax.experimental import pallas as pl
from jax.experimental.pallas import tpu as pltpu
from jax.sharding import Mesh, PartitionSpec as P

GROUPS = 32
EPS = 1e-05
LR_KERNEL = 0.1
LR_VECTOR = 0.01
LANES = 128
BF16 = jnp.bfloat16
F32 = jnp.float32

SMEM_SPEC = pl.BlockSpec(memory_space=pltpu.SMEM)
VMEM_SPEC = pl.BlockSpec(memory_space=pltpu.VMEM)


class Columns:
    def __init__(self, chans):
        tiles = 9 * chans // LANES
        self.total = 9 * chans
        self.lead = (tiles + 1) // 2 * LANES
        self.start = self.total - self.lead
        self.both = 2 * self.lead - self.total
        self.mid = self.lead - 4 * chans
        self.mid_start = chans - self.mid

    def pair(self, core, k, chans):
        first = jnp.where(core == 0, 2 * k, 5 + 2 * k)
        place = jnp.where(core == 0, 2 * k * chans, self.mid + 2 * k * chans)
        return (first, first + 1), pl.multiple_of(place, LANES)

    def middle(self, core, chans):
        place = jnp.where(core == 0, 4 * chans, 0)
        channel = jnp.where(core == 0, 0, self.mid_start)
        return pl.multiple_of(place, LANES), pl.multiple_of(channel, LANES)


def fill_shifts(shifts, row, values):
    width = values.shape[0]
    at = lax.broadcasted_iota(jnp.int32, values.shape, 0)
    left = jnp.where(at == 0, 0.0, pltpu.roll(values, 1, 0))
    right = jnp.where(at == width - 1, 0.0, pltpu.roll(values, width - 1, 0))
    shifts[0, row] = left.astype(BF16)
    shifts[1, row] = values.astype(BF16)
    shifts[2, row] = right.astype(BF16)


def clear_edges(shifts):
    zero = jnp.zeros(shifts.shape[2:], shifts.dtype)
    for b in range(3):
        shifts[b, 0] = zero
        shifts[b, shifts.shape[1] - 1] = zero


def act_kernel(order, dev, table, lat_own, lat_far, cot_own, cot_far, gain, shift,
               stats, acts, cot_t, cot_f):
    me = dev[0]
    core = me % 2
    half, width, chans = lat_own.shape
    cells = 2 * half * width
    group_width = chans // GROUPS
    own_at = core * half
    far_at = half - own_at
    clear_edges(acts)

    def add_row(i, sums):
        total, square = sums
        a = lat_own[i].astype(F32)
        b = lat_far[i].astype(F32)
        return total + (a + b), square + (a * a + b * b)

    zero = jnp.zeros((width, chans), F32)
    total, square = lax.fori_loop(0, half, add_row, (zero, zero))
    sums = jnp.concatenate(
        [jnp.sum(total, axis=0, keepdims=True), jnp.sum(square, axis=0, keepdims=True),
         jnp.zeros((6, chans), F32)], axis=0
    )
    first = lax.broadcasted_iota(jnp.int32, (chans, LANES), 0)
    start = lax.broadcasted_iota(jnp.int32, (chans, LANES), 1) * group_width
    member = jnp.where((first >= start) & (first < start + group_width), 1.0, 0.0)
    exact = partial(lax.dot_general, precision=lax.Precision.HIGHEST, preferred_element_type=F32)
    sums = exact(sums, member, (((1,), (0,)), ((), ()))) / (cells * group_width)
    sums = exact(sums, member, (((1,), (1,)), ((), ())))
    mean = sums[0:1]
    rstd = lax.rsqrt(sums[1:2] - mean * mean + EPS)
    stats[0:1] = mean
    stats[1:2] = rstd
    gain_v, shift_v = gain[...], shift[...]

    def act_rows(i, _):
        for ref, base in ((lat_own, own_at), (lat_far, far_at)):
            pre = gain_v * ((ref[i].astype(F32) - mean) * rstd) + shift_v
            fill_shifts(acts, base + i + 1, pre * (0.5 + 0.5 * jnp.tanh(0.5 * pre)))
        return 0

    lax.fori_loop(0, half, act_rows, 0)

    chunk = LANES // width
    for ref, base in ((cot_own, own_at), (cot_far, far_at)):
        for i in range(half // chunk):
            piece = ref[i * chunk:(i + 1) * chunk].reshape(LANES, chans).astype(F32)
            place = pl.multiple_of(base * width + i * LANES, LANES)
            if order is None:
                cot_t[:, pl.ds(place, LANES)] = piece.T.astype(BF16)
            else:
                cot_f[:, pl.ds(place, LANES)] = piece.T
    if order is not None:
        first_at, part, count = order
        for q in range(count // 2):
            pair = [
                cot_f[pl.ds(pl.multiple_of(table[me, first_at + 2 * q + i], 8), part)]
                for i in range(2)
            ]
            cot_t[2 * q * part:(2 * q + 2) * part] = jnp.concatenate(pair).astype(BF16)


def grad_kernel(cols, carrier, dev, acts, cot_t, mine, theirs, *pieces):
    core = dev[0] % 2
    rows, width, chans = acts.shape[1] - 2, acts.shape[2], acts.shape[3]
    cells = rows * width

    def emit(window, place, wide):
        value = jnp.dot(cot_t[...], window, preferred_element_type=F32)
        at = 0
        for i, piece in enumerate(pieces):
            count = piece.shape[0] - (2 * mine.shape[0] if i == carrier else 0)
            piece[:count, pl.ds(place, wide)] = value[at:at + count].astype(BF16)
            at += count

    def two_taps(k, _):
        taps, place = cols.pair(core, k, chans)
        windows = [acts[t % 3, pl.ds(t // 3, rows)].reshape(cells, chans) for t in taps]
        emit(jnp.concatenate(windows, axis=1), place, 2 * chans)
        return 0

    lax.fori_loop(0, 2, two_taps, 0)
    place, channel = cols.middle(core, chans)
    emit(acts[1, 1:rows + 1, :, pl.ds(channel, cols.mid)].reshape(cells, cols.mid), place, cols.mid)
    if carrier is not None:
        pieces[carrier][-2 * mine.shape[0]:] = jnp.concatenate([mine[...], theirs[...]])


class Stages:
    def __init__(self, counts, rows):
        self.rows = rows
        self.counts = counts
        self.widths = [-(-n * rows // LANES) * LANES for n in counts]
        self.starts = [sum(self.widths[:i]) for i in range(len(counts))]
        self.width = sum(self.widths)

    def lanes(self, stage):
        return slice(self.starts[stage], self.starts[stage] + self.widths[stage])

    def columns(self, stage, blocks, place, wide):
        parts = [ref[:, pl.ds(place, wide)] for ref in blocks]
        if len(parts) == self.counts[stage] + 1:
            parts[-2:] = [jnp.concatenate(parts[-2:])]
        spare = self.widths[stage] - self.counts[stage] * self.rows
        if spare:
            parts.append(jnp.zeros((spare, wide), BF16))
        return jnp.concatenate(parts) if len(parts) > 1 else parts[0]

    def order(self, me, table, order, chans):
        lane = lax.broadcasted_iota(jnp.int32, (1, self.width), 1)
        source = jnp.full((1, self.width), -1, jnp.int32)
        at = 0
        for start, count in zip(self.starts, self.counts):
            for i in range(count):
                first = start + i * self.rows
                inside = (lane >= first) & (lane < first + self.rows)
                source = jnp.where(inside, table[me, at] * self.rows + lane - first, source)
                at += 1
        channel = lax.broadcasted_iota(jnp.int32, (chans, self.width), 0)
        order[...] = jnp.where(channel == source, 1.0, 0.0).astype(BF16)


def slope_kernel(stages, dev, table, stats, gain, shift, lat_own, lat_far, cot_own, cot_far,
                 cots, slope, slope_x, *refs):
    me = dev[0]
    core = me % 2
    half, width, chans = lat_own.shape
    clear_edges(cots)
    mean, rstd = stats[0:1], stats[1:2]
    gain_v, shift_v = gain[...], shift[...]
    far_at = half - core * half
    if len(stages.counts) > 1:
        order, placed = refs
        stages.order(me, table, order, chans)
        for ref, base in ((cot_own, core * half), (cot_far, far_at)):
            value = jnp.dot(ref[...].reshape(half * width, chans), order[...], preferred_element_type=F32)
            placed[pl.ds(base, half)] = value.reshape(half, width, stages.width)

    def one_row(i, _):
        for lat, cot, base in ((lat_own, cot_own, core * half), (lat_far, cot_far, far_at)):
            value = placed[base + i] if len(stages.counts) > 1 else cot[i].astype(F32)
            fill_shifts(cots, base + i + 1, value)
            xhat = (lat[i].astype(F32) - mean) * rstd
            pre = gain_v * xhat + shift_v
            sig = 0.5 + 0.5 * jnp.tanh(0.5 * pre)
            value = sig * (1.0 + pre * (1.0 - sig))
            slope[base + i] = value.astype(BF16)
            slope_x[base + i] = (value * xhat).astype(BF16)
        return 0

    lax.fori_loop(0, half, one_row, 0)


def conv_sum(cols, stages, stage, core, first, half, acts, blocks, total):
    width, chans = acts.shape[2:]
    cells = half * width
    nt = (((1,), (1,)), ((), ()))
    place, channel = cols.middle(core, chans)
    window = acts[1, pl.ds(first + 1, half), :, pl.ds(channel, cols.mid)].reshape(cells, cols.mid)
    lane = lax.broadcasted_iota(jnp.int32, window.shape, 1)
    window = jnp.where((core == 1) & (lane < cols.both), jnp.zeros_like(window), window)
    kernel = stages.columns(stage, blocks, place, cols.mid)
    total[...] = lax.dot_general(window, kernel, nt, preferred_element_type=F32)

    def two_taps(k, _):
        taps, place = cols.pair(core, k, chans)
        windows = [acts[t % 3, pl.ds(first + t // 3, half)].reshape(cells, chans) for t in taps]
        kernel = stages.columns(stage, blocks, place, 2 * chans)
        total[...] += lax.dot_general(
            jnp.concatenate(windows, axis=1), kernel, nt, preferred_element_type=F32
        )
        return 0

    lax.fori_loop(0, 2, two_taps, 0)


def conv_both_kernel(cols, stages, stage, dev, acts, *refs):
    blocks, (own, far, total) = refs[:-3], refs[-3:]
    core = dev[0] % 2
    rows = acts.shape[1] - 2
    conv_sum(cols, stages, stage, core, 0, rows, acts, blocks, total)
    half = own.shape[0]
    own[...] = total[pl.ds(pl.multiple_of(core * half, half), half)]
    far[...] = total[pl.ds(pl.multiple_of((1 - core) * half, half), half)].astype(BF16)


def conv_far_kernel(cols, stages, stage, dev, acts, *refs):
    blocks, (far, total) = refs[:-2], refs[-2:]
    core = dev[0] % 2
    half = (acts.shape[1] - 2) // 2
    conv_sum(cols, stages, stage, core, (1 - core) * half, half, acts, blocks, total)
    far[...] = total[...].astype(BF16)


def conv_own_kernel(cols, stages, dev, acts, got, latent, bias, *refs):
    core = dev[0] % 2
    half, width, chans = latent.shape
    scale = cols.total ** (-0.5)
    stage = len(stages.counts) - 1
    before = 3 * stage
    blocks, (block, total) = refs[before:-2], refs[-2:]
    conv_sum(cols, stages, stage, core, core * half, half, acts, blocks, total)
    conv = total[...] + got[...].astype(F32)
    if stage:
        first_own, first_got, order = refs[:before]
        conv = jnp.concatenate([first_own[...] + first_got[...].astype(F32), conv], axis=1)
        high = conv.astype(BF16)
        low = (conv - high.astype(F32)).astype(BF16)
        nt = (((1,), (1,)), ((), ()))
        conv = sum(
            lax.dot_general(value, order[...], nt, preferred_element_type=F32) for value in (low, high)
        )
    conv = scale * conv + bias[...]
    block[...] = (conv.reshape(half, width, chans) + latent[...].astype(F32)).astype(BF16)


def back_kernel(cols, stages, stage, dev, cots, slope, slope_x, *refs):
    blocks, (sums, total) = refs[:-2], refs[-2:]
    core = dev[0] % 2
    rows, width = cots.shape[1] - 2, cots.shape[2]
    cells, chans = total.shape
    lanes = stages.lanes(stage)

    def taps_from(first, place, count):
        windows, kernels = [], []
        for i in range(count):
            tap = first + i
            window = cots[2 - tap % 3, pl.ds(2 - tap // 3, rows), :, lanes]
            windows.append(window.reshape(cells, stages.widths[stage]))
            kernels.append(stages.columns(stage, blocks, pl.multiple_of(place + i * chans, LANES), chans))
        return jnp.dot(
            jnp.concatenate(windows, axis=1), jnp.concatenate(kernels), preferred_element_type=F32
        )

    if stages.widths[stage] * 4 <= 2 * chans:
        taps, place = cols.pair(core, 0, chans)
        total[...] = taps_from(taps[0], place, 4)
    else:
        total[...] = jnp.zeros_like(total)

        def two_taps(k, _):
            taps, place = cols.pair(core, k, chans)
            total[...] += taps_from(taps[0], place, 2)
            return 0

        lax.fori_loop(0, 2, two_taps, 0)

    place, channel = cols.middle(core, chans)
    window = cots[1, 1:rows + 1, :, lanes].reshape(cells, stages.widths[stage])
    kernel = stages.columns(stage, blocks, place, cols.mid)
    value = jnp.dot(window, kernel, preferred_element_type=F32)
    lane = lax.broadcasted_iota(jnp.int32, value.shape, 1)
    total[:, pl.ds(channel, cols.mid)] += jnp.where((core == 1) & (lane < cols.both), 0.0, value)

    def add_row(i, carry):
        gains, shifts = carry
        value = total[pl.ds(pl.multiple_of(i * width, width), width)]
        return gains + value * slope_x[i].astype(F32), shifts + value * slope[i].astype(F32)

    zero = jnp.zeros((width, chans), F32)
    gains, shifts = lax.fori_loop(0, rows, add_row, (zero, zero))
    scale = cols.total ** (-0.5)
    sums[0:1] = scale * jnp.sum(gains, axis=0, keepdims=True)
    sums[1:2] = scale * jnp.sum(shifts, axis=0, keepdims=True)


def finish_kernel(cols, dev, step, shard, carried, ours, aside, vectors, out, new_bias, new_gain, new_shift):
    lower = dev[0] % 2 == 0
    rate = LR_KERNEL * (1.0 - (step[0] % 1000).astype(F32) / 2000.0)
    factor = 0.5 * cols.total ** (-0.5) * rate
    part = shard.shape[0]
    peer = carried[-2 * part:].astype(F32)
    mine, theirs = peer[:part], peer[part:]
    here = 0.5 * mine - factor * ours[...].astype(F32)
    there = 0.5 * theirs - factor * aside[...].astype(F32)
    left, right = jnp.where(lower, here, there), jnp.where(lower, there, here)
    out[:, :cols.lead] = 0.5 * shard[:, :cols.lead] + left
    out[:, cols.lead:] = 0.5 * shard[:, cols.lead:] + right[:, cols.both:]
    for i, new in enumerate((new_bias, new_gain, new_shift)):
        new[...] = 0.5 * vectors[i:i + 1]


NODE = ("z", "y")


def swap(value, axis):
    return lax.ppermute(value, axis, [(0, 1), (1, 0)])


def from_peer(level, value):
    count = lax.axis_size("replica")
    levels = count.bit_length() - 1
    moves = [[(s, (s + (1 << k)) % count) for s in range(count)] for k in range(levels)]
    if levels == 1:
        return lax.ppermute(value, "replica", moves[0])
    return lax.switch(level, [lambda v, m=m: lax.ppermute(v, "replica", m) for m in moves], value)


class Ring:
    def __init__(self, zs):
        self.count = 2 * zs
        self.reach = zs
        self.nodes = [2 * z for z in range(zs)] + [2 * z + 1 for z in reversed(range(zs))]
        ahead = list(zip(self.nodes, self.nodes[1:] + self.nodes[:1]))
        self.ahead = ahead
        self.behind = [(b, a) for a, b in ahead]

    def node(self, at, offset):
        return self.nodes[(at + offset) % self.count]

    def up(self, value):
        return lax.ppermute(value, NODE, self.ahead)

    def down(self, value):
        return lax.ppermute(value, NODE, self.behind)

    def table(self, part):
        rows = np.zeros((2, self.count, 2, 3 * self.count), np.int32)
        for replica in range(2):
            for at, node in enumerate(self.nodes):
                line = [node]
                for k in range(1, self.reach + 1):
                    line.append(self.node(at, -k))
                    if k < self.reach:
                        line.append(self.node(at, k))
                for which in (replica, 1 - replica):
                    for j in range(self.reach):
                        targets = [self.node(at, self.reach - j), self.node(at, j + 1 - self.reach)]
                        line += [(2 * target + which) * part for target in targets]
                rows[replica, node, :] = line
        return rows.reshape(-1, 3 * self.count)


def hop(value, axis, mask):
    count = lax.axis_size(axis)
    return value + lax.ppermute(value, axis, [(s, s ^ mask) for s in range(count)])


def add(*values):
    total = values[0].astype(F32)
    for value in values[1:]:
        total = total + value.astype(F32)
    return total.astype(BF16)


def tied(*values):
    return lax.optimization_barrier(values)


def per_device(latents, cotangent, kernel, conv_bias, gn_gain, gn_shift, step):
    latent, cotan, shard = latents[0], cotangent[0], kernel[0]
    half, width, chans = latent.shape
    part = shard.shape[0]
    cols = Columns(chans)
    cells = half * width
    zs, replicas = lax.axis_size("z"), lax.axis_size("replica")
    core, z, y, replica = (lax.axis_index(a) for a in ("core", "z", "y", "replica"))
    lower = core == 0
    paired = replicas == 2
    ring = Ring(zs)
    scale = cols.total ** (-0.5)
    params = jnp.concatenate([conv_bias, gn_gain, gn_shift])
    me = ((replica * zs + z) * 2 + y) * 2 + core
    core, lower, same, me = tied(core, lower, replica == core, me)
    dev = me.reshape(1)

    mine = lax.dynamic_slice_in_dim(shard, core * cols.start, cols.lead, 1).astype(BF16)
    theirs = lax.dynamic_slice_in_dim(shard, (1 - core) * cols.start, cols.lead, 1).astype(BF16)
    got = swap(theirs, "core")
    unit = jnp.where(lower, jnp.concatenate([mine, got]), jnp.concatenate([got, mine]))
    lat_far = swap(latent, "core")
    cot_b = cotan.astype(BF16)
    cot_far = swap(cot_b, "core")

    if paired:
        table = jnp.asarray(ring.table(part))
        order = (ring.count, part, 2 * ring.count)
        up1, down1 = ring.up(unit), ring.down(unit)
    else:
        table = jnp.zeros((replicas * zs * 4, 1), jnp.int32)
        order = None

    def call(body, outs, ins, scratch, megabytes, flops):
        return pl.pallas_call(
            body,
            out_shape=outs,
            in_specs=ins,
            out_specs=jax.tree.map(lambda _: VMEM_SPEC, outs),
            scratch_shapes=scratch,
            compiler_params=pltpu.CompilerParams(vmem_limit_bytes=megabytes * 2**20),
            cost_estimate=pl.CostEstimate(flops=flops, bytes_accessed=0, transcendentals=0),
        )

    image = (2 * half, width, chans)
    shifted = jax.ShapeDtypeStruct((3, 2 * half + 2, width, chans), BF16)
    flops = 2 * 2 * cells * chans * cols.lead
    stats, acts, cot_t = call(
        partial(act_kernel, order),
        (jax.ShapeDtypeStruct((2, chans), F32), shifted, jax.ShapeDtypeStruct((chans, 2 * cells), BF16)),
        [SMEM_SPEC] * 2 + [VMEM_SPEC] * 6,
        [pltpu.VMEM((chans, 2 * cells), F32)],
        8, flops // 4,
    )(dev, table, latent, lat_far, cot_b, cot_far, gn_gain, gn_shift)
    counts = [zs, 1, 2] + [1] * (zs - 2) if paired else [2 * zs]
    pieces = call(
        partial(grad_kernel, cols, 2 if paired else None),
        [jax.ShapeDtypeStruct((n * 2 * part, cols.lead), BF16) for n in counts],
        [SMEM_SPEC] + [VMEM_SPEC] * 4,
        [],
        4, flops // 2,
    )(dev, acts, cot_t, mine, theirs)
    stages = Stages([2 * zs - 3, 3] if paired else [1], 2 * part if paired else chans)
    staged = paired

    def slopes_of(stats):
        extra = (jax.ShapeDtypeStruct((chans, stages.width), BF16),) if staged else ()
        return call(
            partial(slope_kernel, stages),
            (jax.ShapeDtypeStruct((3, 2 * half + 2, width, stages.width), BF16),
             jax.ShapeDtypeStruct(image, BF16), jax.ShapeDtypeStruct(image, BF16)) + extra,
            [SMEM_SPEC] * 2 + [VMEM_SPEC] * 7,
            [pltpu.VMEM((2 * half, width, stages.width), F32)] if staged else [],
            8, flops // 4,
        )(dev, table, stats, gn_gain, gn_shift, latent, lat_far, cot_b, cot_far)

    def back(stage, cots, slopes, blocks):
        return call(
            partial(back_kernel, cols, stages, stage), jax.ShapeDtypeStruct((2, chans), F32),
            [SMEM_SPEC] + [VMEM_SPEC] * (3 + len(blocks)),
            [pltpu.VMEM((2 * cells, chans), F32)], 8, flops // 4,
        )(dev, cots, *slopes, *blocks)

    def conv_first(blocks):
        wide = stages.widths[0]
        return call(
            partial(conv_both_kernel, cols, stages, 0),
            (jax.ShapeDtypeStruct((cells, wide), F32), jax.ShapeDtypeStruct((cells, wide), BF16)),
            [SMEM_SPEC] + [VMEM_SPEC] * (1 + len(blocks)),
            [pltpu.VMEM((2 * cells, wide), F32)], 6, flops // 4,
        )(dev, acts, *blocks)

    def conv_far(acts, blocks):
        wide = stages.widths[-1]
        return call(
            partial(conv_far_kernel, cols, stages, len(stages.counts) - 1),
            jax.ShapeDtypeStruct((cells, wide), BF16),
            [SMEM_SPEC] + [VMEM_SPEC] * (1 + len(blocks)),
            [pltpu.VMEM((cells, wide), F32)], 4, flops // 8,
        )(dev, acts, *blocks)

    def conv_own(got, earlier, blocks):
        return call(
            partial(conv_own_kernel, cols, stages), jax.ShapeDtypeStruct((half, width, chans), BF16),
            [SMEM_SPEC] + [VMEM_SPEC] * (4 + len(earlier) + len(blocks)),
            [pltpu.VMEM((cells, stages.widths[-1]), F32)], 8, flops // 4,
        )(dev, acts, got, latent, conv_bias, *earlier, *blocks)

    def chip_sum(sums):
        vectors = jnp.concatenate([jnp.sum(cotan, axis=(0, 1))[None], sums])
        vectors = params / (4 * zs) - LR_VECTOR * vectors
        return vectors + swap(vectors, "core")

    if paired:
        kept, *sent = pieces
        crossed = [swap(piece, "replica") for piece in sent]

        def ring_sums(j, *received):
            parts = kept[2 * j * part:(2 * j + 2) * part], crossed[j]
            ahead, behind = (tuple(x[at:at + part] for x in parts) for at in (0, part))
            ahead = add(*ahead, *received[:1])
            behind = behind + tuple(received[1:])
            return ahead, add(*behind) if j < zs - 1 else behind

        def ring_step(ahead, behind):
            return ring.up(ahead), ring.down(behind)

        up, down, _ = tied(up1, down1, sent[0])
        blocks = [unit, up, down]
        up, down = ring.up(up), ring.down(down)
        cots, *slopes, order = slopes_of(stats)
        up, down, cots, *slopes, order = tied(up, down, cots, *slopes, order)
        blocks += [up, down]

        up, down = ring.up(up), ring.down(down)
        conv_first_own, conv_send = conv_first(blocks)
        crossed[0], conv_send = tied(crossed[0], conv_send)
        received = ring_step(*ring_sums(0))
        cots, conv_send = tied(cots, conv_send)
        first_sums = back(0, cots, slopes, blocks)
        up, down, first_sums = tied(up, down, first_sums)
        late = [up, down]

        halves = ring.up(up[:part]), ring.down(down[part:])
        conv_send, *received = tied(conv_send, *received)
        conv_first_got = swap(conv_send, "core")
        for j in range(1, zs - 2):
            received = ring_step(*ring_sums(j, *received))
        late += halves

        conv_send = conv_far(acts, late)
        cots, conv_send = tied(cots, conv_send)
        conv_got = swap(conv_send, "core")
        sums = back(1, cots, slopes, late)
        crossed[-2], sums, *received = tied(crossed[-2], sums, *received)
        received = ring_step(*ring_sums(zs - 2, *received))
        vectors = chip_sum(first_sums + sums)
        conv_got, vectors = tied(conv_got, vectors)
        block = conv_own(conv_got, [conv_first_own, conv_first_got, order], late)
        vectors = hop(hop(vectors, "replica", 1), "z", 1)
        crossed[-1], block, vectors, *received = tied(crossed[-1], block, vectors, *received)
        ahead, behind = ring_sums(zs - 1, *received)
        last = ring.up(ahead)
        vectors = hop(vectors, "y", 1)
        reach = 2
        while reach < zs:
            vectors = hop(vectors, "z", reach)
            reach *= 2
        last, vectors = tied(last, vectors)
        total = add(*behind, last)
        across = swap(total, "replica")
        ours, others = jnp.where(same, total, across), jnp.where(same, across, total)
        aside = swap(others, "core")
        vector = jax.ShapeDtypeStruct((1, chans), F32)
        new_kernel, *new_v = call(
            partial(finish_kernel, cols),
            (jax.ShapeDtypeStruct(shard.shape, F32), vector, vector, vector),
            [SMEM_SPEC] * 2 + [VMEM_SPEC] * 5, [], 8, flops // 16,
        )(dev, step, shard, crossed[1], ours, aside, vectors)
    else:
        late = [lax.all_gather(unit, NODE, axis=0, tiled=True)]
        cots, slope, slope_x = slopes_of(stats)
        sums = back(0, cots, [slope, slope_x], late)
        vectors = chip_sum(sums)
        block = conv_own(swap(conv_far(acts, late), "core"), [], late)
        terms = pieces[0].reshape(2 * zs, 2, part, cols.lead)
        summed = lax.psum_scatter(terms, NODE, scatter_dimension=0, tiled=False)
        ours = lax.dynamic_index_in_dim(summed, core, 0, keepdims=False)
        got = swap(lax.dynamic_index_in_dim(summed, 1 - core, 0, keepdims=False), "core")
        left, right = jnp.where(lower, ours, got), jnp.where(lower, got, ours)
        kernel_grad = jnp.concatenate([left, right[:, cols.both:]], axis=1).astype(F32)
        level = step[0] % (replicas.bit_length() - 1)
        rate = LR_KERNEL * (1.0 - (step[0] % 1000).astype(F32) / 2000.0)
        stepped = shard - (scale * rate) * kernel_grad
        new_kernel = 0.5 * (stepped + from_peer(level, stepped.astype(BF16)).astype(F32))
        stepped_v = lax.psum(vectors, NODE)
        new_v = jnp.split(0.5 * (stepped_v + from_peer(level, stepped_v)), 3)

    return (
        block[None],
        new_kernel[None],
        new_v[0],
        new_v[1],
        new_v[2],
    )


def solution(mesh):
    replicas, shards = mesh.shape["replica"], mesh.shape["shard"]
    split = Mesh(mesh.devices.reshape(replicas, shards // 4, 2, 2), ("replica", "z", "y", "core"))
    shard = ("z", "y", "core")
    return jax.shard_map(
        per_device,
        mesh=split,
        in_specs=(
            P("replica", shard, None, None),
            P("replica", shard, None, None),
            P("replica", shard, None),
            P("replica", None),
            P("replica", None),
            P("replica", None),
            P(),
        ),
        out_specs=(
            P("replica", shard, None, None),
            P("replica", shard, None),
            P("replica", None),
            P("replica", None),
            P("replica", None),
        ),
        check_vma=False,
    )
```

```python
from functools import partial

import jax
import jax.numpy as jnp
import numpy as np
from jax import lax
from jax.experimental import pallas as pl
from jax.experimental.pallas import tpu as pltpu
from jax.sharding import Mesh, PartitionSpec as P

GROUPS = 32
EPS = 1e-05
LR_KERNEL = 0.1
LR_VECTOR = 0.01
LANES = 128
BF16 = jnp.bfloat16
F32 = jnp.float32

SMEM_SPEC = pl.BlockSpec(memory_space=pltpu.SMEM)
VMEM_SPEC = pl.BlockSpec(memory_space=pltpu.VMEM)


class Columns:
    def __init__(self, chans):
        tiles = 9 * chans // LANES
        self.total = 9 * chans
        self.lead = (tiles + 1) // 2 * LANES
        self.start = self.total - self.lead
        self.both = 2 * self.lead - self.total
        self.mid = self.lead - 4 * chans
        self.mid_start = chans - self.mid

    def pair(self, core, k, chans):
        first = jnp.where(core == 0, 2 * k, 5 + 2 * k)
        place = jnp.where(core == 0, 2 * k * chans, self.mid + 2 * k * chans)
        return (first, first + 1), pl.multiple_of(place, LANES)

    def middle(self, core, chans):
        place = jnp.where(core == 0, 4 * chans, 0)
        channel = jnp.where(core == 0, 0, self.mid_start)
        return pl.multiple_of(place, LANES), pl.multiple_of(channel, LANES)


def fill_shifts(shifts, row, values):
    width = values.shape[0]
    at = lax.broadcasted_iota(jnp.int32, values.shape, 0)
    left = jnp.where(at == 0, 0.0, pltpu.roll(values, 1, 0))
    right = jnp.where(at == width - 1, 0.0, pltpu.roll(values, width - 1, 0))
    shifts[0, row] = left.astype(BF16)
    shifts[1, row] = values.astype(BF16)
    shifts[2, row] = right.astype(BF16)


def clear_edges(shifts):
    zero = jnp.zeros(shifts.shape[2:], shifts.dtype)
    for b in range(3):
        shifts[b, 0] = zero
        shifts[b, shifts.shape[1] - 1] = zero


def act_kernel(order, dev, table, lat_own, lat_far, cot_own, cot_far, gain, shift,
               stats, acts, cot_t, cot_f):
    me = dev[0]
    core = me % 2
    half, width, chans = lat_own.shape
    cells = 2 * half * width
    group_width = chans // GROUPS
    own_at = core * half
    far_at = half - own_at
    clear_edges(acts)

    def add_row(i, sums):
        total, square = sums
        a = lat_own[i].astype(F32)
        b = lat_far[i].astype(F32)
        return total + (a + b), square + (a * a + b * b)

    zero = jnp.zeros((width, chans), F32)
    total, square = lax.fori_loop(0, half, add_row, (zero, zero))
    sums = jnp.concatenate(
        [jnp.sum(total, axis=0, keepdims=True), jnp.sum(square, axis=0, keepdims=True),
         jnp.zeros((6, chans), F32)], axis=0
    )
    first = lax.broadcasted_iota(jnp.int32, (chans, LANES), 0)
    start = lax.broadcasted_iota(jnp.int32, (chans, LANES), 1) * group_width
    member = jnp.where((first >= start) & (first < start + group_width), 1.0, 0.0)
    exact = partial(lax.dot_general, precision=lax.Precision.HIGHEST, preferred_element_type=F32)
    sums = exact(sums, member, (((1,), (0,)), ((), ()))) / (cells * group_width)
    sums = exact(sums, member, (((1,), (1,)), ((), ())))
    mean = sums[0:1]
    rstd = lax.rsqrt(sums[1:2] - mean * mean + EPS)
    stats[0:1] = mean
    stats[1:2] = rstd
    gain_v, shift_v = gain[...], shift[...]

    def act_rows(i, _):
        for ref, base in ((lat_own, own_at), (lat_far, far_at)):
            pre = gain_v * ((ref[i].astype(F32) - mean) * rstd) + shift_v
            fill_shifts(acts, base + i + 1, pre * (0.5 + 0.5 * jnp.tanh(0.5 * pre)))
        return 0

    lax.fori_loop(0, half, act_rows, 0)

    chunk = LANES // width
    for ref, base in ((cot_own, own_at), (cot_far, far_at)):
        for i in range(half // chunk):
            piece = ref[i * chunk:(i + 1) * chunk].reshape(LANES, chans).astype(F32)
            place = pl.multiple_of(base * width + i * LANES, LANES)
            if order is None:
                cot_t[:, pl.ds(place, LANES)] = piece.T.astype(BF16)
            else:
                cot_f[:, pl.ds(place, LANES)] = piece.T
    if order is not None:
        first_at, part, count = order
        for q in range(count // 2):
            pair = [
                cot_f[pl.ds(pl.multiple_of(table[me, first_at + 2 * q + i], 8), part)]
                for i in range(2)
            ]
            cot_t[2 * q * part:(2 * q + 2) * part] = jnp.concatenate(pair).astype(BF16)


def grad_kernel(cols, dev, acts, cot_t, *pieces):
    core = dev[0] % 2
    rows, width, chans = acts.shape[1] - 2, acts.shape[2], acts.shape[3]
    cells = rows * width

    def emit(window, place, wide):
        value = jnp.dot(cot_t[...], window, preferred_element_type=F32)
        at = 0
        for piece in pieces:
            piece[:, pl.ds(place, wide)] = value[at:at + piece.shape[0]].astype(BF16)
            at += piece.shape[0]

    def two_taps(k, _):
        taps, place = cols.pair(core, k, chans)
        windows = [acts[t % 3, pl.ds(t // 3, rows)].reshape(cells, chans) for t in taps]
        emit(jnp.concatenate(windows, axis=1), place, 2 * chans)
        return 0

    lax.fori_loop(0, 2, two_taps, 0)
    place, channel = cols.middle(core, chans)
    emit(acts[1, 1:rows + 1, :, pl.ds(channel, cols.mid)].reshape(cells, cols.mid), place, cols.mid)


class Stages:
    def __init__(self, counts, rows):
        self.rows = rows
        self.counts = counts
        self.widths = [-(-n * rows // LANES) * LANES for n in counts]
        self.starts = [sum(self.widths[:i]) for i in range(len(counts))]
        self.width = sum(self.widths)

    def lanes(self, stage):
        return slice(self.starts[stage], self.starts[stage] + self.widths[stage])

    def columns(self, stage, blocks, place, wide):
        parts = [ref[:, pl.ds(place, wide)] for ref in blocks]
        if len(parts) == self.counts[stage] + 1:
            parts[-2:] = [jnp.concatenate(parts[-2:])]
        spare = self.widths[stage] - self.counts[stage] * self.rows
        if spare:
            parts.append(jnp.zeros((spare, wide), BF16))
        return jnp.concatenate(parts) if len(parts) > 1 else parts[0]

    def order(self, me, table, order, chans):
        lane = lax.broadcasted_iota(jnp.int32, (1, self.width), 1)
        source = jnp.full((1, self.width), -1, jnp.int32)
        at = 0
        for start, count in zip(self.starts, self.counts):
            for i in range(count):
                first = start + i * self.rows
                inside = (lane >= first) & (lane < first + self.rows)
                source = jnp.where(inside, table[me, at] * self.rows + lane - first, source)
                at += 1
        channel = lax.broadcasted_iota(jnp.int32, (chans, self.width), 0)
        order[...] = jnp.where(channel == source, 1.0, 0.0).astype(BF16)


def slope_kernel(stages, dev, table, stats, gain, shift, lat_own, lat_far, cot_own, cot_far,
                 cots, slope, slope_x, *refs):
    me = dev[0]
    core = me % 2
    half, width, chans = lat_own.shape
    clear_edges(cots)
    mean, rstd = stats[0:1], stats[1:2]
    gain_v, shift_v = gain[...], shift[...]
    far_at = half - core * half
    if len(stages.counts) > 1:
        order, placed = refs
        stages.order(me, table, order, chans)
        for ref, base in ((cot_own, core * half), (cot_far, far_at)):
            value = jnp.dot(ref[...].reshape(half * width, chans), order[...], preferred_element_type=F32)
            placed[pl.ds(base, half)] = value.reshape(half, width, stages.width)

    def one_row(i, _):
        for lat, cot, base in ((lat_own, cot_own, core * half), (lat_far, cot_far, far_at)):
            value = placed[base + i] if len(stages.counts) > 1 else cot[i].astype(F32)
            fill_shifts(cots, base + i + 1, value)
            xhat = (lat[i].astype(F32) - mean) * rstd
            pre = gain_v * xhat + shift_v
            sig = 0.5 + 0.5 * jnp.tanh(0.5 * pre)
            value = sig * (1.0 + pre * (1.0 - sig))
            slope[base + i] = value.astype(BF16)
            slope_x[base + i] = (value * xhat).astype(BF16)
        return 0

    lax.fori_loop(0, half, one_row, 0)


def conv_sum(cols, stages, stage, core, first, half, acts, blocks, total):
    width, chans = acts.shape[2:]
    cells = half * width
    nt = (((1,), (1,)), ((), ()))
    place, channel = cols.middle(core, chans)
    window = acts[1, pl.ds(first + 1, half), :, pl.ds(channel, cols.mid)].reshape(cells, cols.mid)
    lane = lax.broadcasted_iota(jnp.int32, window.shape, 1)
    window = jnp.where((core == 1) & (lane < cols.both), jnp.zeros_like(window), window)
    kernel = stages.columns(stage, blocks, place, cols.mid)
    total[...] = lax.dot_general(window, kernel, nt, preferred_element_type=F32)

    def two_taps(k, _):
        taps, place = cols.pair(core, k, chans)
        windows = [acts[t % 3, pl.ds(first + t // 3, half)].reshape(cells, chans) for t in taps]
        kernel = stages.columns(stage, blocks, place, 2 * chans)
        total[...] += lax.dot_general(
            jnp.concatenate(windows, axis=1), kernel, nt, preferred_element_type=F32
        )
        return 0

    lax.fori_loop(0, 2, two_taps, 0)


def conv_both_kernel(cols, stages, stage, dev, acts, *refs):
    blocks, (own, far, total) = refs[:-3], refs[-3:]
    core = dev[0] % 2
    rows = acts.shape[1] - 2
    conv_sum(cols, stages, stage, core, 0, rows, acts, blocks, total)
    half = own.shape[0]
    own[...] = total[pl.ds(pl.multiple_of(core * half, half), half)]
    far[...] = total[pl.ds(pl.multiple_of((1 - core) * half, half), half)].astype(BF16)


def conv_far_kernel(cols, stages, stage, dev, acts, *refs):
    blocks, (far, total) = refs[:-2], refs[-2:]
    core = dev[0] % 2
    half = (acts.shape[1] - 2) // 2
    conv_sum(cols, stages, stage, core, (1 - core) * half, half, acts, blocks, total)
    far[...] = total[...].astype(BF16)


def conv_own_kernel(cols, stages, dev, acts, got, latent, bias, *refs):
    core = dev[0] % 2
    half, width, chans = latent.shape
    scale = cols.total ** (-0.5)
    stage = len(stages.counts) - 1
    before = 3 * stage
    blocks, (block, total) = refs[before:-2], refs[-2:]
    conv_sum(cols, stages, stage, core, core * half, half, acts, blocks, total)
    conv = total[...] + got[...].astype(F32)
    if stage:
        first_own, first_got, order = refs[:before]
        conv = jnp.concatenate([first_own[...] + first_got[...].astype(F32), conv], axis=1)
        high = conv.astype(BF16)
        low = (conv - high.astype(F32)).astype(BF16)
        nt = (((1,), (1,)), ((), ()))
        conv = sum(
            lax.dot_general(value, order[...], nt, preferred_element_type=F32) for value in (low, high)
        )
    conv = scale * conv + bias[...]
    block[...] = (conv.reshape(half, width, chans) + latent[...].astype(F32)).astype(BF16)


def back_kernel(cols, stages, stage, dev, cots, slope, slope_x, *refs):
    blocks, (sums, total) = refs[:-2], refs[-2:]
    core = dev[0] % 2
    rows, width = cots.shape[1] - 2, cots.shape[2]
    cells, chans = total.shape
    lanes = stages.lanes(stage)

    def taps_from(first, place, count):
        windows, kernels = [], []
        for i in range(count):
            tap = first + i
            window = cots[2 - tap % 3, pl.ds(2 - tap // 3, rows), :, lanes]
            windows.append(window.reshape(cells, stages.widths[stage]))
            kernels.append(stages.columns(stage, blocks, pl.multiple_of(place + i * chans, LANES), chans))
        return jnp.dot(
            jnp.concatenate(windows, axis=1), jnp.concatenate(kernels), preferred_element_type=F32
        )

    if stages.widths[stage] * 4 <= 2 * chans:
        taps, place = cols.pair(core, 0, chans)
        total[...] = taps_from(taps[0], place, 4)
    else:
        total[...] = jnp.zeros_like(total)

        def two_taps(k, _):
            taps, place = cols.pair(core, k, chans)
            total[...] += taps_from(taps[0], place, 2)
            return 0

        lax.fori_loop(0, 2, two_taps, 0)

    place, channel = cols.middle(core, chans)
    window = cots[1, 1:rows + 1, :, lanes].reshape(cells, stages.widths[stage])
    kernel = stages.columns(stage, blocks, place, cols.mid)
    value = jnp.dot(window, kernel, preferred_element_type=F32)
    lane = lax.broadcasted_iota(jnp.int32, value.shape, 1)
    total[:, pl.ds(channel, cols.mid)] += jnp.where((core == 1) & (lane < cols.both), 0.0, value)

    def add_row(i, carry):
        gains, shifts = carry
        value = total[pl.ds(pl.multiple_of(i * width, width), width)]
        return gains + value * slope_x[i].astype(F32), shifts + value * slope[i].astype(F32)

    zero = jnp.zeros((width, chans), F32)
    gains, shifts = lax.fori_loop(0, rows, add_row, (zero, zero))
    scale = cols.total ** (-0.5)
    sums[0:1] = scale * jnp.sum(gains, axis=0, keepdims=True)
    sums[1:2] = scale * jnp.sum(shifts, axis=0, keepdims=True)


def finish_kernel(cols, dev, step, shard, mine, theirs, ours, aside, vectors, out, new_bias, new_gain, new_shift):
    lower = dev[0] % 2 == 0
    rate = LR_KERNEL * (1.0 - (step[0] % 1000).astype(F32) / 2000.0)
    factor = 0.5 * cols.total ** (-0.5) * rate
    here = 0.5 * mine[...].astype(F32) - factor * ours[...].astype(F32)
    there = 0.5 * theirs[...].astype(F32) - factor * aside[...].astype(F32)
    left, right = jnp.where(lower, here, there), jnp.where(lower, there, here)
    out[:, :cols.lead] = 0.5 * shard[:, :cols.lead] + left
    out[:, cols.lead:] = 0.5 * shard[:, cols.lead:] + right[:, cols.both:]
    for i, new in enumerate((new_bias, new_gain, new_shift)):
        new[...] = 0.5 * vectors[i:i + 1]


NODE = ("z", "y")


def swap(value, axis):
    return lax.ppermute(value, axis, [(0, 1), (1, 0)])


def from_peer(level, value):
    count = lax.axis_size("replica")
    levels = count.bit_length() - 1
    moves = [[(s, (s + (1 << k)) % count) for s in range(count)] for k in range(levels)]
    if levels == 1:
        return lax.ppermute(value, "replica", moves[0])
    return lax.switch(level, [lambda v, m=m: lax.ppermute(v, "replica", m) for m in moves], value)


class Ring:
    def __init__(self, zs):
        self.count = 2 * zs
        self.reach = zs
        self.nodes = [2 * z for z in range(zs)] + [2 * z + 1 for z in reversed(range(zs))]
        ahead = list(zip(self.nodes, self.nodes[1:] + self.nodes[:1]))
        self.ahead = ahead
        self.behind = [(b, a) for a, b in ahead]

    def node(self, at, offset):
        return self.nodes[(at + offset) % self.count]

    def up(self, value):
        return lax.ppermute(value, NODE, self.ahead)

    def down(self, value):
        return lax.ppermute(value, NODE, self.behind)

    def table(self, part):
        rows = np.zeros((2, self.count, 2, 3 * self.count), np.int32)
        for replica in range(2):
            for at, node in enumerate(self.nodes):
                line = [node]
                for k in range(1, self.reach + 1):
                    line.append(self.node(at, -k))
                    if k < self.reach:
                        line.append(self.node(at, k))
                for which in (replica, 1 - replica):
                    for j in range(self.reach):
                        targets = [self.node(at, self.reach - j), self.node(at, j + 1 - self.reach)]
                        line += [(2 * target + which) * part for target in targets]
                rows[replica, node, :] = line
        return rows.reshape(-1, 3 * self.count)


def hop(value, axis, mask):
    count = lax.axis_size(axis)
    return value + lax.ppermute(value, axis, [(s, s ^ mask) for s in range(count)])


def add(*values):
    total = values[0].astype(F32)
    for value in values[1:]:
        total = total + value.astype(F32)
    return total.astype(BF16)


def tied(*values):
    return lax.optimization_barrier(values)


def per_device(latents, cotangent, kernel, conv_bias, gn_gain, gn_shift, step):
    latent, cotan, shard = latents[0], cotangent[0], kernel[0]
    half, width, chans = latent.shape
    part = shard.shape[0]
    cols = Columns(chans)
    cells = half * width
    zs, replicas = lax.axis_size("z"), lax.axis_size("replica")
    core, z, y, replica = (lax.axis_index(a) for a in ("core", "z", "y", "replica"))
    lower = core == 0
    paired = replicas == 2
    ring = Ring(zs)
    scale = cols.total ** (-0.5)
    params = jnp.concatenate([conv_bias, gn_gain, gn_shift])
    me = ((replica * zs + z) * 2 + y) * 2 + core
    core, lower, same, me = tied(core, lower, replica == core, me)
    dev = me.reshape(1)

    mine = lax.dynamic_slice_in_dim(shard, core * cols.start, cols.lead, 1).astype(BF16)
    theirs = lax.dynamic_slice_in_dim(shard, (1 - core) * cols.start, cols.lead, 1).astype(BF16)
    got = swap(theirs, "core")
    unit = jnp.where(lower, jnp.concatenate([mine, got]), jnp.concatenate([got, mine]))
    lat_far = swap(latent, "core")
    cot_b = cotan.astype(BF16)
    cot_far = swap(cot_b, "core")

    if paired:
        table = jnp.asarray(ring.table(part))
        order = (ring.count, part, 2 * ring.count)
        up1, down1 = ring.up(unit), ring.down(unit)
        peer = swap(mine, "replica"), swap(theirs, "replica")
    else:
        table = jnp.zeros((replicas * zs * 4, 1), jnp.int32)
        order = None

    def call(body, outs, ins, scratch, megabytes, flops):
        return pl.pallas_call(
            body,
            out_shape=outs,
            in_specs=ins,
            out_specs=jax.tree.map(lambda _: VMEM_SPEC, outs),
            scratch_shapes=scratch,
            compiler_params=pltpu.CompilerParams(vmem_limit_bytes=megabytes * 2**20),
            cost_estimate=pl.CostEstimate(flops=flops, bytes_accessed=0, transcendentals=0),
        )

    image = (2 * half, width, chans)
    shifted = jax.ShapeDtypeStruct((3, 2 * half + 2, width, chans), BF16)
    flops = 2 * 2 * cells * chans * cols.lead
    stats, acts, cot_t = call(
        partial(act_kernel, order),
        (jax.ShapeDtypeStruct((2, chans), F32), shifted, jax.ShapeDtypeStruct((chans, 2 * cells), BF16)),
        [SMEM_SPEC] * 2 + [VMEM_SPEC] * 6,
        [pltpu.VMEM((chans, 2 * cells), F32)],
        8, flops // 4,
    )(dev, table, latent, lat_far, cot_b, cot_far, gn_gain, gn_shift)
    counts = [zs] + [1] * zs if paired else [2 * zs]
    pieces = call(
        partial(grad_kernel, cols),
        [jax.ShapeDtypeStruct((n * 2 * part, cols.lead), BF16) for n in counts],
        [SMEM_SPEC] + [VMEM_SPEC] * 2,
        [],
        4, flops // 2,
    )(dev, acts, cot_t)
    stages = Stages([2 * zs - 3, 3] if paired else [1], 2 * part if paired else chans)
    staged = paired

    def slopes_of(stats):
        extra = (jax.ShapeDtypeStruct((chans, stages.width), BF16),) if staged else ()
        return call(
            partial(slope_kernel, stages),
            (jax.ShapeDtypeStruct((3, 2 * half + 2, width, stages.width), BF16),
             jax.ShapeDtypeStruct(image, BF16), jax.ShapeDtypeStruct(image, BF16)) + extra,
            [SMEM_SPEC] * 2 + [VMEM_SPEC] * 7,
            [pltpu.VMEM((2 * half, width, stages.width), F32)] if staged else [],
            8, flops // 4,
        )(dev, table, stats, gn_gain, gn_shift, latent, lat_far, cot_b, cot_far)

    def back(stage, cots, slopes, blocks):
        return call(
            partial(back_kernel, cols, stages, stage), jax.ShapeDtypeStruct((2, chans), F32),
            [SMEM_SPEC] + [VMEM_SPEC] * (3 + len(blocks)),
            [pltpu.VMEM((2 * cells, chans), F32)], 8, flops // 4,
        )(dev, cots, *slopes, *blocks)

    def conv_first(blocks):
        wide = stages.widths[0]
        return call(
            partial(conv_both_kernel, cols, stages, 0),
            (jax.ShapeDtypeStruct((cells, wide), F32), jax.ShapeDtypeStruct((cells, wide), BF16)),
            [SMEM_SPEC] + [VMEM_SPEC] * (1 + len(blocks)),
            [pltpu.VMEM((2 * cells, wide), F32)], 6, flops // 4,
        )(dev, acts, *blocks)

    def conv_far(acts, blocks):
        wide = stages.widths[-1]
        return call(
            partial(conv_far_kernel, cols, stages, len(stages.counts) - 1),
            jax.ShapeDtypeStruct((cells, wide), BF16),
            [SMEM_SPEC] + [VMEM_SPEC] * (1 + len(blocks)),
            [pltpu.VMEM((cells, wide), F32)], 4, flops // 8,
        )(dev, acts, *blocks)

    def conv_own(got, earlier, blocks):
        return call(
            partial(conv_own_kernel, cols, stages), jax.ShapeDtypeStruct((half, width, chans), BF16),
            [SMEM_SPEC] + [VMEM_SPEC] * (4 + len(earlier) + len(blocks)),
            [pltpu.VMEM((cells, stages.widths[-1]), F32)], 8, flops // 4,
        )(dev, acts, got, latent, conv_bias, *earlier, *blocks)

    def chip_sum(sums):
        vectors = jnp.concatenate([jnp.sum(cotan, axis=(0, 1))[None], sums])
        vectors = params / (4 * zs) - LR_VECTOR * vectors
        return vectors + swap(vectors, "core")

    if paired:
        kept, *sent = pieces
        up, down, sent[0], mine, theirs = tied(up1, down1, sent[0], *peer)
        blocks = [unit, up, down]
        crossed = [swap(piece, "replica") for piece in sent]
        up, down = ring.up(up), ring.down(down)
        up, down, cots, *slopes, order = tied(up, down, *slopes_of(stats))
        blocks += [up, down]

        def ring_step(j, *received):
            parts = kept[2 * j * part:(2 * j + 2) * part], crossed[j]
            ahead, behind = (tuple(x[half] for x in parts) for half in (slice(part), slice(part, None)))
            up_sum = ring.up(add(*ahead, *received[:1]))
            if j < zs - 1:
                return up_sum, ring.down(add(*behind, *received[1:]))
            return up_sum, behind + tuple(received[1:])

        up, down = ring.up(up), ring.down(down)
        conv_first_own, conv_send = conv_first(blocks)
        crossed[0], conv_send = tied(crossed[0], conv_send)
        received = ring_step(0)
        cots, conv_send = tied(cots, conv_send)
        first_sums = back(0, cots, slopes, blocks)
        up, down, first_sums, crossed[1] = tied(up, down, first_sums, crossed[1])
        late = [up, down]

        halves = ring.up(up[:part]), ring.down(down[part:])
        conv_send, *received = tied(conv_send, *received)
        conv_first_got = swap(conv_send, "core")
        for j in range(1, zs - 2):
            received = ring_step(j, *received)
        late += halves

        conv_send = conv_far(acts, late)
        crossed[-2], cots, conv_send = tied(crossed[-2], cots, conv_send)
        conv_got = swap(conv_send, "core")
        received = ring_step(zs - 2, *received)
        sums = back(1, cots, slopes, late)
        crossed[-1], conv_got, sums, *received = tied(crossed[-1], conv_got, sums, *received)
        last, behind = ring_step(zs - 1, *received)
        block = conv_own(conv_got, [conv_first_own, conv_first_got, order], late)
        vectors = hop(chip_sum(first_sums + sums), "replica", 1)
        last, block, vectors = tied(last, block, vectors)
        total = add(*behind, last)
        vectors = hop(vectors, "y", 1)
        reach = 1
        while reach < zs:
            vectors = hop(vectors, "z", reach)
            reach *= 2
        across, vectors = tied(swap(total, "replica"), vectors)
        ours, others = jnp.where(same, total, across), jnp.where(same, across, total)
        aside = swap(others, "core")
        vector = jax.ShapeDtypeStruct((1, chans), F32)
        new_kernel, *new_v = call(
            partial(finish_kernel, cols),
            (jax.ShapeDtypeStruct(shard.shape, F32), vector, vector, vector),
            [SMEM_SPEC] * 2 + [VMEM_SPEC] * 6, [], 8, flops // 16,
        )(dev, step, shard, mine, theirs, ours, aside, vectors)
    else:
        late = [lax.all_gather(unit, NODE, axis=0, tiled=True)]
        cots, slope, slope_x = slopes_of(stats)
        sums = back(0, cots, [slope, slope_x], late)
        vectors = chip_sum(sums)
        block = conv_own(swap(conv_far(acts, late), "core"), [], late)
        terms = pieces[0].reshape(2 * zs, 2, part, cols.lead)
        summed = lax.psum_scatter(terms, NODE, scatter_dimension=0, tiled=False)
        ours = lax.dynamic_index_in_dim(summed, core, 0, keepdims=False)
        got = swap(lax.dynamic_index_in_dim(summed, 1 - core, 0, keepdims=False), "core")
        left, right = jnp.where(lower, ours, got), jnp.where(lower, got, ours)
        kernel_grad = jnp.concatenate([left, right[:, cols.both:]], axis=1).astype(F32)
        level = step[0] % (replicas.bit_length() - 1)
        rate = LR_KERNEL * (1.0 - (step[0] % 1000).astype(F32) / 2000.0)
        stepped = shard - (scale * rate) * kernel_grad
        new_kernel = 0.5 * (stepped + from_peer(level, stepped.astype(BF16)).astype(F32))
        stepped_v = lax.psum(vectors, NODE)
        new_v = jnp.split(0.5 * (stepped_v + from_peer(level, stepped_v)), 3)

    return (
        block[None],
        new_kernel[None],
        new_v[0],
        new_v[1],
        new_v[2],
    )


def solution(mesh):
    replicas, shards = mesh.shape["replica"], mesh.shape["shard"]
    split = Mesh(mesh.devices.reshape(replicas, shards // 4, 2, 2), ("replica", "z", "y", "core"))
    shard = ("z", "y", "core")
    return jax.shard_map(
        per_device,
        mesh=split,
        in_specs=(
            P("replica", shard, None, None),
            P("replica", shard, None, None),
            P("replica", shard, None),
            P("replica", None),
            P("replica", None),
            P("replica", None),
            P(),
        ),
        out_specs=(
            P("replica", shard, None, None),
            P("replica", shard, None),
            P("replica", None),
            P("replica", None),
            P("replica", None),
        ),
        check_vma=False,
    )
```

```python
from functools import partial

import jax
import jax.numpy as jnp
import numpy as np
from jax import lax
from jax.experimental import pallas as pl
from jax.experimental.pallas import tpu as pltpu
from jax.sharding import Mesh, PartitionSpec as P

GROUPS = 32
EPS = 1e-05
LR_KERNEL = 0.1
LR_VECTOR = 0.01
LANES = 128
BF16 = jnp.bfloat16
F32 = jnp.float32

SMEM_SPEC = pl.BlockSpec(memory_space=pltpu.SMEM)
VMEM_SPEC = pl.BlockSpec(memory_space=pltpu.VMEM)


class Columns:
    def __init__(self, chans):
        tiles = 9 * chans // LANES
        self.total = 9 * chans
        self.lead = (tiles + 1) // 2 * LANES
        self.start = self.total - self.lead
        self.both = 2 * self.lead - self.total
        self.mid = self.lead - 4 * chans
        self.mid_start = chans - self.mid

    def pair(self, core, k, chans):
        first = jnp.where(core == 0, 2 * k, 5 + 2 * k)
        place = jnp.where(core == 0, 2 * k * chans, self.mid + 2 * k * chans)
        return (first, first + 1), pl.multiple_of(place, LANES)

    def middle(self, core, chans):
        place = jnp.where(core == 0, 4 * chans, 0)
        channel = jnp.where(core == 0, 0, self.mid_start)
        return pl.multiple_of(place, LANES), pl.multiple_of(channel, LANES)


def fill_shifts(shifts, row, values):
    width = values.shape[0]
    at = lax.broadcasted_iota(jnp.int32, values.shape, 0)
    left = jnp.where(at == 0, 0.0, pltpu.roll(values, 1, 0))
    right = jnp.where(at == width - 1, 0.0, pltpu.roll(values, width - 1, 0))
    shifts[0, row] = left.astype(BF16)
    shifts[1, row] = values.astype(BF16)
    shifts[2, row] = right.astype(BF16)


def clear_edges(shifts):
    zero = jnp.zeros(shifts.shape[2:], shifts.dtype)
    for b in range(3):
        shifts[b, 0] = zero
        shifts[b, shifts.shape[1] - 1] = zero


def act_kernel(order, dev, table, lat_own, lat_far, cot_own, cot_far, gain, shift,
               stats, acts, cot_t, cot_f):
    me = dev[0]
    core = me % 2
    half, width, chans = lat_own.shape
    cells = 2 * half * width
    group_width = chans // GROUPS
    own_at = core * half
    far_at = half - own_at
    clear_edges(acts)

    def add_row(i, sums):
        total, square = sums
        a = lat_own[i].astype(F32)
        b = lat_far[i].astype(F32)
        return total + (a + b), square + (a * a + b * b)

    zero = jnp.zeros((width, chans), F32)
    total, square = lax.fori_loop(0, half, add_row, (zero, zero))
    sums = jnp.concatenate(
        [jnp.sum(total, axis=0, keepdims=True), jnp.sum(square, axis=0, keepdims=True),
         jnp.zeros((6, chans), F32)], axis=0
    )
    first = lax.broadcasted_iota(jnp.int32, (chans, LANES), 0)
    start = lax.broadcasted_iota(jnp.int32, (chans, LANES), 1) * group_width
    member = jnp.where((first >= start) & (first < start + group_width), 1.0, 0.0)
    exact = partial(lax.dot_general, precision=lax.Precision.HIGHEST, preferred_element_type=F32)
    sums = exact(sums, member, (((1,), (0,)), ((), ()))) / (cells * group_width)
    sums = exact(sums, member, (((1,), (1,)), ((), ())))
    mean = sums[0:1]
    rstd = lax.rsqrt(sums[1:2] - mean * mean + EPS)
    stats[0:1] = mean
    stats[1:2] = rstd
    gain_v, shift_v = gain[...], shift[...]

    def act_rows(i, _):
        for ref, base in ((lat_own, own_at), (lat_far, far_at)):
            pre = gain_v * ((ref[i].astype(F32) - mean) * rstd) + shift_v
            fill_shifts(acts, base + i + 1, pre * (0.5 + 0.5 * jnp.tanh(0.5 * pre)))
        return 0

    lax.fori_loop(0, half, act_rows, 0)

    chunk = LANES // width
    for ref, base in ((cot_own, own_at), (cot_far, far_at)):
        for i in range(half // chunk):
            piece = ref[i * chunk:(i + 1) * chunk].reshape(LANES, chans).astype(F32)
            place = pl.multiple_of(base * width + i * LANES, LANES)
            if order is None:
                cot_t[:, pl.ds(place, LANES)] = piece.T.astype(BF16)
            else:
                cot_f[:, pl.ds(place, LANES)] = piece.T
    if order is not None:
        first_at, part, count = order
        for q in range(count // 2):
            pair = [
                cot_f[pl.ds(pl.multiple_of(table[me, first_at + 2 * q + i], 8), part)]
                for i in range(2)
            ]
            cot_t[2 * q * part:(2 * q + 2) * part] = jnp.concatenate(pair).astype(BF16)


def grad_kernel(cols, carrier, dev, acts, cot_t, theirs, *pieces):
    core = dev[0] % 2
    rows, width, chans = acts.shape[1] - 2, acts.shape[2], acts.shape[3]
    cells = rows * width

    def emit(window, place, wide):
        value = jnp.dot(cot_t[...], window, preferred_element_type=F32)
        at = 0
        for i, piece in enumerate(pieces):
            count = piece.shape[0] - (theirs.shape[0] if i == carrier else 0)
            piece[:count, pl.ds(place, wide)] = value[at:at + count].astype(BF16)
            at += count

    def two_taps(k, _):
        taps, place = cols.pair(core, k, chans)
        windows = [acts[t % 3, pl.ds(t // 3, rows)].reshape(cells, chans) for t in taps]
        emit(jnp.concatenate(windows, axis=1), place, 2 * chans)
        return 0

    lax.fori_loop(0, 2, two_taps, 0)
    place, channel = cols.middle(core, chans)
    emit(acts[1, 1:rows + 1, :, pl.ds(channel, cols.mid)].reshape(cells, cols.mid), place, cols.mid)
    if carrier is not None:
        pieces[carrier][-theirs.shape[0]:] = theirs[...]


class Stages:
    def __init__(self, counts, rows):
        self.rows = rows
        self.counts = counts
        self.widths = [-(-n * rows // LANES) * LANES for n in counts]
        self.starts = [sum(self.widths[:i]) for i in range(len(counts))]
        self.width = sum(self.widths)

    def lanes(self, stage):
        return slice(self.starts[stage], self.starts[stage] + self.widths[stage])

    def columns(self, stage, blocks, place, wide):
        parts = [ref[:min(self.rows, ref.shape[0]), pl.ds(place, wide)] for ref in blocks]
        if len(parts) == self.counts[stage] + 1:
            parts[-2:] = [jnp.concatenate(parts[-2:])]
        spare = self.widths[stage] - self.counts[stage] * self.rows
        if spare:
            parts.append(jnp.zeros((spare, wide), BF16))
        return jnp.concatenate(parts) if len(parts) > 1 else parts[0]

    def order(self, me, table, order, chans):
        lane = lax.broadcasted_iota(jnp.int32, (1, self.width), 1)
        source = jnp.full((1, self.width), -1, jnp.int32)
        at = 0
        for start, count in zip(self.starts, self.counts):
            for i in range(count):
                first = start + i * self.rows
                inside = (lane >= first) & (lane < first + self.rows)
                source = jnp.where(inside, table[me, at] * self.rows + lane - first, source)
                at += 1
        channel = lax.broadcasted_iota(jnp.int32, (chans, self.width), 0)
        order[...] = jnp.where(channel == source, 1.0, 0.0).astype(BF16)


def slope_kernel(stages, dev, table, stats, gain, shift, lat_own, lat_far, cot_own, cot_far,
                 cots, slope, slope_x, *refs):
    me = dev[0]
    core = me % 2
    half, width, chans = lat_own.shape
    clear_edges(cots)
    mean, rstd = stats[0:1], stats[1:2]
    gain_v, shift_v = gain[...], shift[...]
    far_at = half - core * half
    if len(stages.counts) > 1:
        order, placed = refs
        stages.order(me, table, order, chans)
        for ref, base in ((cot_own, core * half), (cot_far, far_at)):
            value = jnp.dot(ref[...].reshape(half * width, chans), order[...], preferred_element_type=F32)
            placed[pl.ds(base, half)] = value.reshape(half, width, stages.width)

    def one_row(i, _):
        for lat, cot, base in ((lat_own, cot_own, core * half), (lat_far, cot_far, far_at)):
            value = placed[base + i] if len(stages.counts) > 1 else cot[i].astype(F32)
            fill_shifts(cots, base + i + 1, value)
            xhat = (lat[i].astype(F32) - mean) * rstd
            pre = gain_v * xhat + shift_v
            sig = 0.5 + 0.5 * jnp.tanh(0.5 * pre)
            value = sig * (1.0 + pre * (1.0 - sig))
            slope[base + i] = value.astype(BF16)
            slope_x[base + i] = (value * xhat).astype(BF16)
        return 0

    lax.fori_loop(0, half, one_row, 0)


def conv_sum(cols, stages, stage, core, first, half, acts, blocks, total):
    width, chans = acts.shape[2:]
    cells = half * width
    nt = (((1,), (1,)), ((), ()))
    place, channel = cols.middle(core, chans)
    window = acts[1, pl.ds(first + 1, half), :, pl.ds(channel, cols.mid)].reshape(cells, cols.mid)
    lane = lax.broadcasted_iota(jnp.int32, window.shape, 1)
    window = jnp.where((core == 1) & (lane < cols.both), jnp.zeros_like(window), window)
    kernel = stages.columns(stage, blocks, place, cols.mid)
    total[...] = lax.dot_general(window, kernel, nt, preferred_element_type=F32)

    def two_taps(k, _):
        taps, place = cols.pair(core, k, chans)
        windows = [acts[t % 3, pl.ds(first + t // 3, half)].reshape(cells, chans) for t in taps]
        kernel = stages.columns(stage, blocks, place, 2 * chans)
        total[...] += lax.dot_general(
            jnp.concatenate(windows, axis=1), kernel, nt, preferred_element_type=F32
        )
        return 0

    lax.fori_loop(0, 2, two_taps, 0)


def conv_both_kernel(cols, stages, stage, dev, acts, *refs):
    blocks, (own, far, total) = refs[:-3], refs[-3:]
    core = dev[0] % 2
    rows = acts.shape[1] - 2
    conv_sum(cols, stages, stage, core, 0, rows, acts, blocks, total)
    half = own.shape[0]
    own[...] = total[pl.ds(pl.multiple_of(core * half, half), half)]
    far[...] = total[pl.ds(pl.multiple_of((1 - core) * half, half), half)].astype(BF16)


def conv_far_kernel(cols, stages, stage, dev, acts, *refs):
    blocks, (far, total) = refs[:-2], refs[-2:]
    core = dev[0] % 2
    half = (acts.shape[1] - 2) // 2
    conv_sum(cols, stages, stage, core, (1 - core) * half, half, acts, blocks, total)
    far[...] = total[...].astype(BF16)


def conv_own_kernel(cols, stages, dev, acts, got, latent, bias, *refs):
    core = dev[0] % 2
    half, width, chans = latent.shape
    scale = cols.total ** (-0.5)
    stage = len(stages.counts) - 1
    before = 3 * stage
    blocks, (block, total) = refs[before:-2], refs[-2:]
    conv_sum(cols, stages, stage, core, core * half, half, acts, blocks, total)
    conv = total[...] + got[...].astype(F32)
    if stage:
        first_own, first_got, order = refs[:before]
        conv = jnp.concatenate([first_own[...] + first_got[...].astype(F32), conv], axis=1)
        high = conv.astype(BF16)
        low = (conv - high.astype(F32)).astype(BF16)
        nt = (((1,), (1,)), ((), ()))
        conv = sum(
            lax.dot_general(value, order[...], nt, preferred_element_type=F32) for value in (low, high)
        )
    conv = scale * conv + bias[...]
    block[...] = (conv.reshape(half, width, chans) + latent[...].astype(F32)).astype(BF16)


def back_kernel(cols, stages, stage, dev, cots, slope, slope_x, *refs):
    blocks, (sums, total) = refs[:-2], refs[-2:]
    core = dev[0] % 2
    rows, width = cots.shape[1] - 2, cots.shape[2]
    cells, chans = total.shape
    lanes = stages.lanes(stage)

    def taps_from(first, place, count):
        windows, kernels = [], []
        for i in range(count):
            tap = first + i
            window = cots[2 - tap % 3, pl.ds(2 - tap // 3, rows), :, lanes]
            windows.append(window.reshape(cells, stages.widths[stage]))
            kernels.append(stages.columns(stage, blocks, pl.multiple_of(place + i * chans, LANES), chans))
        return jnp.dot(
            jnp.concatenate(windows, axis=1), jnp.concatenate(kernels), preferred_element_type=F32
        )

    if stages.widths[stage] * 4 <= 2 * chans:
        taps, place = cols.pair(core, 0, chans)
        total[...] = taps_from(taps[0], place, 4)
    else:
        total[...] = jnp.zeros_like(total)

        def two_taps(k, _):
            taps, place = cols.pair(core, k, chans)
            total[...] += taps_from(taps[0], place, 2)
            return 0

        lax.fori_loop(0, 2, two_taps, 0)

    place, channel = cols.middle(core, chans)
    window = cots[1, 1:rows + 1, :, lanes].reshape(cells, stages.widths[stage])
    kernel = stages.columns(stage, blocks, place, cols.mid)
    value = jnp.dot(window, kernel, preferred_element_type=F32)
    lane = lax.broadcasted_iota(jnp.int32, value.shape, 1)
    total[:, pl.ds(channel, cols.mid)] += jnp.where((core == 1) & (lane < cols.both), 0.0, value)

    def add_row(i, carry):
        gains, shifts = carry
        value = total[pl.ds(pl.multiple_of(i * width, width), width)]
        return gains + value * slope_x[i].astype(F32), shifts + value * slope[i].astype(F32)

    zero = jnp.zeros((width, chans), F32)
    gains, shifts = lax.fori_loop(0, rows, add_row, (zero, zero))
    scale = cols.total ** (-0.5)
    sums[0:1] = scale * jnp.sum(gains, axis=0, keepdims=True)
    sums[1:2] = scale * jnp.sum(shifts, axis=0, keepdims=True)


def finish_kernel(cols, dev, step, shard, mine, carried, ours, aside, vectors, out, new_bias, new_gain, new_shift):
    lower = dev[0] % 2 == 0
    rate = LR_KERNEL * (1.0 - (step[0] % 1000).astype(F32) / 2000.0)
    factor = 0.5 * cols.total ** (-0.5) * rate
    part = shard.shape[0]
    theirs = carried[-part:].astype(F32)
    here = 0.5 * mine[...].astype(F32) - factor * ours[...].astype(F32)
    there = 0.5 * theirs - factor * aside[...].astype(F32)
    left, right = jnp.where(lower, here, there), jnp.where(lower, there, here)
    out[:, :cols.lead] = 0.5 * shard[:, :cols.lead] + left
    out[:, cols.lead:] = 0.5 * shard[:, cols.lead:] + right[:, cols.both:]
    for i, new in enumerate((new_bias, new_gain, new_shift)):
        new[...] = 0.5 * vectors[i:i + 1]


NODE = ("z", "y")


def swap(value, axis):
    return lax.ppermute(value, axis, [(0, 1), (1, 0)])


def from_peer(level, value):
    count = lax.axis_size("replica")
    levels = count.bit_length() - 1
    moves = [[(s, (s + (1 << k)) % count) for s in range(count)] for k in range(levels)]
    if levels == 1:
        return lax.ppermute(value, "replica", moves[0])
    return lax.switch(level, [lambda v, m=m: lax.ppermute(v, "replica", m) for m in moves], value)


class Ring:
    def __init__(self, zs):
        self.count = 2 * zs
        self.reach = zs
        self.nodes = [2 * z for z in range(zs)] + [2 * z + 1 for z in reversed(range(zs))]
        ahead = list(zip(self.nodes, self.nodes[1:] + self.nodes[:1]))
        self.ahead = ahead
        self.behind = [(b, a) for a, b in ahead]

    def node(self, at, offset):
        return self.nodes[(at + offset) % self.count]

    def up(self, value):
        return lax.ppermute(value, NODE, self.ahead)

    def down(self, value):
        return lax.ppermute(value, NODE, self.behind)

    def table(self, part):
        rows = np.zeros((2, self.count, 2, 3 * self.count), np.int32)
        for replica in range(2):
            for at, node in enumerate(self.nodes):
                line = [node]
                for k in range(1, self.reach + 1):
                    line.append(self.node(at, -k))
                    if k < self.reach:
                        line.append(self.node(at, k))
                for which in (replica, 1 - replica):
                    for j in range(self.reach):
                        targets = [self.node(at, self.reach - j), self.node(at, j + 1 - self.reach)]
                        line += [(2 * target + which) * part for target in targets]
                rows[replica, node, :] = line
        return rows.reshape(-1, 3 * self.count)


def hop(value, axis, mask):
    count = lax.axis_size(axis)
    return value + lax.ppermute(value, axis, [(s, s ^ mask) for s in range(count)])


def add(*values):
    total = values[0].astype(F32)
    for value in values[1:]:
        total = total + value.astype(F32)
    return total.astype(BF16)


def tied(*values):
    return lax.optimization_barrier(values)


def per_device(latents, cotangent, kernel, conv_bias, gn_gain, gn_shift, step):
    latent, cotan, shard = latents[0], cotangent[0], kernel[0]
    half, width, chans = latent.shape
    part = shard.shape[0]
    cols = Columns(chans)
    cells = half * width
    zs, replicas = lax.axis_size("z"), lax.axis_size("replica")
    core, z, y, replica = (lax.axis_index(a) for a in ("core", "z", "y", "replica"))
    lower = core == 0
    paired = replicas == 2
    ring = Ring(zs)
    scale = cols.total ** (-0.5)
    params = jnp.concatenate([conv_bias, gn_gain, gn_shift])
    me = ((replica * zs + z) * 2 + y) * 2 + core
    core, lower, same, me = tied(core, lower, replica == core, me)
    dev = me.reshape(1)

    mine = lax.dynamic_slice_in_dim(shard, core * cols.start, cols.lead, 1).astype(BF16)
    theirs = lax.dynamic_slice_in_dim(shard, (1 - core) * cols.start, cols.lead, 1).astype(BF16)
    got = swap(theirs, "core")
    unit = jnp.where(lower, jnp.concatenate([mine, got]), jnp.concatenate([got, mine]))
    lat_far = swap(latent, "core")
    cot_b = cotan.astype(BF16)
    cot_far = swap(cot_b, "core")

    if paired:
        table = jnp.asarray(ring.table(part))
        order = (ring.count, part, 2 * ring.count)
        up1, down1 = ring.up(unit), ring.down(unit)
        peer = swap(mine, "replica")
    else:
        table = jnp.zeros((replicas * zs * 4, 1), jnp.int32)
        order = None

    def call(body, outs, ins, scratch, megabytes, flops):
        return pl.pallas_call(
            body,
            out_shape=outs,
            in_specs=ins,
            out_specs=jax.tree.map(lambda _: VMEM_SPEC, outs),
            scratch_shapes=scratch,
            compiler_params=pltpu.CompilerParams(vmem_limit_bytes=megabytes * 2**20),
            cost_estimate=pl.CostEstimate(flops=flops * 4, bytes_accessed=0, transcendentals=0),
        )

    image = (2 * half, width, chans)
    shifted = jax.ShapeDtypeStruct((3, 2 * half + 2, width, chans), BF16)
    flops = 2 * 2 * cells * chans * cols.lead
    stats, acts, cot_t = call(
        partial(act_kernel, order),
        (jax.ShapeDtypeStruct((2, chans), F32), shifted, jax.ShapeDtypeStruct((chans, 2 * cells), BF16)),
        [SMEM_SPEC] * 2 + [VMEM_SPEC] * 6,
        [pltpu.VMEM((chans, 2 * cells), F32)],
        8, flops // 4,
    )(dev, table, latent, lat_far, cot_b, cot_far, gn_gain, gn_shift)
    if paired:
        peer, acts = tied(peer, acts)
    counts = [2 * zs, 2, 3] + [2] * (zs - 2) if paired else [4 * zs]
    pieces = call(
        partial(grad_kernel, cols, 2 if paired else None),
        [jax.ShapeDtypeStruct((n * part, cols.lead), BF16) for n in counts],
        [SMEM_SPEC] + [VMEM_SPEC] * 3,
        [],
        4, flops // 2,
    )(dev, acts, cot_t, theirs)
    stages = Stages([2 * zs - 3, 3] if paired else [1], 2 * part if paired else chans)
    staged = paired

    def slopes_of(stats):
        extra = (jax.ShapeDtypeStruct((chans, stages.width), BF16),) if staged else ()
        return call(
            partial(slope_kernel, stages),
            (jax.ShapeDtypeStruct((3, 2 * half + 2, width, stages.width), BF16),
             jax.ShapeDtypeStruct(image, BF16), jax.ShapeDtypeStruct(image, BF16)) + extra,
            [SMEM_SPEC] * 2 + [VMEM_SPEC] * 7,
            [pltpu.VMEM((2 * half, width, stages.width), F32)] if staged else [],
            8, flops // 4,
        )(dev, table, stats, gn_gain, gn_shift, latent, lat_far, cot_b, cot_far)

    def back(stage, cots, slopes, blocks):
        return call(
            partial(back_kernel, cols, stages, stage), jax.ShapeDtypeStruct((2, chans), F32),
            [SMEM_SPEC] + [VMEM_SPEC] * (3 + len(blocks)),
            [pltpu.VMEM((2 * cells, chans), F32)], 8, flops // 4,
        )(dev, cots, *slopes, *blocks)

    def conv_first(blocks):
        wide = stages.widths[0]
        return call(
            partial(conv_both_kernel, cols, stages, 0),
            (jax.ShapeDtypeStruct((cells, wide), F32), jax.ShapeDtypeStruct((cells, wide), BF16)),
            [SMEM_SPEC] + [VMEM_SPEC] * (1 + len(blocks)),
            [pltpu.VMEM((2 * cells, wide), F32)], 6, flops // 4,
        )(dev, acts, *blocks)

    def conv_far(acts, blocks):
        wide = stages.widths[-1]
        return call(
            partial(conv_far_kernel, cols, stages, len(stages.counts) - 1),
            jax.ShapeDtypeStruct((cells, wide), BF16),
            [SMEM_SPEC] + [VMEM_SPEC] * (1 + len(blocks)),
            [pltpu.VMEM((cells, wide), F32)], 4, flops // 8,
        )(dev, acts, *blocks)

    def conv_own(got, earlier, blocks):
        return call(
            partial(conv_own_kernel, cols, stages), jax.ShapeDtypeStruct((half, width, chans), BF16),
            [SMEM_SPEC] + [VMEM_SPEC] * (4 + len(earlier) + len(blocks)),
            [pltpu.VMEM((cells, stages.widths[-1]), F32)], 8, flops // 4,
        )(dev, acts, got, latent, conv_bias, *earlier, *blocks)

    def chip_sum(sums):
        vectors = jnp.concatenate([jnp.sum(cotan, axis=(0, 1))[None], sums])
        vectors = params / (4 * zs) - LR_VECTOR * vectors
        return vectors + swap(vectors, "core")

    if paired:
        kept, *sent = pieces
        crossed = [swap(piece, "replica") for piece in sent]
        theirs = crossed[1]

        def ring_sums(j, *received):
            parts = kept[2 * j * part:(2 * j + 2) * part], crossed[j]
            ahead, behind = (tuple(x[at:at + part] for x in parts) for at in (0, part))
            ahead = add(*ahead, *received[:1])
            behind = behind + tuple(received[1:])
            return ahead, add(*behind) if j < zs - 1 else behind

        def ring_step(ahead, behind):
            return ring.up(ahead), ring.down(behind)

        up, down, stats, _ = tied(up1, down1, stats, sent[0])
        blocks = [unit, up, down]
        up, down = ring.up(up), ring.down(down)
        up, down, cots, *slopes, order = tied(up, down, *slopes_of(stats))
        blocks += [up, down]

        ahead, behind = ring_sums(0)
        up = ring.up(jnp.concatenate([up, ahead]))
        down = ring.down(jnp.concatenate([down, behind]))
        conv_first_own, conv_send = conv_first(blocks)
        cots, conv_send = tied(cots, conv_send)
        first_sums = back(0, cots, slopes, blocks)
        up, down, first_sums, crossed[1] = tied(up, down, first_sums, crossed[1])
        late = [up, down]
        received = up[2 * part:], down[2 * part:]

        halves = ring.up(up[:part]), ring.down(down[part:2 * part])
        conv_first_got = swap(conv_send, "core")
        for j in range(1, zs - 2):
            received = ring_step(*ring_sums(j, *received))
        late += halves

        conv_send = conv_far(acts, late)
        crossed[2], cots, conv_send = tied(crossed[2], cots, conv_send)
        conv_got = swap(conv_send, "core")
        received = ring_step(*ring_sums(zs - 2, *received))
        sums = back(1, cots, slopes, late)
        crossed[3], conv_got, sums, *received = tied(crossed[3], conv_got, sums, *received)
        ahead, behind = ring_sums(zs - 1, *received)
        last = ring.up(ahead)
        block = conv_own(conv_got, [conv_first_own, conv_first_got, order], late)
        vectors = hop(hop(chip_sum(first_sums + sums), "replica", 1), "z", 1)
        last, block, vectors = tied(last, block, vectors)
        total = add(*behind, last)
        vectors = hop(vectors, "y", 1)
        reach = 2
        while reach < zs:
            vectors = hop(vectors, "z", reach)
            reach *= 2
        across, vectors = tied(swap(total, "replica"), vectors)
        ours, others = jnp.where(same, total, across), jnp.where(same, across, total)
        aside = swap(others, "core")
        vector = jax.ShapeDtypeStruct((1, chans), F32)
        new_kernel, *new_v = call(
            partial(finish_kernel, cols),
            (jax.ShapeDtypeStruct(shard.shape, F32), vector, vector, vector),
            [SMEM_SPEC] * 2 + [VMEM_SPEC] * 6, [], 8, flops // 16,
        )(dev, step, shard, peer, theirs, ours, aside, vectors)
    else:
        late = [lax.all_gather(unit, NODE, axis=0, tiled=True)]
        cots, slope, slope_x = slopes_of(stats)
        sums = back(0, cots, [slope, slope_x], late)
        vectors = chip_sum(sums)
        block = conv_own(swap(conv_far(acts, late), "core"), [], late)
        terms = pieces[0].reshape(2 * zs, 2, part, cols.lead)
        summed = lax.psum_scatter(terms, NODE, scatter_dimension=0, tiled=False)
        ours = lax.dynamic_index_in_dim(summed, core, 0, keepdims=False)
        got = swap(lax.dynamic_index_in_dim(summed, 1 - core, 0, keepdims=False), "core")
        left, right = jnp.where(lower, ours, got), jnp.where(lower, got, ours)
        kernel_grad = jnp.concatenate([left, right[:, cols.both:]], axis=1).astype(F32)
        level = step[0] % (replicas.bit_length() - 1)
        rate = LR_KERNEL * (1.0 - (step[0] % 1000).astype(F32) / 2000.0)
        stepped = shard - (scale * rate) * kernel_grad
        new_kernel = 0.5 * (stepped + from_peer(level, stepped.astype(BF16)).astype(F32))
        stepped_v = lax.psum(vectors, NODE)
        new_v = jnp.split(0.5 * (stepped_v + from_peer(level, stepped_v)), 3)

    return (
        block[None],
        new_kernel[None],
        new_v[0],
        new_v[1],
        new_v[2],
    )


def solution(mesh):
    replicas, shards = mesh.shape["replica"], mesh.shape["shard"]
    split = Mesh(mesh.devices.reshape(replicas, shards // 4, 2, 2), ("replica", "z", "y", "core"))
    shard = ("z", "y", "core")
    return jax.shard_map(
        per_device,
        mesh=split,
        in_specs=(
            P("replica", shard, None, None),
            P("replica", shard, None, None),
            P("replica", shard, None),
            P("replica", None),
            P("replica", None),
            P("replica", None),
            P(),
        ),
        out_specs=(
            P("replica", shard, None, None),
            P("replica", shard, None),
            P("replica", None),
            P("replica", None),
            P("replica", None),
        ),
        check_vma=False,
    )
```

```python
from functools import partial

import jax
import jax.numpy as jnp
import numpy as np
from jax import lax
from jax.experimental import pallas as pl
from jax.experimental.pallas import tpu as pltpu
from jax.sharding import Mesh, PartitionSpec as P

GROUPS = 32
EPS = 1e-05
LR_KERNEL = 0.1
LR_VECTOR = 0.01
LANES = 128
BF16 = jnp.bfloat16
F32 = jnp.float32

SMEM_SPEC = pl.BlockSpec(memory_space=pltpu.SMEM)
VMEM_SPEC = pl.BlockSpec(memory_space=pltpu.VMEM)


class Columns:
    def __init__(self, chans):
        tiles = 9 * chans // LANES
        self.total = 9 * chans
        self.lead = (tiles + 1) // 2 * LANES
        self.start = self.total - self.lead
        self.both = 2 * self.lead - self.total
        self.mid = self.lead - 4 * chans
        self.mid_start = chans - self.mid

    def pair(self, core, k, chans):
        first = jnp.where(core == 0, 2 * k, 5 + 2 * k)
        place = jnp.where(core == 0, 2 * k * chans, self.mid + 2 * k * chans)
        return (first, first + 1), pl.multiple_of(place, LANES)

    def middle(self, core, chans):
        place = jnp.where(core == 0, 4 * chans, 0)
        channel = jnp.where(core == 0, 0, self.mid_start)
        return pl.multiple_of(place, LANES), pl.multiple_of(channel, LANES)


def fill_shifts(shifts, row, values):
    width = values.shape[0]
    at = lax.broadcasted_iota(jnp.int32, values.shape, 0)
    left = jnp.where(at == 0, 0.0, pltpu.roll(values, 1, 0))
    right = jnp.where(at == width - 1, 0.0, pltpu.roll(values, width - 1, 0))
    shifts[0, row] = left.astype(BF16)
    shifts[1, row] = values.astype(BF16)
    shifts[2, row] = right.astype(BF16)


def clear_edges(shifts):
    zero = jnp.zeros(shifts.shape[2:], shifts.dtype)
    for b in range(3):
        shifts[b, 0] = zero
        shifts[b, shifts.shape[1] - 1] = zero


def act_kernel(order, dev, table, lat_own, lat_far, cot_own, cot_far, gain, shift,
               stats, acts, cot_t, cot_f):
    me = dev[0]
    core = me % 2
    half, width, chans = lat_own.shape
    cells = 2 * half * width
    group_width = chans // GROUPS
    own_at = core * half
    far_at = half - own_at
    clear_edges(acts)

    def add_row(i, sums):
        total, square = sums
        a = lat_own[i].astype(F32)
        b = lat_far[i].astype(F32)
        return total + (a + b), square + (a * a + b * b)

    zero = jnp.zeros((width, chans), F32)
    total, square = lax.fori_loop(0, half, add_row, (zero, zero))
    sums = jnp.concatenate(
        [jnp.sum(total, axis=0, keepdims=True), jnp.sum(square, axis=0, keepdims=True),
         jnp.zeros((6, chans), F32)], axis=0
    )
    first = lax.broadcasted_iota(jnp.int32, (chans, LANES), 0)
    start = lax.broadcasted_iota(jnp.int32, (chans, LANES), 1) * group_width
    member = jnp.where((first >= start) & (first < start + group_width), 1.0, 0.0)
    exact = partial(lax.dot_general, precision=lax.Precision.HIGHEST, preferred_element_type=F32)
    sums = exact(sums, member, (((1,), (0,)), ((), ()))) / (cells * group_width)
    sums = exact(sums, member, (((1,), (1,)), ((), ())))
    mean = sums[0:1]
    rstd = lax.rsqrt(sums[1:2] - mean * mean + EPS)
    stats[0:1] = mean
    stats[1:2] = rstd
    gain_v, shift_v = gain[...], shift[...]

    def act_rows(i, _):
        for ref, base in ((lat_own, own_at), (lat_far, far_at)):
            pre = gain_v * ((ref[i].astype(F32) - mean) * rstd) + shift_v
            fill_shifts(acts, base + i + 1, pre * (0.5 + 0.5 * jnp.tanh(0.5 * pre)))
        return 0

    lax.fori_loop(0, half, act_rows, 0)

    chunk = LANES // width
    for ref, base in ((cot_own, own_at), (cot_far, far_at)):
        for i in range(half // chunk):
            piece = ref[i * chunk:(i + 1) * chunk].reshape(LANES, chans).astype(F32)
            place = pl.multiple_of(base * width + i * LANES, LANES)
            if order is None:
                cot_t[:, pl.ds(place, LANES)] = piece.T.astype(BF16)
            else:
                cot_f[:, pl.ds(place, LANES)] = piece.T
    if order is not None:
        first_at, part, count = order
        for q in range(count // 2):
            pair = [
                cot_f[pl.ds(pl.multiple_of(table[me, first_at + 2 * q + i], 8), part)]
                for i in range(2)
            ]
            cot_t[2 * q * part:(2 * q + 2) * part] = jnp.concatenate(pair).astype(BF16)


def grad_kernel(cols, carrier, dev, acts, cot_t, theirs, *pieces):
    core = dev[0] % 2
    rows, width, chans = acts.shape[1] - 2, acts.shape[2], acts.shape[3]
    cells = rows * width

    def emit(window, place, wide):
        value = jnp.dot(cot_t[...], window, preferred_element_type=F32)
        at = 0
        for i, piece in enumerate(pieces):
            count = piece.shape[0] - (theirs.shape[0] if i == carrier else 0)
            piece[:count, pl.ds(place, wide)] = value[at:at + count].astype(BF16)
            at += count

    def two_taps(k, _):
        taps, place = cols.pair(core, k, chans)
        windows = [acts[t % 3, pl.ds(t // 3, rows)].reshape(cells, chans) for t in taps]
        emit(jnp.concatenate(windows, axis=1), place, 2 * chans)
        return 0

    lax.fori_loop(0, 2, two_taps, 0)
    place, channel = cols.middle(core, chans)
    emit(acts[1, 1:rows + 1, :, pl.ds(channel, cols.mid)].reshape(cells, cols.mid), place, cols.mid)
    if carrier is not None:
        pieces[carrier][-theirs.shape[0]:] = theirs[...]


class Stages:
    def __init__(self, counts, rows):
        self.rows = rows
        self.counts = counts
        self.widths = [-(-n * rows // LANES) * LANES for n in counts]
        self.starts = [sum(self.widths[:i]) for i in range(len(counts))]
        self.width = sum(self.widths)

    def lanes(self, stage):
        return slice(self.starts[stage], self.starts[stage] + self.widths[stage])

    def columns(self, stage, blocks, place, wide):
        parts = [ref[:min(self.rows, ref.shape[0]), pl.ds(place, wide)] for ref in blocks]
        if len(parts) == self.counts[stage] + 1:
            parts[-2:] = [jnp.concatenate(parts[-2:])]
        spare = self.widths[stage] - self.counts[stage] * self.rows
        if spare:
            parts.append(jnp.zeros((spare, wide), BF16))
        return jnp.concatenate(parts) if len(parts) > 1 else parts[0]

    def order(self, me, table, order, chans):
        lane = lax.broadcasted_iota(jnp.int32, (1, self.width), 1)
        source = jnp.full((1, self.width), -1, jnp.int32)
        at = 0
        for start, count in zip(self.starts, self.counts):
            for i in range(count):
                first = start + i * self.rows
                inside = (lane >= first) & (lane < first + self.rows)
                source = jnp.where(inside, table[me, at] * self.rows + lane - first, source)
                at += 1
        channel = lax.broadcasted_iota(jnp.int32, (chans, self.width), 0)
        order[...] = jnp.where(channel == source, 1.0, 0.0).astype(BF16)


def slope_kernel(stages, dev, table, stats, gain, shift, lat_own, lat_far, cot_own, cot_far,
                 cots, slope, slope_x, *refs):
    me = dev[0]
    core = me % 2
    half, width, chans = lat_own.shape
    clear_edges(cots)
    mean, rstd = stats[0:1], stats[1:2]
    gain_v, shift_v = gain[...], shift[...]
    far_at = half - core * half
    if len(stages.counts) > 1:
        order, placed = refs
        stages.order(me, table, order, chans)
        for ref, base in ((cot_own, core * half), (cot_far, far_at)):
            value = jnp.dot(ref[...].reshape(half * width, chans), order[...], preferred_element_type=F32)
            placed[pl.ds(base, half)] = value.reshape(half, width, stages.width)

    def one_row(i, _):
        for lat, cot, base in ((lat_own, cot_own, core * half), (lat_far, cot_far, far_at)):
            value = placed[base + i] if len(stages.counts) > 1 else cot[i].astype(F32)
            fill_shifts(cots, base + i + 1, value)
            xhat = (lat[i].astype(F32) - mean) * rstd
            pre = gain_v * xhat + shift_v
            sig = 0.5 + 0.5 * jnp.tanh(0.5 * pre)
            value = sig * (1.0 + pre * (1.0 - sig))
            slope[base + i] = value.astype(BF16)
            slope_x[base + i] = (value * xhat).astype(BF16)
        return 0

    lax.fori_loop(0, half, one_row, 0)


def conv_sum(cols, stages, stage, core, first, half, acts, blocks, total):
    width, chans = acts.shape[2:]
    cells = half * width
    nt = (((1,), (1,)), ((), ()))
    place, channel = cols.middle(core, chans)
    window = acts[1, pl.ds(first + 1, half), :, pl.ds(channel, cols.mid)].reshape(cells, cols.mid)
    lane = lax.broadcasted_iota(jnp.int32, window.shape, 1)
    window = jnp.where((core == 1) & (lane < cols.both), jnp.zeros_like(window), window)
    kernel = stages.columns(stage, blocks, place, cols.mid)
    total[...] = lax.dot_general(window, kernel, nt, preferred_element_type=F32)

    def two_taps(k, _):
        taps, place = cols.pair(core, k, chans)
        windows = [acts[t % 3, pl.ds(first + t // 3, half)].reshape(cells, chans) for t in taps]
        kernel = stages.columns(stage, blocks, place, 2 * chans)
        total[...] += lax.dot_general(
            jnp.concatenate(windows, axis=1), kernel, nt, preferred_element_type=F32
        )
        return 0

    lax.fori_loop(0, 2, two_taps, 0)


def conv_both_kernel(cols, stages, stage, dev, acts, *refs):
    blocks, (own, far, total) = refs[:-3], refs[-3:]
    core = dev[0] % 2
    rows = acts.shape[1] - 2
    conv_sum(cols, stages, stage, core, 0, rows, acts, blocks, total)
    half = own.shape[0]
    own[...] = total[pl.ds(pl.multiple_of(core * half, half), half)]
    far[...] = total[pl.ds(pl.multiple_of((1 - core) * half, half), half)].astype(BF16)


def conv_far_kernel(cols, stages, stage, dev, acts, *refs):
    blocks, (far, total) = refs[:-2], refs[-2:]
    core = dev[0] % 2
    half = (acts.shape[1] - 2) // 2
    conv_sum(cols, stages, stage, core, (1 - core) * half, half, acts, blocks, total)
    far[...] = total[...].astype(BF16)


def conv_own_kernel(cols, stages, dev, acts, got, latent, bias, *refs):
    core = dev[0] % 2
    half, width, chans = latent.shape
    scale = cols.total ** (-0.5)
    stage = len(stages.counts) - 1
    before = 3 * stage
    blocks, (block, total) = refs[before:-2], refs[-2:]
    conv_sum(cols, stages, stage, core, core * half, half, acts, blocks, total)
    conv = total[...] + got[...].astype(F32)
    if stage:
        first_own, first_got, order = refs[:before]
        conv = jnp.concatenate([first_own[...] + first_got[...].astype(F32), conv], axis=1)
        high = conv.astype(BF16)
        low = (conv - high.astype(F32)).astype(BF16)
        nt = (((1,), (1,)), ((), ()))
        conv = sum(
            lax.dot_general(value, order[...], nt, preferred_element_type=F32) for value in (low, high)
        )
    conv = scale * conv + bias[...]
    block[...] = (conv.reshape(half, width, chans) + latent[...].astype(F32)).astype(BF16)


def back_kernel(cols, stages, stage, dev, cots, slope, slope_x, *refs):
    blocks, (sums, total) = refs[:-2], refs[-2:]
    core = dev[0] % 2
    rows, width = cots.shape[1] - 2, cots.shape[2]
    cells, chans = total.shape
    lanes = stages.lanes(stage)

    def taps_from(first, place, count):
        windows, kernels = [], []
        for i in range(count):
            tap = first + i
            window = cots[2 - tap % 3, pl.ds(2 - tap // 3, rows), :, lanes]
            windows.append(window.reshape(cells, stages.widths[stage]))
            kernels.append(stages.columns(stage, blocks, pl.multiple_of(place + i * chans, LANES), chans))
        return jnp.dot(
            jnp.concatenate(windows, axis=1), jnp.concatenate(kernels), preferred_element_type=F32
        )

    if stages.widths[stage] * 4 <= 2 * chans:
        taps, place = cols.pair(core, 0, chans)
        total[...] = taps_from(taps[0], place, 4)
    else:
        total[...] = jnp.zeros_like(total)

        def two_taps(k, _):
            taps, place = cols.pair(core, k, chans)
            total[...] += taps_from(taps[0], place, 2)
            return 0

        lax.fori_loop(0, 2, two_taps, 0)

    place, channel = cols.middle(core, chans)
    window = cots[1, 1:rows + 1, :, lanes].reshape(cells, stages.widths[stage])
    kernel = stages.columns(stage, blocks, place, cols.mid)
    value = jnp.dot(window, kernel, preferred_element_type=F32)
    lane = lax.broadcasted_iota(jnp.int32, value.shape, 1)
    total[:, pl.ds(channel, cols.mid)] += jnp.where((core == 1) & (lane < cols.both), 0.0, value)

    def add_row(i, carry):
        gains, shifts = carry
        value = total[pl.ds(pl.multiple_of(i * width, width), width)]
        return gains + value * slope_x[i].astype(F32), shifts + value * slope[i].astype(F32)

    zero = jnp.zeros((width, chans), F32)
    gains, shifts = lax.fori_loop(0, rows, add_row, (zero, zero))
    scale = cols.total ** (-0.5)
    sums[0:1] = scale * jnp.sum(gains, axis=0, keepdims=True)
    sums[1:2] = scale * jnp.sum(shifts, axis=0, keepdims=True)


def finish_kernel(cols, dev, step, shard, mine, carried, ours, aside, vectors, out, new_bias, new_gain, new_shift):
    lower = dev[0] % 2 == 0
    rate = LR_KERNEL * (1.0 - (step[0] % 1000).astype(F32) / 2000.0)
    factor = 0.5 * cols.total ** (-0.5) * rate
    part = shard.shape[0]
    theirs = carried[-part:].astype(F32)
    here = 0.5 * mine[...].astype(F32) - factor * ours[...].astype(F32)
    there = 0.5 * theirs - factor * aside[...].astype(F32)
    left, right = jnp.where(lower, here, there), jnp.where(lower, there, here)
    out[:, :cols.lead] = 0.5 * shard[:, :cols.lead] + left
    out[:, cols.lead:] = 0.5 * shard[:, cols.lead:] + right[:, cols.both:]
    for i, new in enumerate((new_bias, new_gain, new_shift)):
        new[...] = 0.5 * vectors[i:i + 1]


NODE = ("z", "y")


def swap(value, axis):
    return lax.ppermute(value, axis, [(0, 1), (1, 0)])


def from_peer(level, value):
    count = lax.axis_size("replica")
    levels = count.bit_length() - 1
    moves = [[(s, (s + (1 << k)) % count) for s in range(count)] for k in range(levels)]
    if levels == 1:
        return lax.ppermute(value, "replica", moves[0])
    return lax.switch(level, [lambda v, m=m: lax.ppermute(v, "replica", m) for m in moves], value)


class Ring:
    def __init__(self, zs):
        self.count = 2 * zs
        self.reach = zs
        self.nodes = [2 * z for z in range(zs)] + [2 * z + 1 for z in reversed(range(zs))]
        ahead = list(zip(self.nodes, self.nodes[1:] + self.nodes[:1]))
        self.ahead = ahead
        self.behind = [(b, a) for a, b in ahead]

    def node(self, at, offset):
        return self.nodes[(at + offset) % self.count]

    def up(self, value):
        return lax.ppermute(value, NODE, self.ahead)

    def down(self, value):
        return lax.ppermute(value, NODE, self.behind)

    def table(self, part):
        rows = np.zeros((2, self.count, 2, 3 * self.count), np.int32)
        for replica in range(2):
            for at, node in enumerate(self.nodes):
                line = [node]
                for k in range(1, self.reach + 1):
                    line.append(self.node(at, -k))
                    if k < self.reach:
                        line.append(self.node(at, k))
                for which in (replica, 1 - replica):
                    for j in range(self.reach):
                        targets = [self.node(at, self.reach - j), self.node(at, j + 1 - self.reach)]
                        line += [(2 * target + which) * part for target in targets]
                rows[replica, node, :] = line
        return rows.reshape(-1, 3 * self.count)


def hop(value, axis, mask):
    count = lax.axis_size(axis)
    return value + lax.ppermute(value, axis, [(s, s ^ mask) for s in range(count)])


def add(*values):
    total = values[0].astype(F32)
    for value in values[1:]:
        total = total + value.astype(F32)
    return total.astype(BF16)


def tied(*values):
    return lax.optimization_barrier(values)


def per_device(latents, cotangent, kernel, conv_bias, gn_gain, gn_shift, step):
    latent, cotan, shard = latents[0], cotangent[0], kernel[0]
    half, width, chans = latent.shape
    part = shard.shape[0]
    cols = Columns(chans)
    cells = half * width
    zs, replicas = lax.axis_size("z"), lax.axis_size("replica")
    core, z, y, replica = (lax.axis_index(a) for a in ("core", "z", "y", "replica"))
    lower = core == 0
    paired = replicas == 2
    ring = Ring(zs)
    scale = cols.total ** (-0.5)
    params = jnp.concatenate([conv_bias, gn_gain, gn_shift])
    me = ((replica * zs + z) * 2 + y) * 2 + core
    core, lower, same, me = tied(core, lower, replica == core, me)
    dev = me.reshape(1)

    mine = lax.dynamic_slice_in_dim(shard, core * cols.start, cols.lead, 1).astype(BF16)
    theirs = lax.dynamic_slice_in_dim(shard, (1 - core) * cols.start, cols.lead, 1).astype(BF16)
    got = swap(theirs, "core")
    unit = jnp.where(lower, jnp.concatenate([mine, got]), jnp.concatenate([got, mine]))
    lat_far = swap(latent, "core")
    cot_b = cotan.astype(BF16)
    cot_far = swap(cot_b, "core")

    if paired:
        table = jnp.asarray(ring.table(part))
        order = (ring.count, part, 2 * ring.count)
        up1, down1 = ring.up(unit), ring.down(unit)
        peer = swap(mine, "replica")
    else:
        table = jnp.zeros((replicas * zs * 4, 1), jnp.int32)
        order = None

    def call(body, outs, ins, scratch, megabytes, flops):
        return pl.pallas_call(
            body,
            out_shape=outs,
            in_specs=ins,
            out_specs=jax.tree.map(lambda _: VMEM_SPEC, outs),
            scratch_shapes=scratch,
            compiler_params=pltpu.CompilerParams(vmem_limit_bytes=megabytes * 2**20),
            cost_estimate=pl.CostEstimate(flops=flops * 4, bytes_accessed=0, transcendentals=0),
        )

    image = (2 * half, width, chans)
    shifted = jax.ShapeDtypeStruct((3, 2 * half + 2, width, chans), BF16)
    flops = 2 * 2 * cells * chans * cols.lead
    stats, acts, cot_t = call(
        partial(act_kernel, order),
        (jax.ShapeDtypeStruct((2, chans), F32), shifted, jax.ShapeDtypeStruct((chans, 2 * cells), BF16)),
        [SMEM_SPEC] * 2 + [VMEM_SPEC] * 6,
        [pltpu.VMEM((chans, 2 * cells), F32)],
        8, flops // 4,
    )(dev, table, latent, lat_far, cot_b, cot_far, gn_gain, gn_shift)
    if paired:
        peer, acts = tied(peer, acts)
    counts = [2 * zs, 2, 3] + [2] * (zs - 2) if paired else [4 * zs]
    pieces = call(
        partial(grad_kernel, cols, 2 if paired else None),
        [jax.ShapeDtypeStruct((n * part, cols.lead), BF16) for n in counts],
        [SMEM_SPEC] + [VMEM_SPEC] * 3,
        [],
        4, flops // 2,
    )(dev, acts, cot_t, theirs)
    stages = Stages([2 * zs - 3, 3] if paired else [1], 2 * part if paired else chans)
    staged = paired

    def slopes_of(stats):
        extra = (jax.ShapeDtypeStruct((chans, stages.width), BF16),) if staged else ()
        return call(
            partial(slope_kernel, stages),
            (jax.ShapeDtypeStruct((3, 2 * half + 2, width, stages.width), BF16),
             jax.ShapeDtypeStruct(image, BF16), jax.ShapeDtypeStruct(image, BF16)) + extra,
            [SMEM_SPEC] * 2 + [VMEM_SPEC] * 7,
            [pltpu.VMEM((2 * half, width, stages.width), F32)] if staged else [],
            8, flops // 4,
        )(dev, table, stats, gn_gain, gn_shift, latent, lat_far, cot_b, cot_far)

    def back(stage, cots, slopes, blocks):
        return call(
            partial(back_kernel, cols, stages, stage), jax.ShapeDtypeStruct((2, chans), F32),
            [SMEM_SPEC] + [VMEM_SPEC] * (3 + len(blocks)),
            [pltpu.VMEM((2 * cells, chans), F32)], 8, flops // 4,
        )(dev, cots, *slopes, *blocks)

    def conv_first(blocks):
        wide = stages.widths[0]
        return call(
            partial(conv_both_kernel, cols, stages, 0),
            (jax.ShapeDtypeStruct((cells, wide), F32), jax.ShapeDtypeStruct((cells, wide), BF16)),
            [SMEM_SPEC] + [VMEM_SPEC] * (1 + len(blocks)),
            [pltpu.VMEM((2 * cells, wide), F32)], 6, flops // 4,
        )(dev, acts, *blocks)

    def conv_far(acts, blocks):
        wide = stages.widths[-1]
        return call(
            partial(conv_far_kernel, cols, stages, len(stages.counts) - 1),
            jax.ShapeDtypeStruct((cells, wide), BF16),
            [SMEM_SPEC] + [VMEM_SPEC] * (1 + len(blocks)),
            [pltpu.VMEM((cells, wide), F32)], 4, flops // 8,
        )(dev, acts, *blocks)

    def conv_own(got, earlier, blocks):
        return call(
            partial(conv_own_kernel, cols, stages), jax.ShapeDtypeStruct((half, width, chans), BF16),
            [SMEM_SPEC] + [VMEM_SPEC] * (4 + len(earlier) + len(blocks)),
            [pltpu.VMEM((cells, stages.widths[-1]), F32)], 8, flops // 4,
        )(dev, acts, got, latent, conv_bias, *earlier, *blocks)

    def chip_sum(sums):
        vectors = jnp.concatenate([jnp.sum(cotan, axis=(0, 1))[None], sums])
        vectors = params / (4 * zs) - LR_VECTOR * vectors
        return vectors + swap(vectors, "core")

    if paired:
        kept, *sent = pieces
        crossed = [swap(sent[0], "replica")]
        up, down, stats, *sent[:3] = tied(up1, down1, stats, *sent[:3])
        crossed += [swap(piece, "replica") for piece in sent[1:3]]
        theirs = crossed[1]

        def ring_sums(j, *received):
            parts = kept[2 * j * part:(2 * j + 2) * part], crossed[j]
            ahead, behind = (tuple(x[at:at + part] for x in parts) for at in (0, part))
            ahead = add(*ahead, *received[:1])
            behind = behind + tuple(received[1:])
            return ahead, add(*behind) if j < zs - 1 else behind

        def ring_step(ahead, behind):
            return ring.up(ahead), ring.down(behind)

        blocks = [unit, up, down]
        up, down = ring.up(up), ring.down(down)
        up, down, cots, *slopes, order = tied(up, down, *slopes_of(stats))
        blocks += [up, down]

        up, down = ring.up(up), ring.down(down)
        conv_first_own, conv_send = conv_first(blocks)
        crossed[0], conv_send = tied(crossed[0], conv_send)
        received = ring_step(*ring_sums(0))
        cots, conv_send = tied(cots, conv_send)
        first_sums = back(0, cots, slopes, blocks)
        up, down, first_sums, sent[3] = tied(up, down, first_sums, sent[3])
        crossed.append(swap(sent[3], "replica"))
        late = [up, down]

        halves = ring.up(up[:part]), ring.down(down[part:])
        conv_first_got = swap(conv_send, "core")
        for j in range(1, zs - 2):
            received = ring_step(*ring_sums(j, *received))
        late += halves

        conv_send = conv_far(acts, late)
        cots, conv_send = tied(cots, conv_send)
        conv_got = swap(conv_send, "core")
        sums = back(1, cots, slopes, late)
        crossed[2], sums, *received = tied(crossed[2], sums, *received)
        received = ring_step(*ring_sums(zs - 2, *received))
        vectors = hop(chip_sum(first_sums + sums), "replica", 1)
        crossed[3], conv_got, vectors, *received = tied(crossed[3], conv_got, vectors, *received)
        ahead, behind = ring_sums(zs - 1, *received)
        last = ring.up(ahead)
        block = conv_own(conv_got, [conv_first_own, conv_first_got, order], late)
        vectors = hop(vectors, "z", 1)
        last, block, vectors = tied(last, block, vectors)
        total = add(*behind, last)
        vectors = hop(vectors, "y", 1)
        reach = 2
        while reach < zs:
            vectors = hop(vectors, "z", reach)
            reach *= 2
        across, vectors = tied(swap(total, "replica"), vectors)
        ours, others = jnp.where(same, total, across), jnp.where(same, across, total)
        aside = swap(others, "core")
        vector = jax.ShapeDtypeStruct((1, chans), F32)
        new_kernel, *new_v = call(
            partial(finish_kernel, cols),
            (jax.ShapeDtypeStruct(shard.shape, F32), vector, vector, vector),
            [SMEM_SPEC] * 2 + [VMEM_SPEC] * 6, [], 8, flops // 16,
        )(dev, step, shard, peer, theirs, ours, aside, vectors)
    else:
        late = [lax.all_gather(unit, NODE, axis=0, tiled=True)]
        cots, slope, slope_x = slopes_of(stats)
        sums = back(0, cots, [slope, slope_x], late)
        vectors = chip_sum(sums)
        block = conv_own(swap(conv_far(acts, late), "core"), [], late)
        terms = pieces[0].reshape(2 * zs, 2, part, cols.lead)
        summed = lax.psum_scatter(terms, NODE, scatter_dimension=0, tiled=False)
        ours = lax.dynamic_index_in_dim(summed, core, 0, keepdims=False)
        got = swap(lax.dynamic_index_in_dim(summed, 1 - core, 0, keepdims=False), "core")
        left, right = jnp.where(lower, ours, got), jnp.where(lower, got, ours)
        kernel_grad = jnp.concatenate([left, right[:, cols.both:]], axis=1).astype(F32)
        level = step[0] % (replicas.bit_length() - 1)
        rate = LR_KERNEL * (1.0 - (step[0] % 1000).astype(F32) / 2000.0)
        stepped = shard - (scale * rate) * kernel_grad
        new_kernel = 0.5 * (stepped + from_peer(level, stepped.astype(BF16)).astype(F32))
        stepped_v = lax.psum(vectors, NODE)
        new_v = jnp.split(0.5 * (stepped_v + from_peer(level, stepped_v)), 3)

    return (
        block[None],
        new_kernel[None],
        new_v[0],
        new_v[1],
        new_v[2],
    )


def solution(mesh):
    replicas, shards = mesh.shape["replica"], mesh.shape["shard"]
    split = Mesh(mesh.devices.reshape(replicas, shards // 4, 2, 2), ("replica", "z", "y", "core"))
    shard = ("z", "y", "core")
    return jax.shard_map(
        per_device,
        mesh=split,
        in_specs=(
            P("replica", shard, None, None),
            P("replica", shard, None, None),
            P("replica", shard, None),
            P("replica", None),
            P("replica", None),
            P("replica", None),
            P(),
        ),
        out_specs=(
            P("replica", shard, None, None),
            P("replica", shard, None),
            P("replica", None),
            P("replica", None),
            P("replica", None),
        ),
        check_vma=False,
    )
```

```python
from functools import partial

import jax
import jax.numpy as jnp
import numpy as np
from jax import lax
from jax.experimental import pallas as pl
from jax.experimental.pallas import tpu as pltpu
from jax.sharding import Mesh, PartitionSpec as P

GROUPS = 32
EPS = 1e-05
LR_KERNEL = 0.1
LR_VECTOR = 0.01
LANES = 128
BF16 = jnp.bfloat16
F32 = jnp.float32

SMEM_SPEC = pl.BlockSpec(memory_space=pltpu.SMEM)
VMEM_SPEC = pl.BlockSpec(memory_space=pltpu.VMEM)


class Columns:
    def __init__(self, chans):
        tiles = 9 * chans // LANES
        self.total = 9 * chans
        self.lead = (tiles + 1) // 2 * LANES
        self.start = self.total - self.lead
        self.both = 2 * self.lead - self.total
        self.mid = self.lead - 4 * chans
        self.mid_start = chans - self.mid

    def pair(self, core, k, chans):
        first = jnp.where(core == 0, 2 * k, 5 + 2 * k)
        place = jnp.where(core == 0, 2 * k * chans, self.mid + 2 * k * chans)
        return (first, first + 1), pl.multiple_of(place, LANES)

    def middle(self, core, chans):
        place = jnp.where(core == 0, 4 * chans, 0)
        channel = jnp.where(core == 0, 0, self.mid_start)
        return pl.multiple_of(place, LANES), pl.multiple_of(channel, LANES)


def fill_shifts(shifts, row, values):
    width = values.shape[0]
    at = lax.broadcasted_iota(jnp.int32, values.shape, 0)
    left = jnp.where(at == 0, 0.0, pltpu.roll(values, 1, 0))
    right = jnp.where(at == width - 1, 0.0, pltpu.roll(values, width - 1, 0))
    shifts[0, row] = left.astype(BF16)
    shifts[1, row] = values.astype(BF16)
    shifts[2, row] = right.astype(BF16)


def clear_edges(shifts):
    zero = jnp.zeros(shifts.shape[2:], shifts.dtype)
    for b in range(3):
        shifts[b, 0] = zero
        shifts[b, shifts.shape[1] - 1] = zero


def act_kernel(order, dev, table, lat_own, lat_far, cot_own, cot_far, gain, shift,
               stats, acts, cot_t, cot_f):
    me = dev[0]
    core = me % 2
    half, width, chans = lat_own.shape
    cells = 2 * half * width
    group_width = chans // GROUPS
    own_at = core * half
    far_at = half - own_at
    clear_edges(acts)

    def add_row(i, sums):
        total, square = sums
        a = lat_own[i].astype(F32)
        b = lat_far[i].astype(F32)
        return total + (a + b), square + (a * a + b * b)

    zero = jnp.zeros((width, chans), F32)
    total, square = lax.fori_loop(0, half, add_row, (zero, zero))
    sums = jnp.concatenate(
        [jnp.sum(total, axis=0, keepdims=True), jnp.sum(square, axis=0, keepdims=True),
         jnp.zeros((6, chans), F32)], axis=0
    )
    first = lax.broadcasted_iota(jnp.int32, (chans, LANES), 0)
    start = lax.broadcasted_iota(jnp.int32, (chans, LANES), 1) * group_width
    member = jnp.where((first >= start) & (first < start + group_width), 1.0, 0.0)
    exact = partial(lax.dot_general, precision=lax.Precision.HIGHEST, preferred_element_type=F32)
    sums = exact(sums, member, (((1,), (0,)), ((), ()))) / (cells * group_width)
    sums = exact(sums, member, (((1,), (1,)), ((), ())))
    mean = sums[0:1]
    rstd = lax.rsqrt(sums[1:2] - mean * mean + EPS)
    stats[0:1] = mean
    stats[1:2] = rstd
    gain_v, shift_v = gain[...], shift[...]

    def act_rows(i, _):
        for ref, base in ((lat_own, own_at), (lat_far, far_at)):
            pre = gain_v * ((ref[i].astype(F32) - mean) * rstd) + shift_v
            fill_shifts(acts, base + i + 1, pre * (0.5 + 0.5 * jnp.tanh(0.5 * pre)))
        return 0

    lax.fori_loop(0, half, act_rows, 0)

    chunk = LANES // width
    for ref, base in ((cot_own, own_at), (cot_far, far_at)):
        for i in range(half // chunk):
            piece = ref[i * chunk:(i + 1) * chunk].reshape(LANES, chans).astype(F32)
            place = pl.multiple_of(base * width + i * LANES, LANES)
            if order is None:
                cot_t[:, pl.ds(place, LANES)] = piece.T.astype(BF16)
            else:
                cot_f[:, pl.ds(place, LANES)] = piece.T
    if order is not None:
        first_at, part, count = order
        for q in range(count // 2):
            pair = [
                cot_f[pl.ds(pl.multiple_of(table[me, first_at + 2 * q + i], 8), part)]
                for i in range(2)
            ]
            cot_t[2 * q * part:(2 * q + 2) * part] = jnp.concatenate(pair).astype(BF16)


def grad_kernel(cols, carrier, dev, acts, cot_t, theirs, *pieces):
    core = dev[0] % 2
    rows, width, chans = acts.shape[1] - 2, acts.shape[2], acts.shape[3]
    cells = rows * width

    def emit(window, place, wide):
        value = jnp.dot(cot_t[...], window, preferred_element_type=F32)
        at = 0
        for i, piece in enumerate(pieces):
            count = piece.shape[0] - (theirs.shape[0] if i == carrier else 0)
            piece[:count, pl.ds(place, wide)] = value[at:at + count].astype(BF16)
            at += count

    def two_taps(k, _):
        taps, place = cols.pair(core, k, chans)
        windows = [acts[t % 3, pl.ds(t // 3, rows)].reshape(cells, chans) for t in taps]
        emit(jnp.concatenate(windows, axis=1), place, 2 * chans)
        return 0

    lax.fori_loop(0, 2, two_taps, 0)
    place, channel = cols.middle(core, chans)
    emit(acts[1, 1:rows + 1, :, pl.ds(channel, cols.mid)].reshape(cells, cols.mid), place, cols.mid)
    if carrier is not None:
        pieces[carrier][-theirs.shape[0]:] = theirs[...]


class Stages:
    def __init__(self, counts, rows):
        self.rows = rows
        self.counts = counts
        self.widths = [-(-n * rows // LANES) * LANES for n in counts]
        self.starts = [sum(self.widths[:i]) for i in range(len(counts))]
        self.width = sum(self.widths)

    def lanes(self, stage):
        return slice(self.starts[stage], self.starts[stage] + self.widths[stage])

    def columns(self, stage, blocks, place, wide):
        parts = [ref[:min(self.rows, ref.shape[0]), pl.ds(place, wide)] for ref in blocks]
        if len(parts) == self.counts[stage] + 1:
            parts[-2:] = [jnp.concatenate(parts[-2:])]
        spare = self.widths[stage] - self.counts[stage] * self.rows
        if spare:
            parts.append(jnp.zeros((spare, wide), BF16))
        return jnp.concatenate(parts) if len(parts) > 1 else parts[0]

    def order(self, me, table, order, chans):
        lane = lax.broadcasted_iota(jnp.int32, (1, self.width), 1)
        source = jnp.full((1, self.width), -1, jnp.int32)
        at = 0
        for start, count in zip(self.starts, self.counts):
            for i in range(count):
                first = start + i * self.rows
                inside = (lane >= first) & (lane < first + self.rows)
                source = jnp.where(inside, table[me, at] * self.rows + lane - first, source)
                at += 1
        channel = lax.broadcasted_iota(jnp.int32, (chans, self.width), 0)
        order[...] = jnp.where(channel == source, 1.0, 0.0).astype(BF16)


def slope_kernel(stages, dev, table, stats, gain, shift, lat_own, lat_far, cot_own, cot_far,
                 cots, slope, slope_x, *refs):
    me = dev[0]
    core = me % 2
    half, width, chans = lat_own.shape
    clear_edges(cots)
    mean, rstd = stats[0:1], stats[1:2]
    gain_v, shift_v = gain[...], shift[...]
    far_at = half - core * half
    if len(stages.counts) > 1:
        order, placed = refs
        stages.order(me, table, order, chans)
        for ref, base in ((cot_own, core * half), (cot_far, far_at)):
            value = jnp.dot(ref[...].reshape(half * width, chans), order[...], preferred_element_type=F32)
            placed[pl.ds(base, half)] = value.reshape(half, width, stages.width)

    def one_row(i, _):
        for lat, cot, base in ((lat_own, cot_own, core * half), (lat_far, cot_far, far_at)):
            value = placed[base + i] if len(stages.counts) > 1 else cot[i].astype(F32)
            fill_shifts(cots, base + i + 1, value)
            xhat = (lat[i].astype(F32) - mean) * rstd
            pre = gain_v * xhat + shift_v
            sig = 0.5 + 0.5 * jnp.tanh(0.5 * pre)
            value = sig * (1.0 + pre * (1.0 - sig))
            slope[base + i] = value.astype(BF16)
            slope_x[base + i] = (value * xhat).astype(BF16)
        return 0

    lax.fori_loop(0, half, one_row, 0)


def conv_sum(cols, stages, stage, core, first, half, acts, blocks, total):
    width, chans = acts.shape[2:]
    cells = half * width
    nt = (((1,), (1,)), ((), ()))
    place, channel = cols.middle(core, chans)
    window = acts[1, pl.ds(first + 1, half), :, pl.ds(channel, cols.mid)].reshape(cells, cols.mid)
    lane = lax.broadcasted_iota(jnp.int32, window.shape, 1)
    window = jnp.where((core == 1) & (lane < cols.both), jnp.zeros_like(window), window)
    kernel = stages.columns(stage, blocks, place, cols.mid)
    total[...] = lax.dot_general(window, kernel, nt, preferred_element_type=F32)

    def two_taps(k, _):
        taps, place = cols.pair(core, k, chans)
        windows = [acts[t % 3, pl.ds(first + t // 3, half)].reshape(cells, chans) for t in taps]
        kernel = stages.columns(stage, blocks, place, 2 * chans)
        total[...] += lax.dot_general(
            jnp.concatenate(windows, axis=1), kernel, nt, preferred_element_type=F32
        )
        return 0

    lax.fori_loop(0, 2, two_taps, 0)


def conv_both_kernel(cols, stages, stage, dev, acts, *refs):
    blocks, (own, far, total) = refs[:-3], refs[-3:]
    core = dev[0] % 2
    rows = acts.shape[1] - 2
    conv_sum(cols, stages, stage, core, 0, rows, acts, blocks, total)
    half = own.shape[0]
    own[...] = total[pl.ds(pl.multiple_of(core * half, half), half)]
    far[...] = total[pl.ds(pl.multiple_of((1 - core) * half, half), half)].astype(BF16)


def conv_far_kernel(cols, stages, stage, dev, acts, *refs):
    blocks, (far, total) = refs[:-2], refs[-2:]
    core = dev[0] % 2
    half = (acts.shape[1] - 2) // 2
    conv_sum(cols, stages, stage, core, (1 - core) * half, half, acts, blocks, total)
    far[...] = total[...].astype(BF16)


def conv_own_kernel(cols, stages, dev, acts, got, latent, bias, *refs):
    core = dev[0] % 2
    half, width, chans = latent.shape
    scale = cols.total ** (-0.5)
    stage = len(stages.counts) - 1
    before = 3 * stage
    blocks, (block, total) = refs[before:-2], refs[-2:]
    conv_sum(cols, stages, stage, core, core * half, half, acts, blocks, total)
    conv = total[...] + got[...].astype(F32)
    if stage:
        first_own, first_got, order = refs[:before]
        conv = jnp.concatenate([first_own[...] + first_got[...].astype(F32), conv], axis=1)
        high = conv.astype(BF16)
        low = (conv - high.astype(F32)).astype(BF16)
        nt = (((1,), (1,)), ((), ()))
        conv = sum(
            lax.dot_general(value, order[...], nt, preferred_element_type=F32) for value in (low, high)
        )
    conv = scale * conv + bias[...]
    block[...] = (conv.reshape(half, width, chans) + latent[...].astype(F32)).astype(BF16)


def back_kernel(cols, stages, stage, dev, cots, slope, slope_x, *refs):
    blocks, (sums, total) = refs[:-2], refs[-2:]
    core = dev[0] % 2
    rows, width = cots.shape[1] - 2, cots.shape[2]
    cells, chans = total.shape
    lanes = stages.lanes(stage)

    def taps_from(first, place, count):
        windows, kernels = [], []
        for i in range(count):
            tap = first + i
            window = cots[2 - tap % 3, pl.ds(2 - tap // 3, rows), :, lanes]
            windows.append(window.reshape(cells, stages.widths[stage]))
            kernels.append(stages.columns(stage, blocks, pl.multiple_of(place + i * chans, LANES), chans))
        return jnp.dot(
            jnp.concatenate(windows, axis=1), jnp.concatenate(kernels), preferred_element_type=F32
        )

    if stages.widths[stage] * 4 <= 2 * chans:
        taps, place = cols.pair(core, 0, chans)
        total[...] = taps_from(taps[0], place, 4)
    else:
        total[...] = jnp.zeros_like(total)

        def two_taps(k, _):
            taps, place = cols.pair(core, k, chans)
            total[...] += taps_from(taps[0], place, 2)
            return 0

        lax.fori_loop(0, 2, two_taps, 0)

    place, channel = cols.middle(core, chans)
    window = cots[1, 1:rows + 1, :, lanes].reshape(cells, stages.widths[stage])
    kernel = stages.columns(stage, blocks, place, cols.mid)
    value = jnp.dot(window, kernel, preferred_element_type=F32)
    lane = lax.broadcasted_iota(jnp.int32, value.shape, 1)
    total[:, pl.ds(channel, cols.mid)] += jnp.where((core == 1) & (lane < cols.both), 0.0, value)

    def add_row(i, carry):
        gains, shifts = carry
        value = total[pl.ds(pl.multiple_of(i * width, width), width)]
        return gains + value * slope_x[i].astype(F32), shifts + value * slope[i].astype(F32)

    zero = jnp.zeros((width, chans), F32)
    gains, shifts = lax.fori_loop(0, rows, add_row, (zero, zero))
    scale = cols.total ** (-0.5)
    sums[0:1] = scale * jnp.sum(gains, axis=0, keepdims=True)
    sums[1:2] = scale * jnp.sum(shifts, axis=0, keepdims=True)


def finish_kernel(cols, dev, step, shard, mine, carried, ours, aside, vectors, out, new_bias, new_gain, new_shift):
    lower = dev[0] % 2 == 0
    rate = LR_KERNEL * (1.0 - (step[0] % 1000).astype(F32) / 2000.0)
    factor = 0.5 * cols.total ** (-0.5) * rate
    part = shard.shape[0]
    theirs = carried[-part:].astype(F32)
    here = 0.5 * mine[...].astype(F32) - factor * ours[...].astype(F32)
    there = 0.5 * theirs - factor * aside[...].astype(F32)
    left, right = jnp.where(lower, here, there), jnp.where(lower, there, here)
    out[:, :cols.lead] = 0.5 * shard[:, :cols.lead] + left
    out[:, cols.lead:] = 0.5 * shard[:, cols.lead:] + right[:, cols.both:]
    for i, new in enumerate((new_bias, new_gain, new_shift)):
        new[...] = 0.5 * vectors[i:i + 1]


NODE = ("z", "y")


def swap(value, axis):
    return lax.ppermute(value, axis, [(0, 1), (1, 0)])


def from_peer(level, value):
    count = lax.axis_size("replica")
    levels = count.bit_length() - 1
    moves = [[(s, (s + (1 << k)) % count) for s in range(count)] for k in range(levels)]
    if levels == 1:
        return lax.ppermute(value, "replica", moves[0])
    return lax.switch(level, [lambda v, m=m: lax.ppermute(v, "replica", m) for m in moves], value)


class Ring:
    def __init__(self, zs):
        self.count = 2 * zs
        self.reach = zs
        self.nodes = [2 * z for z in range(zs)] + [2 * z + 1 for z in reversed(range(zs))]
        ahead = list(zip(self.nodes, self.nodes[1:] + self.nodes[:1]))
        self.ahead = ahead
        self.behind = [(b, a) for a, b in ahead]

    def node(self, at, offset):
        return self.nodes[(at + offset) % self.count]

    def up(self, value):
        return lax.ppermute(value, NODE, self.ahead)

    def down(self, value):
        return lax.ppermute(value, NODE, self.behind)

    def table(self, part):
        rows = np.zeros((2, self.count, 2, 3 * self.count), np.int32)
        for replica in range(2):
            for at, node in enumerate(self.nodes):
                line = [node]
                for k in range(1, self.reach + 1):
                    line.append(self.node(at, -k))
                    if k < self.reach:
                        line.append(self.node(at, k))
                for which in (replica, 1 - replica):
                    for j in range(self.reach):
                        targets = [self.node(at, self.reach - j), self.node(at, j + 1 - self.reach)]
                        line += [(2 * target + which) * part for target in targets]
                rows[replica, node, :] = line
        return rows.reshape(-1, 3 * self.count)


def hop(value, axis, mask):
    count = lax.axis_size(axis)
    return value + lax.ppermute(value, axis, [(s, s ^ mask) for s in range(count)])


def add(*values):
    total = values[0].astype(F32)
    for value in values[1:]:
        total = total + value.astype(F32)
    return total.astype(BF16)


def tied(*values):
    return lax.optimization_barrier(values)


def per_device(latents, cotangent, kernel, conv_bias, gn_gain, gn_shift, step):
    latent, cotan, shard = latents[0], cotangent[0], kernel[0]
    half, width, chans = latent.shape
    part = shard.shape[0]
    cols = Columns(chans)
    cells = half * width
    zs, replicas = lax.axis_size("z"), lax.axis_size("replica")
    core, z, y, replica = (lax.axis_index(a) for a in ("core", "z", "y", "replica"))
    lower = core == 0
    paired = replicas == 2
    ring = Ring(zs)
    scale = cols.total ** (-0.5)
    params = jnp.concatenate([conv_bias, gn_gain, gn_shift])
    me = ((replica * zs + z) * 2 + y) * 2 + core
    core, lower, same, me = tied(core, lower, replica == core, me)
    dev = me.reshape(1)

    mine = lax.dynamic_slice_in_dim(shard, core * cols.start, cols.lead, 1).astype(BF16)
    theirs = lax.dynamic_slice_in_dim(shard, (1 - core) * cols.start, cols.lead, 1).astype(BF16)
    got = swap(theirs, "core")
    unit = jnp.where(lower, jnp.concatenate([mine, got]), jnp.concatenate([got, mine]))
    lat_far = swap(latent, "core")
    cot_b = cotan.astype(BF16)
    cot_far = swap(cot_b, "core")

    if paired:
        table = jnp.asarray(ring.table(part))
        order = (ring.count, part, 2 * ring.count)
        up1, down1 = ring.up(unit), ring.down(unit)
        peer = swap(tied(mine, unit)[0], "replica")
    else:
        table = jnp.zeros((replicas * zs * 4, 1), jnp.int32)
        order = None

    def call(body, outs, ins, scratch, megabytes, flops):
        return pl.pallas_call(
            body,
            out_shape=outs,
            in_specs=ins,
            out_specs=jax.tree.map(lambda _: VMEM_SPEC, outs),
            scratch_shapes=scratch,
            compiler_params=pltpu.CompilerParams(vmem_limit_bytes=megabytes * 2**20),
            cost_estimate=pl.CostEstimate(flops=flops * 4, bytes_accessed=0, transcendentals=0),
        )

    image = (2 * half, width, chans)
    shifted = jax.ShapeDtypeStruct((3, 2 * half + 2, width, chans), BF16)
    flops = 2 * 2 * cells * chans * cols.lead
    stats, acts, cot_t = call(
        partial(act_kernel, order),
        (jax.ShapeDtypeStruct((2, chans), F32), shifted, jax.ShapeDtypeStruct((chans, 2 * cells), BF16)),
        [SMEM_SPEC] * 2 + [VMEM_SPEC] * 6,
        [pltpu.VMEM((chans, 2 * cells), F32)],
        8, flops // 4,
    )(dev, table, latent, lat_far, cot_b, cot_far, gn_gain, gn_shift)
    if paired:
        peer, acts = tied(peer, acts)
    counts = [2 * zs, 2, 3] + [2] * (zs - 2) if paired else [4 * zs]
    pieces = call(
        partial(grad_kernel, cols, 2 if paired else None),
        [jax.ShapeDtypeStruct((n * part, cols.lead), BF16) for n in counts],
        [SMEM_SPEC] + [VMEM_SPEC] * 3,
        [],
        4, flops // 2,
    )(dev, acts, cot_t, theirs)
    stages = Stages([2 * zs - 3, 3] if paired else [1], 2 * part if paired else chans)
    staged = paired

    def slopes_of(stats):
        extra = (jax.ShapeDtypeStruct((chans, stages.width), BF16),) if staged else ()
        return call(
            partial(slope_kernel, stages),
            (jax.ShapeDtypeStruct((3, 2 * half + 2, width, stages.width), BF16),
             jax.ShapeDtypeStruct(image, BF16), jax.ShapeDtypeStruct(image, BF16)) + extra,
            [SMEM_SPEC] * 2 + [VMEM_SPEC] * 7,
            [pltpu.VMEM((2 * half, width, stages.width), F32)] if staged else [],
            8, flops // 4,
        )(dev, table, stats, gn_gain, gn_shift, latent, lat_far, cot_b, cot_far)

    def back(stage, cots, slopes, blocks):
        return call(
            partial(back_kernel, cols, stages, stage), jax.ShapeDtypeStruct((2, chans), F32),
            [SMEM_SPEC] + [VMEM_SPEC] * (3 + len(blocks)),
            [pltpu.VMEM((2 * cells, chans), F32)], 8, flops // 4,
        )(dev, cots, *slopes, *blocks)

    def conv_first(blocks):
        wide = stages.widths[0]
        return call(
            partial(conv_both_kernel, cols, stages, 0),
            (jax.ShapeDtypeStruct((cells, wide), F32), jax.ShapeDtypeStruct((cells, wide), BF16)),
            [SMEM_SPEC] + [VMEM_SPEC] * (1 + len(blocks)),
            [pltpu.VMEM((2 * cells, wide), F32)], 6, flops // 4,
        )(dev, acts, *blocks)

    def conv_far(acts, blocks):
        wide = stages.widths[-1]
        return call(
            partial(conv_far_kernel, cols, stages, len(stages.counts) - 1),
            jax.ShapeDtypeStruct((cells, wide), BF16),
            [SMEM_SPEC] + [VMEM_SPEC] * (1 + len(blocks)),
            [pltpu.VMEM((cells, wide), F32)], 4, flops // 8,
        )(dev, acts, *blocks)

    def conv_own(got, earlier, blocks):
        return call(
            partial(conv_own_kernel, cols, stages), jax.ShapeDtypeStruct((half, width, chans), BF16),
            [SMEM_SPEC] + [VMEM_SPEC] * (4 + len(earlier) + len(blocks)),
            [pltpu.VMEM((cells, stages.widths[-1]), F32)], 8, flops // 4,
        )(dev, acts, got, latent, conv_bias, *earlier, *blocks)

    def chip_sum(sums):
        vectors = jnp.concatenate([jnp.sum(cotan, axis=(0, 1))[None], sums])
        vectors = params / (4 * zs) - LR_VECTOR * vectors
        return vectors + swap(vectors, "core")

    if paired:
        kept, *sent = pieces
        crossed = [swap(sent[0], "replica")]
        up, down, stats, *sent[:3] = tied(up1, down1, stats, *sent[:3])
        crossed += [swap(piece, "replica") for piece in sent[1:3]]
        theirs = crossed[1]

        def ring_sums(j, *received):
            parts = kept[2 * j * part:(2 * j + 2) * part], crossed[j]
            ahead, behind = (tuple(x[at:at + part] for x in parts) for at in (0, part))
            ahead = add(*ahead, *received[:1])
            behind = behind + tuple(received[1:])
            return ahead, add(*behind) if j < zs - 1 else behind

        def ring_step(ahead, behind):
            return ring.up(ahead), ring.down(behind)

        blocks = [unit, up, down]
        up, down = ring.up(up), ring.down(down)
        up, down, cots, *slopes, order = tied(up, down, *slopes_of(stats))
        blocks += [up, down]

        up, down = ring.up(up), ring.down(down)
        conv_first_own, conv_send = conv_first(blocks)
        crossed[0], conv_send = tied(crossed[0], conv_send)
        received = ring_step(*ring_sums(0))
        cots, conv_send = tied(cots, conv_send)
        first_sums = back(0, cots, slopes, blocks)
        up, down, first_sums, sent[3] = tied(up, down, first_sums, sent[3])
        crossed.append(swap(sent[3], "replica"))
        late = [up, down]

        halves = ring.up(up[:part]), ring.down(down[part:])
        conv_first_got = swap(conv_send, "core")
        for j in range(1, zs - 2):
            received = ring_step(*ring_sums(j, *received))
        late += halves

        conv_send = conv_far(acts, late)
        cots, conv_send = tied(cots, conv_send)
        conv_got = swap(conv_send, "core")
        sums = back(1, cots, slopes, late)
        crossed[2], sums, *received = tied(crossed[2], sums, *received)
        received = ring_step(*ring_sums(zs - 2, *received))
        vectors = hop(hop(chip_sum(first_sums + sums), "replica", 1), "z", 1)
        crossed[3], conv_got, vectors, *received = tied(crossed[3], conv_got, vectors, *received)
        ahead, behind = ring_sums(zs - 1, *received)
        last = ring.up(ahead)
        block = conv_own(conv_got, [conv_first_own, conv_first_got, order], late)
        block, vectors = tied(block, vectors)
        vectors = hop(vectors, "y", 1)
        last, block, vectors = tied(last, block, vectors)
        total = add(*behind, last)
        reach = 2
        while reach < zs:
            vectors = hop(vectors, "z", reach)
            reach *= 2
        across, vectors = tied(swap(total, "replica"), vectors)
        ours, others = jnp.where(same, total, across), jnp.where(same, across, total)
        aside = swap(others, "core")
        vector = jax.ShapeDtypeStruct((1, chans), F32)
        new_kernel, *new_v = call(
            partial(finish_kernel, cols),
            (jax.ShapeDtypeStruct(shard.shape, F32), vector, vector, vector),
            [SMEM_SPEC] * 2 + [VMEM_SPEC] * 6, [], 8, flops // 16,
        )(dev, step, shard, peer, theirs, ours, aside, vectors)
    else:
        late = [lax.all_gather(unit, NODE, axis=0, tiled=True)]
        cots, slope, slope_x = slopes_of(stats)
        sums = back(0, cots, [slope, slope_x], late)
        vectors = chip_sum(sums)
        block = conv_own(swap(conv_far(acts, late), "core"), [], late)
        terms = pieces[0].reshape(2 * zs, 2, part, cols.lead)
        summed = lax.psum_scatter(terms, NODE, scatter_dimension=0, tiled=False)
        ours = lax.dynamic_index_in_dim(summed, core, 0, keepdims=False)
        got = swap(lax.dynamic_index_in_dim(summed, 1 - core, 0, keepdims=False), "core")
        left, right = jnp.where(lower, ours, got), jnp.where(lower, got, ours)
        kernel_grad = jnp.concatenate([left, right[:, cols.both:]], axis=1).astype(F32)
        level = step[0] % (replicas.bit_length() - 1)
        rate = LR_KERNEL * (1.0 - (step[0] % 1000).astype(F32) / 2000.0)
        stepped = shard - (scale * rate) * kernel_grad
        new_kernel = 0.5 * (stepped + from_peer(level, stepped.astype(BF16)).astype(F32))
        stepped_v = lax.psum(vectors, NODE)
        new_v = jnp.split(0.5 * (stepped_v + from_peer(level, stepped_v)), 3)

    return (
        block[None],
        new_kernel[None],
        new_v[0],
        new_v[1],
        new_v[2],
    )


def solution(mesh):
    replicas, shards = mesh.shape["replica"], mesh.shape["shard"]
    split = Mesh(mesh.devices.reshape(replicas, shards // 4, 2, 2), ("replica", "z", "y", "core"))
    shard = ("z", "y", "core")
    return jax.shard_map(
        per_device,
        mesh=split,
        in_specs=(
            P("replica", shard, None, None),
            P("replica", shard, None, None),
            P("replica", shard, None),
            P("replica", None),
            P("replica", None),
            P("replica", None),
            P(),
        ),
        out_specs=(
            P("replica", shard, None, None),
            P("replica", shard, None),
            P("replica", None),
            P("replica", None),
            P("replica", None),
        ),
        check_vma=False,
    )
```

```python
from functools import partial

import jax
import jax.numpy as jnp
import numpy as np
from jax import lax
from jax.experimental import pallas as pl
from jax.experimental.pallas import tpu as pltpu
from jax.sharding import Mesh, PartitionSpec as P

GROUPS = 32
EPS = 1e-05
LR_KERNEL = 0.1
LR_VECTOR = 0.01
LANES = 128
BF16 = jnp.bfloat16
F32 = jnp.float32

SMEM_SPEC = pl.BlockSpec(memory_space=pltpu.SMEM)
VMEM_SPEC = pl.BlockSpec(memory_space=pltpu.VMEM)


class Columns:
    def __init__(self, chans):
        tiles = 9 * chans // LANES
        self.total = 9 * chans
        self.lead = (tiles + 1) // 2 * LANES
        self.start = self.total - self.lead
        self.both = 2 * self.lead - self.total
        self.mid = self.lead - 4 * chans
        self.mid_start = chans - self.mid

    def pair(self, core, k, chans):
        first = jnp.where(core == 0, 2 * k, 5 + 2 * k)
        place = jnp.where(core == 0, 2 * k * chans, self.mid + 2 * k * chans)
        return (first, first + 1), pl.multiple_of(place, LANES)

    def middle(self, core, chans):
        place = jnp.where(core == 0, 4 * chans, 0)
        channel = jnp.where(core == 0, 0, self.mid_start)
        return pl.multiple_of(place, LANES), pl.multiple_of(channel, LANES)


def fill_shifts(shifts, row, values):
    width = values.shape[0]
    at = lax.broadcasted_iota(jnp.int32, values.shape, 0)
    left = jnp.where(at == 0, 0.0, pltpu.roll(values, 1, 0))
    right = jnp.where(at == width - 1, 0.0, pltpu.roll(values, width - 1, 0))
    shifts[0, row] = left.astype(BF16)
    shifts[1, row] = values.astype(BF16)
    shifts[2, row] = right.astype(BF16)


def clear_edges(shifts):
    zero = jnp.zeros(shifts.shape[2:], shifts.dtype)
    for b in range(3):
        shifts[b, 0] = zero
        shifts[b, shifts.shape[1] - 1] = zero


def act_kernel(order, dev, table, lat_own, lat_far, cot_own, cot_far, gain, shift,
               stats, acts, cot_t, cot_f):
    me = dev[0]
    core = me % 2
    half, width, chans = lat_own.shape
    cells = 2 * half * width
    group_width = chans // GROUPS
    own_at = core * half
    far_at = half - own_at
    clear_edges(acts)

    def add_row(i, sums):
        total, square = sums
        a = lat_own[i].astype(F32)
        b = lat_far[i].astype(F32)
        return total + (a + b), square + (a * a + b * b)

    zero = jnp.zeros((width, chans), F32)
    total, square = lax.fori_loop(0, half, add_row, (zero, zero))
    sums = jnp.concatenate(
        [jnp.sum(total, axis=0, keepdims=True), jnp.sum(square, axis=0, keepdims=True),
         jnp.zeros((6, chans), F32)], axis=0
    )
    first = lax.broadcasted_iota(jnp.int32, (chans, LANES), 0)
    start = lax.broadcasted_iota(jnp.int32, (chans, LANES), 1) * group_width
    member = jnp.where((first >= start) & (first < start + group_width), 1.0, 0.0)
    exact = partial(lax.dot_general, precision=lax.Precision.HIGHEST, preferred_element_type=F32)
    sums = exact(sums, member, (((1,), (0,)), ((), ()))) / (cells * group_width)
    sums = exact(sums, member, (((1,), (1,)), ((), ())))
    mean = sums[0:1]
    rstd = lax.rsqrt(sums[1:2] - mean * mean + EPS)
    stats[0:1] = mean
    stats[1:2] = rstd
    gain_v, shift_v = gain[...], shift[...]

    def act_rows(i, _):
        for ref, base in ((lat_own, own_at), (lat_far, far_at)):
            pre = gain_v * ((ref[i].astype(F32) - mean) * rstd) + shift_v
            fill_shifts(acts, base + i + 1, pre * (0.5 + 0.5 * jnp.tanh(0.5 * pre)))
        return 0

    lax.fori_loop(0, half, act_rows, 0)

    chunk = LANES // width
    for ref, base in ((cot_own, own_at), (cot_far, far_at)):
        for i in range(half // chunk):
            piece = ref[i * chunk:(i + 1) * chunk].reshape(LANES, chans).astype(F32)
            place = pl.multiple_of(base * width + i * LANES, LANES)
            if order is None:
                cot_t[:, pl.ds(place, LANES)] = piece.T.astype(BF16)
            else:
                cot_f[:, pl.ds(place, LANES)] = piece.T
    if order is not None:
        first_at, part, count = order
        for q in range(count // 2):
            pair = [
                cot_f[pl.ds(pl.multiple_of(table[me, first_at + 2 * q + i], 8), part)]
                for i in range(2)
            ]
            cot_t[2 * q * part:(2 * q + 2) * part] = jnp.concatenate(pair).astype(BF16)


def grad_kernel(cols, carrier, dev, acts, cot_t, theirs, *pieces):
    core = dev[0] % 2
    rows, width, chans = acts.shape[1] - 2, acts.shape[2], acts.shape[3]
    cells = rows * width

    def emit(window, place, wide):
        value = jnp.dot(cot_t[...], window, preferred_element_type=F32)
        at = 0
        for i, piece in enumerate(pieces):
            count = piece.shape[0] - (theirs.shape[0] if i == carrier else 0)
            piece[:count, pl.ds(place, wide)] = value[at:at + count].astype(BF16)
            at += count

    def two_taps(k, _):
        taps, place = cols.pair(core, k, chans)
        windows = [acts[t % 3, pl.ds(t // 3, rows)].reshape(cells, chans) for t in taps]
        emit(jnp.concatenate(windows, axis=1), place, 2 * chans)
        return 0

    lax.fori_loop(0, 2, two_taps, 0)
    place, channel = cols.middle(core, chans)
    emit(acts[1, 1:rows + 1, :, pl.ds(channel, cols.mid)].reshape(cells, cols.mid), place, cols.mid)
    if carrier is not None:
        pieces[carrier][-theirs.shape[0]:] = theirs[...]


class Stages:
    def __init__(self, counts, rows):
        self.rows = rows
        self.counts = counts
        self.widths = [-(-n * rows // LANES) * LANES for n in counts]
        self.starts = [sum(self.widths[:i]) for i in range(len(counts))]
        self.width = sum(self.widths)

    def lanes(self, stage):
        return slice(self.starts[stage], self.starts[stage] + self.widths[stage])

    def columns(self, stage, blocks, place, wide):
        parts = [ref[:min(self.rows, ref.shape[0]), pl.ds(place, wide)] for ref in blocks]
        if len(parts) == self.counts[stage] + 1:
            parts[-2:] = [jnp.concatenate(parts[-2:])]
        spare = self.widths[stage] - self.counts[stage] * self.rows
        if spare:
            parts.append(jnp.zeros((spare, wide), BF16))
        return jnp.concatenate(parts) if len(parts) > 1 else parts[0]

    def order(self, me, table, order, chans):
        lane = lax.broadcasted_iota(jnp.int32, (1, self.width), 1)
        source = jnp.full((1, self.width), -1, jnp.int32)
        at = 0
        for start, count in zip(self.starts, self.counts):
            for i in range(count):
                first = start + i * self.rows
                inside = (lane >= first) & (lane < first + self.rows)
                source = jnp.where(inside, table[me, at] * self.rows + lane - first, source)
                at += 1
        channel = lax.broadcasted_iota(jnp.int32, (chans, self.width), 0)
        order[...] = jnp.where(channel == source, 1.0, 0.0).astype(BF16)


def slope_kernel(stages, dev, table, stats, gain, shift, lat_own, lat_far, cot_own, cot_far,
                 cots, slope, slope_x, *refs):
    me = dev[0]
    core = me % 2
    half, width, chans = lat_own.shape
    clear_edges(cots)
    mean, rstd = stats[0:1], stats[1:2]
    gain_v, shift_v = gain[...], shift[...]
    far_at = half - core * half
    if len(stages.counts) > 1:
        order, placed = refs
        stages.order(me, table, order, chans)
        for ref, base in ((cot_own, core * half), (cot_far, far_at)):
            value = jnp.dot(ref[...].reshape(half * width, chans), order[...], preferred_element_type=F32)
            placed[pl.ds(base, half)] = value.reshape(half, width, stages.width)

    def one_row(i, _):
        for lat, cot, base in ((lat_own, cot_own, core * half), (lat_far, cot_far, far_at)):
            value = placed[base + i] if len(stages.counts) > 1 else cot[i].astype(F32)
            fill_shifts(cots, base + i + 1, value)
            xhat = (lat[i].astype(F32) - mean) * rstd
            pre = gain_v * xhat + shift_v
            sig = 0.5 + 0.5 * jnp.tanh(0.5 * pre)
            value = sig * (1.0 + pre * (1.0 - sig))
            slope[base + i] = value.astype(BF16)
            slope_x[base + i] = (value * xhat).astype(BF16)
        return 0

    lax.fori_loop(0, half, one_row, 0)


def conv_sum(cols, stages, stage, core, first, half, acts, blocks, total):
    width, chans = acts.shape[2:]
    cells = half * width
    nt = (((1,), (1,)), ((), ()))
    place, channel = cols.middle(core, chans)
    window = acts[1, pl.ds(first + 1, half), :, pl.ds(channel, cols.mid)].reshape(cells, cols.mid)
    lane = lax.broadcasted_iota(jnp.int32, window.shape, 1)
    window = jnp.where((core == 1) & (lane < cols.both), jnp.zeros_like(window), window)
    kernel = stages.columns(stage, blocks, place, cols.mid)
    total[...] = lax.dot_general(window, kernel, nt, preferred_element_type=F32)

    def two_taps(k, _):
        taps, place = cols.pair(core, k, chans)
        windows = [acts[t % 3, pl.ds(first + t // 3, half)].reshape(cells, chans) for t in taps]
        kernel = stages.columns(stage, blocks, place, 2 * chans)
        total[...] += lax.dot_general(
            jnp.concatenate(windows, axis=1), kernel, nt, preferred_element_type=F32
        )
        return 0

    lax.fori_loop(0, 2, two_taps, 0)


def conv_both_kernel(cols, stages, stage, dev, acts, *refs):
    blocks, (own, far, total) = refs[:-3], refs[-3:]
    core = dev[0] % 2
    rows = acts.shape[1] - 2
    conv_sum(cols, stages, stage, core, 0, rows, acts, blocks, total)
    half = own.shape[0]
    own[...] = total[pl.ds(pl.multiple_of(core * half, half), half)]
    far[...] = total[pl.ds(pl.multiple_of((1 - core) * half, half), half)].astype(BF16)


def conv_far_kernel(cols, stages, stage, dev, acts, *refs):
    blocks, (far, total) = refs[:-2], refs[-2:]
    core = dev[0] % 2
    half = (acts.shape[1] - 2) // 2
    conv_sum(cols, stages, stage, core, (1 - core) * half, half, acts, blocks, total)
    far[...] = total[...].astype(BF16)


def conv_own_kernel(cols, stages, dev, acts, got, latent, bias, *refs):
    core = dev[0] % 2
    half, width, chans = latent.shape
    scale = cols.total ** (-0.5)
    stage = len(stages.counts) - 1
    before = 3 * stage
    blocks, (block, total) = refs[before:-2], refs[-2:]
    conv_sum(cols, stages, stage, core, core * half, half, acts, blocks, total)
    conv = total[...] + got[...].astype(F32)
    if stage:
        first_own, first_got, order = refs[:before]
        conv = jnp.concatenate([first_own[...] + first_got[...].astype(F32), conv], axis=1)
        high = conv.astype(BF16)
        low = (conv - high.astype(F32)).astype(BF16)
        nt = (((1,), (1,)), ((), ()))
        conv = sum(
            lax.dot_general(value, order[...], nt, preferred_element_type=F32) for value in (low, high)
        )
    conv = scale * conv + bias[...]
    block[...] = (conv.reshape(half, width, chans) + latent[...].astype(F32)).astype(BF16)


def back_kernel(cols, stages, stage, dev, cots, slope, slope_x, *refs):
    blocks, (sums, total) = refs[:-2], refs[-2:]
    core = dev[0] % 2
    rows, width = cots.shape[1] - 2, cots.shape[2]
    cells, chans = total.shape
    lanes = stages.lanes(stage)

    def taps_from(first, place, count):
        windows, kernels = [], []
        for i in range(count):
            tap = first + i
            window = cots[2 - tap % 3, pl.ds(2 - tap // 3, rows), :, lanes]
            windows.append(window.reshape(cells, stages.widths[stage]))
            kernels.append(stages.columns(stage, blocks, pl.multiple_of(place + i * chans, LANES), chans))
        return jnp.dot(
            jnp.concatenate(windows, axis=1), jnp.concatenate(kernels), preferred_element_type=F32
        )

    if stages.widths[stage] * 4 <= 2 * chans:
        taps, place = cols.pair(core, 0, chans)
        total[...] = taps_from(taps[0], place, 4)
    else:
        total[...] = jnp.zeros_like(total)

        def two_taps(k, _):
            taps, place = cols.pair(core, k, chans)
            total[...] += taps_from(taps[0], place, 2)
            return 0

        lax.fori_loop(0, 2, two_taps, 0)

    place, channel = cols.middle(core, chans)
    window = cots[1, 1:rows + 1, :, lanes].reshape(cells, stages.widths[stage])
    kernel = stages.columns(stage, blocks, place, cols.mid)
    value = jnp.dot(window, kernel, preferred_element_type=F32)
    lane = lax.broadcasted_iota(jnp.int32, value.shape, 1)
    total[:, pl.ds(channel, cols.mid)] += jnp.where((core == 1) & (lane < cols.both), 0.0, value)

    def add_row(i, carry):
        gains, shifts = carry
        value = total[pl.ds(pl.multiple_of(i * width, width), width)]
        return gains + value * slope_x[i].astype(F32), shifts + value * slope[i].astype(F32)

    zero = jnp.zeros((width, chans), F32)
    gains, shifts = lax.fori_loop(0, rows, add_row, (zero, zero))
    scale = cols.total ** (-0.5)
    sums[0:1] = scale * jnp.sum(gains, axis=0, keepdims=True)
    sums[1:2] = scale * jnp.sum(shifts, axis=0, keepdims=True)


def finish_kernel(cols, dev, step, shard, mine, carried, ours, aside, vectors, out, new_bias, new_gain, new_shift):
    lower = dev[0] % 2 == 0
    rate = LR_KERNEL * (1.0 - (step[0] % 1000).astype(F32) / 2000.0)
    factor = 0.5 * cols.total ** (-0.5) * rate
    part = shard.shape[0]
    theirs = carried[-part:].astype(F32)
    here = 0.5 * mine[...].astype(F32) - factor * ours[...].astype(F32)
    there = 0.5 * theirs - factor * aside[...].astype(F32)
    left, right = jnp.where(lower, here, there), jnp.where(lower, there, here)
    out[:, :cols.lead] = 0.5 * shard[:, :cols.lead] + left
    out[:, cols.lead:] = 0.5 * shard[:, cols.lead:] + right[:, cols.both:]
    for i, new in enumerate((new_bias, new_gain, new_shift)):
        new[...] = 0.5 * vectors[i:i + 1]


NODE = ("z", "y")


def swap(value, axis):
    return lax.ppermute(value, axis, [(0, 1), (1, 0)])


def from_peer(level, value):
    count = lax.axis_size("replica")
    levels = count.bit_length() - 1
    moves = [[(s, (s + (1 << k)) % count) for s in range(count)] for k in range(levels)]
    if levels == 1:
        return lax.ppermute(value, "replica", moves[0])
    return lax.switch(level, [lambda v, m=m: lax.ppermute(v, "replica", m) for m in moves], value)


class Ring:
    def __init__(self, zs):
        self.count = 2 * zs
        self.reach = zs
        self.nodes = [2 * z for z in range(zs)] + [2 * z + 1 for z in reversed(range(zs))]
        ahead = list(zip(self.nodes, self.nodes[1:] + self.nodes[:1]))
        self.ahead = ahead
        self.behind = [(b, a) for a, b in ahead]

    def node(self, at, offset):
        return self.nodes[(at + offset) % self.count]

    def up(self, value):
        return lax.ppermute(value, NODE, self.ahead)

    def down(self, value):
        return lax.ppermute(value, NODE, self.behind)

    def table(self, part):
        rows = np.zeros((2, self.count, 2, 3 * self.count), np.int32)
        for replica in range(2):
            for at, node in enumerate(self.nodes):
                line = [node]
                for k in range(1, self.reach + 1):
                    line.append(self.node(at, -k))
                    if k < self.reach:
                        line.append(self.node(at, k))
                for which in (replica, 1 - replica):
                    for j in range(self.reach):
                        targets = [self.node(at, self.reach - j), self.node(at, j + 1 - self.reach)]
                        line += [(2 * target + which) * part for target in targets]
                rows[replica, node, :] = line
        return rows.reshape(-1, 3 * self.count)


def hop(value, axis, mask):
    count = lax.axis_size(axis)
    return value + lax.ppermute(value, axis, [(s, s ^ mask) for s in range(count)])


def add(*values):
    total = values[0].astype(F32)
    for value in values[1:]:
        total = total + value.astype(F32)
    return total.astype(BF16)


def tied(*values):
    return lax.optimization_barrier(values)


def per_device(latents, cotangent, kernel, conv_bias, gn_gain, gn_shift, step):
    latent, cotan, shard = latents[0], cotangent[0], kernel[0]
    half, width, chans = latent.shape
    part = shard.shape[0]
    cols = Columns(chans)
    cells = half * width
    zs, replicas = lax.axis_size("z"), lax.axis_size("replica")
    core, z, y, replica = (lax.axis_index(a) for a in ("core", "z", "y", "replica"))
    lower = core == 0
    paired = replicas == 2
    ring = Ring(zs)
    scale = cols.total ** (-0.5)
    params = jnp.concatenate([conv_bias, gn_gain, gn_shift])
    me = ((replica * zs + z) * 2 + y) * 2 + core
    core, lower, same, me = tied(core, lower, replica == core, me)
    dev = me.reshape(1)

    mine = lax.dynamic_slice_in_dim(shard, core * cols.start, cols.lead, 1).astype(BF16)
    theirs = lax.dynamic_slice_in_dim(shard, (1 - core) * cols.start, cols.lead, 1).astype(BF16)
    theirs, cotan = tied(theirs, cotan)
    got = swap(theirs, "core")
    unit = jnp.where(lower, jnp.concatenate([mine, got]), jnp.concatenate([got, mine]))
    lat_far = swap(latent, "core")
    cot_b = cotan.astype(BF16)
    cot_far = swap(cot_b, "core")

    if paired:
        table = jnp.asarray(ring.table(part))
        order = (ring.count, part, 2 * ring.count)
        up1, down1 = ring.up(unit), ring.down(unit)
        peer = swap(tied(mine, unit)[0], "replica")
    else:
        table = jnp.zeros((replicas * zs * 4, 1), jnp.int32)
        order = None

    def call(body, outs, ins, scratch, megabytes, flops):
        return pl.pallas_call(
            body,
            out_shape=outs,
            in_specs=ins,
            out_specs=jax.tree.map(lambda _: VMEM_SPEC, outs),
            scratch_shapes=scratch,
            compiler_params=pltpu.CompilerParams(vmem_limit_bytes=megabytes * 2**20),
            cost_estimate=pl.CostEstimate(flops=flops * 4, bytes_accessed=0, transcendentals=0),
        )

    image = (2 * half, width, chans)
    shifted = jax.ShapeDtypeStruct((3, 2 * half + 2, width, chans), BF16)
    flops = 2 * 2 * cells * chans * cols.lead
    stats, acts, cot_t = call(
        partial(act_kernel, order),
        (jax.ShapeDtypeStruct((2, chans), F32), shifted, jax.ShapeDtypeStruct((chans, 2 * cells), BF16)),
        [SMEM_SPEC] * 2 + [VMEM_SPEC] * 6,
        [pltpu.VMEM((chans, 2 * cells), F32)],
        8, flops // 4,
    )(dev, table, latent, lat_far, cot_b, cot_far, gn_gain, gn_shift)
    if paired:
        peer, acts = tied(peer, acts)
    counts = [2 * zs, 2, 3] + [2] * (zs - 2) if paired else [4 * zs]
    pieces = call(
        partial(grad_kernel, cols, 2 if paired else None),
        [jax.ShapeDtypeStruct((n * part, cols.lead), BF16) for n in counts],
        [SMEM_SPEC] + [VMEM_SPEC] * 3,
        [],
        4, flops // 2,
    )(dev, acts, cot_t, theirs)
    stages = Stages([2 * zs - 3, 3] if paired else [1], 2 * part if paired else chans)
    staged = paired

    def slopes_of(stats):
        extra = (jax.ShapeDtypeStruct((chans, stages.width), BF16),) if staged else ()
        return call(
            partial(slope_kernel, stages),
            (jax.ShapeDtypeStruct((3, 2 * half + 2, width, stages.width), BF16),
             jax.ShapeDtypeStruct(image, BF16), jax.ShapeDtypeStruct(image, BF16)) + extra,
            [SMEM_SPEC] * 2 + [VMEM_SPEC] * 7,
            [pltpu.VMEM((2 * half, width, stages.width), F32)] if staged else [],
            8, flops // 4,
        )(dev, table, stats, gn_gain, gn_shift, latent, lat_far, cot_b, cot_far)

    def back(stage, cots, slopes, blocks):
        return call(
            partial(back_kernel, cols, stages, stage), jax.ShapeDtypeStruct((2, chans), F32),
            [SMEM_SPEC] + [VMEM_SPEC] * (3 + len(blocks)),
            [pltpu.VMEM((2 * cells, chans), F32)], 8, flops // 4,
        )(dev, cots, *slopes, *blocks)

    def conv_first(blocks):
        wide = stages.widths[0]
        return call(
            partial(conv_both_kernel, cols, stages, 0),
            (jax.ShapeDtypeStruct((cells, wide), F32), jax.ShapeDtypeStruct((cells, wide), BF16)),
            [SMEM_SPEC] + [VMEM_SPEC] * (1 + len(blocks)),
            [pltpu.VMEM((2 * cells, wide), F32)], 6, flops // 4,
        )(dev, acts, *blocks)

    def conv_far(acts, blocks):
        wide = stages.widths[-1]
        return call(
            partial(conv_far_kernel, cols, stages, len(stages.counts) - 1),
            jax.ShapeDtypeStruct((cells, wide), BF16),
            [SMEM_SPEC] + [VMEM_SPEC] * (1 + len(blocks)),
            [pltpu.VMEM((cells, wide), F32)], 4, flops // 8,
        )(dev, acts, *blocks)

    def conv_own(got, earlier, blocks):
        return call(
            partial(conv_own_kernel, cols, stages), jax.ShapeDtypeStruct((half, width, chans), BF16),
            [SMEM_SPEC] + [VMEM_SPEC] * (4 + len(earlier) + len(blocks)),
            [pltpu.VMEM((cells, stages.widths[-1]), F32)], 8, flops // 4,
        )(dev, acts, got, latent, conv_bias, *earlier, *blocks)

    def chip_sum(sums):
        vectors = jnp.concatenate([jnp.sum(cotan, axis=(0, 1))[None], sums])
        vectors = params / (4 * zs) - LR_VECTOR * vectors
        return vectors + swap(vectors, "core")

    if paired:
        kept, *sent = pieces
        crossed = [swap(sent[0], "replica")]
        up, down, stats, *sent[:3] = tied(up1, down1, stats, *sent[:3])
        crossed += [swap(piece, "replica") for piece in sent[1:3]]
        theirs = crossed[1]

        def ring_sums(j, *received):
            parts = kept[2 * j * part:(2 * j + 2) * part], crossed[j]
            ahead, behind = (tuple(x[at:at + part] for x in parts) for at in (0, part))
            ahead = add(*ahead, *received[:1])
            behind = behind + tuple(received[1:])
            return ahead, add(*behind) if j < zs - 1 else behind

        def ring_step(ahead, behind):
            return ring.up(ahead), ring.down(behind)

        blocks = [unit, up, down]
        up, down = ring.up(up), ring.down(down)
        up, down, cots, *slopes, order = tied(up, down, *slopes_of(stats))
        blocks += [up, down]

        ahead, behind = ring_sums(0)
        up = ring.up(jnp.concatenate([up, ahead]))
        down = ring.down(jnp.concatenate([down, behind]))
        conv_first_own, conv_send = conv_first(blocks)
        cots, conv_send = tied(cots, conv_send)
        first_sums = back(0, cots, slopes, blocks)
        up, down, first_sums, crossed[1], sent[3] = tied(up, down, first_sums, crossed[1], sent[3])
        crossed.append(swap(sent[3], "replica"))
        late = [up, down]
        received = up[2 * part:], down[2 * part:]

        halves = ring.up(up[:part]), ring.down(down[part:2 * part])
        conv_first_got = swap(conv_send, "core")
        for j in range(1, zs - 2):
            received = ring_step(*ring_sums(j, *received))
        late += halves

        conv_send = conv_far(acts, late)
        crossed[2], cots, conv_send = tied(crossed[2], cots, conv_send)
        conv_got = swap(conv_send, "core")
        received = ring_step(*ring_sums(zs - 2, *received))
        sums = back(1, cots, slopes, late)
        crossed[3], conv_got, *received = tied(crossed[3], conv_got, *received)
        ahead, behind = ring_sums(zs - 1, *received)
        last = ring.up(ahead)
        block = conv_own(conv_got, [conv_first_own, conv_first_got, order], late)
        vectors = hop(hop(chip_sum(first_sums + sums), "replica", 1), "z", 1)
        last, block, vectors = tied(last, block, vectors)
        total = add(*behind, last)
        vectors = hop(vectors, "y", 1)
        reach = 2
        while reach < zs:
            vectors = hop(vectors, "z", reach)
            reach *= 2
        across, vectors = tied(swap(total, "replica"), vectors)
        ours, others = jnp.where(same, total, across), jnp.where(same, across, total)
        aside = swap(others, "core")
        vector = jax.ShapeDtypeStruct((1, chans), F32)
        new_kernel, *new_v = call(
            partial(finish_kernel, cols),
            (jax.ShapeDtypeStruct(shard.shape, F32), vector, vector, vector),
            [SMEM_SPEC] * 2 + [VMEM_SPEC] * 6, [], 8, flops // 16,
        )(dev, step, shard, peer, theirs, ours, aside, vectors)
    else:
        late = [lax.all_gather(unit, NODE, axis=0, tiled=True)]
        cots, slope, slope_x = slopes_of(stats)
        sums = back(0, cots, [slope, slope_x], late)
        vectors = chip_sum(sums)
        block = conv_own(swap(conv_far(acts, late), "core"), [], late)
        terms = pieces[0].reshape(2 * zs, 2, part, cols.lead)
        summed = lax.psum_scatter(terms, NODE, scatter_dimension=0, tiled=False)
        ours = lax.dynamic_index_in_dim(summed, core, 0, keepdims=False)
        got = swap(lax.dynamic_index_in_dim(summed, 1 - core, 0, keepdims=False), "core")
        left, right = jnp.where(lower, ours, got), jnp.where(lower, got, ours)
        kernel_grad = jnp.concatenate([left, right[:, cols.both:]], axis=1).astype(F32)
        level = step[0] % (replicas.bit_length() - 1)
        rate = LR_KERNEL * (1.0 - (step[0] % 1000).astype(F32) / 2000.0)
        stepped = shard - (scale * rate) * kernel_grad
        new_kernel = 0.5 * (stepped + from_peer(level, stepped.astype(BF16)).astype(F32))
        stepped_v = lax.psum(vectors, NODE)
        new_v = jnp.split(0.5 * (stepped_v + from_peer(level, stepped_v)), 3)

    return (
        block[None],
        new_kernel[None],
        new_v[0],
        new_v[1],
        new_v[2],
    )


def solution(mesh):
    replicas, shards = mesh.shape["replica"], mesh.shape["shard"]
    split = Mesh(mesh.devices.reshape(replicas, shards // 4, 2, 2), ("replica", "z", "y", "core"))
    shard = ("z", "y", "core")
    return jax.shard_map(
        per_device,
        mesh=split,
        in_specs=(
            P("replica", shard, None, None),
            P("replica", shard, None, None),
            P("replica", shard, None),
            P("replica", None),
            P("replica", None),
            P("replica", None),
            P(),
        ),
        out_specs=(
            P("replica", shard, None, None),
            P("replica", shard, None),
            P("replica", None),
            P("replica", None),
            P("replica", None),
        ),
        check_vma=False,
    )
```

```python
from functools import partial

import jax
import jax.numpy as jnp
import numpy as np
from jax import lax
from jax.experimental import pallas as pl
from jax.experimental.pallas import tpu as pltpu
from jax.sharding import Mesh, PartitionSpec as P

GROUPS = 32
EPS = 1e-05
LR_KERNEL = 0.1
LR_VECTOR = 0.01
LANES = 128
BF16 = jnp.bfloat16
F32 = jnp.float32

SMEM_SPEC = pl.BlockSpec(memory_space=pltpu.SMEM)
VMEM_SPEC = pl.BlockSpec(memory_space=pltpu.VMEM)


class Columns:
    def __init__(self, chans):
        tiles = 9 * chans // LANES
        self.total = 9 * chans
        self.lead = (tiles + 1) // 2 * LANES
        self.start = self.total - self.lead
        self.both = 2 * self.lead - self.total
        self.mid = self.lead - 4 * chans
        self.mid_start = chans - self.mid

    def pair(self, core, k, chans):
        first = jnp.where(core == 0, 2 * k, 5 + 2 * k)
        place = jnp.where(core == 0, 2 * k * chans, self.mid + 2 * k * chans)
        return (first, first + 1), pl.multiple_of(place, LANES)

    def middle(self, core, chans):
        place = jnp.where(core == 0, 4 * chans, 0)
        channel = jnp.where(core == 0, 0, self.mid_start)
        return pl.multiple_of(place, LANES), pl.multiple_of(channel, LANES)


def fill_shifts(shifts, row, values):
    width = values.shape[0]
    at = lax.broadcasted_iota(jnp.int32, values.shape, 0)
    left = jnp.where(at == 0, 0.0, pltpu.roll(values, 1, 0))
    right = jnp.where(at == width - 1, 0.0, pltpu.roll(values, width - 1, 0))
    shifts[0, row] = left.astype(BF16)
    shifts[1, row] = values.astype(BF16)
    shifts[2, row] = right.astype(BF16)


def clear_edges(shifts):
    zero = jnp.zeros(shifts.shape[2:], shifts.dtype)
    for b in range(3):
        shifts[b, 0] = zero
        shifts[b, shifts.shape[1] - 1] = zero


def act_kernel(order, dev, table, lat_own, lat_far, cot_own, cot_far, gain, shift,
               stats, acts, cot_t, cot_f):
    me = dev[0]
    core = me % 2
    half, width, chans = lat_own.shape
    cells = 2 * half * width
    group_width = chans // GROUPS
    own_at = core * half
    far_at = half - own_at
    clear_edges(acts)

    def add_row(i, sums):
        total, square = sums
        a = lat_own[i].astype(F32)
        b = lat_far[i].astype(F32)
        return total + (a + b), square + (a * a + b * b)

    zero = jnp.zeros((width, chans), F32)
    total, square = lax.fori_loop(0, half, add_row, (zero, zero))
    sums = jnp.concatenate(
        [jnp.sum(total, axis=0, keepdims=True), jnp.sum(square, axis=0, keepdims=True),
         jnp.zeros((6, chans), F32)], axis=0
    )
    first = lax.broadcasted_iota(jnp.int32, (chans, LANES), 0)
    start = lax.broadcasted_iota(jnp.int32, (chans, LANES), 1) * group_width
    member = jnp.where((first >= start) & (first < start + group_width), 1.0, 0.0)
    exact = partial(lax.dot_general, precision=lax.Precision.HIGHEST, preferred_element_type=F32)
    sums = exact(sums, member, (((1,), (0,)), ((), ()))) / (cells * group_width)
    sums = exact(sums, member, (((1,), (1,)), ((), ())))
    mean = sums[0:1]
    rstd = lax.rsqrt(sums[1:2] - mean * mean + EPS)
    stats[0:1] = mean
    stats[1:2] = rstd
    gain_v, shift_v = gain[...], shift[...]

    def act_rows(i, _):
        for ref, base in ((lat_own, own_at), (lat_far, far_at)):
            pre = gain_v * ((ref[i].astype(F32) - mean) * rstd) + shift_v
            fill_shifts(acts, base + i + 1, pre * (0.5 + 0.5 * jnp.tanh(0.5 * pre)))
        return 0

    lax.fori_loop(0, half, act_rows, 0)

    chunk = LANES // width
    for ref, base in ((cot_own, own_at), (cot_far, far_at)):
        for i in range(half // chunk):
            piece = ref[i * chunk:(i + 1) * chunk].reshape(LANES, chans).astype(F32)
            place = pl.multiple_of(base * width + i * LANES, LANES)
            if order is None:
                cot_t[:, pl.ds(place, LANES)] = piece.T.astype(BF16)
            else:
                cot_f[:, pl.ds(place, LANES)] = piece.T
    if order is not None:
        first_at, part, count = order
        for q in range(count // 2):
            pair = [
                cot_f[pl.ds(pl.multiple_of(table[me, first_at + 2 * q + i], 8), part)]
                for i in range(2)
            ]
            cot_t[2 * q * part:(2 * q + 2) * part] = jnp.concatenate(pair).astype(BF16)


def grad_kernel(cols, carrier, dev, acts, cot_t, theirs, *pieces):
    core = dev[0] % 2
    rows, width, chans = acts.shape[1] - 2, acts.shape[2], acts.shape[3]
    cells = rows * width

    def emit(window, place, wide):
        value = jnp.dot(cot_t[...], window, preferred_element_type=F32)
        at = 0
        for i, piece in enumerate(pieces):
            count = piece.shape[0] - (theirs.shape[0] if i == carrier else 0)
            piece[:count, pl.ds(place, wide)] = value[at:at + count].astype(BF16)
            at += count

    def two_taps(k, _):
        taps, place = cols.pair(core, k, chans)
        windows = [acts[t % 3, pl.ds(t // 3, rows)].reshape(cells, chans) for t in taps]
        emit(jnp.concatenate(windows, axis=1), place, 2 * chans)
        return 0

    lax.fori_loop(0, 2, two_taps, 0)
    place, channel = cols.middle(core, chans)
    emit(acts[1, 1:rows + 1, :, pl.ds(channel, cols.mid)].reshape(cells, cols.mid), place, cols.mid)
    if carrier is not None:
        pieces[carrier][-theirs.shape[0]:] = theirs[...]


class Stages:
    def __init__(self, counts, rows):
        self.rows = rows
        self.counts = counts
        self.widths = [-(-n * rows // LANES) * LANES for n in counts]
        self.starts = [sum(self.widths[:i]) for i in range(len(counts))]
        self.width = sum(self.widths)

    def lanes(self, stage):
        return slice(self.starts[stage], self.starts[stage] + self.widths[stage])

    def columns(self, stage, blocks, place, wide):
        parts = [ref[:, pl.ds(place, wide)] for ref in blocks]
        if len(parts) == self.counts[stage] + 1:
            parts[-2:] = [jnp.concatenate(parts[-2:])]
        spare = self.widths[stage] - self.counts[stage] * self.rows
        if spare:
            parts.append(jnp.zeros((spare, wide), BF16))
        return jnp.concatenate(parts) if len(parts) > 1 else parts[0]

    def order(self, me, table, order, chans):
        lane = lax.broadcasted_iota(jnp.int32, (1, self.width), 1)
        source = jnp.full((1, self.width), -1, jnp.int32)
        at = 0
        for start, count in zip(self.starts, self.counts):
            for i in range(count):
                first = start + i * self.rows
                inside = (lane >= first) & (lane < first + self.rows)
                source = jnp.where(inside, table[me, at] * self.rows + lane - first, source)
                at += 1
        channel = lax.broadcasted_iota(jnp.int32, (chans, self.width), 0)
        order[...] = jnp.where(channel == source, 1.0, 0.0).astype(BF16)


def slope_kernel(stages, dev, table, stats, gain, shift, lat_own, lat_far, cot_own, cot_far,
                 cots, slope, slope_x, *refs):
    me = dev[0]
    core = me % 2
    half, width, chans = lat_own.shape
    clear_edges(cots)
    mean, rstd = stats[0:1], stats[1:2]
    gain_v, shift_v = gain[...], shift[...]
    far_at = half - core * half
    if len(stages.counts) > 1:
        order, placed = refs
        stages.order(me, table, order, chans)
        for ref, base in ((cot_own, core * half), (cot_far, far_at)):
            value = jnp.dot(ref[...].reshape(half * width, chans), order[...], preferred_element_type=F32)
            placed[pl.ds(base, half)] = value.reshape(half, width, stages.width)

    def one_row(i, _):
        for lat, cot, base in ((lat_own, cot_own, core * half), (lat_far, cot_far, far_at)):
            value = placed[base + i] if len(stages.counts) > 1 else cot[i].astype(F32)
            fill_shifts(cots, base + i + 1, value)
            xhat = (lat[i].astype(F32) - mean) * rstd
            pre = gain_v * xhat + shift_v
            sig = 0.5 + 0.5 * jnp.tanh(0.5 * pre)
            value = sig * (1.0 + pre * (1.0 - sig))
            slope[base + i] = value.astype(BF16)
            slope_x[base + i] = (value * xhat).astype(BF16)
        return 0

    lax.fori_loop(0, half, one_row, 0)


def conv_sum(cols, stages, stage, core, first, half, acts, blocks, total):
    width, chans = acts.shape[2:]
    cells = half * width
    nt = (((1,), (1,)), ((), ()))
    place, channel = cols.middle(core, chans)
    window = acts[1, pl.ds(first + 1, half), :, pl.ds(channel, cols.mid)].reshape(cells, cols.mid)
    lane = lax.broadcasted_iota(jnp.int32, window.shape, 1)
    window = jnp.where((core == 1) & (lane < cols.both), jnp.zeros_like(window), window)
    kernel = stages.columns(stage, blocks, place, cols.mid)
    total[...] = lax.dot_general(window, kernel, nt, preferred_element_type=F32)

    def two_taps(k, _):
        taps, place = cols.pair(core, k, chans)
        windows = [acts[t % 3, pl.ds(first + t // 3, half)].reshape(cells, chans) for t in taps]
        kernel = stages.columns(stage, blocks, place, 2 * chans)
        total[...] += lax.dot_general(
            jnp.concatenate(windows, axis=1), kernel, nt, preferred_element_type=F32
        )
        return 0

    lax.fori_loop(0, 2, two_taps, 0)


def conv_both_kernel(cols, stages, stage, dev, acts, *refs):
    blocks, (own, far, total) = refs[:-3], refs[-3:]
    core = dev[0] % 2
    rows = acts.shape[1] - 2
    conv_sum(cols, stages, stage, core, 0, rows, acts, blocks, total)
    half = own.shape[0]
    own[...] = total[pl.ds(pl.multiple_of(core * half, half), half)]
    far[...] = total[pl.ds(pl.multiple_of((1 - core) * half, half), half)].astype(BF16)


def conv_far_kernel(cols, stages, stage, dev, acts, *refs):
    blocks, (far, total) = refs[:-2], refs[-2:]
    core = dev[0] % 2
    half = (acts.shape[1] - 2) // 2
    conv_sum(cols, stages, stage, core, (1 - core) * half, half, acts, blocks, total)
    far[...] = total[...].astype(BF16)


def conv_own_kernel(cols, stages, dev, acts, got, latent, bias, *refs):
    core = dev[0] % 2
    half, width, chans = latent.shape
    scale = cols.total ** (-0.5)
    stage = len(stages.counts) - 1
    before = 3 * stage
    blocks, (block, total) = refs[before:-2], refs[-2:]
    conv_sum(cols, stages, stage, core, core * half, half, acts, blocks, total)
    conv = total[...] + got[...].astype(F32)
    if stage:
        first_own, first_got, order = refs[:before]
        conv = jnp.concatenate([first_own[...] + first_got[...].astype(F32), conv], axis=1)
        high = conv.astype(BF16)
        low = (conv - high.astype(F32)).astype(BF16)
        nt = (((1,), (1,)), ((), ()))
        conv = sum(
            lax.dot_general(value, order[...], nt, preferred_element_type=F32) for value in (low, high)
        )
    conv = scale * conv + bias[...]
    block[...] = (conv.reshape(half, width, chans) + latent[...].astype(F32)).astype(BF16)


def back_kernel(cols, stages, stage, dev, cots, slope, slope_x, *refs):
    blocks, (sums, total) = refs[:-2], refs[-2:]
    core = dev[0] % 2
    rows, width = cots.shape[1] - 2, cots.shape[2]
    cells, chans = total.shape
    lanes = stages.lanes(stage)

    def taps_from(first, place, count):
        windows, kernels = [], []
        for i in range(count):
            tap = first + i
            window = cots[2 - tap % 3, pl.ds(2 - tap // 3, rows), :, lanes]
            windows.append(window.reshape(cells, stages.widths[stage]))
            kernels.append(stages.columns(stage, blocks, pl.multiple_of(place + i * chans, LANES), chans))
        return jnp.dot(
            jnp.concatenate(windows, axis=1), jnp.concatenate(kernels), preferred_element_type=F32
        )

    if stages.widths[stage] * 4 <= 2 * chans:
        taps, place = cols.pair(core, 0, chans)
        total[...] = taps_from(taps[0], place, 4)
    else:
        total[...] = jnp.zeros_like(total)

        def two_taps(k, _):
            taps, place = cols.pair(core, k, chans)
            total[...] += taps_from(taps[0], place, 2)
            return 0

        lax.fori_loop(0, 2, two_taps, 0)

    place, channel = cols.middle(core, chans)
    window = cots[1, 1:rows + 1, :, lanes].reshape(cells, stages.widths[stage])
    kernel = stages.columns(stage, blocks, place, cols.mid)
    value = jnp.dot(window, kernel, preferred_element_type=F32)
    lane = lax.broadcasted_iota(jnp.int32, value.shape, 1)
    total[:, pl.ds(channel, cols.mid)] += jnp.where((core == 1) & (lane < cols.both), 0.0, value)

    def add_row(i, carry):
        gains, shifts = carry
        value = total[pl.ds(pl.multiple_of(i * width, width), width)]
        return gains + value * slope_x[i].astype(F32), shifts + value * slope[i].astype(F32)

    zero = jnp.zeros((width, chans), F32)
    gains, shifts = lax.fori_loop(0, rows, add_row, (zero, zero))
    scale = cols.total ** (-0.5)
    sums[0:1] = scale * jnp.sum(gains, axis=0, keepdims=True)
    sums[1:2] = scale * jnp.sum(shifts, axis=0, keepdims=True)


def finish_kernel(cols, dev, step, shard, mine, carried, ours, aside, out):
    lower = dev[0] % 2 == 0
    rate = LR_KERNEL * (1.0 - (step[0] % 1000).astype(F32) / 2000.0)
    factor = 0.5 * cols.total ** (-0.5) * rate
    here = 0.5 * mine[...].astype(F32) - factor * ours[...].astype(F32)
    theirs = carried[-shard.shape[0]:].astype(F32)
    there = 0.5 * theirs - factor * aside[...].astype(F32)
    left, right = jnp.where(lower, here, there), jnp.where(lower, there, here)
    out[:, :cols.lead] = 0.5 * shard[:, :cols.lead] + left
    out[:, cols.lead:] = 0.5 * shard[:, cols.lead:] + right[:, cols.both:]


NODE = ("z", "y")


def swap(value, axis):
    return lax.ppermute(value, axis, [(0, 1), (1, 0)])


def from_peer(level, value):
    count = lax.axis_size("replica")
    levels = count.bit_length() - 1
    moves = [[(s, (s + (1 << k)) % count) for s in range(count)] for k in range(levels)]
    if levels == 1:
        return lax.ppermute(value, "replica", moves[0])
    return lax.switch(level, [lambda v, m=m: lax.ppermute(v, "replica", m) for m in moves], value)


class Ring:
    def __init__(self, zs):
        self.count = 2 * zs
        self.reach = zs
        self.nodes = [2 * z for z in range(zs)] + [2 * z + 1 for z in reversed(range(zs))]
        ahead = list(zip(self.nodes, self.nodes[1:] + self.nodes[:1]))
        self.ahead = ahead
        self.behind = [(b, a) for a, b in ahead]

    def node(self, at, offset):
        return self.nodes[(at + offset) % self.count]

    def up(self, value):
        return lax.ppermute(value, NODE, self.ahead)

    def down(self, value):
        return lax.ppermute(value, NODE, self.behind)

    def table(self, part):
        rows = np.zeros((2, self.count, 2, 3 * self.count), np.int32)
        for replica in range(2):
            for at, node in enumerate(self.nodes):
                line = [node]
                for k in range(1, self.reach + 1):
                    line.append(self.node(at, -k))
                    if k < self.reach:
                        line.append(self.node(at, k))
                for which in (replica, 1 - replica):
                    for j in range(self.reach):
                        targets = [self.node(at, self.reach - j), self.node(at, j + 1 - self.reach)]
                        line += [(2 * target + which) * part for target in targets]
                rows[replica, node, :] = line
        return rows.reshape(-1, 3 * self.count)


def hop(value, axis, mask):
    count = lax.axis_size(axis)
    return value + lax.ppermute(value, axis, [(s, s ^ mask) for s in range(count)])


def add(*values):
    total = values[0].astype(F32)
    for value in values[1:]:
        total = total + value.astype(F32)
    return total.astype(BF16)


def tied(*values):
    return lax.optimization_barrier(values)


def per_device(latents, cotangent, kernel, conv_bias, gn_gain, gn_shift, step):
    latent, cotan, shard = latents[0], cotangent[0], kernel[0]
    half, width, chans = latent.shape
    part = shard.shape[0]
    cols = Columns(chans)
    cells = half * width
    zs, replicas = lax.axis_size("z"), lax.axis_size("replica")
    core, z, y, replica = (lax.axis_index(a) for a in ("core", "z", "y", "replica"))
    lower = core == 0
    paired = replicas == 2
    ring = Ring(zs)
    scale = cols.total ** (-0.5)
    params = jnp.concatenate([conv_bias, gn_gain, gn_shift])
    me = ((replica * zs + z) * 2 + y) * 2 + core
    core, lower, same, me = tied(core, lower, replica == core, me)
    dev = me.reshape(1)

    mine = lax.dynamic_slice_in_dim(shard, core * cols.start, cols.lead, 1).astype(BF16)
    theirs = lax.dynamic_slice_in_dim(shard, (1 - core) * cols.start, cols.lead, 1).astype(BF16)
    got = swap(theirs, "core")
    unit = jnp.where(lower, jnp.concatenate([mine, got]), jnp.concatenate([got, mine]))
    lat_far = swap(latent, "core")
    cot_b = cotan.astype(BF16)
    cot_far = swap(cot_b, "core")

    if paired:
        table = jnp.asarray(ring.table(part))
        order = (ring.count, part, 2 * ring.count)
        up1, down1 = ring.up(unit), ring.down(unit)
        peer = swap(mine, "replica")
    else:
        table = jnp.zeros((replicas * zs * 4, 1), jnp.int32)
        order = None

    def call(body, outs, ins, scratch, megabytes, flops):
        return pl.pallas_call(
            body,
            out_shape=outs,
            in_specs=ins,
            out_specs=jax.tree.map(lambda _: VMEM_SPEC, outs),
            scratch_shapes=scratch,
            compiler_params=pltpu.CompilerParams(vmem_limit_bytes=megabytes * 2**20),
            cost_estimate=pl.CostEstimate(flops=flops, bytes_accessed=0, transcendentals=0),
        )

    image = (2 * half, width, chans)
    shifted = jax.ShapeDtypeStruct((3, 2 * half + 2, width, chans), BF16)
    flops = 2 * 2 * cells * chans * cols.lead
    stats, acts, cot_t = call(
        partial(act_kernel, order),
        (jax.ShapeDtypeStruct((2, chans), F32), shifted, jax.ShapeDtypeStruct((chans, 2 * cells), BF16)),
        [SMEM_SPEC] * 2 + [VMEM_SPEC] * 6,
        [pltpu.VMEM((chans, 2 * cells), F32)],
        8, flops // 4,
    )(dev, table, latent, lat_far, cot_b, cot_far, gn_gain, gn_shift)
    counts = [2 * zs, 2, 3] + [2] * (zs - 2) if paired else [4 * zs]
    pieces = call(
        partial(grad_kernel, cols, 2 if paired else None),
        [jax.ShapeDtypeStruct((n * part, cols.lead), BF16) for n in counts],
        [SMEM_SPEC] + [VMEM_SPEC] * 3,
        [],
        4, flops // 2,
    )(dev, acts, cot_t, theirs)
    stages = Stages([2 * zs - 3, 3] if paired else [1], 2 * part if paired else chans)
    staged = paired

    def slopes_of(stats):
        extra = (jax.ShapeDtypeStruct((chans, stages.width), BF16),) if staged else ()
        return call(
            partial(slope_kernel, stages),
            (jax.ShapeDtypeStruct((3, 2 * half + 2, width, stages.width), BF16),
             jax.ShapeDtypeStruct(image, BF16), jax.ShapeDtypeStruct(image, BF16)) + extra,
            [SMEM_SPEC] * 2 + [VMEM_SPEC] * 7,
            [pltpu.VMEM((2 * half, width, stages.width), F32)] if staged else [],
            8, flops // 4,
        )(dev, table, stats, gn_gain, gn_shift, latent, lat_far, cot_b, cot_far)

    def back(stage, cots, slopes, blocks):
        return call(
            partial(back_kernel, cols, stages, stage), jax.ShapeDtypeStruct((2, chans), F32),
            [SMEM_SPEC] + [VMEM_SPEC] * (3 + len(blocks)),
            [pltpu.VMEM((2 * cells, chans), F32)], 8, flops // 4,
        )(dev, cots, *slopes, *blocks)

    def conv_first(blocks):
        wide = stages.widths[0]
        return call(
            partial(conv_both_kernel, cols, stages, 0),
            (jax.ShapeDtypeStruct((cells, wide), F32), jax.ShapeDtypeStruct((cells, wide), BF16)),
            [SMEM_SPEC] + [VMEM_SPEC] * (1 + len(blocks)),
            [pltpu.VMEM((2 * cells, wide), F32)], 6, flops // 4,
        )(dev, acts, *blocks)

    def conv_far(acts, blocks):
        wide = stages.widths[-1]
        return call(
            partial(conv_far_kernel, cols, stages, len(stages.counts) - 1),
            jax.ShapeDtypeStruct((cells, wide), BF16),
            [SMEM_SPEC] + [VMEM_SPEC] * (1 + len(blocks)),
            [pltpu.VMEM((cells, wide), F32)], 4, flops // 8,
        )(dev, acts, *blocks)

    def conv_own(got, earlier, blocks):
        return call(
            partial(conv_own_kernel, cols, stages), jax.ShapeDtypeStruct((half, width, chans), BF16),
            [SMEM_SPEC] + [VMEM_SPEC] * (4 + len(earlier) + len(blocks)),
            [pltpu.VMEM((cells, stages.widths[-1]), F32)], 8, flops // 4,
        )(dev, acts, got, latent, conv_bias, *earlier, *blocks)

    def chip_sum(sums):
        vectors = jnp.concatenate([jnp.sum(cotan, axis=(0, 1))[None], sums])
        vectors = params / (4 * zs) - LR_VECTOR * vectors
        return vectors + swap(vectors, "core")

    if paired:
        kept, *sent = pieces
        up, down, sent[0], mine = tied(up1, down1, sent[0], peer)
        blocks = [unit, up, down]
        crossed = [swap(piece, "replica") for piece in sent]
        up, down = ring.up(up), ring.down(down)
        up, down, cots, *slopes, order = tied(up, down, *slopes_of(stats))
        blocks += [up, down]

        def ring_step(j, *received):
            parts = kept[2 * j * part:(2 * j + 2) * part], crossed[j]
            ahead, behind = (tuple(x[at:at + part] for x in parts) for at in (0, part))
            up_sum = ring.up(add(*ahead, *received[:1]))
            if j < zs - 1:
                return up_sum, ring.down(add(*behind, *received[1:]))
            return up_sum, behind + tuple(received[1:])

        up, down = ring.up(up), ring.down(down)
        conv_first_own, conv_send = conv_first(blocks)
        crossed[0], conv_send = tied(crossed[0], conv_send)
        received = ring_step(0)
        cots, conv_send = tied(cots, conv_send)
        first_sums = back(0, cots, slopes, blocks)
        up, down, first_sums, crossed[1] = tied(up, down, first_sums, crossed[1])
        late = [up, down]

        halves = ring.up(up[:part]), ring.down(down[part:])
        conv_send, *received = tied(conv_send, *received)
        conv_first_got = swap(conv_send, "core")
        for j in range(1, zs - 2):
            received = ring_step(j, *received)
        late += halves

        sums = back(1, cots, slopes, late)
        crossed[-2], sums, *received = tied(crossed[-2], sums, *received)
        acts_last, *_ = tied(acts, sums, *received)
        received = ring_step(zs - 2, *received)
        conv_got = swap(conv_far(acts_last, late), "core")
        vectors = hop(chip_sum(first_sums + sums), "replica", 1)
        crossed[-1], conv_got, vectors, *received = tied(crossed[-1], conv_got, vectors, *received)
        last, behind = ring_step(zs - 1, *received)
        block = conv_own(conv_got, [conv_first_own, conv_first_got, order], late)
        vectors = hop(vectors, "z", 1)
        last, block, vectors = tied(last, block, vectors)
        total = add(*behind, last)
        across = swap(total, "replica")
        ours, others = jnp.where(same, total, across), jnp.where(same, across, total)
        aside = swap(others, "core")
        new_kernel = call(
            partial(finish_kernel, cols), jax.ShapeDtypeStruct(shard.shape, F32),
            [SMEM_SPEC] * 2 + [VMEM_SPEC] * 5, [], 8, flops // 16,
        )(dev, step, shard, mine, crossed[1], ours, aside)
        vectors = hop(vectors, "y", 1)
        reach = 2
        while reach < zs:
            vectors = hop(vectors, "z", reach)
            reach *= 2
        new_v = 0.5 * vectors
    else:
        late = [lax.all_gather(unit, NODE, axis=0, tiled=True)]
        cots, slope, slope_x = slopes_of(stats)
        sums = back(0, cots, [slope, slope_x], late)
        vectors = chip_sum(sums)
        block = conv_own(swap(conv_far(acts, late), "core"), [], late)
        terms = pieces[0].reshape(2 * zs, 2, part, cols.lead)
        summed = lax.psum_scatter(terms, NODE, scatter_dimension=0, tiled=False)
        ours = lax.dynamic_index_in_dim(summed, core, 0, keepdims=False)
        got = swap(lax.dynamic_index_in_dim(summed, 1 - core, 0, keepdims=False), "core")
        left, right = jnp.where(lower, ours, got), jnp.where(lower, got, ours)
        kernel_grad = jnp.concatenate([left, right[:, cols.both:]], axis=1).astype(F32)
        level = step[0] % (replicas.bit_length() - 1)
        rate = LR_KERNEL * (1.0 - (step[0] % 1000).astype(F32) / 2000.0)
        stepped = shard - (scale * rate) * kernel_grad
        new_kernel = 0.5 * (stepped + from_peer(level, stepped.astype(BF16)).astype(F32))
        stepped_v = lax.psum(vectors, NODE)
        new_v = 0.5 * (stepped_v + from_peer(level, stepped_v))

    return (
        block[None],
        new_kernel[None],
        new_v[0][None],
        new_v[1][None],
        new_v[2][None],
    )


def solution(mesh):
    replicas, shards = mesh.shape["replica"], mesh.shape["shard"]
    split = Mesh(mesh.devices.reshape(replicas, shards // 4, 2, 2), ("replica", "z", "y", "core"))
    shard = ("z", "y", "core")
    return jax.shard_map(
        per_device,
        mesh=split,
        in_specs=(
            P("replica", shard, None, None),
            P("replica", shard, None, None),
            P("replica", shard, None),
            P("replica", None),
            P("replica", None),
            P("replica", None),
            P(),
        ),
        out_specs=(
            P("replica", shard, None, None),
            P("replica", shard, None),
            P("replica", None),
            P("replica", None),
            P("replica", None),
        ),
        check_vma=False,
    )
```

```python
from functools import partial

import jax
import jax.numpy as jnp
import numpy as np
from jax import lax
from jax.experimental import pallas as pl
from jax.experimental.pallas import tpu as pltpu
from jax.sharding import Mesh, PartitionSpec as P

GROUPS = 32
EPS = 1e-05
LR_KERNEL = 0.1
LR_VECTOR = 0.01
LANES = 128
BF16 = jnp.bfloat16
F32 = jnp.float32

SMEM_SPEC = pl.BlockSpec(memory_space=pltpu.SMEM)
VMEM_SPEC = pl.BlockSpec(memory_space=pltpu.VMEM)


class Columns:
    def __init__(self, chans):
        tiles = 9 * chans // LANES
        self.total = 9 * chans
        self.lead = (tiles + 1) // 2 * LANES
        self.start = self.total - self.lead
        self.both = 2 * self.lead - self.total
        self.mid = self.lead - 4 * chans
        self.mid_start = chans - self.mid

    def pair(self, core, k, chans):
        first = jnp.where(core == 0, 2 * k, 5 + 2 * k)
        place = jnp.where(core == 0, 2 * k * chans, self.mid + 2 * k * chans)
        return (first, first + 1), pl.multiple_of(place, LANES)

    def middle(self, core, chans):
        place = jnp.where(core == 0, 4 * chans, 0)
        channel = jnp.where(core == 0, 0, self.mid_start)
        return pl.multiple_of(place, LANES), pl.multiple_of(channel, LANES)


def fill_shifts(shifts, row, values):
    width = values.shape[0]
    at = lax.broadcasted_iota(jnp.int32, values.shape, 0)
    left = jnp.where(at == 0, 0.0, pltpu.roll(values, 1, 0))
    right = jnp.where(at == width - 1, 0.0, pltpu.roll(values, width - 1, 0))
    shifts[0, row] = left.astype(BF16)
    shifts[1, row] = values.astype(BF16)
    shifts[2, row] = right.astype(BF16)


def clear_edges(shifts):
    zero = jnp.zeros(shifts.shape[2:], shifts.dtype)
    for b in range(3):
        shifts[b, 0] = zero
        shifts[b, shifts.shape[1] - 1] = zero


def act_kernel(order, dev, table, lat_own, lat_far, cot_own, cot_far, gain, shift,
               stats, acts, cot_t, cot_f):
    me = dev[0]
    core = me % 2
    half, width, chans = lat_own.shape
    cells = 2 * half * width
    group_width = chans // GROUPS
    own_at = core * half
    far_at = half - own_at
    clear_edges(acts)

    def add_row(i, sums):
        total, square = sums
        a = lat_own[i].astype(F32)
        b = lat_far[i].astype(F32)
        return total + (a + b), square + (a * a + b * b)

    zero = jnp.zeros((width, chans), F32)
    total, square = lax.fori_loop(0, half, add_row, (zero, zero))
    sums = jnp.concatenate(
        [jnp.sum(total, axis=0, keepdims=True), jnp.sum(square, axis=0, keepdims=True),
         jnp.zeros((6, chans), F32)], axis=0
    )
    first = lax.broadcasted_iota(jnp.int32, (chans, LANES), 0)
    start = lax.broadcasted_iota(jnp.int32, (chans, LANES), 1) * group_width
    member = jnp.where((first >= start) & (first < start + group_width), 1.0, 0.0)
    exact = partial(lax.dot_general, precision=lax.Precision.HIGHEST, preferred_element_type=F32)
    sums = exact(sums, member, (((1,), (0,)), ((), ()))) / (cells * group_width)
    sums = exact(sums, member, (((1,), (1,)), ((), ())))
    mean = sums[0:1]
    rstd = lax.rsqrt(sums[1:2] - mean * mean + EPS)
    stats[0:1] = mean
    stats[1:2] = rstd
    gain_v, shift_v = gain[...], shift[...]

    def act_rows(i, _):
        for ref, base in ((lat_own, own_at), (lat_far, far_at)):
            pre = gain_v * ((ref[i].astype(F32) - mean) * rstd) + shift_v
            fill_shifts(acts, base + i + 1, pre * (0.5 + 0.5 * jnp.tanh(0.5 * pre)))
        return 0

    lax.fori_loop(0, half, act_rows, 0)

    chunk = LANES // width
    for ref, base in ((cot_own, own_at), (cot_far, far_at)):
        for i in range(half // chunk):
            piece = ref[i * chunk:(i + 1) * chunk].reshape(LANES, chans).astype(F32)
            place = pl.multiple_of(base * width + i * LANES, LANES)
            if order is None:
                cot_t[:, pl.ds(place, LANES)] = piece.T.astype(BF16)
            else:
                cot_f[:, pl.ds(place, LANES)] = piece.T
    if order is not None:
        first_at, part, count = order
        for q in range(count // 2):
            pair = [
                cot_f[pl.ds(pl.multiple_of(table[me, first_at + 2 * q + i], 8), part)]
                for i in range(2)
            ]
            cot_t[2 * q * part:(2 * q + 2) * part] = jnp.concatenate(pair).astype(BF16)


def grad_kernel(cols, dev, acts, cot_t, *pieces):
    core = dev[0] % 2
    rows, width, chans = acts.shape[1] - 2, acts.shape[2], acts.shape[3]
    cells = rows * width

    def emit(window, place, wide):
        value = jnp.dot(cot_t[...], window, preferred_element_type=F32)
        at = 0
        for piece in pieces:
            piece[:, pl.ds(place, wide)] = value[at:at + piece.shape[0]].astype(BF16)
            at += piece.shape[0]

    def two_taps(k, _):
        taps, place = cols.pair(core, k, chans)
        windows = [acts[t % 3, pl.ds(t // 3, rows)].reshape(cells, chans) for t in taps]
        emit(jnp.concatenate(windows, axis=1), place, 2 * chans)
        return 0

    lax.fori_loop(0, 2, two_taps, 0)
    place, channel = cols.middle(core, chans)
    emit(acts[1, 1:rows + 1, :, pl.ds(channel, cols.mid)].reshape(cells, cols.mid), place, cols.mid)


class Stages:
    def __init__(self, counts, rows):
        self.rows = rows
        self.counts = counts
        self.widths = [-(-n * rows // LANES) * LANES for n in counts]
        self.starts = [sum(self.widths[:i]) for i in range(len(counts))]
        self.width = sum(self.widths)

    def lanes(self, stage):
        return slice(self.starts[stage], self.starts[stage] + self.widths[stage])

    def columns(self, stage, blocks, place, wide):
        parts = [ref[:, pl.ds(place, wide)] for ref in blocks]
        if len(parts) == self.counts[stage] + 1:
            parts[-2:] = [jnp.concatenate(parts[-2:])]
        spare = self.widths[stage] - self.counts[stage] * self.rows
        if spare:
            parts.append(jnp.zeros((spare, wide), BF16))
        return jnp.concatenate(parts) if len(parts) > 1 else parts[0]

    def order(self, me, table, order, chans):
        lane = lax.broadcasted_iota(jnp.int32, (1, self.width), 1)
        source = jnp.full((1, self.width), -1, jnp.int32)
        at = 0
        for start, count in zip(self.starts, self.counts):
            for i in range(count):
                first = start + i * self.rows
                inside = (lane >= first) & (lane < first + self.rows)
                source = jnp.where(inside, table[me, at] * self.rows + lane - first, source)
                at += 1
        channel = lax.broadcasted_iota(jnp.int32, (chans, self.width), 0)
        order[...] = jnp.where(channel == source, 1.0, 0.0).astype(BF16)


def slope_kernel(stages, dev, table, stats, gain, shift, lat_own, lat_far, cot_own, cot_far,
                 cots, slope, slope_x, *refs):
    me = dev[0]
    core = me % 2
    half, width, chans = lat_own.shape
    clear_edges(cots)
    mean, rstd = stats[0:1], stats[1:2]
    gain_v, shift_v = gain[...], shift[...]
    far_at = half - core * half
    if len(stages.counts) > 1:
        order, placed = refs
        stages.order(me, table, order, chans)
        for ref, base in ((cot_own, core * half), (cot_far, far_at)):
            value = jnp.dot(ref[...].reshape(half * width, chans), order[...], preferred_element_type=F32)
            placed[pl.ds(base, half)] = value.reshape(half, width, stages.width)

    def one_row(i, _):
        for lat, cot, base in ((lat_own, cot_own, core * half), (lat_far, cot_far, far_at)):
            value = placed[base + i] if len(stages.counts) > 1 else cot[i].astype(F32)
            fill_shifts(cots, base + i + 1, value)
            xhat = (lat[i].astype(F32) - mean) * rstd
            pre = gain_v * xhat + shift_v
            sig = 0.5 + 0.5 * jnp.tanh(0.5 * pre)
            value = sig * (1.0 + pre * (1.0 - sig))
            slope[base + i] = value.astype(BF16)
            slope_x[base + i] = (value * xhat).astype(BF16)
        return 0

    lax.fori_loop(0, half, one_row, 0)


def conv_sum(cols, stages, stage, core, first, half, acts, blocks, total):
    width, chans = acts.shape[2:]
    cells = half * width
    nt = (((1,), (1,)), ((), ()))
    place, channel = cols.middle(core, chans)
    window = acts[1, pl.ds(first + 1, half), :, pl.ds(channel, cols.mid)].reshape(cells, cols.mid)
    lane = lax.broadcasted_iota(jnp.int32, window.shape, 1)
    window = jnp.where((core == 1) & (lane < cols.both), jnp.zeros_like(window), window)
    kernel = stages.columns(stage, blocks, place, cols.mid)
    total[...] = lax.dot_general(window, kernel, nt, preferred_element_type=F32)

    def two_taps(k, _):
        taps, place = cols.pair(core, k, chans)
        windows = [acts[t % 3, pl.ds(first + t // 3, half)].reshape(cells, chans) for t in taps]
        kernel = stages.columns(stage, blocks, place, 2 * chans)
        total[...] += lax.dot_general(
            jnp.concatenate(windows, axis=1), kernel, nt, preferred_element_type=F32
        )
        return 0

    lax.fori_loop(0, 2, two_taps, 0)


def conv_both_kernel(cols, stages, stage, dev, acts, *refs):
    blocks, (own, far, total) = refs[:-3], refs[-3:]
    core = dev[0] % 2
    rows = acts.shape[1] - 2
    conv_sum(cols, stages, stage, core, 0, rows, acts, blocks, total)
    half = own.shape[0]
    own[...] = total[pl.ds(pl.multiple_of(core * half, half), half)]
    far[...] = total[pl.ds(pl.multiple_of((1 - core) * half, half), half)].astype(BF16)


def conv_far_kernel(cols, stages, stage, dev, acts, *refs):
    blocks, (far, total) = refs[:-2], refs[-2:]
    core = dev[0] % 2
    half = (acts.shape[1] - 2) // 2
    conv_sum(cols, stages, stage, core, (1 - core) * half, half, acts, blocks, total)
    far[...] = total[...].astype(BF16)


def conv_own_kernel(cols, stages, dev, acts, got, latent, bias, *refs):
    core = dev[0] % 2
    half, width, chans = latent.shape
    scale = cols.total ** (-0.5)
    stage = len(stages.counts) - 1
    before = 3 * stage
    blocks, (block, total) = refs[before:-2], refs[-2:]
    conv_sum(cols, stages, stage, core, core * half, half, acts, blocks, total)
    conv = total[...] + got[...].astype(F32)
    if stage:
        first_own, first_got, order = refs[:before]
        conv = jnp.concatenate([first_own[...] + first_got[...].astype(F32), conv], axis=1)
        high = conv.astype(BF16)
        low = (conv - high.astype(F32)).astype(BF16)
        nt = (((1,), (1,)), ((), ()))
        conv = sum(
            lax.dot_general(value, order[...], nt, preferred_element_type=F32) for value in (low, high)
        )
    conv = scale * conv + bias[...]
    block[...] = (conv.reshape(half, width, chans) + latent[...].astype(F32)).astype(BF16)


def back_kernel(cols, stages, stage, dev, cots, slope, slope_x, *refs):
    blocks, (sums, total) = refs[:-2], refs[-2:]
    core = dev[0] % 2
    rows, width = cots.shape[1] - 2, cots.shape[2]
    cells, chans = total.shape
    lanes = stages.lanes(stage)

    def taps_from(first, place, count):
        windows, kernels = [], []
        for i in range(count):
            tap = first + i
            window = cots[2 - tap % 3, pl.ds(2 - tap // 3, rows), :, lanes]
            windows.append(window.reshape(cells, stages.widths[stage]))
            kernels.append(stages.columns(stage, blocks, pl.multiple_of(place + i * chans, LANES), chans))
        return jnp.dot(
            jnp.concatenate(windows, axis=1), jnp.concatenate(kernels), preferred_element_type=F32
        )

    if stages.widths[stage] * 4 <= 2 * chans:
        taps, place = cols.pair(core, 0, chans)
        total[...] = taps_from(taps[0], place, 4)
    else:
        total[...] = jnp.zeros_like(total)

        def two_taps(k, _):
            taps, place = cols.pair(core, k, chans)
            total[...] += taps_from(taps[0], place, 2)
            return 0

        lax.fori_loop(0, 2, two_taps, 0)

    place, channel = cols.middle(core, chans)
    window = cots[1, 1:rows + 1, :, lanes].reshape(cells, stages.widths[stage])
    kernel = stages.columns(stage, blocks, place, cols.mid)
    value = jnp.dot(window, kernel, preferred_element_type=F32)
    lane = lax.broadcasted_iota(jnp.int32, value.shape, 1)
    total[:, pl.ds(channel, cols.mid)] += jnp.where((core == 1) & (lane < cols.both), 0.0, value)

    def add_row(i, carry):
        gains, shifts = carry
        value = total[pl.ds(pl.multiple_of(i * width, width), width)]
        return gains + value * slope_x[i].astype(F32), shifts + value * slope[i].astype(F32)

    zero = jnp.zeros((width, chans), F32)
    gains, shifts = lax.fori_loop(0, rows, add_row, (zero, zero))
    scale = cols.total ** (-0.5)
    sums[0:1] = scale * jnp.sum(gains, axis=0, keepdims=True)
    sums[1:2] = scale * jnp.sum(shifts, axis=0, keepdims=True)


def finish_kernel(cols, dev, step, shard, mine, theirs, ours, aside, out):
    lower = dev[0] % 2 == 0
    rate = LR_KERNEL * (1.0 - (step[0] % 1000).astype(F32) / 2000.0)
    factor = 0.5 * cols.total ** (-0.5) * rate
    here = 0.5 * mine[...].astype(F32) - factor * ours[...].astype(F32)
    there = 0.5 * theirs[...].astype(F32) - factor * aside[...].astype(F32)
    left, right = jnp.where(lower, here, there), jnp.where(lower, there, here)
    out[:, :cols.lead] = 0.5 * shard[:, :cols.lead] + left
    out[:, cols.lead:] = 0.5 * shard[:, cols.lead:] + right[:, cols.both:]


NODE = ("z", "y")


def swap(value, axis):
    return lax.ppermute(value, axis, [(0, 1), (1, 0)])


def from_peer(level, value):
    count = lax.axis_size("replica")
    levels = count.bit_length() - 1
    moves = [[(s, (s + (1 << k)) % count) for s in range(count)] for k in range(levels)]
    if levels == 1:
        return lax.ppermute(value, "replica", moves[0])
    return lax.switch(level, [lambda v, m=m: lax.ppermute(v, "replica", m) for m in moves], value)


class Ring:
    def __init__(self, zs):
        self.count = 2 * zs
        self.reach = zs
        self.nodes = [2 * z for z in range(zs)] + [2 * z + 1 for z in reversed(range(zs))]
        ahead = list(zip(self.nodes, self.nodes[1:] + self.nodes[:1]))
        self.ahead = ahead
        self.behind = [(b, a) for a, b in ahead]

    def node(self, at, offset):
        return self.nodes[(at + offset) % self.count]

    def up(self, value):
        return lax.ppermute(value, NODE, self.ahead)

    def down(self, value):
        return lax.ppermute(value, NODE, self.behind)

    def table(self, part):
        rows = np.zeros((2, self.count, 2, 3 * self.count), np.int32)
        for replica in range(2):
            for at, node in enumerate(self.nodes):
                line = [node]
                for k in range(1, self.reach + 1):
                    line.append(self.node(at, -k))
                    if k < self.reach:
                        line.append(self.node(at, k))
                for which in (replica, 1 - replica):
                    for j in range(self.reach):
                        targets = [self.node(at, self.reach - j), self.node(at, j + 1 - self.reach)]
                        line += [(2 * target + which) * part for target in targets]
                rows[replica, node, :] = line
        return rows.reshape(-1, 3 * self.count)


def hop(value, axis, mask):
    count = lax.axis_size(axis)
    return value + lax.ppermute(value, axis, [(s, s ^ mask) for s in range(count)])


def add(*values):
    total = values[0].astype(F32)
    for value in values[1:]:
        total = total + value.astype(F32)
    return total.astype(BF16)


def tied(*values):
    return lax.optimization_barrier(values)


def per_device(latents, cotangent, kernel, conv_bias, gn_gain, gn_shift, step):
    latent, cotan, shard = latents[0], cotangent[0], kernel[0]
    half, width, chans = latent.shape
    part = shard.shape[0]
    cols = Columns(chans)
    cells = half * width
    zs, replicas = lax.axis_size("z"), lax.axis_size("replica")
    core, z, y, replica = (lax.axis_index(a) for a in ("core", "z", "y", "replica"))
    lower = core == 0
    paired = replicas == 2
    ring = Ring(zs)
    scale = cols.total ** (-0.5)
    params = jnp.concatenate([conv_bias, gn_gain, gn_shift])
    me = ((replica * zs + z) * 2 + y) * 2 + core
    core, lower, same, me = tied(core, lower, replica == core, me)
    dev = me.reshape(1)

    mine = lax.dynamic_slice_in_dim(shard, core * cols.start, cols.lead, 1).astype(BF16)
    theirs = lax.dynamic_slice_in_dim(shard, (1 - core) * cols.start, cols.lead, 1).astype(BF16)
    got = swap(theirs, "core")
    unit = jnp.where(lower, jnp.concatenate([mine, got]), jnp.concatenate([got, mine]))
    lat_far = swap(latent, "core")
    cot_b = cotan.astype(BF16)
    cot_far = swap(cot_b, "core")

    if paired:
        table = jnp.asarray(ring.table(part))
        order = (ring.count, part, 2 * ring.count)
        up1, down1 = ring.up(unit), ring.down(unit)
        peer = swap(mine, "replica"), swap(theirs, "replica")
    else:
        table = jnp.zeros((replicas * zs * 4, 1), jnp.int32)
        order = None

    def call(body, outs, ins, scratch, megabytes, flops):
        return pl.pallas_call(
            body,
            out_shape=outs,
            in_specs=ins,
            out_specs=jax.tree.map(lambda _: VMEM_SPEC, outs),
            scratch_shapes=scratch,
            compiler_params=pltpu.CompilerParams(vmem_limit_bytes=megabytes * 2**20),
            cost_estimate=pl.CostEstimate(flops=flops, bytes_accessed=0, transcendentals=0),
        )

    image = (2 * half, width, chans)
    shifted = jax.ShapeDtypeStruct((3, 2 * half + 2, width, chans), BF16)
    flops = 2 * 2 * cells * chans * cols.lead
    stats, acts, cot_t = call(
        partial(act_kernel, order),
        (jax.ShapeDtypeStruct((2, chans), F32), shifted, jax.ShapeDtypeStruct((chans, 2 * cells), BF16)),
        [SMEM_SPEC] * 2 + [VMEM_SPEC] * 6,
        [pltpu.VMEM((chans, 2 * cells), F32)],
        8, flops // 4,
    )(dev, table, latent, lat_far, cot_b, cot_far, gn_gain, gn_shift)
    counts = [zs] + [1] * zs if paired else [2 * zs]
    pieces = call(
        partial(grad_kernel, cols),
        [jax.ShapeDtypeStruct((n * 2 * part, cols.lead), BF16) for n in counts],
        [SMEM_SPEC] + [VMEM_SPEC] * 2,
        [],
        4, flops // 2,
    )(dev, acts, cot_t)
    stages = Stages([2 * zs - 3, 3] if paired else [1], 2 * part if paired else chans)
    staged = paired

    def slopes_of(stats):
        extra = (jax.ShapeDtypeStruct((chans, stages.width), BF16),) if staged else ()
        return call(
            partial(slope_kernel, stages),
            (jax.ShapeDtypeStruct((3, 2 * half + 2, width, stages.width), BF16),
             jax.ShapeDtypeStruct(image, BF16), jax.ShapeDtypeStruct(image, BF16)) + extra,
            [SMEM_SPEC] * 2 + [VMEM_SPEC] * 7,
            [pltpu.VMEM((2 * half, width, stages.width), F32)] if staged else [],
            8, flops // 4,
        )(dev, table, stats, gn_gain, gn_shift, latent, lat_far, cot_b, cot_far)

    def back(stage, cots, slopes, blocks):
        return call(
            partial(back_kernel, cols, stages, stage), jax.ShapeDtypeStruct((2, chans), F32),
            [SMEM_SPEC] + [VMEM_SPEC] * (3 + len(blocks)),
            [pltpu.VMEM((2 * cells, chans), F32)], 8, flops // 4,
        )(dev, cots, *slopes, *blocks)

    def conv_first(blocks):
        wide = stages.widths[0]
        return call(
            partial(conv_both_kernel, cols, stages, 0),
            (jax.ShapeDtypeStruct((cells, wide), F32), jax.ShapeDtypeStruct((cells, wide), BF16)),
            [SMEM_SPEC] + [VMEM_SPEC] * (1 + len(blocks)),
            [pltpu.VMEM((2 * cells, wide), F32)], 6, flops // 4,
        )(dev, acts, *blocks)

    def conv_far(acts, blocks):
        wide = stages.widths[-1]
        return call(
            partial(conv_far_kernel, cols, stages, len(stages.counts) - 1),
            jax.ShapeDtypeStruct((cells, wide), BF16),
            [SMEM_SPEC] + [VMEM_SPEC] * (1 + len(blocks)),
            [pltpu.VMEM((cells, wide), F32)], 4, flops // 8,
        )(dev, acts, *blocks)

    def conv_own(got, earlier, blocks):
        return call(
            partial(conv_own_kernel, cols, stages), jax.ShapeDtypeStruct((half, width, chans), BF16),
            [SMEM_SPEC] + [VMEM_SPEC] * (4 + len(earlier) + len(blocks)),
            [pltpu.VMEM((cells, stages.widths[-1]), F32)], 8, flops // 4,
        )(dev, acts, got, latent, conv_bias, *earlier, *blocks)

    def chip_sum(sums):
        vectors = jnp.concatenate([jnp.sum(cotan, axis=(0, 1))[None], sums])
        vectors = params / (4 * zs) - LR_VECTOR * vectors
        return vectors + swap(vectors, "core")

    if paired:
        kept, *sent = pieces
        up, down, sent[0], mine, theirs = tied(up1, down1, sent[0], *peer)
        blocks = [unit, up, down]
        crossed = [swap(piece, "replica") for piece in sent]
        up, down = ring.up(up), ring.down(down)
        up, down, cots, *slopes, order = tied(up, down, *slopes_of(stats))
        blocks += [up, down]

        def ring_step(j, *received):
            parts = kept[2 * j * part:(2 * j + 2) * part], crossed[j]
            ahead, behind = (tuple(x[half] for x in parts) for half in (slice(part), slice(part, None)))
            up_sum = ring.up(add(*ahead, *received[:1]))
            if j < zs - 1:
                return up_sum, ring.down(add(*behind, *received[1:]))
            return up_sum, behind + tuple(received[1:])

        up, down = ring.up(up), ring.down(down)
        conv_first_own, conv_send = conv_first(blocks)
        crossed[0], conv_send = tied(crossed[0], conv_send)
        received = ring_step(0)
        cots, conv_send = tied(cots, conv_send)
        first_sums = back(0, cots, slopes, blocks)
        up, down, first_sums, crossed[1] = tied(up, down, first_sums, crossed[1])
        late = [up, down]

        halves = ring.up(up[:part]), ring.down(down[part:])
        conv_send, *received = tied(conv_send, *received)
        conv_first_got = swap(conv_send, "core")
        for j in range(1, zs - 2):
            received = ring_step(j, *received)
        late += halves

        sums = back(1, cots, slopes, late)
        crossed[-2], sums, *received = tied(crossed[-2], sums, *received)
        acts_last, *_ = tied(acts, sums, *received)
        received = ring_step(zs - 2, *received)
        conv_send = conv_far(acts_last, late)
        vectors = hop(chip_sum(first_sums + sums), "replica", 1)
        crossed[-1], conv_send, vectors, *received = tied(crossed[-1], conv_send, vectors, *received)
        conv_got = swap(conv_send, "core")
        last, behind = ring_step(zs - 1, *received)
        block = conv_own(conv_got, [conv_first_own, conv_first_got, order], late)
        vectors = hop(vectors, "z", 1)
        last, block, vectors = tied(last, block, vectors)
        total = add(*behind, last)
        across = swap(total, "replica")
        ours, others = jnp.where(same, total, across), jnp.where(same, across, total)
        aside = swap(others, "core")
        new_kernel = call(
            partial(finish_kernel, cols), jax.ShapeDtypeStruct(shard.shape, F32),
            [SMEM_SPEC] * 2 + [VMEM_SPEC] * 5, [], 8, flops // 16,
        )(dev, step, shard, mine, theirs, ours, aside)
        vectors = hop(vectors, "y", 1)
        reach = 2
        while reach < zs:
            vectors = hop(vectors, "z", reach)
            reach *= 2
        new_v = 0.5 * vectors
    else:
        late = [lax.all_gather(unit, NODE, axis=0, tiled=True)]
        cots, slope, slope_x = slopes_of(stats)
        sums = back(0, cots, [slope, slope_x], late)
        vectors = chip_sum(sums)
        block = conv_own(swap(conv_far(acts, late), "core"), [], late)
        terms = pieces[0].reshape(2 * zs, 2, part, cols.lead)
        summed = lax.psum_scatter(terms, NODE, scatter_dimension=0, tiled=False)
        ours = lax.dynamic_index_in_dim(summed, core, 0, keepdims=False)
        got = swap(lax.dynamic_index_in_dim(summed, 1 - core, 0, keepdims=False), "core")
        left, right = jnp.where(lower, ours, got), jnp.where(lower, got, ours)
        kernel_grad = jnp.concatenate([left, right[:, cols.both:]], axis=1).astype(F32)
        level = step[0] % (replicas.bit_length() - 1)
        rate = LR_KERNEL * (1.0 - (step[0] % 1000).astype(F32) / 2000.0)
        stepped = shard - (scale * rate) * kernel_grad
        new_kernel = 0.5 * (stepped + from_peer(level, stepped.astype(BF16)).astype(F32))
        stepped_v = lax.psum(vectors, NODE)
        new_v = 0.5 * (stepped_v + from_peer(level, stepped_v))

    return (
        block[None],
        new_kernel[None],
        new_v[0][None],
        new_v[1][None],
        new_v[2][None],
    )


def solution(mesh):
    replicas, shards = mesh.shape["replica"], mesh.shape["shard"]
    split = Mesh(mesh.devices.reshape(replicas, shards // 4, 2, 2), ("replica", "z", "y", "core"))
    shard = ("z", "y", "core")
    return jax.shard_map(
        per_device,
        mesh=split,
        in_specs=(
            P("replica", shard, None, None),
            P("replica", shard, None, None),
            P("replica", shard, None),
            P("replica", None),
            P("replica", None),
            P("replica", None),
            P(),
        ),
        out_specs=(
            P("replica", shard, None, None),
            P("replica", shard, None),
            P("replica", None),
            P("replica", None),
            P("replica", None),
        ),
        check_vma=False,
    )
```

```python
from functools import partial

import jax
import jax.numpy as jnp
import numpy as np
from jax import lax
from jax.experimental import pallas as pl
from jax.experimental.pallas import tpu as pltpu
from jax.sharding import Mesh, PartitionSpec as P

GROUPS = 32
EPS = 1e-05
LR_KERNEL = 0.1
LR_VECTOR = 0.01
LANES = 128
BF16 = jnp.bfloat16
F32 = jnp.float32

SMEM_SPEC = pl.BlockSpec(memory_space=pltpu.SMEM)
VMEM_SPEC = pl.BlockSpec(memory_space=pltpu.VMEM)


class Columns:
    def __init__(self, chans):
        tiles = 9 * chans // LANES
        self.total = 9 * chans
        self.lead = (tiles + 1) // 2 * LANES
        self.start = self.total - self.lead
        self.both = 2 * self.lead - self.total
        self.mid = self.lead - 4 * chans
        self.mid_start = chans - self.mid

    def pair(self, core, k, chans):
        first = jnp.where(core == 0, 2 * k, 5 + 2 * k)
        place = jnp.where(core == 0, 2 * k * chans, self.mid + 2 * k * chans)
        return (first, first + 1), pl.multiple_of(place, LANES)

    def middle(self, core, chans):
        place = jnp.where(core == 0, 4 * chans, 0)
        channel = jnp.where(core == 0, 0, self.mid_start)
        return pl.multiple_of(place, LANES), pl.multiple_of(channel, LANES)


def fill_shifts(shifts, row, values):
    width = values.shape[0]
    at = lax.broadcasted_iota(jnp.int32, values.shape, 0)
    left = jnp.where(at == 0, 0.0, pltpu.roll(values, 1, 0))
    right = jnp.where(at == width - 1, 0.0, pltpu.roll(values, width - 1, 0))
    shifts[0, row] = left.astype(BF16)
    shifts[1, row] = values.astype(BF16)
    shifts[2, row] = right.astype(BF16)


def clear_edges(shifts):
    zero = jnp.zeros(shifts.shape[2:], shifts.dtype)
    for b in range(3):
        shifts[b, 0] = zero
        shifts[b, shifts.shape[1] - 1] = zero


def act_kernel(order, dev, table, lat_own, lat_far, cot_own, cot_far, gain, shift,
               stats, acts, cot_t, cot_f):
    me = dev[0]
    core = me % 2
    half, width, chans = lat_own.shape
    cells = 2 * half * width
    group_width = chans // GROUPS
    own_at = core * half
    far_at = half - own_at
    clear_edges(acts)

    def add_row(i, sums):
        total, square = sums
        a = lat_own[i].astype(F32)
        b = lat_far[i].astype(F32)
        return total + (a + b), square + (a * a + b * b)

    zero = jnp.zeros((width, chans), F32)
    total, square = lax.fori_loop(0, half, add_row, (zero, zero))
    sums = jnp.concatenate(
        [jnp.sum(total, axis=0, keepdims=True), jnp.sum(square, axis=0, keepdims=True),
         jnp.zeros((6, chans), F32)], axis=0
    )
    first = lax.broadcasted_iota(jnp.int32, (chans, LANES), 0)
    start = lax.broadcasted_iota(jnp.int32, (chans, LANES), 1) * group_width
    member = jnp.where((first >= start) & (first < start + group_width), 1.0, 0.0)
    exact = partial(lax.dot_general, precision=lax.Precision.HIGHEST, preferred_element_type=F32)
    sums = exact(sums, member, (((1,), (0,)), ((), ()))) / (cells * group_width)
    sums = exact(sums, member, (((1,), (1,)), ((), ())))
    mean = sums[0:1]
    rstd = lax.rsqrt(sums[1:2] - mean * mean + EPS)
    stats[0:1] = mean
    stats[1:2] = rstd
    gain_v, shift_v = gain[...], shift[...]

    def act_rows(i, _):
        for ref, base in ((lat_own, own_at), (lat_far, far_at)):
            pre = gain_v * ((ref[i].astype(F32) - mean) * rstd) + shift_v
            fill_shifts(acts, base + i + 1, pre * (0.5 + 0.5 * jnp.tanh(0.5 * pre)))
        return 0

    lax.fori_loop(0, half, act_rows, 0)

    chunk = LANES // width
    for ref, base in ((cot_own, own_at), (cot_far, far_at)):
        for i in range(half // chunk):
            piece = ref[i * chunk:(i + 1) * chunk].reshape(LANES, chans).astype(F32)
            place = pl.multiple_of(base * width + i * LANES, LANES)
            if order is None:
                cot_t[:, pl.ds(place, LANES)] = piece.T.astype(BF16)
            else:
                cot_f[:, pl.ds(place, LANES)] = piece.T
    if order is not None:
        first_at, part, count = order
        for q in range(count // 2):
            pair = [
                cot_f[pl.ds(pl.multiple_of(table[me, first_at + 2 * q + i], 8), part)]
                for i in range(2)
            ]
            cot_t[2 * q * part:(2 * q + 2) * part] = jnp.concatenate(pair).astype(BF16)


def grad_kernel(cols, dev, acts, cot_t, *pieces):
    core = dev[0] % 2
    rows, width, chans = acts.shape[1] - 2, acts.shape[2], acts.shape[3]
    cells = rows * width

    def emit(window, place, wide):
        value = jnp.dot(cot_t[...], window, preferred_element_type=F32)
        at = 0
        for piece in pieces:
            piece[:, pl.ds(place, wide)] = value[at:at + piece.shape[0]].astype(BF16)
            at += piece.shape[0]

    def two_taps(k, _):
        taps, place = cols.pair(core, k, chans)
        windows = [acts[t % 3, pl.ds(t // 3, rows)].reshape(cells, chans) for t in taps]
        emit(jnp.concatenate(windows, axis=1), place, 2 * chans)
        return 0

    lax.fori_loop(0, 2, two_taps, 0)
    place, channel = cols.middle(core, chans)
    emit(acts[1, 1:rows + 1, :, pl.ds(channel, cols.mid)].reshape(cells, cols.mid), place, cols.mid)


class Stages:
    def __init__(self, counts, rows):
        self.rows = rows
        self.counts = counts
        self.widths = [-(-n * rows // LANES) * LANES for n in counts]
        self.starts = [sum(self.widths[:i]) for i in range(len(counts))]
        self.width = sum(self.widths)

    def lanes(self, stage):
        return slice(self.starts[stage], self.starts[stage] + self.widths[stage])

    def columns(self, stage, blocks, place, wide):
        parts = [ref[:, pl.ds(place, wide)] for ref in blocks]
        if len(parts) == self.counts[stage] + 1:
            parts[-2:] = [jnp.concatenate(parts[-2:])]
        spare = self.widths[stage] - self.counts[stage] * self.rows
        if spare:
            parts.append(jnp.zeros((spare, wide), BF16))
        return jnp.concatenate(parts) if len(parts) > 1 else parts[0]

    def order(self, me, table, order, chans):
        lane = lax.broadcasted_iota(jnp.int32, (1, self.width), 1)
        source = jnp.full((1, self.width), -1, jnp.int32)
        at = 0
        for start, count in zip(self.starts, self.counts):
            for i in range(count):
                first = start + i * self.rows
                inside = (lane >= first) & (lane < first + self.rows)
                source = jnp.where(inside, table[me, at] * self.rows + lane - first, source)
                at += 1
        channel = lax.broadcasted_iota(jnp.int32, (chans, self.width), 0)
        order[...] = jnp.where(channel == source, 1.0, 0.0).astype(BF16)


def slope_kernel(stages, dev, table, stats, gain, shift, lat_own, lat_far, cot_own, cot_far,
                 cots, slope, slope_x, *refs):
    me = dev[0]
    core = me % 2
    half, width, chans = lat_own.shape
    clear_edges(cots)
    mean, rstd = stats[0:1], stats[1:2]
    gain_v, shift_v = gain[...], shift[...]
    far_at = half - core * half
    if len(stages.counts) > 1:
        order, placed = refs
        stages.order(me, table, order, chans)
        for ref, base in ((cot_own, core * half), (cot_far, far_at)):
            value = jnp.dot(ref[...].reshape(half * width, chans), order[...], preferred_element_type=F32)
            placed[pl.ds(base, half)] = value.reshape(half, width, stages.width)

    def one_row(i, _):
        for lat, cot, base in ((lat_own, cot_own, core * half), (lat_far, cot_far, far_at)):
            value = placed[base + i] if len(stages.counts) > 1 else cot[i].astype(F32)
            fill_shifts(cots, base + i + 1, value)
            xhat = (lat[i].astype(F32) - mean) * rstd
            pre = gain_v * xhat + shift_v
            sig = 0.5 + 0.5 * jnp.tanh(0.5 * pre)
            value = sig * (1.0 + pre * (1.0 - sig))
            slope[base + i] = value.astype(BF16)
            slope_x[base + i] = (value * xhat).astype(BF16)
        return 0

    lax.fori_loop(0, half, one_row, 0)


def conv_sum(cols, stages, stage, core, first, half, acts, blocks, total):
    width, chans = acts.shape[2:]
    cells = half * width
    nt = (((1,), (1,)), ((), ()))
    place, channel = cols.middle(core, chans)
    window = acts[1, pl.ds(first + 1, half), :, pl.ds(channel, cols.mid)].reshape(cells, cols.mid)
    lane = lax.broadcasted_iota(jnp.int32, window.shape, 1)
    window = jnp.where((core == 1) & (lane < cols.both), jnp.zeros_like(window), window)
    kernel = stages.columns(stage, blocks, place, cols.mid)
    total[...] = lax.dot_general(window, kernel, nt, preferred_element_type=F32)

    def two_taps(k, _):
        taps, place = cols.pair(core, k, chans)
        windows = [acts[t % 3, pl.ds(first + t // 3, half)].reshape(cells, chans) for t in taps]
        kernel = stages.columns(stage, blocks, place, 2 * chans)
        total[...] += lax.dot_general(
            jnp.concatenate(windows, axis=1), kernel, nt, preferred_element_type=F32
        )
        return 0

    lax.fori_loop(0, 2, two_taps, 0)


def conv_both_kernel(cols, stages, stage, dev, acts, *refs):
    blocks, (own, far, total) = refs[:-3], refs[-3:]
    core = dev[0] % 2
    rows = acts.shape[1] - 2
    conv_sum(cols, stages, stage, core, 0, rows, acts, blocks, total)
    half = own.shape[0]
    own[...] = total[pl.ds(pl.multiple_of(core * half, half), half)]
    far[...] = total[pl.ds(pl.multiple_of((1 - core) * half, half), half)].astype(BF16)


def conv_far_kernel(cols, stages, stage, dev, acts, *refs):
    blocks, (far, total) = refs[:-2], refs[-2:]
    core = dev[0] % 2
    half = (acts.shape[1] - 2) // 2
    conv_sum(cols, stages, stage, core, (1 - core) * half, half, acts, blocks, total)
    far[...] = total[...].astype(BF16)


def conv_own_kernel(cols, stages, dev, acts, got, latent, bias, *refs):
    core = dev[0] % 2
    half, width, chans = latent.shape
    scale = cols.total ** (-0.5)
    stage = len(stages.counts) - 1
    before = 3 * stage
    blocks, (block, total) = refs[before:-2], refs[-2:]
    conv_sum(cols, stages, stage, core, core * half, half, acts, blocks, total)
    conv = total[...] + got[...].astype(F32)
    if stage:
        first_own, first_got, order = refs[:before]
        conv = jnp.concatenate([first_own[...] + first_got[...].astype(F32), conv], axis=1)
        high = conv.astype(BF16)
        low = (conv - high.astype(F32)).astype(BF16)
        nt = (((1,), (1,)), ((), ()))
        conv = sum(
            lax.dot_general(value, order[...], nt, preferred_element_type=F32) for value in (low, high)
        )
    conv = scale * conv + bias[...]
    block[...] = (conv.reshape(half, width, chans) + latent[...].astype(F32)).astype(BF16)


def back_kernel(cols, stages, stage, dev, cots, slope, slope_x, *refs):
    blocks, (sums, total) = refs[:-2], refs[-2:]
    core = dev[0] % 2
    rows, width = cots.shape[1] - 2, cots.shape[2]
    cells, chans = total.shape
    lanes = stages.lanes(stage)

    def taps_from(first, place, count):
        windows, kernels = [], []
        for i in range(count):
            tap = first + i
            window = cots[2 - tap % 3, pl.ds(2 - tap // 3, rows), :, lanes]
            windows.append(window.reshape(cells, stages.widths[stage]))
            kernels.append(stages.columns(stage, blocks, pl.multiple_of(place + i * chans, LANES), chans))
        return jnp.dot(
            jnp.concatenate(windows, axis=1), jnp.concatenate(kernels), preferred_element_type=F32
        )

    if stages.widths[stage] * 4 <= 2 * chans:
        taps, place = cols.pair(core, 0, chans)
        total[...] = taps_from(taps[0], place, 4)
    else:
        total[...] = jnp.zeros_like(total)

        def two_taps(k, _):
            taps, place = cols.pair(core, k, chans)
            total[...] += taps_from(taps[0], place, 2)
            return 0

        lax.fori_loop(0, 2, two_taps, 0)

    place, channel = cols.middle(core, chans)
    window = cots[1, 1:rows + 1, :, lanes].reshape(cells, stages.widths[stage])
    kernel = stages.columns(stage, blocks, place, cols.mid)
    value = jnp.dot(window, kernel, preferred_element_type=F32)
    lane = lax.broadcasted_iota(jnp.int32, value.shape, 1)
    total[:, pl.ds(channel, cols.mid)] += jnp.where((core == 1) & (lane < cols.both), 0.0, value)

    def add_row(i, carry):
        gains, shifts = carry
        value = total[pl.ds(pl.multiple_of(i * width, width), width)]
        return gains + value * slope_x[i].astype(F32), shifts + value * slope[i].astype(F32)

    zero = jnp.zeros((width, chans), F32)
    gains, shifts = lax.fori_loop(0, rows, add_row, (zero, zero))
    scale = cols.total ** (-0.5)
    sums[0:1] = scale * jnp.sum(gains, axis=0, keepdims=True)
    sums[1:2] = scale * jnp.sum(shifts, axis=0, keepdims=True)


def finish_kernel(cols, dev, step, shard, mine, theirs, ours, aside, out):
    lower = dev[0] % 2 == 0
    rate = LR_KERNEL * (1.0 - (step[0] % 1000).astype(F32) / 2000.0)
    factor = 0.5 * cols.total ** (-0.5) * rate
    here = 0.5 * mine[...].astype(F32) - factor * ours[...].astype(F32)
    there = 0.5 * theirs[...].astype(F32) - factor * aside[...].astype(F32)
    left, right = jnp.where(lower, here, there), jnp.where(lower, there, here)
    out[:, :cols.lead] = 0.5 * shard[:, :cols.lead] + left
    out[:, cols.lead:] = 0.5 * shard[:, cols.lead:] + right[:, cols.both:]


NODE = ("z", "y")


def swap(value, axis):
    return lax.ppermute(value, axis, [(0, 1), (1, 0)])


def from_peer(level, value):
    count = lax.axis_size("replica")
    levels = count.bit_length() - 1
    moves = [[(s, (s + (1 << k)) % count) for s in range(count)] for k in range(levels)]
    if levels == 1:
        return lax.ppermute(value, "replica", moves[0])
    return lax.switch(level, [lambda v, m=m: lax.ppermute(v, "replica", m) for m in moves], value)


class Ring:
    def __init__(self, zs):
        self.count = 2 * zs
        self.reach = zs
        self.nodes = [2 * z for z in range(zs)] + [2 * z + 1 for z in reversed(range(zs))]
        ahead = list(zip(self.nodes, self.nodes[1:] + self.nodes[:1]))
        self.ahead = ahead
        self.behind = [(b, a) for a, b in ahead]

    def node(self, at, offset):
        return self.nodes[(at + offset) % self.count]

    def up(self, value):
        return lax.ppermute(value, NODE, self.ahead)

    def down(self, value):
        return lax.ppermute(value, NODE, self.behind)

    def table(self, part):
        rows = np.zeros((2, self.count, 2, 3 * self.count), np.int32)
        for replica in range(2):
            for at, node in enumerate(self.nodes):
                line = [node]
                for k in range(1, self.reach + 1):
                    line.append(self.node(at, -k))
                    if k < self.reach:
                        line.append(self.node(at, k))
                for which in (replica, 1 - replica):
                    for j in range(self.reach):
                        targets = [self.node(at, self.reach - j), self.node(at, j + 1 - self.reach)]
                        line += [(2 * target + which) * part for target in targets]
                rows[replica, node, :] = line
        return rows.reshape(-1, 3 * self.count)


def hop(value, axis, mask):
    count = lax.axis_size(axis)
    return value + lax.ppermute(value, axis, [(s, s ^ mask) for s in range(count)])


def add(*values):
    total = values[0].astype(F32)
    for value in values[1:]:
        total = total + value.astype(F32)
    return total.astype(BF16)


def tied(*values):
    return lax.optimization_barrier(values)


def per_device(latents, cotangent, kernel, conv_bias, gn_gain, gn_shift, step):
    latent, cotan, shard = latents[0], cotangent[0], kernel[0]
    half, width, chans = latent.shape
    part = shard.shape[0]
    cols = Columns(chans)
    cells = half * width
    zs, replicas = lax.axis_size("z"), lax.axis_size("replica")
    core, z, y, replica = (lax.axis_index(a) for a in ("core", "z", "y", "replica"))
    lower = core == 0
    paired = replicas == 2
    ring = Ring(zs)
    scale = cols.total ** (-0.5)
    params = jnp.concatenate([conv_bias, gn_gain, gn_shift])
    me = ((replica * zs + z) * 2 + y) * 2 + core
    core, lower, same, me = tied(core, lower, replica == core, me)
    dev = me.reshape(1)

    mine = lax.dynamic_slice_in_dim(shard, core * cols.start, cols.lead, 1).astype(BF16)
    theirs = lax.dynamic_slice_in_dim(shard, (1 - core) * cols.start, cols.lead, 1).astype(BF16)
    got = swap(theirs, "core")
    unit = jnp.where(lower, jnp.concatenate([mine, got]), jnp.concatenate([got, mine]))
    lat_far = swap(latent, "core")
    cot_b = cotan.astype(BF16)
    cot_far = swap(cot_b, "core")

    if paired:
        table = jnp.asarray(ring.table(part))
        order = (ring.count, part, 2 * ring.count)
        up1, down1 = ring.up(unit), ring.down(unit)
        peer = swap(mine, "replica"), swap(theirs, "replica")
    else:
        table = jnp.zeros((replicas * zs * 4, 1), jnp.int32)
        order = None

    def call(body, outs, ins, scratch, megabytes, flops):
        return pl.pallas_call(
            body,
            out_shape=outs,
            in_specs=ins,
            out_specs=jax.tree.map(lambda _: VMEM_SPEC, outs),
            scratch_shapes=scratch,
            compiler_params=pltpu.CompilerParams(vmem_limit_bytes=megabytes * 2**20),
            cost_estimate=pl.CostEstimate(flops=flops, bytes_accessed=0, transcendentals=0),
        )

    image = (2 * half, width, chans)
    shifted = jax.ShapeDtypeStruct((3, 2 * half + 2, width, chans), BF16)
    flops = 2 * 2 * cells * chans * cols.lead
    stats, acts, cot_t = call(
        partial(act_kernel, order),
        (jax.ShapeDtypeStruct((2, chans), F32), shifted, jax.ShapeDtypeStruct((chans, 2 * cells), BF16)),
        [SMEM_SPEC] * 2 + [VMEM_SPEC] * 6,
        [pltpu.VMEM((chans, 2 * cells), F32)],
        8, flops // 4,
    )(dev, table, latent, lat_far, cot_b, cot_far, gn_gain, gn_shift)
    counts = [zs] + [1] * zs if paired else [2 * zs]
    pieces = call(
        partial(grad_kernel, cols),
        [jax.ShapeDtypeStruct((n * 2 * part, cols.lead), BF16) for n in counts],
        [SMEM_SPEC] + [VMEM_SPEC] * 2,
        [],
        4, flops // 2,
    )(dev, acts, cot_t)
    stages = Stages([2 * zs - 3, 3] if paired else [1], 2 * part if paired else chans)
    staged = paired

    def slopes_of(stats):
        extra = (jax.ShapeDtypeStruct((chans, stages.width), BF16),) if staged else ()
        return call(
            partial(slope_kernel, stages),
            (jax.ShapeDtypeStruct((3, 2 * half + 2, width, stages.width), BF16),
             jax.ShapeDtypeStruct(image, BF16), jax.ShapeDtypeStruct(image, BF16)) + extra,
            [SMEM_SPEC] * 2 + [VMEM_SPEC] * 7,
            [pltpu.VMEM((2 * half, width, stages.width), F32)] if staged else [],
            8, flops // 4,
        )(dev, table, stats, gn_gain, gn_shift, latent, lat_far, cot_b, cot_far)

    def back(stage, cots, slopes, blocks):
        return call(
            partial(back_kernel, cols, stages, stage), jax.ShapeDtypeStruct((2, chans), F32),
            [SMEM_SPEC] + [VMEM_SPEC] * (3 + len(blocks)),
            [pltpu.VMEM((2 * cells, chans), F32)], 8, flops // 4,
        )(dev, cots, *slopes, *blocks)

    def conv_first(blocks):
        wide = stages.widths[0]
        return call(
            partial(conv_both_kernel, cols, stages, 0),
            (jax.ShapeDtypeStruct((cells, wide), F32), jax.ShapeDtypeStruct((cells, wide), BF16)),
            [SMEM_SPEC] + [VMEM_SPEC] * (1 + len(blocks)),
            [pltpu.VMEM((2 * cells, wide), F32)], 6, flops // 4,
        )(dev, acts, *blocks)

    def conv_far(acts, blocks):
        wide = stages.widths[-1]
        return call(
            partial(conv_far_kernel, cols, stages, len(stages.counts) - 1),
            jax.ShapeDtypeStruct((cells, wide), BF16),
            [SMEM_SPEC] + [VMEM_SPEC] * (1 + len(blocks)),
            [pltpu.VMEM((cells, wide), F32)], 4, flops // 8,
        )(dev, acts, *blocks)

    def conv_own(got, earlier, blocks):
        return call(
            partial(conv_own_kernel, cols, stages), jax.ShapeDtypeStruct((half, width, chans), BF16),
            [SMEM_SPEC] + [VMEM_SPEC] * (4 + len(earlier) + len(blocks)),
            [pltpu.VMEM((cells, stages.widths[-1]), F32)], 8, flops // 4,
        )(dev, acts, got, latent, conv_bias, *earlier, *blocks)

    def chip_sum(sums):
        vectors = jnp.concatenate([jnp.sum(cotan, axis=(0, 1))[None], sums])
        vectors = params / (4 * zs) - LR_VECTOR * vectors
        return vectors + swap(vectors, "core")

    if paired:
        kept, *sent = pieces
        up, down, sent[0], mine, theirs = tied(up1, down1, sent[0], *peer)
        blocks = [unit, up, down]
        crossed = [swap(piece, "replica") for piece in sent]
        up, down = ring.up(up), ring.down(down)
        up, down, cots, *slopes, order = tied(up, down, *slopes_of(stats))
        blocks += [up, down]

        def ring_step(j, *received):
            parts = kept[2 * j * part:(2 * j + 2) * part], crossed[j]
            ahead, behind = (tuple(x[half] for x in parts) for half in (slice(part), slice(part, None)))
            up_sum = ring.up(add(*ahead, *received[:1]))
            if j < zs - 1:
                return up_sum, ring.down(add(*behind, *received[1:]))
            return up_sum, behind + tuple(received[1:])

        up, down = ring.up(up), ring.down(down)
        conv_first_own, conv_send = conv_first(blocks)
        crossed[0], conv_send = tied(crossed[0], conv_send)
        received = ring_step(0)
        cots, conv_send = tied(cots, conv_send)
        first_sums = back(0, cots, slopes, blocks)
        up, down, first_sums, crossed[1] = tied(up, down, first_sums, crossed[1])
        late = [up, down]

        halves = ring.up(up[:part]), ring.down(down[part:])
        conv_send, *received = tied(conv_send, *received)
        conv_first_got = swap(conv_send, "core")
        for j in range(1, zs - 2):
            received = ring_step(j, *received)
        late += halves

        conv_send = conv_far(acts, late)
        cots, conv_send = tied(cots, conv_send)
        conv_got = swap(conv_send, "core")
        sums = back(1, cots, slopes, late)
        crossed[-2], sums, *received = tied(crossed[-2], sums, *received)
        received = ring_step(zs - 2, *received)
        vectors = hop(chip_sum(first_sums + sums), "replica", 1)
        crossed[-1], conv_got, vectors, *received = tied(crossed[-1], conv_got, vectors, *received)
        last, behind = ring_step(zs - 1, *received)
        block = conv_own(conv_got, [conv_first_own, conv_first_got, order], late)
        vectors = hop(vectors, "z", 1)
        last, block, vectors = tied(last, block, vectors)
        total = add(*behind, last)
        across = swap(total, "replica")
        ours, others = jnp.where(same, total, across), jnp.where(same, across, total)
        aside = swap(others, "core")
        new_kernel = call(
            partial(finish_kernel, cols), jax.ShapeDtypeStruct(shard.shape, F32),
            [SMEM_SPEC] * 2 + [VMEM_SPEC] * 5, [], 8, flops // 16,
        )(dev, step, shard, mine, theirs, ours, aside)
        vectors = hop(vectors, "y", 1)
        reach = 2
        while reach < zs:
            vectors = hop(vectors, "z", reach)
            reach *= 2
        new_v = 0.5 * vectors
    else:
        late = [lax.all_gather(unit, NODE, axis=0, tiled=True)]
        cots, slope, slope_x = slopes_of(stats)
        sums = back(0, cots, [slope, slope_x], late)
        vectors = chip_sum(sums)
        block = conv_own(swap(conv_far(acts, late), "core"), [], late)
        terms = pieces[0].reshape(2 * zs, 2, part, cols.lead)
        summed = lax.psum_scatter(terms, NODE, scatter_dimension=0, tiled=False)
        ours = lax.dynamic_index_in_dim(summed, core, 0, keepdims=False)
        got = swap(lax.dynamic_index_in_dim(summed, 1 - core, 0, keepdims=False), "core")
        left, right = jnp.where(lower, ours, got), jnp.where(lower, got, ours)
        kernel_grad = jnp.concatenate([left, right[:, cols.both:]], axis=1).astype(F32)
        level = step[0] % (replicas.bit_length() - 1)
        rate = LR_KERNEL * (1.0 - (step[0] % 1000).astype(F32) / 2000.0)
        stepped = shard - (scale * rate) * kernel_grad
        new_kernel = 0.5 * (stepped + from_peer(level, stepped.astype(BF16)).astype(F32))
        stepped_v = lax.psum(vectors, NODE)
        new_v = 0.5 * (stepped_v + from_peer(level, stepped_v))

    return (
        block[None],
        new_kernel[None],
        new_v[0][None],
        new_v[1][None],
        new_v[2][None],
    )


def solution(mesh):
    replicas, shards = mesh.shape["replica"], mesh.shape["shard"]
    split = Mesh(mesh.devices.reshape(replicas, shards // 4, 2, 2), ("replica", "z", "y", "core"))
    shard = ("z", "y", "core")
    return jax.shard_map(
        per_device,
        mesh=split,
        in_specs=(
            P("replica", shard, None, None),
            P("replica", shard, None, None),
            P("replica", shard, None),
            P("replica", None),
            P("replica", None),
            P("replica", None),
            P(),
        ),
        out_specs=(
            P("replica", shard, None, None),
            P("replica", shard, None),
            P("replica", None),
            P("replica", None),
            P("replica", None),
        ),
        check_vma=False,
    )
```

```python
from functools import partial

import jax
import jax.numpy as jnp
import numpy as np
from jax import lax
from jax.experimental import pallas as pl
from jax.experimental.pallas import tpu as pltpu
from jax.sharding import Mesh, PartitionSpec as P

GROUPS = 32
EPS = 1e-05
LR_KERNEL = 0.1
LR_VECTOR = 0.01
LANES = 128
BF16 = jnp.bfloat16
F32 = jnp.float32

SMEM_SPEC = pl.BlockSpec(memory_space=pltpu.SMEM)
VMEM_SPEC = pl.BlockSpec(memory_space=pltpu.VMEM)


class Columns:
    def __init__(self, chans):
        tiles = 9 * chans // LANES
        self.total = 9 * chans
        self.lead = (tiles + 1) // 2 * LANES
        self.start = self.total - self.lead
        self.both = 2 * self.lead - self.total
        self.mid = self.lead - 4 * chans
        self.mid_start = chans - self.mid

    def pair(self, core, k, chans):
        first = jnp.where(core == 0, 2 * k, 5 + 2 * k)
        place = jnp.where(core == 0, 2 * k * chans, self.mid + 2 * k * chans)
        return (first, first + 1), pl.multiple_of(place, LANES)

    def middle(self, core, chans):
        place = jnp.where(core == 0, 4 * chans, 0)
        channel = jnp.where(core == 0, 0, self.mid_start)
        return pl.multiple_of(place, LANES), pl.multiple_of(channel, LANES)


def fill_shifts(shifts, row, values):
    width = values.shape[0]
    at = lax.broadcasted_iota(jnp.int32, values.shape, 0)
    left = jnp.where(at == 0, 0.0, pltpu.roll(values, 1, 0))
    right = jnp.where(at == width - 1, 0.0, pltpu.roll(values, width - 1, 0))
    shifts[0, row] = left.astype(BF16)
    shifts[1, row] = values.astype(BF16)
    shifts[2, row] = right.astype(BF16)


def clear_edges(shifts):
    zero = jnp.zeros(shifts.shape[2:], shifts.dtype)
    for b in range(3):
        shifts[b, 0] = zero
        shifts[b, shifts.shape[1] - 1] = zero


def act_kernel(order, dev, table, lat_own, lat_far, cot_own, cot_far, gain, shift,
               stats, acts, cot_t, cot_f):
    me = dev[0]
    core = me % 2
    half, width, chans = lat_own.shape
    cells = 2 * half * width
    group_width = chans // GROUPS
    own_at = core * half
    far_at = half - own_at
    clear_edges(acts)

    def add_row(i, sums):
        total, square = sums
        a = lat_own[i].astype(F32)
        b = lat_far[i].astype(F32)
        return total + (a + b), square + (a * a + b * b)

    zero = jnp.zeros((width, chans), F32)
    total, square = lax.fori_loop(0, half, add_row, (zero, zero))
    sums = jnp.concatenate(
        [jnp.sum(total, axis=0, keepdims=True), jnp.sum(square, axis=0, keepdims=True),
         jnp.zeros((6, chans), F32)], axis=0
    )
    first = lax.broadcasted_iota(jnp.int32, (chans, LANES), 0)
    start = lax.broadcasted_iota(jnp.int32, (chans, LANES), 1) * group_width
    member = jnp.where((first >= start) & (first < start + group_width), 1.0, 0.0)
    exact = partial(lax.dot_general, precision=lax.Precision.HIGHEST, preferred_element_type=F32)
    sums = exact(sums, member, (((1,), (0,)), ((), ()))) / (cells * group_width)
    sums = exact(sums, member, (((1,), (1,)), ((), ())))
    mean = sums[0:1]
    rstd = lax.rsqrt(sums[1:2] - mean * mean + EPS)
    stats[0:1] = mean
    stats[1:2] = rstd
    gain_v, shift_v = gain[...], shift[...]

    def act_rows(i, _):
        for ref, base in ((lat_own, own_at), (lat_far, far_at)):
            pre = gain_v * ((ref[i].astype(F32) - mean) * rstd) + shift_v
            fill_shifts(acts, base + i + 1, pre * (0.5 + 0.5 * jnp.tanh(0.5 * pre)))
        return 0

    lax.fori_loop(0, half, act_rows, 0)

    chunk = LANES // width
    for ref, base in ((cot_own, own_at), (cot_far, far_at)):
        for i in range(half // chunk):
            piece = ref[i * chunk:(i + 1) * chunk].reshape(LANES, chans).astype(F32)
            place = pl.multiple_of(base * width + i * LANES, LANES)
            if order is None:
                cot_t[:, pl.ds(place, LANES)] = piece.T.astype(BF16)
            else:
                cot_f[:, pl.ds(place, LANES)] = piece.T
    if order is not None:
        first_at, part, count = order
        for q in range(count // 2):
            pair = [
                cot_f[pl.ds(pl.multiple_of(table[me, first_at + 2 * q + i], 8), part)]
                for i in range(2)
            ]
            cot_t[2 * q * part:(2 * q + 2) * part] = jnp.concatenate(pair).astype(BF16)


def grad_kernel(cols, dev, acts, cot_t, *pieces):
    core = dev[0] % 2
    rows, width, chans = acts.shape[1] - 2, acts.shape[2], acts.shape[3]
    cells = rows * width

    def emit(window, place, wide):
        value = jnp.dot(cot_t[...], window, preferred_element_type=F32)
        at = 0
        for piece in pieces:
            piece[:, pl.ds(place, wide)] = value[at:at + piece.shape[0]].astype(BF16)
            at += piece.shape[0]

    def two_taps(k, _):
        taps, place = cols.pair(core, k, chans)
        windows = [acts[t % 3, pl.ds(t // 3, rows)].reshape(cells, chans) for t in taps]
        emit(jnp.concatenate(windows, axis=1), place, 2 * chans)
        return 0

    lax.fori_loop(0, 2, two_taps, 0)
    place, channel = cols.middle(core, chans)
    emit(acts[1, 1:rows + 1, :, pl.ds(channel, cols.mid)].reshape(cells, cols.mid), place, cols.mid)


class Stages:
    def __init__(self, counts, rows):
        self.rows = rows
        self.counts = counts
        self.widths = [-(-n * rows // LANES) * LANES for n in counts]
        self.starts = [sum(self.widths[:i]) for i in range(len(counts))]
        self.width = sum(self.widths)

    def lanes(self, stage):
        return slice(self.starts[stage], self.starts[stage] + self.widths[stage])

    def columns(self, stage, blocks, place, wide):
        parts = [ref[:, pl.ds(place, wide)] for ref in blocks]
        if len(parts) == self.counts[stage] + 1:
            parts[-2:] = [jnp.concatenate(parts[-2:])]
        spare = self.widths[stage] - self.counts[stage] * self.rows
        if spare:
            parts.append(jnp.zeros((spare, wide), BF16))
        return jnp.concatenate(parts) if len(parts) > 1 else parts[0]

    def order(self, me, table, order, chans):
        lane = lax.broadcasted_iota(jnp.int32, (1, self.width), 1)
        source = jnp.full((1, self.width), -1, jnp.int32)
        at = 0
        for start, count in zip(self.starts, self.counts):
            for i in range(count):
                first = start + i * self.rows
                inside = (lane >= first) & (lane < first + self.rows)
                source = jnp.where(inside, table[me, at] * self.rows + lane - first, source)
                at += 1
        channel = lax.broadcasted_iota(jnp.int32, (chans, self.width), 0)
        order[...] = jnp.where(channel == source, 1.0, 0.0).astype(BF16)


def slope_kernel(stages, dev, table, stats, gain, shift, lat_own, lat_far, cot_own, cot_far,
                 cots, slope, slope_x, *refs):
    me = dev[0]
    core = me % 2
    half, width, chans = lat_own.shape
    clear_edges(cots)
    mean, rstd = stats[0:1], stats[1:2]
    gain_v, shift_v = gain[...], shift[...]
    far_at = half - core * half
    if len(stages.counts) > 1:
        order, placed = refs
        stages.order(me, table, order, chans)
        for ref, base in ((cot_own, core * half), (cot_far, far_at)):
            value = jnp.dot(ref[...].reshape(half * width, chans), order[...], preferred_element_type=F32)
            placed[pl.ds(base, half)] = value.reshape(half, width, stages.width)

    def one_row(i, _):
        for lat, cot, base in ((lat_own, cot_own, core * half), (lat_far, cot_far, far_at)):
            value = placed[base + i] if len(stages.counts) > 1 else cot[i].astype(F32)
            fill_shifts(cots, base + i + 1, value)
            xhat = (lat[i].astype(F32) - mean) * rstd
            pre = gain_v * xhat + shift_v
            sig = 0.5 + 0.5 * jnp.tanh(0.5 * pre)
            value = sig * (1.0 + pre * (1.0 - sig))
            slope[base + i] = value.astype(BF16)
            slope_x[base + i] = (value * xhat).astype(BF16)
        return 0

    lax.fori_loop(0, half, one_row, 0)


def conv_sum(cols, stages, stage, core, first, half, acts, blocks, total):
    width, chans = acts.shape[2:]
    cells = half * width
    nt = (((1,), (1,)), ((), ()))
    place, channel = cols.middle(core, chans)
    window = acts[1, pl.ds(first + 1, half), :, pl.ds(channel, cols.mid)].reshape(cells, cols.mid)
    lane = lax.broadcasted_iota(jnp.int32, window.shape, 1)
    window = jnp.where((core == 1) & (lane < cols.both), jnp.zeros_like(window), window)
    kernel = stages.columns(stage, blocks, place, cols.mid)
    total[...] = lax.dot_general(window, kernel, nt, preferred_element_type=F32)

    def two_taps(k, _):
        taps, place = cols.pair(core, k, chans)
        windows = [acts[t % 3, pl.ds(first + t // 3, half)].reshape(cells, chans) for t in taps]
        kernel = stages.columns(stage, blocks, place, 2 * chans)
        total[...] += lax.dot_general(
            jnp.concatenate(windows, axis=1), kernel, nt, preferred_element_type=F32
        )
        return 0

    lax.fori_loop(0, 2, two_taps, 0)


def conv_both_kernel(cols, stages, stage, dev, acts, *refs):
    blocks, (own, far, total) = refs[:-3], refs[-3:]
    core = dev[0] % 2
    rows = acts.shape[1] - 2
    conv_sum(cols, stages, stage, core, 0, rows, acts, blocks, total)
    half = own.shape[0]
    own[...] = total[pl.ds(pl.multiple_of(core * half, half), half)]
    far[...] = total[pl.ds(pl.multiple_of((1 - core) * half, half), half)].astype(BF16)


def conv_far_kernel(cols, stages, stage, dev, acts, *refs):
    blocks, (far, total) = refs[:-2], refs[-2:]
    core = dev[0] % 2
    half = (acts.shape[1] - 2) // 2
    conv_sum(cols, stages, stage, core, (1 - core) * half, half, acts, blocks, total)
    far[...] = total[...].astype(BF16)


def conv_own_kernel(cols, stages, dev, acts, got, latent, bias, *refs):
    core = dev[0] % 2
    half, width, chans = latent.shape
    scale = cols.total ** (-0.5)
    stage = len(stages.counts) - 1
    before = 3 * stage
    blocks, (block, total) = refs[before:-2], refs[-2:]
    conv_sum(cols, stages, stage, core, core * half, half, acts, blocks, total)
    conv = total[...] + got[...].astype(F32)
    if stage:
        first_own, first_got, order = refs[:before]
        conv = jnp.concatenate([first_own[...] + first_got[...].astype(F32), conv], axis=1)
        high = conv.astype(BF16)
        low = (conv - high.astype(F32)).astype(BF16)
        nt = (((1,), (1,)), ((), ()))
        conv = sum(
            lax.dot_general(value, order[...], nt, preferred_element_type=F32) for value in (low, high)
        )
    conv = scale * conv + bias[...]
    block[...] = (conv.reshape(half, width, chans) + latent[...].astype(F32)).astype(BF16)


def back_kernel(cols, stages, stage, dev, cots, slope, slope_x, *refs):
    blocks, (sums, total) = refs[:-2], refs[-2:]
    core = dev[0] % 2
    rows, width = cots.shape[1] - 2, cots.shape[2]
    cells, chans = total.shape
    lanes = stages.lanes(stage)

    def taps_from(first, place, count):
        windows, kernels = [], []
        for i in range(count):
            tap = first + i
            window = cots[2 - tap % 3, pl.ds(2 - tap // 3, rows), :, lanes]
            windows.append(window.reshape(cells, stages.widths[stage]))
            kernels.append(stages.columns(stage, blocks, pl.multiple_of(place + i * chans, LANES), chans))
        return jnp.dot(
            jnp.concatenate(windows, axis=1), jnp.concatenate(kernels), preferred_element_type=F32
        )

    if stages.widths[stage] * 4 <= 2 * chans:
        taps, place = cols.pair(core, 0, chans)
        total[...] = taps_from(taps[0], place, 4)
    else:
        total[...] = jnp.zeros_like(total)

        def two_taps(k, _):
            taps, place = cols.pair(core, k, chans)
            total[...] += taps_from(taps[0], place, 2)
            return 0

        lax.fori_loop(0, 2, two_taps, 0)

    place, channel = cols.middle(core, chans)
    window = cots[1, 1:rows + 1, :, lanes].reshape(cells, stages.widths[stage])
    kernel = stages.columns(stage, blocks, place, cols.mid)
    value = jnp.dot(window, kernel, preferred_element_type=F32)
    lane = lax.broadcasted_iota(jnp.int32, value.shape, 1)
    total[:, pl.ds(channel, cols.mid)] += jnp.where((core == 1) & (lane < cols.both), 0.0, value)

    def add_row(i, carry):
        gains, shifts = carry
        value = total[pl.ds(pl.multiple_of(i * width, width), width)]
        return gains + value * slope_x[i].astype(F32), shifts + value * slope[i].astype(F32)

    zero = jnp.zeros((width, chans), F32)
    gains, shifts = lax.fori_loop(0, rows, add_row, (zero, zero))
    scale = cols.total ** (-0.5)
    sums[0:1] = scale * jnp.sum(gains, axis=0, keepdims=True)
    sums[1:2] = scale * jnp.sum(shifts, axis=0, keepdims=True)


def finish_kernel(cols, dev, step, shard, mine, theirs, ours, aside, out):
    lower = dev[0] % 2 == 0
    rate = LR_KERNEL * (1.0 - (step[0] % 1000).astype(F32) / 2000.0)
    factor = 0.5 * cols.total ** (-0.5) * rate
    here = 0.5 * mine[...].astype(F32) - factor * ours[...].astype(F32)
    there = 0.5 * theirs[...].astype(F32) - factor * aside[...].astype(F32)
    left, right = jnp.where(lower, here, there), jnp.where(lower, there, here)
    out[:, :cols.lead] = 0.5 * shard[:, :cols.lead] + left
    out[:, cols.lead:] = 0.5 * shard[:, cols.lead:] + right[:, cols.both:]


NODE = ("z", "y")


def swap(value, axis):
    return lax.ppermute(value, axis, [(0, 1), (1, 0)])


def from_peer(level, value):
    count = lax.axis_size("replica")
    levels = count.bit_length() - 1
    moves = [[(s, (s + (1 << k)) % count) for s in range(count)] for k in range(levels)]
    if levels == 1:
        return lax.ppermute(value, "replica", moves[0])
    return lax.switch(level, [lambda v, m=m: lax.ppermute(v, "replica", m) for m in moves], value)


class Ring:
    def __init__(self, zs):
        self.count = 2 * zs
        self.reach = zs
        self.nodes = [2 * z for z in range(zs)] + [2 * z + 1 for z in reversed(range(zs))]
        ahead = list(zip(self.nodes, self.nodes[1:] + self.nodes[:1]))
        self.ahead = ahead
        self.behind = [(b, a) for a, b in ahead]

    def node(self, at, offset):
        return self.nodes[(at + offset) % self.count]

    def up(self, value):
        return lax.ppermute(value, NODE, self.ahead)

    def down(self, value):
        return lax.ppermute(value, NODE, self.behind)

    def table(self, part):
        rows = np.zeros((2, self.count, 2, 3 * self.count), np.int32)
        for replica in range(2):
            for at, node in enumerate(self.nodes):
                line = [node]
                for k in range(1, self.reach + 1):
                    line.append(self.node(at, -k))
                    if k < self.reach:
                        line.append(self.node(at, k))
                for which in (replica, 1 - replica):
                    for j in range(self.reach):
                        targets = [self.node(at, self.reach - j), self.node(at, j + 1 - self.reach)]
                        line += [(2 * target + which) * part for target in targets]
                rows[replica, node, :] = line
        return rows.reshape(-1, 3 * self.count)


def hop(value, axis, mask):
    count = lax.axis_size(axis)
    return value + lax.ppermute(value, axis, [(s, s ^ mask) for s in range(count)])


def add(*values):
    total = values[0].astype(F32)
    for value in values[1:]:
        total = total + value.astype(F32)
    return total.astype(BF16)


def tied(*values):
    return lax.optimization_barrier(values)


def per_device(latents, cotangent, kernel, conv_bias, gn_gain, gn_shift, step):
    latent, cotan, shard = latents[0], cotangent[0], kernel[0]
    half, width, chans = latent.shape
    part = shard.shape[0]
    cols = Columns(chans)
    cells = half * width
    zs, replicas = lax.axis_size("z"), lax.axis_size("replica")
    core, z, y, replica = (lax.axis_index(a) for a in ("core", "z", "y", "replica"))
    lower = core == 0
    paired = replicas == 2
    ring = Ring(zs)
    scale = cols.total ** (-0.5)
    params = jnp.concatenate([conv_bias, gn_gain, gn_shift])
    me = ((replica * zs + z) * 2 + y) * 2 + core
    core, lower, same, me = tied(core, lower, replica == core, me)
    dev = me.reshape(1)

    mine = lax.dynamic_slice_in_dim(shard, core * cols.start, cols.lead, 1).astype(BF16)
    theirs = lax.dynamic_slice_in_dim(shard, (1 - core) * cols.start, cols.lead, 1).astype(BF16)
    got = swap(theirs, "core")
    unit = jnp.where(lower, jnp.concatenate([mine, got]), jnp.concatenate([got, mine]))
    lat_far = swap(latent, "core")
    cot_b = cotan.astype(BF16)
    cot_far = swap(cot_b, "core")

    if paired:
        table = jnp.asarray(ring.table(part))
        order = (ring.count, part, 2 * ring.count)
        up1, down1 = ring.up(unit), ring.down(unit)
        peer = swap(mine, "replica"), swap(theirs, "replica")
    else:
        table = jnp.zeros((replicas * zs * 4, 1), jnp.int32)
        order = None

    def call(body, outs, ins, scratch, megabytes, flops):
        return pl.pallas_call(
            body,
            out_shape=outs,
            in_specs=ins,
            out_specs=jax.tree.map(lambda _: VMEM_SPEC, outs),
            scratch_shapes=scratch,
            compiler_params=pltpu.CompilerParams(vmem_limit_bytes=megabytes * 2**20),
            cost_estimate=pl.CostEstimate(flops=flops, bytes_accessed=0, transcendentals=0),
        )

    image = (2 * half, width, chans)
    shifted = jax.ShapeDtypeStruct((3, 2 * half + 2, width, chans), BF16)
    flops = 2 * 2 * cells * chans * cols.lead
    stats, acts, cot_t = call(
        partial(act_kernel, order),
        (jax.ShapeDtypeStruct((2, chans), F32), shifted, jax.ShapeDtypeStruct((chans, 2 * cells), BF16)),
        [SMEM_SPEC] * 2 + [VMEM_SPEC] * 6,
        [pltpu.VMEM((chans, 2 * cells), F32)],
        8, flops // 4,
    )(dev, table, latent, lat_far, cot_b, cot_far, gn_gain, gn_shift)
    counts = [zs] + [1] * zs if paired else [2 * zs]
    pieces = call(
        partial(grad_kernel, cols),
        [jax.ShapeDtypeStruct((n * 2 * part, cols.lead), BF16) for n in counts],
        [SMEM_SPEC] + [VMEM_SPEC] * 2,
        [],
        4, flops // 2,
    )(dev, acts, cot_t)
    stages = Stages([2 * zs - 3, 3] if paired else [1], 2 * part if paired else chans)
    staged = paired

    def slopes_of(stats):
        extra = (jax.ShapeDtypeStruct((chans, stages.width), BF16),) if staged else ()
        return call(
            partial(slope_kernel, stages),
            (jax.ShapeDtypeStruct((3, 2 * half + 2, width, stages.width), BF16),
             jax.ShapeDtypeStruct(image, BF16), jax.ShapeDtypeStruct(image, BF16)) + extra,
            [SMEM_SPEC] * 2 + [VMEM_SPEC] * 7,
            [pltpu.VMEM((2 * half, width, stages.width), F32)] if staged else [],
            8, flops // 4,
        )(dev, table, stats, gn_gain, gn_shift, latent, lat_far, cot_b, cot_far)

    def back(stage, cots, slopes, blocks):
        return call(
            partial(back_kernel, cols, stages, stage), jax.ShapeDtypeStruct((2, chans), F32),
            [SMEM_SPEC] + [VMEM_SPEC] * (3 + len(blocks)),
            [pltpu.VMEM((2 * cells, chans), F32)], 8, flops // 4,
        )(dev, cots, *slopes, *blocks)

    def conv_first(blocks):
        wide = stages.widths[0]
        return call(
            partial(conv_both_kernel, cols, stages, 0),
            (jax.ShapeDtypeStruct((cells, wide), F32), jax.ShapeDtypeStruct((cells, wide), BF16)),
            [SMEM_SPEC] + [VMEM_SPEC] * (1 + len(blocks)),
            [pltpu.VMEM((2 * cells, wide), F32)], 6, flops // 4,
        )(dev, acts, *blocks)

    def conv_far(acts, blocks):
        wide = stages.widths[-1]
        return call(
            partial(conv_far_kernel, cols, stages, len(stages.counts) - 1),
            jax.ShapeDtypeStruct((cells, wide), BF16),
            [SMEM_SPEC] + [VMEM_SPEC] * (1 + len(blocks)),
            [pltpu.VMEM((cells, wide), F32)], 4, flops // 8,
        )(dev, acts, *blocks)

    def conv_own(got, earlier, blocks):
        return call(
            partial(conv_own_kernel, cols, stages), jax.ShapeDtypeStruct((half, width, chans), BF16),
            [SMEM_SPEC] + [VMEM_SPEC] * (4 + len(earlier) + len(blocks)),
            [pltpu.VMEM((cells, stages.widths[-1]), F32)], 8, flops // 4,
        )(dev, acts, got, latent, conv_bias, *earlier, *blocks)

    def chip_sum(sums):
        vectors = jnp.concatenate([jnp.sum(cotan, axis=(0, 1))[None], sums])
        vectors = params / (4 * zs) - LR_VECTOR * vectors
        return vectors + swap(vectors, "core")

    if paired:
        kept, *sent = pieces
        up, down, sent[0], mine, theirs = tied(up1, down1, sent[0], *peer)
        blocks = [unit, up, down]
        crossed = [swap(piece, "replica") for piece in sent]
        up, down = ring.up(up), ring.down(down)
        up, down, cots, *slopes, order = tied(up, down, *slopes_of(stats))
        blocks += [up, down]

        def ring_step(j, *received):
            parts = kept[2 * j * part:(2 * j + 2) * part], crossed[j]
            ahead, behind = (tuple(x[half] for x in parts) for half in (slice(part), slice(part, None)))
            up_sum = ring.up(add(*ahead, *received[:1]))
            if j < zs - 1:
                return up_sum, ring.down(add(*behind, *received[1:]))
            return up_sum, behind + tuple(received[1:])

        up, down = ring.up(up), ring.down(down)
        conv_first_own, conv_send = conv_first(blocks)
        crossed[0], conv_send = tied(crossed[0], conv_send)
        received = ring_step(0)
        cots, conv_send = tied(cots, conv_send)
        first_sums = back(0, cots, slopes, blocks)
        up, down, first_sums, crossed[1] = tied(up, down, first_sums, crossed[1])
        late = [up, down]

        halves = ring.up(up[:part]), ring.down(down[part:])
        conv_send, *received = tied(conv_send, *received)
        conv_first_got = swap(conv_send, "core")
        for j in range(1, zs - 2):
            received = ring_step(j, *received)
        late += halves

        conv_send = conv_far(acts, late)
        cots, conv_send = tied(cots, conv_send)
        conv_got = swap(conv_send, "core")
        sums = back(1, cots, slopes, late)
        crossed[-2], sums, *received = tied(crossed[-2], sums, *received)
        received = ring_step(zs - 2, *received)
        vectors = hop(chip_sum(first_sums + sums), "replica", 1)
        crossed[-1], conv_got, vectors, *received = tied(crossed[-1], conv_got, vectors, *received)
        last, behind = ring_step(zs - 1, *received)
        block = conv_own(conv_got, [conv_first_own, conv_first_got, order], late)
        vectors = hop(vectors, "z", 1)
        last, block, vectors = tied(last, block, vectors)
        total = add(*behind, last)
        across = swap(total, "replica")
        ours, others = jnp.where(same, total, across), jnp.where(same, across, total)
        aside = swap(others, "core")
        new_kernel = call(
            partial(finish_kernel, cols), jax.ShapeDtypeStruct(shard.shape, F32),
            [SMEM_SPEC] * 2 + [VMEM_SPEC] * 5, [], 8, flops // 16,
        )(dev, step, shard, mine, theirs, ours, aside)
        reach = 2
        while reach < zs:
            vectors = hop(vectors, "z", reach)
            reach *= 2
        vectors = hop(vectors, "y", 1)
        new_v = 0.5 * vectors
    else:
        late = [lax.all_gather(unit, NODE, axis=0, tiled=True)]
        cots, slope, slope_x = slopes_of(stats)
        sums = back(0, cots, [slope, slope_x], late)
        vectors = chip_sum(sums)
        block = conv_own(swap(conv_far(acts, late), "core"), [], late)
        terms = pieces[0].reshape(2 * zs, 2, part, cols.lead)
        summed = lax.psum_scatter(terms, NODE, scatter_dimension=0, tiled=False)
        ours = lax.dynamic_index_in_dim(summed, core, 0, keepdims=False)
        got = swap(lax.dynamic_index_in_dim(summed, 1 - core, 0, keepdims=False), "core")
        left, right = jnp.where(lower, ours, got), jnp.where(lower, got, ours)
        kernel_grad = jnp.concatenate([left, right[:, cols.both:]], axis=1).astype(F32)
        level = step[0] % (replicas.bit_length() - 1)
        rate = LR_KERNEL * (1.0 - (step[0] % 1000).astype(F32) / 2000.0)
        stepped = shard - (scale * rate) * kernel_grad
        new_kernel = 0.5 * (stepped + from_peer(level, stepped.astype(BF16)).astype(F32))
        stepped_v = lax.psum(vectors, NODE)
        new_v = 0.5 * (stepped_v + from_peer(level, stepped_v))

    return (
        block[None],
        new_kernel[None],
        new_v[0][None],
        new_v[1][None],
        new_v[2][None],
    )


def solution(mesh):
    replicas, shards = mesh.shape["replica"], mesh.shape["shard"]
    split = Mesh(mesh.devices.reshape(replicas, shards // 4, 2, 2), ("replica", "z", "y", "core"))
    shard = ("z", "y", "core")
    return jax.shard_map(
        per_device,
        mesh=split,
        in_specs=(
            P("replica", shard, None, None),
            P("replica", shard, None, None),
            P("replica", shard, None),
            P("replica", None),
            P("replica", None),
            P("replica", None),
            P(),
        ),
        out_specs=(
            P("replica", shard, None, None),
            P("replica", shard, None),
            P("replica", None),
            P("replica", None),
            P("replica", None),
        ),
        check_vma=False,
    )
```
